32 devices in a mesh: rows: 4 (over x, core), batch: 8 (over z, y).
Axes of the slice: x: 2, y: 2, z: 4, core: 2. Of those that a mesh axis runs over, the one named last changes fastest.
Arguments:
- features: bfloat16 [256, 16, 16, 512], P('batch', 'rows'), may hold values from -6 to 6
- target: float32 [256, 8, 8, 12], P('batch', 'rows'), may hold values from -6 to 6
- mask: int32 [256, 8, 8, 4], P('batch', 'rows'), may hold values 0 or 1
- codes: int32 [256, 8, 8, 4], P('batch', 'rows'), may hold values from 0 to 16383
- conv_w: float32 [4608, 3, 512], P('batch'), may hold values from -0.09375 to 0.09375
- proj_w: float32 [512, 256], P('batch'), may hold values from -0.25 to 0.25
- code_w: float32 [16384, 256], P('batch'), may hold values from -3 to 3
- head_w: float32 [256, 12], P('batch'), may hold values from -0.375 to 0.375
- gains: float32 [4, 512], replicated, may hold values from 0.1 to 1.9
- conv_row: float32 [4608, 3], P('batch'), may hold values from 5.811453e-10 to 9.834766e-08
- conv_col: float32 [3, 512], replicated, may hold values from 5.811453e-10 to 9.834766e-08
- proj_row: float32 [512], P('batch'), may hold values from 1.0728836e-07 to 1.7285347e-06
- proj_col: float32 [256], replicated, may hold values from 1.0728836e-07 to 1.7285347e-06
- code_row: float32 [16384], P('batch'), may hold values from 2.9296875e-12 to 1.4648437e-11
- code_col: float32 [256], replicated, may hold values from 2.9296875e-12 to 1.4648437e-11
- head_row: float32 [256], P('batch'), may hold values from 1.5625e-06 to 2.5e-05
- head_col: float32 [12], replicated, may hold values from 1.5625e-06 to 2.5e-05
- gain_state: float32 [4, 512], replicated, may hold values from 6.8359374e-11 to 3.4179687e-10
Outputs:
- loss: float32 [], replicated
- conv_grad: float32 [4608, 3, 512], P('batch')
- conv_row_new: float32 [4608, 3], P('batch')
- conv_col_new: float32 [3, 512], replicated
- conv_new: float32 [4608, 3, 512], P('batch')
- conv_low: bfloat16 [4608, 3, 512], P('batch')
- proj_grad: float32 [512, 256], P('batch')
- proj_row_new: float32 [512], P('batch')
- proj_col_new: float32 [256], replicated
- proj_new: float32 [512, 256], P('batch')
- proj_low: bfloat16 [512, 256], P('batch')
- code_grad: float32 [16384, 256], P('batch')
- code_row_new: float32 [16384], P('batch')
- code_col_new: float32 [256], replicated
- code_new: float32 [16384, 256], P('batch')
- code_low: bfloat16 [16384, 256], P('batch')
- head_grad: float32 [256, 12], P('batch')
- head_row_new: float32 [256], P('batch')
- head_col_new: float32 [12], replicated
- head_new: float32 [256, 12], P('batch')
- head_low: bfloat16 [256, 12], P('batch')
- gain_grad: float32 [4, 512], replicated
- gain_state_new: float32 [4, 512], replicated
- gains_new: float32 [4, 512], replicated
The draws below stay inside these ranges and needn't reach their ends.
All inputs are finite; a program needn't handle non-finite values. No bound on the sum of `mask` on one device may be relied on, other than what follows from the above.
Results may differ from the reference program's by a relative error of at most 0.0095.
Values may be sent and summed in bfloat16 or wider, within the bound.
A program may use at most 256 MiB of HBM per device.

```python
import math
import jax
import jax.numpy as jnp
from jax import lax

C = 512
GROUPS = 32
LAT = 256
CODES = 16384
DEPTHS = 4
H = 16
W = 16
RGB = 12
CROPS = 256


def kernel_levels():
    return jnp.array([0.08, 0.08, 0.82], jnp.float32) / (LAT * C * C)


def draw_conv_row(key, part):
    key = jax.random.fold_in(key, 11)
    spread = jax.random.uniform(key, (9 * C, 3), jnp.float32, math.log(0.5), math.log(8.0))
    return kernel_levels()[None, :] * jnp.exp(spread)


def draw_conv_col(key, part):
    key = jax.random.fold_in(key, 23)
    spread = jax.random.uniform(key, (3, C), jnp.float32, math.log(0.5), math.log(8.0))
    return kernel_levels()[:, None] * jnp.exp(spread)


def plant(entries, own_key, smallest, largest):
    spot = [jax.random.randint(jax.random.fold_in(own_key, axis), (), 0, length) for axis, length in enumerate(entries.shape)]
    widest = entries.shape.index(max(entries.shape))
    beside = spot[:widest] + [(spot[widest] + 1) % entries.shape[widest]] + spot[widest + 1:]
    return entries.at[tuple(spot)].set(smallest).at[tuple(beside)].set(largest)


def levels(rng, dims, split, least, top_value):
    level, own = 1.0, jax.random.fold_in(rng, 6)
    for position, shards_of in split:
        heights = jnp.exp(jax.random.uniform(jax.random.fold_in(own, position), (shards_of,), jnp.float32, least / len(split), top_value / len(split)))
        level = level * jnp.repeat(heights, dims[position] // shards_of).reshape([-1 if axis == position else 1 for axis in range(len(dims))])
    return level


def normal_values(key, shape, deviation, limit, split=(), held_as=jnp.bfloat16):
    values = deviation * jax.random.normal(key, shape, jnp.float32)
    if split:
        values = values * levels(key, shape, split, -0.22, 0.18)
    return jnp.clip(values, -limit, limit).astype(held_as)


def setup_inputs(seed: int = 0) -> dict:
    key_list = jax.random.split(jax.random.key(seed), 19)
    return {
        "features": normal_values(key_list[0], (CROPS, H, W, C), 1.0, 6.0, ((0, 8), (1, 4))),
        "target": normal_values(key_list[1], (CROPS, H // 2, W // 2, RGB), 1.0, 6.0, ((0, 8), (1, 4)), jnp.float32),
        "mask": plant((jax.random.randint(key_list[2], (CROPS, H // 2, W // 2, 4), 0, 4) < 3).astype(jnp.int32), jax.random.fold_in(key_list[2], 1), 0, 1),
        "codes": plant(jax.random.randint(key_list[3], (CROPS, H // 2, W // 2, DEPTHS), 0, CODES), jax.random.fold_in(key_list[3], 1), 0, CODES - 1).astype(jnp.int32),
        "conv_w": normal_values(key_list[4], (9 * C, 3, C), (9 * C) ** -0.5, 0.09375, ((0, 8),), jnp.float32),
        "proj_w": normal_values(key_list[5], (C, LAT), C ** -0.5, 0.25, ((0, 8),), jnp.float32),
        "code_w": normal_values(key_list[6], (CODES, LAT), 0.5, 3.0, ((0, 8),), jnp.float32),
        "head_w": normal_values(key_list[7], (LAT, RGB), LAT ** -0.5, 0.375, ((0, 8),), jnp.float32),
        "gains": jnp.clip(1.0 + 0.18 * jax.random.normal(key_list[8], (4, C), jnp.float32), 0.1, 1.9),
        "conv_row": draw_conv_row(jax.random.fold_in(key_list[18], 71), 0),
        "conv_col": draw_conv_col(jax.random.fold_in(key_list[18], 71), 0),
        "proj_row": jnp.clip(jnp.exp(math.log(1.7285346984863281e-06) - 2.7795092 * jax.random.uniform(key_list[11], (C,), jnp.float32) ** levels(key_list[11], (C,), ((0, 8),), -0.2, 0.2)), 1.0728835775353218e-07, 1.7285346984863281e-06),
        "proj_col": jnp.clip(jnp.exp(jax.random.uniform(key_list[12], (LAT,), jnp.float32, math.log(1.0728835775353218e-07), math.log(1.7285346984863281e-06))), 1.0728835775353218e-07, 1.7285346984863281e-06),
        "code_row": jnp.clip(jnp.exp(math.log(1.4648436977293677e-11) - 1.60943787 * jax.random.uniform(key_list[13], (CODES,), jnp.float32) ** levels(key_list[13], (CODES,), ((0, 8),), -0.2, 0.2)), 2.929687525562996e-12, 1.4648436977293677e-11),
        "code_col": jnp.clip(jnp.exp(jax.random.uniform(key_list[14], (LAT,), jnp.float32, math.log(2.929687525562996e-12), math.log(1.4648436977293677e-11))), 2.929687525562996e-12, 1.4648436977293677e-11),
        "head_row": jnp.clip(jnp.exp(math.log(2.499999936844688e-05) - 2.7725887 * jax.random.uniform(key_list[15], (LAT,), jnp.float32) ** levels(key_list[15], (LAT,), ((0, 8),), -0.2, 0.2)), 1.56249996052793e-06, 2.499999936844688e-05),
        "head_col": jnp.clip(jnp.exp(jax.random.uniform(key_list[16], (RGB,), jnp.float32, math.log(1.56249996052793e-06), math.log(2.499999936844688e-05))), 1.56249996052793e-06, 2.499999936844688e-05),
        "gain_state": jnp.clip(jnp.exp(jax.random.uniform(key_list[17], (4, C), jnp.float32, math.log(6.835937371718614e-11), math.log(3.417968685859307e-10))), 6.835937371718614e-11, 3.417968685859307e-10),
    }


HIGH = lax.Precision.HIGHEST
BETA = 0.25
RATE = 0.5
EPS_NORM = 1e-05
EPS_SQ = 1e-30

@jax.custom_vjp
def low(v):
    return lax.optimization_barrier(v.astype(jnp.bfloat16)).astype(jnp.float32)

@jax.custom_vjp
def low_back(v):
    return v

def low_keep(v):
    return (low(v), None)

def low_pass(kept, grad):
    return (grad,)

def back_keep(v):
    return (v, None)

def back_low(kept, grad):
    return (low(grad),)
low.defvjp(low_keep, low_pass)
low_back.defvjp(back_keep, back_low)

def silu(v):
    return v * jax.nn.sigmoid(v)

def group_norm(input_tensor, norm_gain, norm_shift):
    crops, height, width, channel_total = input_tensor.shape
    view = input_tensor.reshape(crops, height, width, GROUPS, channel_total // GROUPS)
    mean = lax.optimization_barrier(jnp.mean(view, axis=(1, 2, 4), keepdims=True))
    square = lax.optimization_barrier(jnp.mean(view * view, axis=(1, 2, 4), keepdims=True))
    rstd = lax.rsqrt(square - mean * mean + EPS_NORM)
    return ((view - mean) * rstd).reshape(crops, height, width, channel_total) * norm_gain + norm_shift

def conv_with(act, weight, stride):
    channels = act.shape[-1]
    height, width = (act.shape[1], act.shape[2])
    padded = jnp.pad(act, ((0, 0), (1, 1), (1, 1), (0, 0)))
    total = None
    for place in range(9):
        down, right = divmod(place, 3)
        window = padded[:, down:down + height:stride, right:right + width:stride, :]
        taps = weight[place * channels:(place + 1) * channels, :]
        term = jnp.einsum('bhwc,co->bhwo', window, taps, precision=HIGH)
        total = term if total is None else total + term
    return total

def encode(enc, feats):
    conv_w, proj_w, gains = enc
    conv_l = low(conv_w)
    a_one = low(silu(group_norm(feats, gains[0], gains[1])))
    c_one = low_back(conv_with(a_one, conv_l[:, 0, :], 1))
    a_two = low(silu(group_norm(c_one, gains[2], gains[3])))
    c_two = low_back(conv_with(a_two, conv_l[:, 1, :], 1))
    summed = low(feats + c_two)
    strided = low_back(conv_with(summed, conv_l[:, 2, :], 2))
    return low_back(jnp.einsum('bhwc,cl->bhwl', low(strided), low(proj_w), precision=HIGH))

def decode(latent, code_w, head_w, latent_fixed, cum_fixed, target, mask, codes):
    element_count = CROPS * (H // 2) * (W // 2) * LAT
    picked = low(code_w)[codes]
    cum = jnp.cumsum(picked, axis=3)
    book = jnp.sum((latent_fixed[:, :, :, None, :] - cum) ** 2) / element_count
    commit = BETA * jnp.sum((latent[:, :, :, None, :] - cum_fixed) ** 2) / element_count
    zq = cum_fixed[:, :, :, DEPTHS - 1, :] + (latent - latent_fixed)
    pred = low_back(jnp.einsum('bhwl,lo->bhwo', low(zq), low(head_w), precision=HIGH))
    weight_mask = jnp.repeat(mask.astype(jnp.float32), 3, axis=-1)
    diff = pred - target
    recon = jnp.sum(weight_mask * (jnp.sqrt(diff * diff + 1.0) - 1.0)) / (CROPS * H * W * 3)
    return recon + book + commit

def factored(grad, weight, row, col):
    g_sq = grad * grad + EPS_SQ
    row_new = 0.5 * row + 0.5 * lax.optimization_barrier(jnp.mean(g_sq, axis=1))
    col_new = 0.5 * col + 0.5 * lax.optimization_barrier(jnp.mean(g_sq, axis=0))
    vhat = row_new[:, None] * col_new[None, :] / jnp.mean(row_new)
    update = grad * lax.rsqrt(vhat)
    rms_u = jnp.sqrt(jnp.mean(update * update))
    scale = jnp.sqrt(jnp.mean(weight * weight))
    return (row_new, col_new, weight - RATE * scale * update / jnp.maximum(1.0, rms_u))

def reference(features, target, mask, codes, conv_w, proj_w, code_w, head_w, gains, conv_row, conv_col, proj_row, proj_col, code_row, code_col, head_row, head_col, gain_state):
    params = (conv_w, proj_w, code_w, head_w, gains)
    block = math.gcd(CROPS, 16)
    steps_count = CROPS // block

    def step(carry, index):
        loss_sum, grads = carry

        def piece(a):
            return lax.dynamic_slice_in_dim(a, index * block, block, 0)
        feats = piece(features).astype(jnp.float32)
        codes_now = piece(codes)
        latent, pull_enc = jax.vjp(lambda e: encode(e, feats), (conv_w, proj_w, gains))
        cum_fixed = jnp.cumsum(low(code_w)[codes_now], axis=3)
        value, pull_dec = jax.vjp(lambda l, c, h: decode(l, c, h, latent, cum_fixed, piece(target), piece(mask), codes_now), latent, code_w, head_w)
        d_lat, d_code, d_head = pull_dec(jnp.ones((), value.dtype))
        (d_conv, d_proj, gain_gradient), = pull_enc(d_lat)
        grad_now = (d_conv, d_proj, d_code, d_head, gain_gradient)
        grads = jax.tree.map(lambda a, b: a + b, grads, grad_now)
        return ((loss_sum + value, grads), None)
    zeros = jax.tree.map(jnp.zeros_like, params)
    (loss, grads), _ = lax.scan(step, (jnp.zeros((), conv_w.dtype), zeros), jnp.arange(steps_count, dtype=jnp.int32))
    g_conv, g_proj, g_code, g_head, g_gain = grads
    rows_c, cols_c, news_c = ([], [], [])
    for layer in range(3):
        r_new, c_new, w_new = factored(g_conv[:, layer, :], conv_w[:, layer, :], conv_row[:, layer], conv_col[layer])
        rows_c.append(r_new)
        cols_c.append(c_new)
        news_c.append(w_new)
    conv_row_new = jnp.stack(rows_c, axis=1)
    conv_col_new = jnp.stack(cols_c, axis=0)
    conv_new = jnp.stack(news_c, axis=1)
    proj_row_new, proj_col_new, proj_new = factored(g_proj, proj_w, proj_row, proj_col)
    code_row_new, code_col_new, code_new = factored(g_code, code_w, code_row, code_col)
    head_row_new, head_col_new, head_new = factored(g_head, head_w, head_row, head_col)
    state_new = 0.5 * gain_state + 0.5 * (g_gain * g_gain + EPS_SQ)
    update = g_gain * lax.rsqrt(state_new)
    rms_u = jnp.sqrt(jnp.mean(update * update))
    scale = jnp.sqrt(jnp.mean(gains * gains))
    gains_new = gains - RATE * scale * update / jnp.maximum(1.0, rms_u)
    bf = jnp.bfloat16
    return (loss, g_conv, conv_row_new, conv_col_new, conv_new, conv_new.astype(bf), g_proj, proj_row_new, proj_col_new, proj_new, proj_new.astype(bf), g_code, code_row_new, code_col_new, code_new, code_new.astype(bf), g_head, head_row_new, head_col_new, head_new, head_new.astype(bf), g_gain, state_new, gains_new)
```

```python
import functools

import jax
import jax.numpy as jnp
from jax import lax
from jax.experimental import pallas as pl
from jax.experimental.pallas import tpu as pltpu
from jax.sharding import PartitionSpec as P

GROUPS = 32
BETA = 0.25
RATE = 0.5
EPS_NORM = 1e-05
EPS_SQ = 1e-30
BF = jnp.bfloat16
F32 = jnp.float32
BOTH = ("batch", "rows")
MIB = 1 << 20
VM = pl.BlockSpec(memory_space=pltpu.VMEM)


def group_sum(v):
    lane = lax.broadcasted_iota(jnp.int32, v.shape, 1)
    width = v.shape[1]
    for k in (1, 2, 4, 8):
        up = pltpu.roll(v, k, 1)
        down = pltpu.roll(v, width - k, 1)
        v = v + jnp.where((lane & k) != 0, up, down)
    return v


def moments(v):
    count = v.shape[0] * (v.shape[1] // GROUPS)
    sums = jnp.concatenate(
        [jnp.sum(v, axis=0, keepdims=True), jnp.sum(v * v, axis=0, keepdims=True)]
        + [jnp.zeros((6, v.shape[1]), F32)],
        axis=0,
    )
    sums = group_sum(sums) / count
    mean = sums[0:1]
    return mean, lax.rsqrt(sums[1:2] - mean * mean + EPS_NORM)


def shifted(v, by):
    cells = v.shape[0]
    col = lax.broadcasted_iota(jnp.int32, v.shape, 0) & 15
    edge = 0 if by == 1 else 15
    return jnp.where(col == edge, 0.0, pltpu.roll(v, by % cells, 0))


def fill_three(dst, left, mid, right):
    ch = mid.shape[1]
    for k, v in enumerate((left, mid, right)):
        dst[1:17, :, k * ch : (k + 1) * ch] = v.astype(BF).reshape(16, 16, ch)


def zero_edges(dst):
    dst[0] = jnp.zeros(dst.shape[1:], dst.dtype)
    dst[17] = jnp.zeros(dst.shape[1:], dst.dtype)


def put_lanes(dst, rows, v):
    for k in range(dst.shape[0]):
        dst[k, rows, :] = v[:, k * 128 : (k + 1) * 128]


def get_lanes(src, rows):
    return jnp.concatenate([src[k, rows, :] for k in range(src.shape[0])], axis=1)


def conv_rows(src, w_ref):
    acc = None
    width = src.shape[2]
    for dy in range(3):
        lhs = src[dy : dy + 16].reshape(256, width)
        d = jnp.dot(lhs, w_ref[dy * width : (dy + 1) * width, :], preferred_element_type=F32)
        acc = d if acc is None else acc + d
    return acc


def conv_rows_back(src, w_ref):
    acc = None
    ch = src.shape[2] // 3
    for dy in range(3):
        for dx in range(3):
            lhs = src[2 - dy : 18 - dy, :, dx * ch : (dx + 1) * ch].reshape(256, ch)
            t = (dy * 3 + dx) * ch
            d = lax.dot_general(
                lhs, w_ref[t : t + ch, :], (((1,), (1,)), ((), ())), preferred_element_type=F32
            )
            acc = d if acc is None else acc + d
    return acc


def conv_weight_grad(a_ref, d3_ref, dw_ref):
    crops, cells, ch = a_ref.shape
    nb = 256

    def block(j, carry):
        dx = j // (ch // nb)
        n = j % (ch // nb)
        lane = pl.multiple_of(j * nb, nb)
        for dy in range(3):
            rhs = d3_ref[:, 2 - dy : 18 - dy, :, pl.ds(lane, nb)].reshape(crops * cells, nb)
            d = lax.dot_general(
                a_ref[...].reshape(crops * cells, ch),
                rhs,
                (((0,), (0,)), ((), ())),
                preferred_element_type=F32,
            )
            row = pl.multiple_of((dy * 3 + dx) * ch, ch)
            dw_ref[pl.ds(row, ch), pl.ds(pl.multiple_of(n * nb, nb), nb)] = d.astype(dw_ref.dtype)
        return carry

    lax.fori_loop(0, 3 * (ch // nb), block, 0)


def silu(h):
    return h * jax.nn.sigmoid(h)


def first_conv_kernel(x_ref, gains_ref, w_ref, a_ref, c_ref, a3):
    zero_edges(a3)

    def crop(i, carry):
        v = x_ref[i].astype(F32)
        mean, rstd = moments(v)
        a = silu((v - mean) * rstd * gains_ref[0:1, :] + gains_ref[1:2, :])
        a_ref[i] = a.astype(BF)
        fill_three(a3, shifted(a, 1), a, shifted(a, -1))
        c_ref[i] = conv_rows(a3, w_ref)
        return carry

    lax.fori_loop(0, x_ref.shape[0], crop, 0)


def second_conv_kernel(c_in_ref, x_ref, gains_ref, w_ref, a_ref, l_ref, a3, y32):
    zero_edges(a3)
    ch = x_ref.shape[2]

    def crop(i, carry):
        v = c_in_ref[i]
        mean, rstd = moments(v)
        a = silu((v - mean) * rstd * gains_ref[2:3, :] + gains_ref[3:4, :])
        a_ref[i] = a.astype(BF)
        fill_three(a3, shifted(a, 1), a, shifted(a, -1))
        put_lanes(y32, slice(None), conv_rows(a3, w_ref) + x_ref[i].astype(F32))
        even = get_lanes(y32, pl.ds(0, 128, stride=2))
        odd = get_lanes(y32, pl.ds(1, 128, stride=2))
        cell = lax.broadcasted_iota(jnp.int32, odd.shape, 0) & 7
        before = jnp.where(cell == 0, 0.0, pltpu.roll(odd, 1, 0))
        for dx, part in enumerate((before, even, odd)):
            part = part.reshape(8, 2, 8, ch)
            upper = part[:, 0].reshape(64, ch)
            lower = part[:, 1].reshape(64, ch)
            above = jnp.concatenate([jnp.zeros((8, ch), F32), lower[:56]], axis=0)
            for dy, rows in enumerate((above, upper, lower)):
                lane = (dy * 3 + dx) * ch
                l_ref[pl.ds(pl.multiple_of(i * 64, 64), 64), lane : lane + ch] = rows.astype(BF)
        return carry

    lax.fori_loop(0, x_ref.shape[0], crop, 0)


def down_back_kernel(ds_ref, l_ref, w_ref, dc_ref, dw_ref, y32):
    cells, ch = ds_ref.shape
    crops = cells // 64

    def dot_t(lhs, tap):
        return lax.dot_general(
            lhs.astype(BF),
            w_ref[tap * ch : (tap + 1) * ch, :],
            (((1,), (1,)), ((), ())),
            preferred_element_type=F32,
        )

    def crop(i, carry):
        here = ds_ref[pl.ds(pl.multiple_of(i * 64, 64), 64), :].astype(F32)
        at = lax.broadcasted_iota(jnp.int32, here.shape, 0)

        def next_col(v):
            return jnp.where((at & 7) == 7, 0.0, pltpu.roll(v, 63, 0))

        right = next_col(here)
        under = jnp.concatenate([here[8:], jnp.zeros((8, ch), F32)], axis=0)
        corner = next_col(under)
        ee = dot_t(here, 4)
        eo = dot_t(here, 5) + dot_t(right, 3)
        oe = dot_t(here, 7) + dot_t(under, 1)
        oo = dot_t(here, 8) + dot_t(right, 6) + dot_t(under, 2) + dot_t(corner, 0)

        def both_rows(top, bottom):
            top, bottom = top.reshape(8, 1, 8, ch), bottom.reshape(8, 1, 8, ch)
            return jnp.concatenate([top, bottom], axis=1).reshape(128, ch)

        put_lanes(y32, pl.ds(0, 128, stride=2), both_rows(ee, oe))
        put_lanes(y32, pl.ds(1, 128, stride=2), both_rows(eo, oo))
        dc_ref[i] = get_lanes(y32, slice(None)).astype(BF)
        return carry

    lax.fori_loop(0, crops, crop, 0)

    def block(t, carry):
        lane = pl.multiple_of(t * ch, ch)
        d = lax.dot_general(
            l_ref[:, pl.ds(lane, ch)],
            ds_ref[...],
            (((0,), (0,)), ((), ())),
            preferred_element_type=F32,
        )
        dw_ref[pl.ds(lane, ch), :] = d.astype(BF)
        return carry

    lax.fori_loop(0, 9, block, 0)


def hidden_grad(v, gain, shift, d_act):
    mean, rstd = moments(v)
    vhat = (v - mean) * rstd
    h = vhat * gain + shift
    sig = jax.nn.sigmoid(h)
    return d_act * sig * (1.0 + h * (1.0 - sig)), vhat, rstd


def unit_back_kernel(dc_ref, v_ref, gains_ref, w_ref, a_ref, *outs, row, inner):
    if inner:
        din_ref, dw_ref, dg_ref, d3 = outs
    else:
        dw_ref, dg_ref, d3 = outs
    crops, cells, ch = dc_ref.shape
    dg_ref[...] = jnp.zeros_like(dg_ref)

    def crop(i, carry):
        d = dc_ref[i].astype(F32)
        slot = d3.at[i]
        zero_edges(slot)
        fill_three(slot, shifted(d, -1), d, shifted(d, 1))
        d_act = conv_rows_back(slot, w_ref)
        gain = gains_ref[row : row + 1, :]
        hg, vhat, rstd = hidden_grad(
            v_ref[i].astype(F32), gain, gains_ref[row + 1 : row + 2, :], d_act
        )
        one = jnp.sum(hg * vhat, axis=0, keepdims=True)
        two = jnp.sum(hg, axis=0, keepdims=True)
        dg_ref[0:1, :] += one
        dg_ref[1:2, :] += two
        if inner:
            count = cells * (ch // GROUPS)
            sums = jnp.concatenate([two * gain, one * gain, jnp.zeros((6, ch), F32)], axis=0)
            sums = group_sum(sums) / count
            din_ref[i] = (rstd * (hg * gain - sums[0:1] - vhat * sums[1:2])).astype(BF)
        return carry

    lax.fori_loop(0, crops, crop, 0)
    conv_weight_grad(a_ref, d3, dw_ref)


def kernel_call(body, outs, scratch, flops, *args):
    bytes_accessed = sum(a.size * a.dtype.itemsize for a in args)
    bytes_accessed += sum(o.size * o.dtype.itemsize for o in outs)
    return pl.pallas_call(
        body,
        out_shape=outs,
        in_specs=[VM] * len(args),
        out_specs=[VM] * len(outs),
        scratch_shapes=scratch,
        compiler_params=pltpu.CompilerParams(vmem_limit_bytes=56 * MIB),
        cost_estimate=pl.CostEstimate(
            flops=flops, bytes_accessed=bytes_accessed, transcendentals=0
        ),
    )(*args)


def contract_last(left, right):
    return lax.dot_general(left, right, (((1,), (0,)), ((), ())), preferred_element_type=F32)


def contract_back(left, right):
    return lax.dot_general(left, right, (((1,), (1,)), ((), ())), preferred_element_type=F32)


def contract_rows(left, right):
    return lax.dot_general(left, right, (((0,), (0,)), ((), ())), preferred_element_type=F32)


def row_part(grad, row):
    g_sq = grad * grad + EPS_SQ
    row_new = 0.5 * row + 0.5 * jnp.mean(g_sq, axis=2)
    over_row = jnp.sum(grad * grad / row_new[:, :, None], axis=0)
    return row_new, jnp.sum(g_sq, axis=0), jnp.sum(row_new, axis=0), over_row


def finish(grad, weight, row_new, col, col_sum, row_sum, over_row, wt_sq):
    total = grad.shape[0] * lax.axis_size("batch")
    count = total * grad.shape[2]
    col_new = 0.5 * col + 0.5 * col_sum / total
    row_mean = row_sum / total
    upd_sq = row_mean * jnp.sum(over_row / col_new, axis=1)
    rms_u = jnp.sqrt(upd_sq / count)
    scale = jnp.sqrt(wt_sq / count)
    vhat = row_new[:, :, None] * col_new[None] / row_mean[None, :, None]
    update = grad * lax.rsqrt(vhat)
    new = weight - RATE * (scale / jnp.maximum(1.0, rms_u))[None, :, None] * update
    return col_new, new


def local(
    features,
    target,
    mask,
    codes,
    conv_w,
    proj_w,
    code_w,
    head_w,
    gains,
    conv_row,
    conv_col,
    proj_row,
    proj_col,
    code_row,
    code_col,
    head_row,
    head_col,
    gain_state,
):
    ranks = lax.axis_size("rows")
    shards = lax.axis_size("batch")
    me = lax.axis_index("rows")
    crops_all = features.shape[0] * shards
    ch = features.shape[3]
    lat = proj_w.shape[1]
    rgb = head_w.shape[1]
    height = features.shape[1] * ranks
    width = features.shape[2]

    def whole_crops(v):
        return lax.all_to_all(v, "rows", split_axis=0, concat_axis=1, tiled=True)

    def my_part(v):
        size = v.shape[0] // ranks
        return lax.dynamic_slice_in_dim(v, me * size, size, 0)

    conv_piece = jnp.transpose(my_part(conv_w).astype(BF), (1, 0, 2))
    head_wide = jnp.pad(head_w, ((0, 0), (0, lat - rgb)))
    rest_piece = jnp.concatenate(
        [my_part(code_w).astype(BF), my_part(proj_w).astype(BF), my_part(head_wide).astype(BF)]
    )
    n_code, n_proj, n_head = (v.shape[0] // ranks for v in (code_w, proj_w, head_w))
    w_all = [lax.all_gather(conv_piece[0], BOTH, axis=0, tiled=True)]
    later = lax.all_gather(conv_piece[1:], BOTH, axis=0)
    later = jnp.transpose(later, (1, 0, 2, 3)).reshape(2, -1, ch)
    w_all += [later[0], later[1]]
    rest = lax.all_gather(rest_piece, BOTH, axis=0)
    code_all = rest[:, :n_code].reshape(-1, lat)
    proj_all = rest[:, n_code : n_code + n_proj].reshape(-1, lat)
    head_all = rest[:, n_code + n_proj :, :rgb].reshape(-1, rgb)

    x = whole_crops(features)
    target, mask, codes = whole_crops(target), whole_crops(mask), whole_crops(codes)
    crops = x.shape[0]
    cells = height * width
    x = x.reshape(crops, cells, ch)
    lat_cells = crops * cells // 4
    target = target.reshape(lat_cells, rgb)
    mask = mask.reshape(lat_cells, -1)
    codes = codes.reshape(lat_cells, -1)

    conv_flops = 2 * crops * cells * 9 * ch * ch
    three = pltpu.VMEM((18, 16, 3 * ch), BF)
    fold = pltpu.VMEM((ch // 128, cells, 128), F32)

    def big(dtype):
        return jax.ShapeDtypeStruct((crops, cells, ch), dtype)

    dw_shape = jax.ShapeDtypeStruct((9 * ch, ch), BF)
    dg_shape = jax.ShapeDtypeStruct((2, ch), F32)

    a_one, c_one = kernel_call(
        first_conv_kernel, [big(BF), big(F32)], [three], conv_flops, x, gains, w_all[0]
    )
    a_two, windows = kernel_call(
        second_conv_kernel,
        [big(BF), jax.ShapeDtypeStruct((lat_cells, 9 * ch), BF)],
        [three, fold],
        conv_flops,
        c_one,
        x,
        gains,
        w_all[1],
    )
    s_low = contract_last(windows, w_all[2]).astype(BF)

    lat_count = crops_all * cells // 4 * lat
    pix_count = crops_all * cells * 3
    latent = contract_last(s_low, proj_all)
    picked = code_all[codes].astype(F32)
    cum = jnp.cumsum(picked, axis=1)
    resid = latent[:, None, :] - cum
    quant_part = (1.0 + BETA) * jnp.sum(resid * resid) / lat_count
    zq_low = cum[:, -1].astype(BF)
    pred = contract_last(zq_low, head_all)
    diff = pred - target
    weight_mask = jnp.repeat(mask.astype(F32), 3, axis=-1)
    smooth = jnp.sqrt(diff * diff + 1.0)
    recon_part = jnp.sum(weight_mask * (smooth - 1.0)) / pix_count
    d_pred = (weight_mask * (diff / smooth) / pix_count).astype(BF)
    d_head = contract_rows(zq_low, d_pred)
    d_zq = contract_back(d_pred, head_all)
    d_cum = -2.0 / lat_count * resid
    d_picked = jnp.flip(jnp.cumsum(jnp.flip(d_cum, 1), axis=1), 1)
    d_code = jax.ops.segment_sum(
        d_picked.reshape(-1, lat), codes.reshape(-1), num_segments=code_all.shape[0]
    )
    d_lat_low = (jnp.sum(resid, axis=1) * (2.0 * BETA / lat_count) + d_zq).astype(BF)
    d_proj = contract_rows(s_low, d_lat_low)
    d_s_low = contract_back(d_lat_low, proj_all).astype(BF)

    d_c_two, d_down = kernel_call(
        down_back_kernel,
        [big(BF), dw_shape],
        [fold],
        conv_flops // 2,
        d_s_low,
        windows,
        w_all[2],
    )
    d_three = pltpu.VMEM((crops, 18, 16, 3 * ch), BF)
    d_c_one, d_second, gain_two = kernel_call(
        functools.partial(unit_back_kernel, row=2, inner=True),
        [big(BF), dw_shape, dg_shape],
        [d_three],
        2 * conv_flops,
        d_c_two,
        c_one,
        gains,
        w_all[1],
        a_two,
    )
    d_first, gain_one = kernel_call(
        functools.partial(unit_back_kernel, row=0, inner=False),
        [dw_shape, dg_shape],
        [d_three],
        2 * conv_flops,
        d_c_one,
        x,
        gains,
        w_all[0],
        a_one,
    )
    d_gains = jnp.concatenate([gain_one, gain_two], axis=0)

    devices = ranks * shards

    def to_owner(v):
        return lax.psum_scatter(v, BOTH, scatter_dimension=0, tiled=True)

    def to_rows(v):
        return lax.all_gather(v, "rows", axis=0)

    pad = jnp.pad(d_head, ((0, 0), (0, lat - rgb)))
    rest_grad = jnp.concatenate(
        [v.astype(BF).reshape(devices, -1, lat) for v in (d_code, d_proj, pad)], axis=1
    )
    rest_mine = to_owner(rest_grad.reshape(-1, lat))
    conv_mine = [to_owner(v) for v in (d_first, d_second, d_down)]
    rest_full = to_rows(rest_mine).astype(F32)
    conv_full = to_rows(jnp.stack(conv_mine)).astype(F32)
    g_conv = jnp.transpose(conv_full, (0, 2, 1, 3)).reshape(-1, 3, ch)
    g_code = rest_full[:, :n_code].reshape(-1, lat)
    g_proj = rest_full[:, n_code : n_code + n_proj].reshape(-1, lat)
    g_head = rest_full[:, n_code + n_proj :, :rgb].reshape(-1, rgb)

    mats = [
        (g_conv, conv_w, conv_row, conv_col),
        (g_proj[:, None, :], proj_w[:, None, :], proj_row[:, None], proj_col[None, :]),
        (g_code[:, None, :], code_w[:, None, :], code_row[:, None], code_col[None, :]),
        (g_head[:, None, :], head_w[:, None, :], head_row[:, None], head_col[None, :]),
    ]
    rows_new = [row_part(grad, row) for grad, weight, row, col in mats]
    wt_sq = [jnp.sum(weight * weight, axis=(0, 2)) for grad, weight, row, col in mats]
    sums = lax.psum([r[1:] + (w,) for r, w in zip(rows_new, wt_sq)], "batch")
    loss, g_gain = lax.psum((recon_part + quant_part, d_gains), BOTH)
    done = [
        finish(m[0], m[1], r[0], m[3], *s) for m, r, s in zip(mats, rows_new, sums)
    ]

    state_new = 0.5 * gain_state + 0.5 * (g_gain * g_gain + EPS_SQ)
    update = g_gain * lax.rsqrt(state_new)
    rms_u = jnp.sqrt(jnp.mean(update * update))
    scale = jnp.sqrt(jnp.mean(gains * gains))
    gains_new = gains - RATE * scale * update / jnp.maximum(1.0, rms_u)
    conv_new = done[0][1]
    proj_new, code_new, head_new = (d[1][:, 0, :] for d in done[1:])
    return (
        loss,
        g_conv,
        rows_new[0][0],
        done[0][0],
        conv_new,
        conv_new.astype(BF),
        g_proj,
        rows_new[1][0][:, 0],
        done[1][0][0],
        proj_new,
        proj_new.astype(BF),
        g_code,
        rows_new[2][0][:, 0],
        done[2][0][0],
        code_new,
        code_new.astype(BF),
        g_head,
        rows_new[3][0][:, 0],
        done[3][0][0],
        head_new,
        head_new.astype(BF),
        g_gain,
        state_new,
        gains_new,
    )


def solution(mesh):
    cell = P("batch", "rows", None, None)
    mat, vec = P("batch", None), P("batch")
    placed = (cell,) * 4 + (P("batch", None, None), mat, mat, mat, P())
    placed += (mat, P()) + (vec, P()) * 3 + (P(),)
    conv_outs = (P("batch", None, None), mat, P(), P("batch", None, None), P("batch", None, None))
    mat_outs = (mat, vec, P(), mat, mat)
    return jax.shard_map(
        local,
        mesh=mesh,
        in_specs=placed,
        out_specs=(P(),) + conv_outs + mat_outs * 3 + (P(),) * 3,
        check_vma=False,
    )
```

```python
import functools

import jax
import jax.numpy as jnp
from jax import lax
from jax.experimental import pallas as pl
from jax.experimental.pallas import tpu as pltpu
from jax.sharding import PartitionSpec as P

GROUPS = 32
BETA = 0.25
RATE = 0.5
EPS_NORM = 1e-05
EPS_SQ = 1e-30
BF = jnp.bfloat16
F32 = jnp.float32
BOTH = ("batch", "rows")
MIB = 1 << 20
VM = pl.BlockSpec(memory_space=pltpu.VMEM)
ANY = pl.BlockSpec(memory_space=pl.ANY)
MESH = pl.DeviceIdType.MESH


def group_sum(v):
    lane = lax.broadcasted_iota(jnp.int32, v.shape, 1)
    width = v.shape[1]
    for k in (1, 2, 4, 8):
        up = pltpu.roll(v, k, 1)
        down = pltpu.roll(v, width - k, 1)
        v = v + jnp.where((lane & k) != 0, up, down)
    return v


def moments(v):
    count = v.shape[0] * (v.shape[1] // GROUPS)
    sums = jnp.concatenate(
        [jnp.sum(v, axis=0, keepdims=True), jnp.sum(v * v, axis=0, keepdims=True)]
        + [jnp.zeros((6, v.shape[1]), F32)],
        axis=0,
    )
    sums = group_sum(sums) / count
    mean = sums[0:1]
    return mean, lax.rsqrt(sums[1:2] - mean * mean + EPS_NORM)


def shifted(v, by):
    cells = v.shape[0]
    col = lax.broadcasted_iota(jnp.int32, v.shape, 0) & 15
    edge = 0 if by == 1 else 15
    return jnp.where(col == edge, 0.0, pltpu.roll(v, by % cells, 0))


def fill_three(dst, left, mid, right):
    ch = mid.shape[1]
    for k, v in enumerate((left, mid, right)):
        dst[1:17, :, k * ch : (k + 1) * ch] = v.astype(BF).reshape(16, 16, ch)


def zero_edges(dst):
    dst[0] = jnp.zeros(dst.shape[1:], dst.dtype)
    dst[17] = jnp.zeros(dst.shape[1:], dst.dtype)


def put_lanes(dst, rows, v):
    for k in range(dst.shape[0]):
        dst[k, rows, :] = v[:, k * 128 : (k + 1) * 128]


def get_lanes(src, rows):
    return jnp.concatenate([src[k, rows, :] for k in range(src.shape[0])], axis=1)


def conv_rows(src, w_ref):
    acc = None
    width = src.shape[2]
    for dy in range(3):
        lhs = src[dy : dy + 16].reshape(256, width)
        d = jnp.dot(lhs, w_ref[dy * width : (dy + 1) * width, :], preferred_element_type=F32)
        acc = d if acc is None else acc + d
    return acc


def conv_rows_back(src, w_ref):
    acc = None
    ch = src.shape[2] // 3
    for dy in range(3):
        for dx in range(3):
            lhs = src[2 - dy : 18 - dy, :, dx * ch : (dx + 1) * ch].reshape(256, ch)
            t = (dy * 3 + dx) * ch
            d = lax.dot_general(
                lhs, w_ref[t : t + ch, :], (((1,), (1,)), ((), ())), preferred_element_type=F32
            )
            acc = d if acc is None else acc + d
    return acc


def conv_weight_grad(a_ref, d3_ref, dw_ref):
    crops, cells, ch = a_ref.shape
    nb = 256

    def block(j, carry):
        dx = j // (ch // nb)
        n = j % (ch // nb)
        lane = pl.multiple_of(j * nb, nb)
        for dy in range(3):
            rhs = d3_ref[:, 2 - dy : 18 - dy, :, pl.ds(lane, nb)].reshape(crops * cells, nb)
            d = lax.dot_general(
                a_ref[...].reshape(crops * cells, ch),
                rhs,
                (((0,), (0,)), ((), ())),
                preferred_element_type=F32,
            )
            row = pl.multiple_of((dy * 3 + dx) * ch, ch)
            dw_ref[pl.ds(row, ch), pl.ds(pl.multiple_of(n * nb, nb), nb)] = d.astype(dw_ref.dtype)
        return carry

    lax.fori_loop(0, 3 * (ch // nb), block, 0)


def silu(h):
    return h * jax.nn.sigmoid(h)


def first_crop(v, gains_ref, w_ref, a3):
    mean, rstd = moments(v)
    a = silu((v - mean) * rstd * gains_ref[0:1, :] + gains_ref[1:2, :])
    fill_three(a3, shifted(a, 1), a, shifted(a, -1))
    return a.astype(BF), conv_rows(a3, w_ref)


def second_crop(v, x, gains_ref, w_ref, l_ref, a3, y32):
    ch = v.shape[1]
    mean, rstd = moments(v)
    a = silu((v - mean) * rstd * gains_ref[2:3, :] + gains_ref[3:4, :])
    fill_three(a3, shifted(a, 1), a, shifted(a, -1))
    put_lanes(y32, slice(None), conv_rows(a3, w_ref) + x)
    even = get_lanes(y32, pl.ds(0, 128, stride=2))
    odd = get_lanes(y32, pl.ds(1, 128, stride=2))
    cell = lax.broadcasted_iota(jnp.int32, odd.shape, 0) & 7
    before = jnp.where(cell == 0, 0.0, pltpu.roll(odd, 1, 0))
    for dx, part in enumerate((before, even, odd)):
        part = part.reshape(8, 2, 8, ch)
        upper = part[:, 0].reshape(64, ch)
        lower = part[:, 1].reshape(64, ch)
        above = jnp.concatenate([jnp.zeros((8, ch), F32), lower[:56]], axis=0)
        for dy, rows in enumerate((above, upper, lower)):
            lane = (dy * 3 + dx) * ch
            l_ref[:, lane : lane + ch] = rows.astype(BF)
    return a.astype(BF)


def down_dot(l_ref, w_ref, s_ref):
    ch = s_ref.shape[1]
    nb = 256

    def block(j, carry):
        lane = pl.ds(pl.multiple_of(j * nb, nb), nb)
        d = jnp.dot(l_ref[...], w_ref[:, lane], preferred_element_type=F32)
        s_ref[:, lane] = d.astype(BF)
        return carry

    lax.fori_loop(0, ch // nb, block, 0)


def crop_rows(i):
    return pl.ds(pl.multiple_of(i * 64, 64), 64)


def first_conv_kernel(x_ref, gains_ref, w_ref, a_ref, c_ref, a3):
    zero_edges(a3)

    def crop(i, carry):
        a_ref[i], c_ref[i] = first_crop(x_ref[i].astype(F32), gains_ref, w_ref, a3)
        return carry

    lax.fori_loop(0, x_ref.shape[0], crop, 0)


def second_conv_kernel(c_in_ref, x_ref, gains_ref, w_ref, w_down_ref, a_ref, l_ref, s_ref, a3, y32):
    zero_edges(a3)

    def crop(i, carry):
        a_ref[i] = second_crop(
            c_in_ref[i],
            x_ref[i].astype(F32),
            gains_ref,
            w_ref,
            l_ref.at[crop_rows(i)],
            a3,
            y32,
        )
        return carry

    lax.fori_loop(0, x_ref.shape[0], crop, 0)
    down_dot(l_ref, w_down_ref, s_ref)


def down_back_kernel(ds_ref, l_ref, w_ref, dc_ref, dw_ref, y32):
    cells, ch = ds_ref.shape
    crops = cells // 64

    def dot_t(lhs, tap):
        return lax.dot_general(
            lhs.astype(BF),
            w_ref[tap * ch : (tap + 1) * ch, :],
            (((1,), (1,)), ((), ())),
            preferred_element_type=F32,
        )

    def crop(i, carry):
        here = ds_ref[pl.ds(pl.multiple_of(i * 64, 64), 64), :].astype(F32)
        at = lax.broadcasted_iota(jnp.int32, here.shape, 0)

        def next_col(v):
            return jnp.where((at & 7) == 7, 0.0, pltpu.roll(v, 63, 0))

        right = next_col(here)
        under = jnp.concatenate([here[8:], jnp.zeros((8, ch), F32)], axis=0)
        corner = next_col(under)
        ee = dot_t(here, 4)
        eo = dot_t(here, 5) + dot_t(right, 3)
        oe = dot_t(here, 7) + dot_t(under, 1)
        oo = dot_t(here, 8) + dot_t(right, 6) + dot_t(under, 2) + dot_t(corner, 0)

        def both_rows(top, bottom):
            top, bottom = top.reshape(8, 1, 8, ch), bottom.reshape(8, 1, 8, ch)
            return jnp.concatenate([top, bottom], axis=1).reshape(128, ch)

        put_lanes(y32, pl.ds(0, 128, stride=2), both_rows(ee, oe))
        put_lanes(y32, pl.ds(1, 128, stride=2), both_rows(eo, oo))
        dc_ref[i] = get_lanes(y32, slice(None)).astype(BF)
        return carry

    lax.fori_loop(0, crops, crop, 0)

    def block(t, carry):
        lane = pl.multiple_of(t * ch, ch)
        d = lax.dot_general(
            l_ref[:, pl.ds(lane, ch)],
            ds_ref[...],
            (((0,), (0,)), ((), ())),
            preferred_element_type=F32,
        )
        dw_ref[pl.ds(lane, ch), :] = d.astype(BF)
        return carry

    lax.fori_loop(0, 9, block, 0)


def hidden_grad(v, gain, shift, d_act):
    mean, rstd = moments(v)
    vhat = (v - mean) * rstd
    h = vhat * gain + shift
    sig = jax.nn.sigmoid(h)
    return d_act * sig * (1.0 + h * (1.0 - sig)), vhat, rstd


def unit_back_kernel(dc_ref, v_ref, gains_ref, w_ref, a_ref, *outs, row, inner):
    if inner:
        din_ref, dw_ref, dg_ref, d3 = outs
    else:
        dw_ref, dg_ref, d3 = outs
    crops, cells, ch = dc_ref.shape
    dg_ref[...] = jnp.zeros_like(dg_ref)

    def crop(i, carry):
        d = dc_ref[i].astype(F32)
        slot = d3.at[i]
        zero_edges(slot)
        fill_three(slot, shifted(d, -1), d, shifted(d, 1))
        d_act = conv_rows_back(slot, w_ref)
        gain = gains_ref[row : row + 1, :]
        hg, vhat, rstd = hidden_grad(
            v_ref[i].astype(F32), gain, gains_ref[row + 1 : row + 2, :], d_act
        )
        one = jnp.sum(hg * vhat, axis=0, keepdims=True)
        two = jnp.sum(hg, axis=0, keepdims=True)
        dg_ref[0:1, :] += one
        dg_ref[1:2, :] += two
        if inner:
            count = cells * (ch // GROUPS)
            sums = jnp.concatenate([two * gain, one * gain, jnp.zeros((6, ch), F32)], axis=0)
            sums = group_sum(sums) / count
            din_ref[i] = (rstd * (hg * gain - sums[0:1] - vhat * sums[1:2])).astype(BF)
        return carry

    lax.fori_loop(0, crops, crop, 0)
    conv_weight_grad(a_ref, d3, dw_ref)


def kernel_call(body, outs, scratch, flops, *args):
    bytes_accessed = sum(a.size * a.dtype.itemsize for a in args)
    bytes_accessed += sum(o.size * o.dtype.itemsize for o in outs)
    return pl.pallas_call(
        body,
        out_shape=outs,
        in_specs=[VM] * len(args),
        out_specs=[VM] * len(outs),
        scratch_shapes=scratch,
        compiler_params=pltpu.CompilerParams(vmem_limit_bytes=56 * MIB),
        cost_estimate=pl.CostEstimate(
            flops=flops, bytes_accessed=bytes_accessed, transcendentals=0
        ),
    )(*args)


class Place:
    def __init__(self):
        rows, batch = lax.axis_index("rows"), lax.axis_index("batch")
        self.x, self.c = rows // 2, rows % 2
        self.z, self.y = batch // 2, batch % 2
        self.part = self.c * 2 + self.x

    def at(self, x=None, c=None, z=None, y=None):
        x = self.x if x is None else x
        c = self.c if c is None else c
        z = self.z if z is None else z
        y = self.y if y is None else y
        return {"rows": 2 * x + c, "batch": 2 * z + y}

    def row_peers(self):
        return [
            self.at(c=1 - self.c),
            self.at(x=1 - self.x),
            self.at(x=1 - self.x, c=1 - self.c),
        ]

    def z_peers(self):
        return [self.at(z=(self.z + d) % 4) for d in (1, 2, 3)]

    def greet(self):
        barrier = pltpu.get_barrier_semaphore()
        peers = self.row_peers() + self.z_peers() + [self.at(y=1 - self.y)]
        for peer in peers:
            pl.semaphore_signal(barrier, inc=1, device_id=peer, device_id_type=MESH)
        pl.semaphore_wait(barrier, len(peers))


def remote(src, dst, send, recv, peer):
    return pltpu.make_async_remote_copy(
        src_ref=src, dst_ref=dst, send_sem=send, recv_sem=recv, device_id=peer, device_id_type=MESH
    )


class Gather:
    def __init__(self, place, src, dst, send, recv, by_x):
        self.p, self.src, self.dst, self.send, self.recv = place, src, dst, send, recv
        self.by_x = by_x
        self.steps = 4 if by_x else 3

    def copies(self, step):
        p, src, dst, send, recv = self.p, self.src, self.dst, self.send, self.recv
        if step == 0:
            mine = (p.c, p.x) if self.by_x else (p.c,)
            here, there = src.at[mine], dst.at[(p.z, p.y) + mine]
            out = [
                remote(here, there, send.at[k], recv.at[k], q) for k, q in enumerate(p.z_peers())
            ]
            return out + [pltpu.make_async_copy(here, there, recv.at[6])]
        if step == 1:
            part = dst.at[:, p.y, p.c, p.x] if self.by_x else dst.at[:, p.y, p.c]
            return [remote(part, part, send.at[3], recv.at[3], p.at(y=1 - p.y))]
        if step == 2 and self.by_x:
            part = dst.at[:, :, p.c, p.x]
            return [remote(part, part, send.at[4], recv.at[4], p.at(x=1 - p.x))]
        part = dst.at[:, :, p.c]
        return [remote(part, part, send.at[5], recv.at[5], p.at(c=1 - p.c))]

    def start(self, step):
        for copy in self.copies(step):
            copy.start()

    def arrive(self, step):
        for copy in self.copies(step):
            copy.wait_recv()

    def go(self, step):
        self.arrive(step - 1)
        self.start(step)

    def finish(self):
        for step in range(self.steps):
            for copy in self.copies(step):
                if copy.is_remote:
                    copy.wait_send()


class Reduce:
    steps = 5

    def __init__(self, place, src, out, mine, one, two, three, four, send, recv):
        self.p, self.src, self.out = place, src, out
        self.mine, self.one, self.two, self.three, self.four = mine, one, two, three, four
        self.send, self.recv = send, recv
        first_x = place.c == 0
        self.f = jnp.where(first_x, place.x, place.y)
        self.g = jnp.where(first_x, place.y, place.x)
        self.f_peer = place.at(
            x=jnp.where(first_x, 1 - place.x, place.x), y=jnp.where(first_x, place.y, 1 - place.y)
        )
        self.g_peer = place.at(
            x=jnp.where(first_x, place.x, 1 - place.x), y=jnp.where(first_x, 1 - place.y, place.y)
        )
        self.slot = 2 * self.f + self.g

    @staticmethod
    def scratch(rows, lanes):
        def buf(*lead):
            return pltpu.VMEM(lead + (rows, lanes), BF)

        return [
            buf(4, 4),
            buf(4, 4),
            buf(2, 4),
            buf(4),
            buf(3),
            pltpu.SemaphoreType.DMA((12,)),
            pltpu.SemaphoreType.DMA((16,)),
        ]

    def copies(self, step):
        p, src, mine = self.p, self.src, self.mine
        if step == 0:
            out = []
            for k in range(4):
                y, x = k // 2, k % 2
                there = jnp.where(p.c == 1, 2 * x + y, 2 * y + x)
                here = jnp.where(p.c == 0, 2 * x + y, 2 * y + x)
                out.append(
                    remote(
                        src.at[:, y, 1 - p.c, x],
                        self.one.at[there],
                        self.send.at[k],
                        self.recv.at[k],
                        p.at(c=1 - p.c),
                    )
                )
                out.append(
                    pltpu.make_async_copy(src.at[:, y, p.c, x], mine.at[here], self.recv.at[12 + k])
                )
            return out
        if step == 1:
            return [
                remote(
                    mine.at[pl.ds(2 * (1 - self.f), 2)],
                    self.two,
                    self.send.at[4],
                    self.recv.at[4],
                    self.f_peer,
                )
            ]
        if step == 2:
            return [
                remote(
                    mine.at[2 * self.f + 1 - self.g],
                    self.three,
                    self.send.at[5],
                    self.recv.at[5],
                    self.g_peer,
                )
            ]
        if step == 3:
            return [
                remote(
                    mine.at[self.slot, (p.z + d) % 4],
                    self.four.at[d - 1],
                    self.send.at[5 + d],
                    self.recv.at[5 + d],
                    peer,
                )
                for d, peer in zip((1, 2, 3), p.z_peers())
            ]
        return [
            remote(
                self.out.at[p.part], self.out.at[p.part], self.send.at[9 + k], self.recv.at[9 + k], q
            )
            for k, q in enumerate(p.row_peers())
        ]

    def start(self, step):
        for copy in self.copies(step):
            copy.start()

    def arrive(self, step):
        p, mine = self.p, self.mine
        for copy in self.copies(step):
            copy.wait_recv()

        def add(dst, src):
            dst[...] = (dst[...].astype(F32) + src[...].astype(F32)).astype(BF)

        if step == 0:

            def body(i, carry):
                add(mine.at[i // 4, i % 4], self.one.at[i // 4, i % 4])
                return carry

            lax.fori_loop(0, 16, body, 0)
        if step == 1:

            def body(i, carry):
                add(mine.at[2 * self.f + i // 4, i % 4], self.two.at[i // 4, i % 4])
                return carry

            lax.fori_loop(0, 8, body, 0)
        if step == 2:

            def body(i, carry):
                add(mine.at[self.slot, i], self.three.at[i])
                return carry

            lax.fori_loop(0, 4, body, 0)
        if step == 3:
            total = mine[self.slot, p.z].astype(F32)
            for d in range(3):
                total = total + self.four[d].astype(F32)
            self.out[p.part] = total.astype(BF)

    def end(self):
        for step in range(self.steps):
            for copy in self.copies(step):
                if copy.is_remote:
                    copy.wait_send()


def forward_kernel(
    feat,
    side,
    w_mine,
    rest_mine,
    gains_ref,
    x_out,
    side_out,
    w_out0,
    w_out1,
    w_out2,
    rest_out,
    a_one_ref,
    c_one_ref,
    a_two_ref,
    l_ref,
    s_ref,
    xv,
    wv0,
    wv1,
    wv2,
    a3,
    y32,
    x_send,
    x_recv,
    g_send,
    g_recv,
    o_sem,
):
    place = Place()
    rank = 2 * place.x + place.c
    place.greet()

    def view(ref, lanes):
        n = ref.shape[0] // 32
        return ref.reshape(4, 2, 2, 2, n, ref.shape[1]).at[..., lanes]

    def job(k, src, dst, by_x):
        return Gather(place, src, dst, g_send.at[k], g_recv.at[k], by_x)

    halves = [slice(0, 256), slice(256, 512)]
    w0 = [job(k, w_mine.at[0, ..., h], view(wv0, h), False) for k, h in enumerate(halves)]
    w1 = [job(2 + k, w_mine.at[1, ..., h], view(wv1, h), False) for k, h in enumerate(halves)]
    w2 = [job(4 + k, w_mine.at[2, ..., h], view(wv2, h), True) for k, h in enumerate(halves)]
    ends = [slice(0, 128), slice(128, 256)]
    rest = [
        job(6 + k, rest_mine.at[..., h], rest_out.at[..., h], k == 0) for k, h in enumerate(ends)
    ]

    cells = []
    for src, dst, base in ((feat, xv, 0), (side, side_out, 4)):
        for k, q in enumerate(place.row_peers()):
            to = q["rows"]
            cells.append(
                remote(src.at[to], dst.at[:, rank], x_send.at[base + k], x_recv.at[base + k], q)
            )
        cells.append(pltpu.make_async_copy(src.at[rank], dst.at[:, rank], x_recv.at[base + 3]))

    w0[0].start(0)
    for copy in cells:
        copy.start()
    w0[1].start(0)
    w0[0].go(1)
    w0[1].arrive(0)
    w1[0].start(0)
    rest[0].start(0)
    w0[0].go(2)
    w0[1].start(1)
    w0[0].arrive(2)
    w0[1].go(2)
    zero_edges(a3)
    for copy in cells:
        copy.wait_recv()
    keep_x = pltpu.make_async_copy(xv, x_out, o_sem.at[0])
    keep_x.start()
    w0[1].arrive(2)
    keep_w = [
        pltpu.make_async_copy(v, o, o_sem.at[1 + k])
        for k, (v, o) in enumerate(((wv0, w_out0), (wv1, w_out1), (wv2, w_out2)))
    ]
    keep_w[0].start()
    count, _, _, ch = xv.shape

    def crop_x(i):
        return xv[i].reshape(256, ch).astype(F32)

    def first(i, carry):
        @pl.when(i == 1)
        def _():
            w1[0].go(1)
            w1[1].start(0)

        @pl.when(i == 2)
        def _():
            rest[0].go(1)
            w2[0].start(0)

        @pl.when(i == 5)
        def _():
            w1[0].go(2)
            w1[1].go(1)
            rest[0].go(2)
            w2[1].start(0)

        @pl.when(i == 7)
        def _():
            w2[0].go(1)

        a_one_ref[i], c_one_ref[i] = first_crop(crop_x(i), gains_ref, wv0, a3)
        return carry

    lax.fori_loop(0, count, first, 0)
    w1[0].arrive(2)
    rest[1].start(0)
    w1[1].go(2)
    w1[1].arrive(2)
    keep_w[1].start()

    def second(i, carry):
        @pl.when(i == 0)
        def _():
            w2[0].go(2)
            w2[1].go(1)

        @pl.when(i == 2)
        def _():
            w2[1].go(2)
            rest[0].go(3)

        @pl.when(i == 3)
        def _():
            rest[1].go(1)

        @pl.when(i == 5)
        def _():
            w2[0].go(3)

        @pl.when(i == 7)
        def _():
            w2[1].go(3)

        a_two_ref[i] = second_crop(
            c_one_ref[i], crop_x(i), gains_ref, wv1, l_ref.at[crop_rows(i)], a3, y32
        )
        return carry

    lax.fori_loop(0, count, second, 0)
    rest[1].go(2)
    w2[0].arrive(3)
    w2[1].arrive(3)
    keep_w[2].start()
    down_dot(l_ref, wv2, s_ref)
    for part in (w0, w1, w2):
        for g in part:
            g.finish()
    for g in rest:
        g.arrive(g.steps - 1)
        g.finish()
    for copy in cells:
        if copy.is_remote:
            copy.wait_send()
    keep_x.wait()
    for copy in keep_w:
        copy.wait()


def forward_call(feat, side, w_mine, rest_mine, gains):
    ranks, crops, cells, ch = feat.shape
    lat_cells = crops * ranks * cells // 4
    whole = 8 * w_mine.shape[1] * w_mine.shape[2] * w_mine.shape[3]

    def shape(*dims, dtype=BF):
        return jax.ShapeDtypeStruct(dims, dtype)

    outs = [
        shape(crops, ranks, cells, ch),
        shape(crops, ranks, *side.shape[2:], dtype=F32),
        shape(whole, ch),
        shape(whole, ch),
        shape(whole, ch),
        shape(4, 2, *rest_mine.shape),
        shape(crops, ranks * cells, ch),
        shape(crops, ranks * cells, ch, dtype=F32),
        shape(crops, ranks * cells, ch),
        shape(lat_cells, 9 * ch),
        shape(lat_cells, ch),
    ]
    return pl.pallas_call(
        forward_kernel,
        out_shape=outs,
        in_specs=[ANY] * 4 + [VM],
        out_specs=[ANY] * 6 + [VM] * 5,
        scratch_shapes=[pltpu.VMEM((crops, ranks, cells, ch), BF)]
        + [pltpu.VMEM((whole, ch), BF)] * 3
        + [
            pltpu.VMEM((18, 16, 3 * ch), BF),
            pltpu.VMEM((ch // 128, ranks * cells, 128), F32),
            pltpu.SemaphoreType.DMA((8,)),
            pltpu.SemaphoreType.DMA((8,)),
            pltpu.SemaphoreType.DMA((8, 8)),
            pltpu.SemaphoreType.DMA((8, 8)),
            pltpu.SemaphoreType.DMA((4,)),
        ],
        compiler_params=pltpu.CompilerParams(
            vmem_limit_bytes=58 * MIB, collective_id=2, has_side_effects=True
        ),
        cost_estimate=pl.CostEstimate(
            flops=45 * crops * ranks * cells * ch * ch,
            bytes_accessed=0,
            transcendentals=0,
        ),
    )(feat, side, w_mine, rest_mine, gains)


def reduce_kernel(parts, *refs):
    n_code, n_proj, n_head, rgb = parts
    sources, refs = refs[:4], refs[4:]
    vec_ref, conv_row_ref, rest_row_ref, refs = refs[0], refs[1], refs[2], refs[3:]
    g_refs, refs = refs[:4], refs[4:]
    conv_new_ref, rest_new_ref, tv_ref, refs = refs[0], refs[1], refs[2], refs[3:]
    vec_in, tv_in, s_send, s_recv, refs = refs[0], refs[1], refs[2], refs[3], refs[4:]
    place = Place()
    per = len(refs) // 4
    jobs = [
        Reduce(place, sources[k], g_refs[k], *refs[k * per : (k + 1) * per]) for k in (3, 2, 1, 0)
    ]
    place.greet()
    small = [
        remote(vec_ref, vec_in.at[k], s_send.at[k], s_recv.at[k], q)
        for k, q in enumerate(place.row_peers())
    ]
    for copy in small:
        copy.start()
    for job in jobs:
        job.start(0)
    for tick in range(len(jobs) + Reduce.steps - 1):
        for k, job in enumerate(jobs):
            step = tick - k
            if 0 <= step < Reduce.steps:
                job.arrive(step)
                if step + 1 < Reduce.steps:
                    job.start(step + 1)
    for copy in small:
        copy.wait_recv()
    tv_ref[...] = jnp.zeros_like(tv_ref)
    tv_ref[16:24, :] = vec_ref[...] + vec_in[0] + vec_in[1] + vec_in[2]
    ch = tv_ref.shape[1]

    def fold(g, row, width):
        sq = g * g
        new = 0.5 * row + 0.5 * (jnp.sum(sq, axis=1, keepdims=True) / width + EPS_SQ)
        return (
            new,
            jnp.sum(sq, axis=0, keepdims=True),
            jnp.sum(sq / new, axis=0, keepdims=True),
            jnp.sum(new, axis=0, keepdims=True),
        )

    for j in range(3):
        for k in range(4):
            g = g_refs[j][k].astype(F32)
            new, col, over, total = fold(g, conv_row_ref[j, k], ch)
            conv_new_ref[j, k] = new
            tv_ref[j : j + 1, :] += col
            tv_ref[3 + j : 4 + j, :] += over
            tv_ref[6 + j : 7 + j, :] += total
    half = ch // 2
    spans = ((0, n_code, half), (n_code, n_proj, half), (n_code + n_proj, n_head, rgb))
    for k in range(4):
        for m, (low, size, width) in enumerate(spans):
            g = g_refs[3][k, low : low + size].astype(F32)
            new, col, over, total = fold(g, rest_row_ref[k, low : low + size], width)
            rest_new_ref[k, low : low + size] = new
            tv_ref[9 + m : 10 + m, :half] += col
            tv_ref[9 + m : 10 + m, half:] += over
            tv_ref[12 + m : 13 + m, :half] += total
    sends = [
        remote(tv_ref, tv_in.at[k], s_send.at[3 + k], s_recv.at[3 + k], q)
        for k, q in enumerate(
            (place.at(y=1 - place.y), place.at(z=place.z ^ 1), place.at(z=place.z ^ 2))
        )
    ]
    for k, copy in enumerate(sends):
        copy.start()
        copy.wait()
        tv_ref[...] += tv_in[k]
    for copy in small:
        copy.wait_send()
    for job in jobs:
        job.end()


def reduce_call(sources, vec, conv_row, rest_row, parts):
    scratch = [
        pltpu.VMEM((3,) + vec.shape, F32),
        pltpu.VMEM((3, 24, vec.shape[1]), F32),
        pltpu.SemaphoreType.DMA((6,)),
        pltpu.SemaphoreType.DMA((6,)),
    ]
    for s in sources:
        scratch += Reduce.scratch(*s.shape[-2:])
    outs = [jax.ShapeDtypeStruct((4,) + s.shape[-2:], BF) for s in sources]
    outs += [jax.ShapeDtypeStruct(v.shape, F32) for v in (conv_row, rest_row)]
    outs += [jax.ShapeDtypeStruct((24, vec.shape[1]), F32)]
    return pl.pallas_call(
        functools.partial(reduce_kernel, parts),
        out_shape=outs,
        in_specs=[ANY] * len(sources) + [VM] * 3,
        out_specs=[VM] * len(outs),
        scratch_shapes=scratch,
        compiler_params=pltpu.CompilerParams(
            vmem_limit_bytes=56 * MIB, collective_id=1, has_side_effects=True
        ),
        cost_estimate=pl.CostEstimate(
            flops=0, bytes_accessed=sum(s.size * 2 for s in sources), transcendentals=0
        ),
    )(*sources, vec, conv_row, rest_row)


def contract_last(left, right):
    return lax.dot_general(left, right, (((1,), (0,)), ((), ())), preferred_element_type=F32)


def contract_back(left, right):
    return lax.dot_general(left, right, (((1,), (1,)), ((), ())), preferred_element_type=F32)


def contract_rows(left, right):
    return lax.dot_general(left, right, (((0,), (0,)), ((), ())), preferred_element_type=F32)


def row_part(grad, row):
    g_sq = grad * grad + EPS_SQ
    row_new = 0.5 * row + 0.5 * jnp.mean(g_sq, axis=2)
    over_row = jnp.sum(grad * grad / row_new[:, :, None], axis=0)
    return row_new, jnp.sum(g_sq, axis=0), jnp.sum(row_new, axis=0), over_row


def finish(grad, weight, row_new, col, col_sum, row_sum, over_row, wt_sq):
    total = grad.shape[0] * lax.axis_size("batch")
    count = total * grad.shape[2]
    col_new = 0.5 * col + 0.5 * col_sum / total
    row_mean = row_sum / total
    upd_sq = row_mean * jnp.sum(over_row / col_new, axis=1)
    rms_u = jnp.sqrt(upd_sq / count)
    scale = jnp.sqrt(wt_sq / count)
    vhat = row_new[:, :, None] * col_new[None] / row_mean[None, :, None]
    update = grad * lax.rsqrt(vhat)
    new = weight - RATE * (scale / jnp.maximum(1.0, rms_u))[None, :, None] * update
    return col_new, new


def local(
    features,
    target,
    mask,
    codes,
    conv_w,
    proj_w,
    code_w,
    head_w,
    gains,
    conv_row,
    conv_col,
    proj_row,
    proj_col,
    code_row,
    code_col,
    head_row,
    head_col,
    gain_state,
):
    ranks = lax.axis_size("rows")
    shards = lax.axis_size("batch")
    fast = (ranks, shards) == (4, 8)
    me = lax.axis_index("rows")
    crops_all = features.shape[0] * shards
    ch = features.shape[3]
    lat = proj_w.shape[1]
    rgb = head_w.shape[1]
    height = features.shape[1] * ranks
    width = features.shape[2]

    def whole_crops(v):
        return lax.all_to_all(v, "rows", split_axis=0, concat_axis=1, tiled=True)

    def my_part(v):
        size = v.shape[0] // ranks
        return lax.dynamic_slice_in_dim(v, me * size, size, 0)

    n_code, n_proj, n_head = (v.shape[0] // ranks for v in (code_w, proj_w, head_w))
    head_wide = jnp.pad(head_w, ((0, 0), (0, lat - rgb)))
    crops = features.shape[0] // ranks
    cells = height * width
    lat_cells = crops * cells // 4
    conv_flops = 2 * crops * cells * 9 * ch * ch
    three = pltpu.VMEM((18, 16, 3 * ch), BF)
    fold = pltpu.VMEM((ch // 128, cells, 128), F32)

    def big(dtype):
        return jax.ShapeDtypeStruct((crops, cells, ch), dtype)

    dw_shape = jax.ShapeDtypeStruct((9 * ch, ch), BF)
    dg_shape = jax.ShapeDtypeStruct((2, ch), F32)
    wide_shape = jax.ShapeDtypeStruct((lat_cells, 9 * ch), BF)
    s_shape = jax.ShapeDtypeStruct((lat_cells, ch), BF)

    if fast:
        w_mine = jnp.transpose(conv_w.astype(BF), (1, 0, 2)).reshape(3, 2, 2, -1, ch)
        rest_piece = jnp.concatenate(
            [v.astype(BF).reshape(ranks, -1, lat) for v in (code_w, proj_w, head_wide)]
            + [jnp.zeros((ranks, 16 - n_head, lat), BF)],
            axis=1,
        )
        side = jnp.concatenate(
            [target, mask.astype(F32), codes.astype(F32)], axis=-1
        ).reshape(ranks, crops, -1, rgb + 8)
        out = forward_call(
            features.reshape(ranks, crops, -1, ch),
            side,
            w_mine,
            rest_piece.reshape(2, 2, -1, lat),
            gains,
        )
        x = out[0].reshape(crops, cells, ch)
        w_all = out[2:5]
        rest = out[5].reshape(ranks * shards, -1, lat)
        side = out[1].reshape(lat_cells, -1)
        target, mask, codes = (side[:, :rgb], side[:, rgb : rgb + 4], side[:, rgb + 4 :])
        codes = codes.astype(jnp.int32)
        a_one, c_one, a_two, windows, s_low = out[6:]
    else:

        def whole_crops(v):
            return lax.all_to_all(v, "rows", split_axis=0, concat_axis=1, tiled=True)

        def my_part(v):
            size = v.shape[0] // ranks
            return lax.dynamic_slice_in_dim(v, me * size, size, 0)

        conv_piece = jnp.transpose(my_part(conv_w).astype(BF), (1, 0, 2))
        rest_piece = jnp.concatenate(
            [my_part(code_w).astype(BF), my_part(proj_w).astype(BF), my_part(head_wide).astype(BF)]
        )
        w_all = [lax.all_gather(conv_piece[0], BOTH, axis=0, tiled=True)]
        later = lax.all_gather(conv_piece[1:], BOTH, axis=0)
        later = jnp.transpose(later, (1, 0, 2, 3)).reshape(2, -1, ch)
        w_all += [later[0], later[1]]
        rest = lax.all_gather(rest_piece, BOTH, axis=0)
        x = whole_crops(features).reshape(crops, cells, ch)
        target = whole_crops(target).reshape(lat_cells, rgb)
        mask = whole_crops(mask).reshape(lat_cells, -1)
        codes = whole_crops(codes).reshape(lat_cells, -1)
        a_one, c_one = kernel_call(
            first_conv_kernel, [big(BF), big(F32)], [three], conv_flops, x, gains, w_all[0]
        )
        a_two, windows, s_low = kernel_call(
            second_conv_kernel,
            [big(BF), wide_shape, s_shape],
            [three, fold],
            conv_flops,
            c_one,
            x,
            gains,
            w_all[1],
            w_all[2],
        )
    code_all = rest[:, :n_code].reshape(-1, lat)
    proj_all = rest[:, n_code : n_code + n_proj].reshape(-1, lat)
    head_all = rest[:, n_code + n_proj : n_code + n_proj + n_head, :rgb].reshape(-1, rgb)

    lat_count = crops_all * cells // 4 * lat
    pix_count = crops_all * cells * 3
    latent = contract_last(s_low, proj_all)
    picked = code_all[codes].astype(F32)
    cum = jnp.cumsum(picked, axis=1)
    resid = latent[:, None, :] - cum
    quant_part = (1.0 + BETA) * jnp.sum(resid * resid) / lat_count
    zq_low = cum[:, -1].astype(BF)
    pred = contract_last(zq_low, head_all)
    diff = pred - target
    weight_mask = jnp.repeat(mask.astype(F32), 3, axis=-1)
    smooth = jnp.sqrt(diff * diff + 1.0)
    recon_part = jnp.sum(weight_mask * (smooth - 1.0)) / pix_count
    d_pred = (weight_mask * (diff / smooth) / pix_count).astype(BF)
    d_head = contract_rows(zq_low, d_pred)
    d_zq = contract_back(d_pred, head_all)
    d_cum = -2.0 / lat_count * resid
    d_picked = jnp.flip(jnp.cumsum(jnp.flip(d_cum, 1), axis=1), 1)
    d_code = jax.ops.segment_sum(
        d_picked.reshape(-1, lat), codes.reshape(-1), num_segments=code_all.shape[0]
    )
    d_lat_low = (jnp.sum(resid, axis=1) * (2.0 * BETA / lat_count) + d_zq).astype(BF)
    d_proj = contract_rows(s_low, d_lat_low)
    d_s_low = contract_back(d_lat_low, proj_all).astype(BF)

    d_c_two, d_down = kernel_call(
        down_back_kernel,
        [big(BF), dw_shape],
        [fold],
        conv_flops // 2,
        d_s_low,
        windows,
        w_all[2],
    )
    d_three = pltpu.VMEM((crops, 18, 16, 3 * ch), BF)
    d_c_one, d_second, gain_two = kernel_call(
        functools.partial(unit_back_kernel, row=2, inner=True),
        [big(BF), dw_shape, dg_shape],
        [d_three],
        2 * conv_flops,
        d_c_two,
        c_one,
        gains,
        w_all[1],
        a_two,
    )
    d_first, gain_one = kernel_call(
        functools.partial(unit_back_kernel, row=0, inner=False),
        [dw_shape, dg_shape],
        [d_three],
        2 * conv_flops,
        d_c_one,
        x,
        gains,
        w_all[0],
        a_one,
    )
    d_gains = jnp.concatenate([gain_one, gain_two], axis=0)

    devices = ranks * shards
    pad = jnp.pad(d_head, ((0, 0), (0, lat - rgb)))
    loss_part = recon_part + quant_part
    mats_old = [
        (conv_w, conv_row, conv_col),
        (proj_w[:, None, :], proj_row[:, None], proj_col[None, :]),
        (code_w[:, None, :], code_row[:, None], code_col[None, :]),
        (head_w[:, None, :], head_row[:, None], head_col[None, :]),
    ]
    wt_sq = [jnp.sum(m[0] * m[0], axis=(0, 2)) for m in mats_old]
    if fast:
        packed = jnp.zeros((devices, 16 - n_head, lat), BF)
        rest_grad = jnp.concatenate(
            [v.astype(BF).reshape(devices, -1, lat) for v in (d_code, d_proj, pad)] + [packed],
            axis=1,
        )
        sources = [d.reshape(4, 2, 2, 2, -1, ch) for d in (d_first, d_second, d_down)]
        sources.append(rest_grad.reshape(4, 2, 2, 2, -1, lat))
        quarter = jnp.concatenate(wt_sq) / 4
        row5 = jnp.pad(jnp.concatenate([loss_part[None], quarter]), (0, ch - 1 - quarter.shape[0]))
        vec = jnp.concatenate([d_gains, row5[None], jnp.zeros((3, ch), F32)])
        conv_rows4 = jnp.transpose(conv_row).reshape(3, 4, -1, 1)
        rest_rows4 = jnp.concatenate(
            [v.reshape(4, -1) for v in (code_row, proj_row, head_row)]
            + [jnp.ones((4, 16 - n_head), F32)],
            axis=1,
        )[:, :, None]
        out = reduce_call(sources, vec, conv_rows4, rest_rows4, (n_code, n_proj, n_head, rgb))
        conv_new_rows = jnp.transpose(out[4].reshape(3, -1))
        rest_new = out[5][:, :, 0]
        cuts = (n_code, n_code + n_proj, n_code + n_proj + n_head)
        code_rn, proj_rn, head_rn = (
            v.reshape(-1, 1) for v in jnp.split(rest_new, cuts, axis=1)[:3]
        )
        rows_one = [conv_new_rows, proj_rn, code_rn, head_rn]
        tv = out[6]
        loss = tv[20, 0]
        g_gain = tv[16:20]
        wt_all = tv[20, 1:7]
        shard_rows = [m[0].shape[0] for m in mats_old]
        eps = [EPS_SQ * n * shards for n in shard_rows]
        sums = [
            (tv[0:3] + eps[0], tv[6:9, 0], tv[3:6], wt_all[0:3]),
            (tv[10:11, :lat] + eps[1], tv[13:14, 0], tv[10:11, lat:], wt_all[3:4]),
            (tv[9:10, :lat] + eps[2], tv[12:13, 0], tv[9:10, lat:], wt_all[4:5]),
            (tv[11:12, :rgb] + eps[3], tv[14:15, 0], tv[11:12, lat : lat + rgb], wt_all[5:6]),
        ]
        g_conv = jnp.transpose(
            jnp.stack([v.reshape(-1, ch) for v in out[:3]]).astype(F32), (1, 0, 2)
        )
        rest_full = out[3].astype(F32)
    else:

        def to_owner(v):
            return lax.psum_scatter(v, BOTH, scatter_dimension=0, tiled=True)

        def to_rows(v):
            return lax.all_gather(v, "rows", axis=0)

        rest_grad = jnp.concatenate(
            [v.astype(BF).reshape(devices, -1, lat) for v in (d_code, d_proj, pad)], axis=1
        )
        rest_mine = to_owner(rest_grad.reshape(-1, lat))
        conv_mine = [to_owner(v) for v in (d_first, d_second, d_down)]
        rest_full = to_rows(rest_mine).astype(F32)
        conv_full = to_rows(jnp.stack(conv_mine)).astype(F32)
        g_conv = jnp.transpose(conv_full, (0, 2, 1, 3)).reshape(-1, 3, ch)
        loss, g_gain = lax.psum((loss_part, d_gains), BOTH)

    g_code = rest_full[:, :n_code].reshape(-1, lat)
    g_proj = rest_full[:, n_code : n_code + n_proj].reshape(-1, lat)
    g_head = rest_full[:, n_code + n_proj : n_code + n_proj + n_head, :rgb].reshape(-1, rgb)
    grads = [g_conv, g_proj[:, None, :], g_code[:, None, :], g_head[:, None, :]]
    if not fast:
        rows_new = [row_part(grad, m[1]) for grad, m in zip(grads, mats_old)]
        rows_one = [r[0] for r in rows_new]
        sums = lax.psum([r[1:] for r in rows_new], "batch")
        sums = [
            (s[0], s[1], s[2], w) for s, w in zip(sums, lax.psum(wt_sq, "batch"))
        ]
    done = [
        finish(g, m[0], r, m[2], *s) for g, m, r, s in zip(grads, mats_old, rows_one, sums)
    ]

    state_new = 0.5 * gain_state + 0.5 * (g_gain * g_gain + EPS_SQ)
    update = g_gain * lax.rsqrt(state_new)
    rms_u = jnp.sqrt(jnp.mean(update * update))
    scale = jnp.sqrt(jnp.mean(gains * gains))
    gains_new = gains - RATE * scale * update / jnp.maximum(1.0, rms_u)
    conv_new = done[0][1]
    proj_new, code_new, head_new = (d[1][:, 0, :] for d in done[1:])
    return (
        loss,
        g_conv,
        rows_one[0],
        done[0][0],
        conv_new,
        conv_new.astype(BF),
        g_proj,
        rows_one[1][:, 0],
        done[1][0][0],
        proj_new,
        proj_new.astype(BF),
        g_code,
        rows_one[2][:, 0],
        done[2][0][0],
        code_new,
        code_new.astype(BF),
        g_head,
        rows_one[3][:, 0],
        done[3][0][0],
        head_new,
        head_new.astype(BF),
        g_gain,
        state_new,
        gains_new,
    )


def solution(mesh):
    cell = P("batch", "rows", None, None)
    mat, vec = P("batch", None), P("batch")
    placed = (cell,) * 4 + (P("batch", None, None), mat, mat, mat, P())
    placed += (mat, P()) + (vec, P()) * 3 + (P(),)
    conv_outs = (P("batch", None, None), mat, P(), P("batch", None, None), P("batch", None, None))
    mat_outs = (mat, vec, P(), mat, mat)
    return jax.shard_map(
        local,
        mesh=mesh,
        in_specs=placed,
        out_specs=(P(),) + conv_outs + mat_outs * 3 + (P(),) * 3,
        check_vma=False,
    )
```

```python
import functools

import jax
import jax.numpy as jnp
from jax import lax
from jax.experimental import pallas as pl
from jax.experimental.pallas import tpu as pltpu
from jax.sharding import PartitionSpec as P

GROUPS = 32
BETA = 0.25
RATE = 0.5
EPS_NORM = 1e-05
EPS_SQ = 1e-30
BF = jnp.bfloat16
F32 = jnp.float32
BOTH = ("batch", "rows")
MIB = 1 << 20
VM = pl.BlockSpec(memory_space=pltpu.VMEM)
ANY = pl.BlockSpec(memory_space=pl.ANY)
MESH = pl.DeviceIdType.MESH


def group_sum(v):
    lane = lax.broadcasted_iota(jnp.int32, v.shape, 1)
    width = v.shape[1]
    for k in (1, 2, 4, 8):
        up = pltpu.roll(v, k, 1)
        down = pltpu.roll(v, width - k, 1)
        v = v + jnp.where((lane & k) != 0, up, down)
    return v


def moments(v):
    count = v.shape[0] * (v.shape[1] // GROUPS)
    sums = jnp.concatenate(
        [jnp.sum(v, axis=0, keepdims=True), jnp.sum(v * v, axis=0, keepdims=True)]
        + [jnp.zeros((6, v.shape[1]), F32)],
        axis=0,
    )
    sums = group_sum(sums) / count
    mean = sums[0:1]
    return mean, lax.rsqrt(sums[1:2] - mean * mean + EPS_NORM)


def shifted(v, by):
    cells = v.shape[0]
    col = lax.broadcasted_iota(jnp.int32, v.shape, 0) & 15
    edge = 0 if by == 1 else 15
    return jnp.where(col == edge, 0.0, pltpu.roll(v, by % cells, 0))


def fill_three(dst, left, mid, right):
    ch = mid.shape[1]
    for k, v in enumerate((left, mid, right)):
        dst[1:17, :, k * ch : (k + 1) * ch] = v.astype(BF).reshape(16, 16, ch)


def zero_edges(dst):
    dst[0] = jnp.zeros(dst.shape[1:], dst.dtype)
    dst[17] = jnp.zeros(dst.shape[1:], dst.dtype)


def put_lanes(dst, rows, v):
    for k in range(dst.shape[0]):
        dst[k, rows, :] = v[:, k * 128 : (k + 1) * 128]


def get_lanes(src, rows):
    return jnp.concatenate([src[k, rows, :] for k in range(src.shape[0])], axis=1)


def conv_rows(src, w_ref):
    acc = None
    width = src.shape[2]
    for dy in range(3):
        lhs = src[dy : dy + 16].reshape(256, width)
        d = jnp.dot(lhs, w_ref[dy * width : (dy + 1) * width, :], preferred_element_type=F32)
        acc = d if acc is None else acc + d
    return acc


def conv_rows_back(src, w_ref):
    acc = None
    ch = src.shape[2] // 3
    for dy in range(3):
        for dx in range(3):
            lhs = src[2 - dy : 18 - dy, :, dx * ch : (dx + 1) * ch].reshape(256, ch)
            t = (dy * 3 + dx) * ch
            d = lax.dot_general(
                lhs, w_ref[t : t + ch, :], (((1,), (1,)), ((), ())), preferred_element_type=F32
            )
            acc = d if acc is None else acc + d
    return acc


def conv_weight_grad(a_ref, d3_ref, dw_ref, half, tick=None):
    crops, cells, ch = a_ref.shape
    nb = 256
    out = slice(half * nb, (half + 1) * nb)

    def block(dx, carry):
        if tick is not None:
            tick(dx)
        lane = pl.multiple_of(dx * ch + half * nb, nb)
        for dy in range(3):
            rhs = d3_ref[:, 2 - dy : 18 - dy, :, pl.ds(lane, nb)].reshape(crops * cells, nb)
            d = lax.dot_general(
                a_ref[...].reshape(crops * cells, ch),
                rhs,
                (((0,), (0,)), ((), ())),
                preferred_element_type=F32,
            )
            row = pl.multiple_of((dy * 3 + dx) * ch, ch)
            dw_ref[pl.ds(row, ch), out] = d.astype(dw_ref.dtype)
        return carry

    lax.fori_loop(0, 3, block, 0)


def silu(h):
    return h * jax.nn.sigmoid(h)


def first_crop(v, gains_ref, w_ref, a3):
    mean, rstd = moments(v)
    a = silu((v - mean) * rstd * gains_ref[0:1, :] + gains_ref[1:2, :])
    fill_three(a3, shifted(a, 1), a, shifted(a, -1))
    return a.astype(BF), conv_rows(a3, w_ref)


def second_crop(v, x, gains_ref, w_ref, l_ref, a3, y32):
    ch = v.shape[1]
    mean, rstd = moments(v)
    a = silu((v - mean) * rstd * gains_ref[2:3, :] + gains_ref[3:4, :])
    fill_three(a3, shifted(a, 1), a, shifted(a, -1))
    put_lanes(y32, slice(None), conv_rows(a3, w_ref) + x)
    even = get_lanes(y32, pl.ds(0, 128, stride=2))
    odd = get_lanes(y32, pl.ds(1, 128, stride=2))
    cell = lax.broadcasted_iota(jnp.int32, odd.shape, 0) & 7
    before = jnp.where(cell == 0, 0.0, pltpu.roll(odd, 1, 0))
    for dx, part in enumerate((before, even, odd)):
        part = part.reshape(8, 2, 8, ch)
        upper = part[:, 0].reshape(64, ch)
        lower = part[:, 1].reshape(64, ch)
        above = jnp.concatenate([jnp.zeros((8, ch), F32), lower[:56]], axis=0)
        for dy, rows in enumerate((above, upper, lower)):
            lane = (dy * 3 + dx) * ch
            l_ref[:, lane : lane + ch] = rows.astype(BF)
    return a.astype(BF)


def down_dot(l_ref, w_ref, s_ref):
    ch = s_ref.shape[1]
    nb = 256

    def block(j, carry):
        lane = pl.ds(pl.multiple_of(j * nb, nb), nb)
        d = jnp.dot(l_ref[...], w_ref[:, lane], preferred_element_type=F32)
        s_ref[:, lane] = d.astype(BF)
        return carry

    lax.fori_loop(0, ch // nb, block, 0)


def crop_rows(i):
    return pl.ds(pl.multiple_of(i * 64, 64), 64)


def first_conv_kernel(x_ref, gains_ref, w_ref, a_ref, c_ref, a3):
    zero_edges(a3)

    def crop(i, carry):
        a_ref[i], c_ref[i] = first_crop(x_ref[i].astype(F32), gains_ref, w_ref, a3)
        return carry

    lax.fori_loop(0, x_ref.shape[0], crop, 0)


def second_conv_kernel(c_in_ref, x_ref, gains_ref, w_ref, w_down_ref, a_ref, l_ref, s_ref, a3, y32):
    zero_edges(a3)

    def crop(i, carry):
        a_ref[i] = second_crop(
            c_in_ref[i],
            x_ref[i].astype(F32),
            gains_ref,
            w_ref,
            l_ref.at[crop_rows(i)],
            a3,
            y32,
        )
        return carry

    lax.fori_loop(0, x_ref.shape[0], crop, 0)
    down_dot(l_ref, w_down_ref, s_ref)


def down_input_grad(ds_ref, w_ref, dc_ref, y32, tick=None):
    cells, ch = ds_ref.shape
    crops = cells // 64

    def dot_t(lhs, tap):
        return lax.dot_general(
            lhs.astype(BF),
            w_ref[tap * ch : (tap + 1) * ch, :],
            (((1,), (1,)), ((), ())),
            preferred_element_type=F32,
        )

    def crop(i, carry):
        if tick is not None:
            tick(i)
        here = ds_ref[pl.ds(pl.multiple_of(i * 64, 64), 64), :].astype(F32)
        at = lax.broadcasted_iota(jnp.int32, here.shape, 0)

        def next_col(v):
            return jnp.where((at & 7) == 7, 0.0, pltpu.roll(v, 63, 0))

        right = next_col(here)
        under = jnp.concatenate([here[8:], jnp.zeros((8, ch), F32)], axis=0)
        corner = next_col(under)
        ee = dot_t(here, 4)
        eo = dot_t(here, 5) + dot_t(right, 3)
        oe = dot_t(here, 7) + dot_t(under, 1)
        oo = dot_t(here, 8) + dot_t(right, 6) + dot_t(under, 2) + dot_t(corner, 0)

        def both_rows(top, bottom):
            top, bottom = top.reshape(8, 1, 8, ch), bottom.reshape(8, 1, 8, ch)
            return jnp.concatenate([top, bottom], axis=1).reshape(128, ch)

        put_lanes(y32, pl.ds(0, 128, stride=2), both_rows(ee, oe))
        put_lanes(y32, pl.ds(1, 128, stride=2), both_rows(eo, oo))
        dc_ref[i] = get_lanes(y32, slice(None)).astype(BF)
        return carry

    lax.fori_loop(0, crops, crop, 0)


def down_weight_grad(l_ref, ds_ref, dw_ref):
    ch = ds_ref.shape[1]

    def block(t, carry):
        lane = pl.multiple_of(t * ch, ch)
        d = lax.dot_general(
            l_ref[:, pl.ds(lane, ch)],
            ds_ref[...],
            (((0,), (0,)), ((), ())),
            preferred_element_type=F32,
        )
        dw_ref[pl.ds(lane, ch), :] = d.astype(BF)
        return carry

    lax.fori_loop(0, 9, block, 0)


def down_back_kernel(ds_ref, l_ref, w_ref, dc_ref, dw_ref, y32):
    down_weight_grad(l_ref, ds_ref, dw_ref)
    down_input_grad(ds_ref, w_ref, dc_ref, y32)


def hidden_grad(v, gain, shift, d_act):
    mean, rstd = moments(v)
    vhat = (v - mean) * rstd
    h = vhat * gain + shift
    sig = jax.nn.sigmoid(h)
    return d_act * sig * (1.0 + h * (1.0 - sig)), vhat, rstd


def unit_back(dc_ref, v_of, gains_ref, w_ref, dg_ref, d3, row, din_ref=None, tick=None):
    crops, cells, ch = dc_ref.shape
    dg_ref[...] = jnp.zeros_like(dg_ref)

    def crop(i, carry):
        if tick is not None:
            tick(i)
        d = dc_ref[i].astype(F32)
        slot = d3.at[i]
        zero_edges(slot)
        fill_three(slot, shifted(d, -1), d, shifted(d, 1))
        d_act = conv_rows_back(slot, w_ref)
        gain = gains_ref[row : row + 1, :]
        hg, vhat, rstd = hidden_grad(v_of(i), gain, gains_ref[row + 1 : row + 2, :], d_act)
        one = jnp.sum(hg * vhat, axis=0, keepdims=True)
        two = jnp.sum(hg, axis=0, keepdims=True)
        dg_ref[0:1, :] += one
        dg_ref[1:2, :] += two
        if din_ref is not None:
            count = cells * (ch // GROUPS)
            sums = jnp.concatenate([two * gain, one * gain, jnp.zeros((6, ch), F32)], axis=0)
            sums = group_sum(sums) / count
            din_ref[i] = (rstd * (hg * gain - sums[0:1] - vhat * sums[1:2])).astype(BF)
        return carry

    lax.fori_loop(0, crops, crop, 0)


def unit_back_kernel(dc_ref, v_ref, gains_ref, w_ref, a_ref, *outs, row, inner):
    if inner:
        din_ref, dw_ref, dg_ref, d3 = outs
    else:
        dw_ref, dg_ref, d3 = outs
        din_ref = None

    def v_of(i):
        return v_ref[i].astype(F32)

    unit_back(dc_ref, v_of, gains_ref, w_ref, dg_ref, d3, row, din_ref)
    for half in range(2):
        conv_weight_grad(a_ref, d3, dw_ref, half)


def kernel_call(body, outs, scratch, flops, *args):
    bytes_accessed = sum(a.size * a.dtype.itemsize for a in args)
    bytes_accessed += sum(o.size * o.dtype.itemsize for o in outs)
    return pl.pallas_call(
        body,
        out_shape=outs,
        in_specs=[VM] * len(args),
        out_specs=[VM] * len(outs),
        scratch_shapes=scratch,
        compiler_params=pltpu.CompilerParams(vmem_limit_bytes=56 * MIB),
        cost_estimate=pl.CostEstimate(
            flops=flops, bytes_accessed=bytes_accessed, transcendentals=0
        ),
    )(*args)


class Place:
    def __init__(self):
        rows, batch = lax.axis_index("rows"), lax.axis_index("batch")
        self.x, self.c = rows // 2, rows % 2
        self.z, self.y = batch // 2, batch % 2
        self.part = self.c * 2 + self.x

    def at(self, x=None, c=None, z=None, y=None):
        x = self.x if x is None else x
        c = self.c if c is None else c
        z = self.z if z is None else z
        y = self.y if y is None else y
        return {"rows": 2 * x + c, "batch": 2 * z + y}

    def row_peers(self):
        return [
            self.at(c=1 - self.c),
            self.at(x=1 - self.x),
            self.at(x=1 - self.x, c=1 - self.c),
        ]

    def z_peers(self):
        return [self.at(z=(self.z + d) % 4) for d in (1, 2, 3)]

    def greet(self):
        barrier = pltpu.get_barrier_semaphore()
        peers = self.row_peers() + self.z_peers() + [self.at(y=1 - self.y)]
        for peer in peers:
            pl.semaphore_signal(barrier, inc=1, device_id=peer, device_id_type=MESH)
        pl.semaphore_wait(barrier, len(peers))


def remote(src, dst, send, recv, peer):
    return pltpu.make_async_remote_copy(
        src_ref=src, dst_ref=dst, send_sem=send, recv_sem=recv, device_id=peer, device_id_type=MESH
    )


class Gather:
    def __init__(self, place, src, dst, send, recv, by_x):
        self.p, self.src, self.dst, self.send, self.recv = place, src, dst, send, recv
        self.by_x = by_x
        self.steps = 4 if by_x else 3

    def copies(self, step):
        p, src, dst, send, recv = self.p, self.src, self.dst, self.send, self.recv
        if step == 0:
            mine = (p.c, p.x) if self.by_x else (p.c,)
            here, there = src.at[mine], dst.at[(p.z, p.y) + mine]
            out = [
                remote(here, there, send.at[k], recv.at[k], q) for k, q in enumerate(p.z_peers())
            ]
            return out + [pltpu.make_async_copy(here, there, recv.at[6])]
        if step == 1:
            part = dst.at[:, p.y, p.c, p.x] if self.by_x else dst.at[:, p.y, p.c]
            return [remote(part, part, send.at[3], recv.at[3], p.at(y=1 - p.y))]
        if step == 2 and self.by_x:
            part = dst.at[:, :, p.c, p.x]
            return [remote(part, part, send.at[4], recv.at[4], p.at(x=1 - p.x))]
        part = dst.at[:, :, p.c]
        return [remote(part, part, send.at[5], recv.at[5], p.at(c=1 - p.c))]

    def start(self, step):
        for copy in self.copies(step):
            copy.start()

    def arrive(self, step):
        for copy in self.copies(step):
            copy.wait_recv()

    def go(self, step):
        self.arrive(step - 1)
        self.start(step)

    def finish(self):
        for step in range(self.steps):
            for copy in self.copies(step):
                if copy.is_remote:
                    copy.wait_send()


class Reduce:
    steps = 6

    def __init__(self, place, src, out, mine, one, two, three, kept, four, send, recv):
        self.p, self.src, self.out = place, src, out
        self.mine, self.one, self.two, self.three, self.four = mine, one, two, three, four
        self.send, self.recv = send, recv
        first_x = place.c == 0
        self.f = jnp.where(first_x, place.x, place.y)
        self.g = jnp.where(first_x, place.y, place.x)
        self.f_peer = place.at(
            x=jnp.where(first_x, 1 - place.x, place.x), y=jnp.where(first_x, place.y, 1 - place.y)
        )
        self.g_peer = place.at(
            x=jnp.where(first_x, place.x, 1 - place.x), y=jnp.where(first_x, 1 - place.y, place.y)
        )
        self.slot = 2 * self.f + self.g
        self.kept = kept

    @staticmethod
    def early(rows, lanes):
        return [pltpu.VMEM(lead + (rows, lanes), BF) for lead in ((4, 4), (4, 4), (2, 4), (4,))]

    @staticmethod
    def late(rows, lanes, kept):
        return [pltpu.VMEM(lead + (rows, lanes), BF) for lead in ((4,),) * kept + ((3,),)]

    @staticmethod
    def sems():
        return [pltpu.SemaphoreType.DMA((11,)), pltpu.SemaphoreType.DMA((15,))]

    def copies(self, step):
        p, src, mine, send, recv = self.p, self.src, self.mine, self.send, self.recv
        if step == 0:
            out = []
            for k in range(4):
                y, x = k // 2, k % 2
                there = jnp.where(p.c == 1, 2 * x + y, 2 * y + x)
                here = jnp.where(p.c == 0, 2 * x + y, 2 * y + x)
                part = src.at[:, y, 1 - p.c, x]
                peer = p.at(c=1 - p.c)
                out.append(remote(part, self.one.at[there], send.at[k], recv.at[k], peer))
                local = src.at[:, y, p.c, x]
                out.append(pltpu.make_async_copy(local, mine.at[here], recv.at[10 + k]))
            return out
        if step == 1:
            part = mine.at[pl.ds(2 * (1 - self.f), 2)]
            return [remote(part, self.two, send.at[4], recv.at[4], self.f_peer)]
        if step == 2:
            part = mine.at[2 * self.f + 1 - self.g]
            return [remote(part, self.three, send.at[5], recv.at[5], self.g_peer)]
        if step == 3:
            out = []
            for d, peer in zip((1, 2, 3), p.z_peers()):
                part = self.kept.at[(p.z + d) % 4]
                out.append(remote(part, self.four.at[d - 1], send.at[5 + d], recv.at[5 + d], peer))
            return out
        if step == 4:
            part = self.out.at[p.part]
            return [remote(part, part, send.at[9], recv.at[9], p.at(x=1 - p.x))]
        part = self.out.at[pl.ds(2 * p.c, 2)]
        return [remote(part, part, send.at[10], recv.at[14], p.at(c=1 - p.c))]

    def start(self, step):
        for copy in self.copies(step):
            copy.start()

    def arrive(self, step):
        p, mine = self.p, self.mine
        for copy in self.copies(step):
            copy.wait_recv()

        def add(dst, a, b):
            dst[...] = (a[...].astype(F32) + b[...].astype(F32)).astype(BF)

        if step == 0:

            def body(i, carry):
                at = (i // 4, i % 4)
                add(mine.at[at], mine.at[at], self.one.at[at])
                return carry

            lax.fori_loop(0, 16, body, 0)
        if step == 1:
            for copy in self.copies(step):
                copy.wait_send()

            def body(i, carry):
                at = (2 * self.f + i // 4, i % 4)
                add(mine.at[at], mine.at[at], self.two.at[i // 4, i % 4])
                return carry

            lax.fori_loop(0, 8, body, 0)
        if step == 2:

            def body(i, carry):
                add(self.kept.at[i], mine.at[self.slot, i], self.three.at[i])
                return carry

            lax.fori_loop(0, 4, body, 0)
        if step == 3:
            total = self.kept[p.z].astype(F32)
            for d in range(3):
                total = total + self.four[d].astype(F32)
            self.out[p.part] = total.astype(BF)

    def go(self, step):
        self.arrive(step - 1)
        self.start(step)

    def sent(self, first, last):
        for step in range(first, last):
            if step == 1:
                continue
            for copy in self.copies(step):
                if copy.is_remote:
                    copy.wait_send()


def forward_kernel(
    feat,
    side,
    conv_ref,
    code_ref,
    proj_ref,
    head_ref,
    gains_ref,
    x_out,
    side_out,
    w_out0,
    w_out1,
    w_out2,
    rest_out,
    a_one_ref,
    c_one_ref,
    a_two_ref,
    l_ref,
    s_ref,
    wt_ref,
    w_mine,
    rest_mine,
    xv,
    wv0,
    wv1,
    wv2,
    a3,
    y32,
    x_send,
    x_recv,
    g_send,
    g_recv,
    o_sem,
):
    place = Place()
    rank = 2 * place.x + place.c
    ch, lat = conv_ref.shape[2], code_ref.shape[1]
    n_code, n_proj, n_head = (v.shape[0] // 4 for v in (code_ref, proj_ref, head_ref))
    wt_ref[...] = jnp.zeros_like(wt_ref)

    def cast_conv(j):
        n = w_mine.shape[3]
        for k in range(4):
            v = conv_ref[j, k * n : (k + 1) * n, :]
            w_mine[j, k // 2, k % 2] = v.astype(BF)
            wt_ref[j : j + 1, :] += jnp.sum(v * v, axis=0, keepdims=True)

    def cast_rest():
        for k in range(4):
            low = 0
            for m, (ref, n) in enumerate(
                ((code_ref, n_code), (proj_ref, n_proj), (head_ref, n_head))
            ):
                v = ref[k * n : (k + 1) * n, :]
                wt_ref[3 + m : 4 + m, :lat] += jnp.sum(v * v, axis=0, keepdims=True)
                if n % 16:
                    v = jnp.concatenate([v, jnp.zeros((-n % 16, lat), F32)], axis=0)
                rest_mine[k // 2, k % 2, low : low + v.shape[0]] = v.astype(BF)
                low += v.shape[0]

    cast_conv(0)
    place.greet()

    def view(ref, lanes):
        n = ref.shape[0] // 32
        return ref.reshape(4, 2, 2, 2, n, ref.shape[1]).at[..., lanes]

    def job(k, src, dst, by_x):
        return Gather(place, src, dst, g_send.at[k], g_recv.at[k], by_x)

    halves = [slice(0, 256), slice(256, 512)]
    w0 = [job(k, w_mine.at[0, ..., h], view(wv0, h), False) for k, h in enumerate(halves)]
    w1 = [job(2 + k, w_mine.at[1, ..., h], view(wv1, h), False) for k, h in enumerate(halves)]
    w2 = [job(4 + k, w_mine.at[2, ..., h], view(wv2, h), True) for k, h in enumerate(halves)]
    ends = [slice(0, 128), slice(128, 256)]
    rest = [
        job(6 + k, rest_mine.at[..., h], rest_out.at[..., h], k == 0) for k, h in enumerate(ends)
    ]

    cells = []
    for src, dst, base in ((feat, xv, 0), (side, side_out, 4)):
        for k, q in enumerate(place.row_peers()):
            to = q["rows"]
            cells.append(
                remote(src.at[to], dst.at[:, rank], x_send.at[base + k], x_recv.at[base + k], q)
            )
        cells.append(pltpu.make_async_copy(src.at[rank], dst.at[:, rank], x_recv.at[base + 3]))

    w0[0].start(0)
    for copy in cells:
        copy.start()
    w0[1].start(0)
    cast_rest()
    cast_conv(1)
    cast_conv(2)
    w0[0].go(1)
    w0[1].arrive(0)
    w1[0].start(0)
    rest[0].start(0)
    w0[0].go(2)
    w0[1].start(1)
    w0[0].arrive(2)
    w0[1].go(2)
    zero_edges(a3)
    for copy in cells:
        copy.wait_recv()
    keep_x = pltpu.make_async_copy(xv, x_out, o_sem.at[0])
    keep_x.start()
    w0[1].arrive(2)
    keep_w = [
        pltpu.make_async_copy(v, o, o_sem.at[1 + k])
        for k, (v, o) in enumerate(((wv0, w_out0), (wv1, w_out1), (wv2, w_out2)))
    ]
    keep_w[0].start()
    count = xv.shape[0]

    def crop_x(i):
        return xv[i].reshape(256, ch).astype(F32)

    def first(i, carry):
        @pl.when(i == 1)
        def _():
            w1[0].go(1)
            w1[1].start(0)

        @pl.when(i == 2)
        def _():
            rest[0].go(1)
            w2[0].start(0)

        @pl.when(i == 5)
        def _():
            w1[0].go(2)
            w1[1].go(1)
            rest[0].go(2)
            w2[1].start(0)

        @pl.when(i == 7)
        def _():
            w2[0].go(1)

        a_one_ref[i], c_one_ref[i] = first_crop(crop_x(i), gains_ref, wv0, a3)
        return carry

    lax.fori_loop(0, count, first, 0)
    w1[0].arrive(2)
    rest[1].start(0)
    w1[1].go(2)
    w1[1].arrive(2)
    keep_w[1].start()

    def second(i, carry):
        @pl.when(i == 0)
        def _():
            w2[0].go(2)
            w2[1].go(1)

        @pl.when(i == 2)
        def _():
            w2[1].go(2)
            rest[0].go(3)

        @pl.when(i == 3)
        def _():
            rest[1].go(1)

        @pl.when(i == 5)
        def _():
            w2[0].go(3)

        @pl.when(i == 7)
        def _():
            w2[1].go(3)

        a_two_ref[i] = second_crop(
            c_one_ref[i], crop_x(i), gains_ref, wv1, l_ref.at[crop_rows(i)], a3, y32
        )
        return carry

    lax.fori_loop(0, count, second, 0)
    rest[1].go(2)
    w2[0].arrive(3)
    w2[1].arrive(3)
    keep_w[2].start()
    down_dot(l_ref, wv2, s_ref)
    for part in (w0, w1, w2):
        for g in part:
            g.finish()
    for g in rest:
        g.arrive(g.steps - 1)
        g.finish()
    for copy in cells:
        if copy.is_remote:
            copy.wait_send()
    keep_x.wait()
    for copy in keep_w:
        copy.wait()


def forward_call(feat, side, conv_w, code_w, proj_w, head_w, gains):
    ranks, crops, cells, ch = feat.shape
    lat = code_w.shape[1]
    lat_cells = crops * ranks * cells // 4
    n_conv = conv_w.shape[1] // 4
    n_rest = code_w.shape[0] // 4 + proj_w.shape[0] // 4 + 16
    whole = 32 * n_conv

    def shape(*dims, dtype=BF):
        return jax.ShapeDtypeStruct(dims, dtype)

    outs = [
        shape(crops, ranks, cells, ch),
        shape(crops, ranks, *side.shape[2:], dtype=F32),
        shape(whole, ch),
        shape(whole, ch),
        shape(whole, ch),
        shape(4, 2, 2, 2, n_rest, lat),
        shape(crops, ranks * cells, ch),
        shape(crops, ranks * cells, ch, dtype=F32),
        shape(crops, ranks * cells, ch),
        shape(lat_cells, 9 * ch),
        shape(lat_cells, ch),
        shape(8, ch, dtype=F32),
    ]
    return pl.pallas_call(
        forward_kernel,
        out_shape=outs,
        in_specs=[ANY] * 2 + [VM] * 5,
        out_specs=[ANY] * 6 + [VM] * 6,
        scratch_shapes=[
            pltpu.VMEM((3, 2, 2, n_conv, ch), BF),
            pltpu.VMEM((2, 2, n_rest, lat), BF),
            pltpu.VMEM((crops, ranks, cells, ch), BF),
        ]
        + [pltpu.VMEM((whole, ch), BF)] * 3
        + [
            pltpu.VMEM((18, 16, 3 * ch), BF),
            pltpu.VMEM((ch // 128, ranks * cells, 128), F32),
            pltpu.SemaphoreType.DMA((8,)),
            pltpu.SemaphoreType.DMA((8,)),
            pltpu.SemaphoreType.DMA((8, 8)),
            pltpu.SemaphoreType.DMA((8, 8)),
            pltpu.SemaphoreType.DMA((4,)),
        ],
        compiler_params=pltpu.CompilerParams(
            vmem_limit_bytes=58 * MIB, collective_id=2, has_side_effects=True
        ),
        cost_estimate=pl.CostEstimate(
            flops=45 * crops * ranks * cells * ch * ch,
            bytes_accessed=0,
            transcendentals=0,
        ),
    )(feat, side, conv_w, code_w, proj_w, head_w, gains)


def quantizer_kernel(
    consts,
    codes_ref,
    rest,
    side_ref,
    sl_ref,
    l_ref,
    ds_ref,
    loss_ref,
    rg_ref,
    dw_ref,
    tab,
    stage,
    proj_v,
    head_v,
    e_ref,
    sems,
):
    lat_count, pix_count, rgb, n_code = consts
    cells = sl_ref.shape[0]
    pieces = rest.shape[0]
    slots = stage.shape[0]
    lat = tab.shape[1]
    small = [
        pltpu.make_async_copy(rest.at[:, n_code : n_code + 16], proj_v, sems.at[slots]),
        pltpu.make_async_copy(rest.at[:, n_code + 16 :], head_v, sems.at[slots + 1]),
    ]
    for copy in small:
        copy.start()

    def fetch(p):
        slot = p % slots
        return pltpu.make_async_copy(rest.at[p, :n_code], stage.at[slot], sems.at[slot])

    for p in range(slots):
        fetch(p).start()

    def widen(p, carry):
        fetch(p).wait()
        tab[pl.ds(pl.multiple_of(p * n_code, n_code), n_code), :] = stage[p % slots].astype(F32)

        @pl.when(p + slots < pieces)
        def _():
            fetch(p + slots).start()

        return carry

    lax.fori_loop(0, pieces, widen, 0)
    for copy in small:
        copy.wait()
    proj = proj_v[...].reshape(-1, lat)
    head = head_v[...].astype(F32)[:, :8, :128].reshape(-1, 128).astype(BF)

    def pick(b, carry):
        for j in range(8):
            for k in range(4):
                row = codes_ref[(b * 8 + j) * 4 + k]
                e_ref[k, pl.ds(b * 8 + j, 1), :] = tab[pl.ds(row, 1), :]
        return carry

    lax.fori_loop(0, cells // 8, pick, 0)

    latent = jnp.dot(sl_ref[...], proj, preferred_element_type=F32)
    cum = e_ref[0]
    resid = []
    square = None
    for k in range(4):
        if k:
            cum = cum + e_ref[k]
        r = latent - cum
        resid.append(r)
        part = jnp.sum(r * r, axis=0, keepdims=True)
        square = part if square is None else square + part
    zq = cum.astype(BF)
    side = side_ref[...]
    valid = lax.broadcasted_iota(jnp.int32, side.shape, 1) < rgb
    weight = jnp.where(valid, pltpu.roll(side, 128 - 16, 1), 0.0)
    diff = jnp.where(valid, jnp.dot(zq, head, preferred_element_type=F32) - side, 0.0)
    smooth = jnp.sqrt(diff * diff + 1.0)
    recon = jnp.sum(weight * (smooth - 1.0), axis=0, keepdims=True)
    loss_ref[...] = jnp.zeros_like(loss_ref)
    loss_ref[0:1, 0:lat] = square * ((1.0 + BETA) / lat_count)
    loss_ref[0:1, lat : lat + 128] = recon / pix_count
    d_pred = (weight * (diff / smooth) / pix_count).astype(BF)
    back = (((1,), (1,)), ((), ()))
    rows = (((0,), (0,)), ((), ()))
    d_head = lax.dot_general(zq, d_pred, rows, preferred_element_type=F32)
    total = resid[0] + resid[1] + resid[2] + resid[3]
    d_zq = lax.dot_general(d_pred, head, back, preferred_element_type=F32)
    d_lat = (total * (2.0 * BETA / lat_count) + d_zq).astype(BF)
    d_proj = lax.dot_general(sl_ref[...], d_lat, rows, preferred_element_type=F32)
    d_s = lax.dot_general(d_lat, proj, back, preferred_element_type=F32)
    ds_ref[...] = d_s.astype(BF)
    tail = None
    for k in (3, 2, 1, 0):
        tail = resid[k] if tail is None else tail + resid[k]
        e_ref[k] = tail * (-2.0 / lat_count)

    def clear(p, carry):
        tab[pl.ds(pl.multiple_of(p * n_code, n_code), n_code), :] = jnp.zeros((n_code, lat), F32)
        return carry

    lax.fori_loop(0, pieces, clear, 0)

    def scatter(b, carry):
        for j in range(8):
            for k in range(4):
                row = codes_ref[(b * 8 + j) * 4 + k]
                tab[pl.ds(row, 1), :] += e_ref[k, pl.ds(b * 8 + j, 1), :]
        return carry

    lax.fori_loop(0, cells // 8, scatter, 0)

    def narrow(p, carry):
        at = pl.ds(pl.multiple_of(p * n_code, n_code), n_code)
        rg_ref[p, :n_code] = tab[at, :].astype(BF)
        return carry

    lax.fori_loop(0, pieces, narrow, 0)
    rg_ref[:, n_code : n_code + 16] = d_proj.astype(BF).reshape(pieces, 16, lat)
    d_head = jnp.concatenate([d_head, jnp.zeros((d_head.shape[0], lat - 128), F32)], axis=1)
    d_head = d_head.reshape(pieces, 8, lat)
    d_head = jnp.concatenate([d_head, jnp.zeros((pieces, 8, lat), F32)], axis=1)
    rg_ref[:, n_code + 16 :] = d_head.astype(BF)
    down_weight_grad(l_ref, ds_ref, dw_ref)


def quantizer_call(codes, rest, side, s_low, windows, lat_count, pix_count, rgb, n_code):
    pieces, rows, lat = rest.shape
    cells, ch = s_low.shape
    outs = [
        jax.ShapeDtypeStruct((cells, ch), BF),
        jax.ShapeDtypeStruct((8, ch), F32),
        jax.ShapeDtypeStruct((pieces, rows, lat), BF),
        jax.ShapeDtypeStruct((9 * ch, ch), BF),
    ]
    return pl.pallas_call(
        functools.partial(quantizer_kernel, (lat_count, pix_count, rgb, n_code)),
        out_shape=outs,
        in_specs=[pl.BlockSpec(memory_space=pltpu.SMEM), ANY, VM, VM, VM],
        out_specs=[VM] * 4,
        scratch_shapes=[
            pltpu.VMEM((pieces * n_code, lat), F32),
            pltpu.VMEM((4, n_code, lat), BF),
            pltpu.VMEM((pieces, 16, lat), BF),
            pltpu.VMEM((pieces, rows - n_code - 16, lat), BF),
            pltpu.VMEM((4, cells, lat), F32),
            pltpu.SemaphoreType.DMA((6,)),
        ],
        compiler_params=pltpu.CompilerParams(vmem_limit_bytes=58 * MIB),
        cost_estimate=pl.CostEstimate(flops=10**10, bytes_accessed=10**7, transcendentals=0),
    )(codes, rest, side, s_low, windows)


def second_back_kernel(
    ds_ref,
    w_down_ref,
    w_ref,
    c_ref,
    a_ref,
    gains_ref,
    down_src,
    rest_src,
    din_ref,
    dw_ref,
    dg_ref,
    g_down_ref,
    rest_kept_ref,
    dc,
    d3,
    y32,
    *bufs,
):
    place = Place()
    down = Reduce(place, down_src, g_down_ref, *bufs[:8])
    early, sems = bufs[8:12], bufs[12:]
    rest = Reduce(place, rest_src.at[..., :128], None, *early, rest_kept_ref, None, *sems)
    place.greet()
    down.start(0)
    rest.start(0)

    def tick_down(i):
        @pl.when(i == 4)
        def _():
            down.go(1)

    def tick_crop(i):
        @pl.when(i == 0)
        def _():
            rest.arrive(0)

        @pl.when(i == 3)
        def _():
            down.go(2)
            rest.start(1)

        @pl.when(i == 6)
        def _():
            down.go(3)

    down_input_grad(ds_ref, w_down_ref, dc, y32, tick_down)
    unit_back(dc, lambda i: c_ref[i], gains_ref, w_ref, dg_ref, d3, 2, din_ref, tick_crop)
    conv_weight_grad(a_ref, d3, dw_ref, 0)
    rest.go(2)
    conv_weight_grad(a_ref, d3, dw_ref, 1)
    down.go(4)
    rest.arrive(2)
    down.go(5)
    down.arrive(5)
    down.sent(0, 6)
    rest.sent(0, 3)


def second_back_call(ds, w_down, w, c_one, a_two, gains, down_src, rest_src):
    crops, cells, ch = c_one.shape
    n_conv, n_rest = down_src.shape[-2], rest_src.shape[-2]
    outs = [
        jax.ShapeDtypeStruct((crops, cells, ch), BF),
        jax.ShapeDtypeStruct(w.shape, BF),
        jax.ShapeDtypeStruct((2, ch), F32),
        jax.ShapeDtypeStruct((4, n_conv, ch), BF),
        jax.ShapeDtypeStruct((4, n_rest, 128), BF),
    ]
    return pl.pallas_call(
        second_back_kernel,
        out_shape=outs,
        in_specs=[VM] * 6 + [ANY] * 2,
        out_specs=[VM] * 5,
        scratch_shapes=[
            pltpu.VMEM((crops, cells, ch), BF),
            pltpu.VMEM((crops, 18, 16, 3 * ch), BF),
            pltpu.VMEM((ch // 128, cells, 128), F32),
        ]
        + Reduce.early(n_conv, ch)
        + Reduce.late(n_conv, ch, 1)
        + Reduce.sems()
        + Reduce.early(n_rest, 128)
        + Reduce.sems(),
        compiler_params=pltpu.CompilerParams(
            vmem_limit_bytes=58 * MIB, collective_id=3, has_side_effects=True
        ),
        cost_estimate=pl.CostEstimate(flops=2 * 10**10, bytes_accessed=0, transcendentals=0),
    )(ds, w_down, w, c_one, a_two, gains, down_src, rest_src)


def first_back_kernel(
    sizes,
    dc_ref,
    x_ref,
    gains_ref,
    w_ref,
    a_ref,
    rest_kept_ref,
    g_down_ref,
    dg_two_ref,
    loss_ref,
    wt_ref,
    conv_row_ref,
    rest_row_ref,
    rest_src,
    second_src,
    g_first0,
    g_first1,
    g_second,
    g_rest0,
    g_rest1,
    conv_new_ref,
    rest_new_ref,
    tv_ref,
    dw,
    d3,
    dg,
    vec,
    vec_in,
    tv_in,
    s_send,
    s_recv,
    *bufs,
):
    n_code, n_proj, n_head, rgb = sizes
    place = Place()
    bufs = list(bufs)

    def take(n):
        out = bufs[:n]
        del bufs[:n]
        return out

    half = rest_src.shape[-1] // 2
    ch = tv_ref.shape[1]
    view = dw.reshape(4, 2, 2, 2, dw.shape[0] // 32, ch)
    four, sems = take(1), take(2)
    rest0 = Reduce(place, None, g_rest0, *[None] * 4, rest_kept_ref, *four, *sems)
    rest1 = Reduce(place, rest_src.at[..., half:], g_rest1, *take(8))
    second = Reduce(place, second_src, g_second, *take(8))
    low = Reduce(place, view.at[..., : ch // 2], g_first0, *take(8))
    high = Reduce(place, view.at[..., ch // 2 :], g_first1, *take(8))
    place.greet()
    rest0.start(3)
    rest1.start(0)
    second.start(0)

    def tick_crop(i):
        @pl.when(i == 2)
        def _():
            rest1.go(1)
            second.arrive(0)

        @pl.when(i == 6)
        def _():
            rest0.go(4)

    def tick_low(dx):
        @pl.when(dx == 0)
        def _():
            rest1.go(2)
            second.start(1)

        @pl.when(dx == 1)
        def _():
            rest0.go(5)

    def tick_high(dx):
        @pl.when(dx == 0)
        def _():
            rest1.go(3)

        @pl.when(dx == 1)
        def _():
            low.go(1)

    def v_of(i):
        return x_ref[i].astype(F32)

    unit_back(dc_ref, v_of, gains_ref, w_ref, dg, d3, 0, None, tick_crop)
    vec[...] = jnp.zeros_like(vec)
    vec[0:2] = dg[...]
    vec[2:4] = dg_two_ref[...]
    vec[4:5] = loss_ref[0:1]
    small = [
        remote(vec, vec_in.at[k], s_send.at[k], s_recv.at[k], q)
        for k, q in enumerate(place.row_peers())
    ]
    for copy in small:
        copy.start()
    conv_weight_grad(a_ref, d3, dw, 0, tick_low)
    low.start(0)
    conv_weight_grad(a_ref, d3, dw, 1, tick_high)
    high.start(0)
    second.go(2)
    high.go(1)

    tv_ref[...] = jnp.zeros_like(tv_ref)
    for copy in small:
        copy.wait_recv()
    tv_ref[16:24, :] = vec[...] + vec_in[0] + vec_in[1] + vec_in[2]
    tv_ref[24:32, :] = wt_ref[...]

    def fold(parts, row, width):
        squares = [g.astype(F32) for g in parts]
        squares = [g * g for g in squares]
        total = sum(jnp.sum(q, axis=1, keepdims=True) for q in squares)
        new = 0.5 * row + 0.5 * (total / width + EPS_SQ)
        inverse = 1.0 / new
        col = [jnp.sum(q, axis=0, keepdims=True) for q in squares]
        over = [jnp.sum(q * inverse, axis=0, keepdims=True) for q in squares]
        return (
            new,
            jnp.concatenate(col, axis=1),
            jnp.concatenate(over, axis=1),
            jnp.sum(new, axis=0, keepdims=True),
        )

    def fold_conv(j, refs):
        for k in range(4):
            new, col, over, total = fold([r[k] for r in refs], conv_row_ref[j, k], ch)
            conv_new_ref[j, k] = new
            tv_ref[j : j + 1, :] += col
            tv_ref[3 + j : 4 + j, :] += over
            tv_ref[6 + j : 7 + j, :] += total

    def fold_rest():
        lat = 2 * half
        spans = ((0, n_code, lat), (n_code, n_proj, lat), (n_code + n_proj, n_head, rgb))
        for k in range(4):
            both = [r[k] for r in (g_rest0, g_rest1)]
            for m, (start, size, width) in enumerate(spans):
                parts = [v.astype(F32)[start : start + size] for v in both]
                row = rest_row_ref[k, start : start + size]
                new, col, over, total = fold(parts, row, width)
                rest_new_ref[k, start : start + size] = new
                tv_ref[9 + m : 10 + m, :lat] += col
                tv_ref[9 + m : 10 + m, lat:] += over
                tv_ref[12 + m : 13 + m, :] += total
            size = rest_row_ref.shape[1] - n_code - n_proj - n_head
            rest_new_ref[k, rest_row_ref.shape[1] - size :] = jnp.ones((size, 1), F32)

    fold_conv(2, [g_down_ref])
    rest0.arrive(5)
    rest1.go(4)
    second.go(3)
    low.go(2)
    low.go(3)
    high.go(2)
    rest1.go(5)
    high.go(3)
    rest1.arrive(5)
    fold_rest()
    second.go(4)
    second.go(5)
    low.go(4)
    second.arrive(5)
    fold_conv(1, [g_second])
    low.go(5)
    high.go(4)
    low.arrive(5)
    high.go(5)
    high.arrive(5)
    fold_conv(0, [g_first0, g_first1])

    across = remote(tv_ref, tv_in.at[0], s_send.at[3], s_recv.at[3], place.at(y=1 - place.y))
    across.start()
    across.wait()
    tv_ref[...] += tv_in[0]
    along = [
        remote(tv_ref, tv_in.at[k], s_send.at[3 + k], s_recv.at[3 + k], q)
        for k, q in zip((1, 2, 3), place.z_peers())
    ]
    for copy in along:
        copy.start()
    for copy in along:
        copy.wait()
    tv_ref[...] += tv_in[1] + tv_in[2] + tv_in[3]
    for copy in small:
        copy.wait_send()
    rest0.sent(3, 6)
    for job in (rest1, second, low, high):
        job.sent(0, 6)


def first_back_call(
    sizes, dc, x, gains, w, a_one, rest_kept, g_down, dg_two, loss, wt, conv_row, rest_row,
    rest_src, second_src
):
    crops, cells, ch = x.shape
    n_conv, n_rest = second_src.shape[-2], rest_src.shape[-2]

    def shape(*dims, dtype=BF):
        return jax.ShapeDtypeStruct(dims, dtype)

    outs = [
        shape(4, n_conv, ch // 2),
        shape(4, n_conv, ch // 2),
        shape(4, n_conv, ch),
        shape(4, n_rest, 128),
        shape(4, n_rest, 128),
        shape(*conv_row.shape, dtype=F32),
        shape(*rest_row.shape, dtype=F32),
        shape(32, ch, dtype=F32),
    ]

    def job(rows, lanes):
        return Reduce.early(rows, lanes) + Reduce.late(rows, lanes, 1) + Reduce.sems()

    return pl.pallas_call(
        functools.partial(first_back_kernel, sizes),
        out_shape=outs,
        in_specs=[VM] * 12 + [ANY] * 2,
        out_specs=[VM] * 8,
        scratch_shapes=[
            pltpu.VMEM(w.shape, BF),
            pltpu.VMEM((crops, 18, 16, 3 * ch), BF),
            pltpu.VMEM((2, ch), F32),
            pltpu.VMEM((8, ch), F32),
            pltpu.VMEM((3, 8, ch), F32),
            pltpu.VMEM((4, 32, ch), F32),
            pltpu.SemaphoreType.DMA((7,)),
            pltpu.SemaphoreType.DMA((7,)),
        ]
        + Reduce.late(n_rest, 128, 0)
        + Reduce.sems()
        + job(n_rest, 128)
        + job(n_conv, ch)
        + job(n_conv, ch // 2)
        + job(n_conv, ch // 2),
        compiler_params=pltpu.CompilerParams(
            vmem_limit_bytes=60 * MIB, collective_id=4, has_side_effects=True
        ),
        cost_estimate=pl.CostEstimate(flops=2 * 10**10, bytes_accessed=0, transcendentals=0),
    )(
        dc, x, gains, w, a_one, rest_kept, g_down, dg_two, loss, wt, conv_row, rest_row,
        rest_src, second_src
    )


def finish_kernel(
    sizes,
    g_first0,
    g_first1,
    g_second,
    g_down,
    g_rest0,
    g_rest1,
    conv_ref,
    code_ref,
    proj_ref,
    head_ref,
    conv_row_ref,
    rest_row_ref,
    tv_ref,
    conv_col_ref,
    code_col_ref,
    proj_col_ref,
    head_col_ref,
    gains_ref,
    state_ref,
    loss_ref,
    conv_outs,
    rest_outs,
    gain_outs,
):
    n_code, n_proj, n_head, rgb, shards = sizes
    ch = conv_ref.shape[2]
    lat = code_ref.shape[1]

    def scales(col, col_sum, over, row_sum, weights, rows, width):
        rows = rows * shards
        col_new = 0.5 * col + 0.5 * (col_sum / rows + EPS_SQ)
        row_mean = row_sum / rows
        upd_sq = row_mean * jnp.sum(over / col_new, axis=1, keepdims=True)
        rms_u = jnp.sqrt(upd_sq / (rows * width))
        scale = jnp.sqrt(jnp.sum(weights, axis=1, keepdims=True) / (rows * width))
        factor = RATE * scale / jnp.maximum(1.0, rms_u)
        return col_new, factor * lax.rsqrt(col_new), row_mean

    def line(k):
        return tv_ref[k : k + 1, :]

    cg, cc, cn, cl = conv_outs
    for j, parts in enumerate(((g_first0, g_first1), (g_second,), (g_down,))):
        n = conv_ref.shape[1]
        col_new, q, row_mean = scales(
            conv_col_ref[j : j + 1, :], line(j), line(3 + j), line(6 + j)[:, :1], line(24 + j), n, ch
        )
        cc[j : j + 1, :] = col_new
        m = n // 4
        for k in range(4):
            r = lax.rsqrt(conv_row_ref[j, k] / row_mean)
            rows = slice(k * m, (k + 1) * m)
            for p, part in enumerate(parts):
                width = part.shape[2]
                lanes = slice(p * width, (p + 1) * width)
                g = part[k].astype(F32)
                new = conv_ref[j, rows, lanes] - g * r * q[:, lanes]
                cg[j, rows, lanes] = g
                cn[j, rows, lanes] = new
                cl[j, rows, lanes] = new.astype(BF)
    cols = (code_col_ref, proj_col_ref, head_col_ref)
    spans = ((0, n_code, lat), (n_code, n_proj, lat), (n_code + n_proj, n_head, rgb))
    for m, (w_ref, (start, size, width)) in enumerate(zip((code_ref, proj_ref, head_ref), spans)):
        og, oc, on, ol = rest_outs[m]
        col_new, q, row_mean = scales(
            cols[m][...],
            line(9 + m)[:, :lat],
            line(9 + m)[:, lat:],
            line(12 + m)[:, :1],
            line(27 + m)[:, :lat],
            w_ref.shape[0],
            width,
        )
        oc[...] = col_new
        news = []
        for k in range(4):
            g = jnp.concatenate([g_rest0[k].astype(F32), g_rest1[k].astype(F32)], axis=1)
            g = g[start : start + size]
            r = lax.rsqrt(rest_row_ref[k, start : start + size] / row_mean)
            rows = slice(k * size, (k + 1) * size)
            new = w_ref[rows, :] - g * r * q
            og[rows, :] = g
            on[rows, :] = new
            if size % 16:
                news.append(new)
            else:
                ol[rows, :] = new.astype(BF)
        if news:
            ol[...] = jnp.concatenate(news, axis=0).astype(BF)
    loss_ref[...] = jnp.sum(line(20), axis=1, keepdims=True)
    grad = tv_ref[16:20, :]
    state = 0.5 * state_ref[...] + 0.5 * (grad * grad + EPS_SQ)
    update = grad * lax.rsqrt(state)
    gains = gains_ref[...]

    def rms(v):
        return jnp.sqrt(
            jnp.sum(jnp.sum(v * v, axis=1, keepdims=True), axis=0, keepdims=True) / v.size
        )

    gain_outs[0][...] = grad
    gain_outs[1][...] = state
    gain_outs[2][...] = gains - RATE * rms(gains) * update / jnp.maximum(1.0, rms(update))


def finish_call(sizes, grads, weights, rows, tv, cols, gains, state):
    conv_w, code_w, proj_w, head_w = weights
    lat = code_w.shape[1]

    def shape(dims, dtype=F32):
        return jax.ShapeDtypeStruct(dims, dtype)

    def matrix(w, col):
        return [shape(w.shape), shape(col), shape(w.shape), shape(w.shape, BF)]

    outs = [shape((1, 1)), matrix(conv_w, (3, conv_w.shape[2]))]
    outs += [[matrix(w, (1, lat)) for w in (code_w, proj_w, head_w)]]
    outs += [[shape(gains.shape)] * 3]
    args = [*grads, *weights, *rows, tv, *cols, gains, state]
    return pl.pallas_call(
        functools.partial(finish_kernel, sizes),
        out_shape=outs,
        in_specs=[VM] * len(args),
        out_specs=jax.tree.map(lambda _: VM, outs),
        compiler_params=pltpu.CompilerParams(vmem_limit_bytes=56 * MIB),
        cost_estimate=pl.CostEstimate(flops=10**7, bytes_accessed=2 * 10**7, transcendentals=0),
    )(*args)


def contract_last(left, right):
    return lax.dot_general(left, right, (((1,), (0,)), ((), ())), preferred_element_type=F32)


def contract_back(left, right):
    return lax.dot_general(left, right, (((1,), (1,)), ((), ())), preferred_element_type=F32)


def contract_rows(left, right):
    return lax.dot_general(left, right, (((0,), (0,)), ((), ())), preferred_element_type=F32)


def row_part(grad, row):
    g_sq = grad * grad + EPS_SQ
    row_new = 0.5 * row + 0.5 * jnp.mean(g_sq, axis=2)
    over_row = jnp.sum(grad * grad / row_new[:, :, None], axis=0)
    return row_new, jnp.sum(g_sq, axis=0), jnp.sum(row_new, axis=0), over_row


def finish(grad, weight, row_new, col, col_sum, row_sum, over_row, wt_sq):
    total = grad.shape[0] * lax.axis_size("batch")
    count = total * grad.shape[2]
    col_new = 0.5 * col + 0.5 * col_sum / total
    row_mean = row_sum / total
    upd_sq = row_mean * jnp.sum(over_row / col_new, axis=1)
    rms_u = jnp.sqrt(upd_sq / count)
    scale = jnp.sqrt(wt_sq / count)
    vhat = row_new[:, :, None] * col_new[None] / row_mean[None, :, None]
    update = grad * lax.rsqrt(vhat)
    new = weight - RATE * (scale / jnp.maximum(1.0, rms_u))[None, :, None] * update
    return col_new, new


def local_any(
    features,
    target,
    mask,
    codes,
    conv_w,
    proj_w,
    code_w,
    head_w,
    gains,
    conv_row,
    conv_col,
    proj_row,
    proj_col,
    code_row,
    code_col,
    head_row,
    head_col,
    gain_state,
):
    ranks = lax.axis_size("rows")
    shards = lax.axis_size("batch")
    me = lax.axis_index("rows")
    crops_all = features.shape[0] * shards
    ch = features.shape[3]
    lat = proj_w.shape[1]
    rgb = head_w.shape[1]
    height = features.shape[1] * ranks
    width = features.shape[2]

    def whole_crops(v):
        return lax.all_to_all(v, "rows", split_axis=0, concat_axis=1, tiled=True)

    def my_part(v):
        size = v.shape[0] // ranks
        return lax.dynamic_slice_in_dim(v, me * size, size, 0)

    conv_piece = jnp.transpose(my_part(conv_w).astype(BF), (1, 0, 2))
    head_wide = jnp.pad(head_w, ((0, 0), (0, lat - rgb)))
    rest_piece = jnp.concatenate(
        [my_part(code_w).astype(BF), my_part(proj_w).astype(BF), my_part(head_wide).astype(BF)]
    )
    n_code, n_proj, n_head = (v.shape[0] // ranks for v in (code_w, proj_w, head_w))
    w_all = [lax.all_gather(conv_piece[0], BOTH, axis=0, tiled=True)]
    later = lax.all_gather(conv_piece[1:], BOTH, axis=0)
    later = jnp.transpose(later, (1, 0, 2, 3)).reshape(2, -1, ch)
    w_all += [later[0], later[1]]
    rest = lax.all_gather(rest_piece, BOTH, axis=0)
    code_all = rest[:, :n_code].reshape(-1, lat)
    proj_all = rest[:, n_code : n_code + n_proj].reshape(-1, lat)
    head_all = rest[:, n_code + n_proj :, :rgb].reshape(-1, rgb)

    x = whole_crops(features)
    target, mask, codes = whole_crops(target), whole_crops(mask), whole_crops(codes)
    crops = x.shape[0]
    cells = height * width
    x = x.reshape(crops, cells, ch)
    lat_cells = crops * cells // 4
    target = target.reshape(lat_cells, rgb)
    mask = mask.reshape(lat_cells, -1)
    codes = codes.reshape(lat_cells, -1)

    conv_flops = 2 * crops * cells * 9 * ch * ch
    three = pltpu.VMEM((18, 16, 3 * ch), BF)
    fold = pltpu.VMEM((ch // 128, cells, 128), F32)

    def big(dtype):
        return jax.ShapeDtypeStruct((crops, cells, ch), dtype)

    dw_shape = jax.ShapeDtypeStruct((9 * ch, ch), BF)
    dg_shape = jax.ShapeDtypeStruct((2, ch), F32)

    a_one, c_one = kernel_call(
        first_conv_kernel, [big(BF), big(F32)], [three], conv_flops, x, gains, w_all[0]
    )
    a_two, windows, s_low = kernel_call(
        second_conv_kernel,
        [
            big(BF),
            jax.ShapeDtypeStruct((lat_cells, 9 * ch), BF),
            jax.ShapeDtypeStruct((lat_cells, ch), BF),
        ],
        [three, fold],
        conv_flops,
        c_one,
        x,
        gains,
        w_all[1],
        w_all[2],
    )

    lat_count = crops_all * cells // 4 * lat
    pix_count = crops_all * cells * 3
    latent = contract_last(s_low, proj_all)
    picked = code_all[codes].astype(F32)
    cum = jnp.cumsum(picked, axis=1)
    resid = latent[:, None, :] - cum
    quant_part = (1.0 + BETA) * jnp.sum(resid * resid) / lat_count
    zq_low = cum[:, -1].astype(BF)
    pred = contract_last(zq_low, head_all)
    diff = pred - target
    weight_mask = jnp.repeat(mask.astype(F32), 3, axis=-1)
    smooth = jnp.sqrt(diff * diff + 1.0)
    recon_part = jnp.sum(weight_mask * (smooth - 1.0)) / pix_count
    d_pred = (weight_mask * (diff / smooth) / pix_count).astype(BF)
    d_head = contract_rows(zq_low, d_pred)
    d_zq = contract_back(d_pred, head_all)
    d_cum = -2.0 / lat_count * resid
    d_picked = jnp.flip(jnp.cumsum(jnp.flip(d_cum, 1), axis=1), 1)
    d_code = jax.ops.segment_sum(
        d_picked.reshape(-1, lat), codes.reshape(-1), num_segments=code_all.shape[0]
    )
    d_lat_low = (jnp.sum(resid, axis=1) * (2.0 * BETA / lat_count) + d_zq).astype(BF)
    d_proj = contract_rows(s_low, d_lat_low)
    d_s_low = contract_back(d_lat_low, proj_all).astype(BF)

    d_c_two, d_down = kernel_call(
        down_back_kernel,
        [big(BF), dw_shape],
        [fold],
        conv_flops // 2,
        d_s_low,
        windows,
        w_all[2],
    )
    d_three = pltpu.VMEM((crops, 18, 16, 3 * ch), BF)
    d_c_one, d_second, gain_two = kernel_call(
        functools.partial(unit_back_kernel, row=2, inner=True),
        [big(BF), dw_shape, dg_shape],
        [d_three],
        2 * conv_flops,
        d_c_two,
        c_one,
        gains,
        w_all[1],
        a_two,
    )
    d_first, gain_one = kernel_call(
        functools.partial(unit_back_kernel, row=0, inner=False),
        [dw_shape, dg_shape],
        [d_three],
        2 * conv_flops,
        d_c_one,
        x,
        gains,
        w_all[0],
        a_one,
    )
    d_gains = jnp.concatenate([gain_one, gain_two], axis=0)

    devices = ranks * shards

    def to_owner(v):
        return lax.psum_scatter(v, BOTH, scatter_dimension=0, tiled=True)

    def to_rows(v):
        return lax.all_gather(v, "rows", axis=0)

    pad = jnp.pad(d_head, ((0, 0), (0, lat - rgb)))
    rest_grad = jnp.concatenate(
        [v.astype(BF).reshape(devices, -1, lat) for v in (d_code, d_proj, pad)], axis=1
    )
    rest_mine = to_owner(rest_grad.reshape(-1, lat))
    conv_mine = [to_owner(v) for v in (d_first, d_second, d_down)]
    rest_full = to_rows(rest_mine).astype(F32)
    conv_full = to_rows(jnp.stack(conv_mine)).astype(F32)
    g_conv = jnp.transpose(conv_full, (0, 2, 1, 3)).reshape(-1, 3, ch)
    g_code = rest_full[:, :n_code].reshape(-1, lat)
    g_proj = rest_full[:, n_code : n_code + n_proj].reshape(-1, lat)
    g_head = rest_full[:, n_code + n_proj :, :rgb].reshape(-1, rgb)

    mats = [
        (g_conv, conv_w, conv_row, conv_col),
        (g_proj[:, None, :], proj_w[:, None, :], proj_row[:, None], proj_col[None, :]),
        (g_code[:, None, :], code_w[:, None, :], code_row[:, None], code_col[None, :]),
        (g_head[:, None, :], head_w[:, None, :], head_row[:, None], head_col[None, :]),
    ]
    rows_new = [row_part(grad, row) for grad, weight, row, col in mats]
    wt_sq = [jnp.sum(weight * weight, axis=(0, 2)) for grad, weight, row, col in mats]
    sums = lax.psum([r[1:] + (w,) for r, w in zip(rows_new, wt_sq)], "batch")
    loss, g_gain = lax.psum((recon_part + quant_part, d_gains), BOTH)
    done = [
        finish(m[0], m[1], r[0], m[3], *s) for m, r, s in zip(mats, rows_new, sums)
    ]

    state_new = 0.5 * gain_state + 0.5 * (g_gain * g_gain + EPS_SQ)
    update = g_gain * lax.rsqrt(state_new)
    rms_u = jnp.sqrt(jnp.mean(update * update))
    scale = jnp.sqrt(jnp.mean(gains * gains))
    gains_new = gains - RATE * scale * update / jnp.maximum(1.0, rms_u)
    conv_new = done[0][1]
    proj_new, code_new, head_new = (d[1][:, 0, :] for d in done[1:])
    return (
        loss,
        g_conv,
        rows_new[0][0],
        done[0][0],
        conv_new,
        conv_new.astype(BF),
        g_proj,
        rows_new[1][0][:, 0],
        done[1][0][0],
        proj_new,
        proj_new.astype(BF),
        g_code,
        rows_new[2][0][:, 0],
        done[2][0][0],
        code_new,
        code_new.astype(BF),
        g_head,
        rows_new[3][0][:, 0],
        done[3][0][0],
        head_new,
        head_new.astype(BF),
        g_gain,
        state_new,
        gains_new,
    )


def local_fast(
    features,
    target,
    mask,
    codes,
    conv_w,
    proj_w,
    code_w,
    head_w,
    gains,
    conv_row,
    conv_col,
    proj_row,
    proj_col,
    code_row,
    code_col,
    head_row,
    head_col,
    gain_state,
):
    ranks = lax.axis_size("rows")
    shards = lax.axis_size("batch")
    crops_all = features.shape[0] * shards
    crops = features.shape[0] // ranks
    ch = features.shape[3]
    cells = features.shape[1] * ranks * features.shape[2]
    lat, rgb = proj_w.shape[1], head_w.shape[1]
    lat_cells = crops * cells // 4
    n_code, n_proj, n_head = (v.shape[0] // ranks for v in (code_w, proj_w, head_w))
    sizes = (n_code, n_proj, n_head, rgb)
    conv_rows = jnp.transpose(conv_w, (1, 0, 2))
    head_wide = jnp.pad(head_w, ((0, 0), (0, lat - rgb)))

    def lanes(v, n):
        return jnp.pad(v, ((0, 0),) * (v.ndim - 1) + ((0, n - v.shape[-1]),))

    side = [lanes(target, 16), lanes(jnp.repeat(mask.astype(F32), 3, axis=-1), 16)]
    side = lanes(jnp.concatenate(side + [codes.astype(F32)], axis=-1), 128)
    out = forward_call(
        features.reshape(ranks, crops, -1, ch),
        side.reshape(ranks, crops, -1, 128),
        conv_rows,
        code_w,
        proj_w,
        head_wide,
        gains,
    )
    x = out[0].reshape(crops, cells, ch)
    side = out[1].reshape(lat_cells, 128)
    w_all, rest = out[2:5], out[5]
    a_one, c_one, a_two, windows, s_low, wt = out[6:]
    codes = side[:, 32:36].astype(jnp.int32).reshape(-1)
    n_rest = rest.shape[-2]
    d_s, loss, rest_grad, d_down = quantizer_call(
        codes,
        rest.reshape(-1, n_rest, lat),
        side,
        s_low,
        windows,
        crops_all * cells // 4 * lat,
        crops_all * cells * 3,
        rgb,
        n_code,
    )

    def shards_of(v):
        return v.reshape(4, 2, 2, 2, -1, v.shape[-1])

    rest_src = shards_of(rest_grad)
    d_c_one, d_second, dg_two, g_down, rest_kept = second_back_call(
        d_s, w_all[2], w_all[1], c_one, a_two, gains, shards_of(d_down), rest_src
    )
    conv_row4 = jnp.transpose(conv_row).reshape(3, 4, -1, 1)
    rest_row4 = [v.reshape(4, -1) for v in (code_row, proj_row, head_row)]
    rest_row4.append(jnp.ones((4, n_rest - n_code - n_proj - n_head), F32))
    rest_row4 = jnp.concatenate(rest_row4, axis=1)[:, :, None]
    out = first_back_call(
        sizes,
        d_c_one,
        x,
        gains,
        w_all[0],
        a_one,
        rest_kept,
        g_down,
        dg_two,
        loss,
        wt,
        conv_row4,
        rest_row4,
        rest_src,
        shards_of(d_second),
    )
    g_first0, g_first1, g_second, g_rest0, g_rest1, conv_rn, rest_rn, tv = out
    head_col_wide = jnp.pad(head_col, (0, lat - rgb), constant_values=1.0)
    loss, conv_outs, rest_outs, gain_outs = finish_call(
        sizes + (shards,),
        (g_first0, g_first1, g_second, g_down, g_rest0, g_rest1),
        (conv_rows, code_w, proj_w, head_wide),
        (conv_rn, rest_rn),
        tv,
        (conv_col, code_col[None], proj_col[None], head_col_wide[None]),
        gains,
        gain_state,
    )
    conv_g, conv_c, conv_n, conv_l = conv_outs
    code_o, proj_o, head_o = rest_outs
    cuts = (n_code, n_code + n_proj, n_code + n_proj + n_head)
    code_r, proj_r, head_r = (
        v.reshape(-1) for v in jnp.split(rest_rn[:, :, 0], cuts, axis=1)[:3]
    )

    def back(v):
        return jnp.transpose(v, (1, 0, 2))

    return (
        loss[0, 0],
        back(conv_g),
        jnp.transpose(conv_rn.reshape(3, -1)),
        conv_c,
        back(conv_n),
        back(conv_l),
        proj_o[0],
        proj_r,
        proj_o[1][0],
        proj_o[2],
        proj_o[3],
        code_o[0],
        code_r,
        code_o[1][0],
        code_o[2],
        code_o[3],
        head_o[0][:, :rgb],
        head_r,
        head_o[1][0, :rgb],
        head_o[2][:, :rgb],
        head_o[3][:, :rgb],
        *gain_outs,
    )


def solution(mesh):
    cell = P("batch", "rows", None, None)
    mat, vec = P("batch", None), P("batch")
    placed = (cell,) * 4 + (P("batch", None, None), mat, mat, mat, P())
    placed += (mat, P()) + (vec, P()) * 3 + (P(),)
    conv_outs = (P("batch", None, None), mat, P(), P("batch", None, None), P("batch", None, None))
    mat_outs = (mat, vec, P(), mat, mat)
    fast = (mesh.shape["rows"], mesh.shape["batch"]) == (4, 8)
    return jax.shard_map(
        local_fast if fast else local_any,
        mesh=mesh,
        in_specs=placed,
        out_specs=(P(),) + conv_outs + mat_outs * 3 + (P(),) * 3,
        check_vma=False,
    )
```

```python
import functools

import jax
import jax.numpy as jnp
from jax import lax
from jax.experimental import pallas as pl
from jax.experimental.pallas import tpu as pltpu
from jax.sharding import PartitionSpec as P

GROUPS = 32
BETA = 0.25
RATE = 0.5
EPS_NORM = 1e-05
EPS_SQ = 1e-30
BF = jnp.bfloat16
F32 = jnp.float32
BOTH = ("batch", "rows")
MIB = 1 << 20
VM = pl.BlockSpec(memory_space=pltpu.VMEM)
ANY = pl.BlockSpec(memory_space=pl.ANY)
MESH = pl.DeviceIdType.MESH


def group_sum(v):
    lane = lax.broadcasted_iota(jnp.int32, v.shape, 1)
    width = v.shape[1]
    for k in (1, 2, 4, 8):
        up = pltpu.roll(v, k, 1)
        down = pltpu.roll(v, width - k, 1)
        v = v + jnp.where((lane & k) != 0, up, down)
    return v


def moments(v):
    count = v.shape[0] * (v.shape[1] // GROUPS)
    sums = jnp.concatenate(
        [jnp.sum(v, axis=0, keepdims=True), jnp.sum(v * v, axis=0, keepdims=True)]
        + [jnp.zeros((6, v.shape[1]), F32)],
        axis=0,
    )
    sums = group_sum(sums) / count
    mean = sums[0:1]
    return mean, lax.rsqrt(sums[1:2] - mean * mean + EPS_NORM)


def shifted(v, by):
    cells = v.shape[0]
    col = lax.broadcasted_iota(jnp.int32, v.shape, 0) & 15
    edge = 0 if by == 1 else 15
    return jnp.where(col == edge, 0.0, pltpu.roll(v, by % cells, 0))


def fill_three(dst, left, mid, right):
    ch = mid.shape[1]
    for k, v in enumerate((left, mid, right)):
        dst[1:17, :, k * ch : (k + 1) * ch] = v.astype(BF).reshape(16, 16, ch)


def zero_edges(dst):
    dst[0] = jnp.zeros(dst.shape[1:], dst.dtype)
    dst[17] = jnp.zeros(dst.shape[1:], dst.dtype)


def put_lanes(dst, rows, v):
    for k in range(dst.shape[0]):
        dst[k, rows, :] = v[:, k * 128 : (k + 1) * 128]


def get_lanes(src, rows):
    return jnp.concatenate([src[k, rows, :] for k in range(src.shape[0])], axis=1)


def conv_rows(src, w_ref):
    acc = None
    width = src.shape[2]
    for dy in range(3):
        lhs = src[dy : dy + 16].reshape(256, width)
        d = jnp.dot(lhs, w_ref[dy * width : (dy + 1) * width, :], preferred_element_type=F32)
        acc = d if acc is None else acc + d
    return acc


def conv_rows_back(src, w_ref):
    acc = None
    ch = src.shape[2] // 3
    for dy in range(3):
        for dx in range(3):
            lhs = src[2 - dy : 18 - dy, :, dx * ch : (dx + 1) * ch].reshape(256, ch)
            t = (dy * 3 + dx) * ch
            d = lax.dot_general(
                lhs, w_ref[t : t + ch, :], (((1,), (1,)), ((), ())), preferred_element_type=F32
            )
            acc = d if acc is None else acc + d
    return acc


def conv_weight_grad(a_ref, d3_ref, dw_ref, half, tick=None):
    crops, cells, ch = a_ref.shape
    nb = 256
    out = slice(half * nb, (half + 1) * nb)

    def block(dx, carry):
        if tick is not None:
            tick(dx)
        lane = pl.multiple_of(dx * ch + half * nb, nb)
        for dy in range(3):
            rhs = d3_ref[:, 2 - dy : 18 - dy, :, pl.ds(lane, nb)].reshape(crops * cells, nb)
            d = lax.dot_general(
                a_ref[...].reshape(crops * cells, ch),
                rhs,
                (((0,), (0,)), ((), ())),
                preferred_element_type=F32,
            )
            row = pl.multiple_of((dy * 3 + dx) * ch, ch)
            dw_ref[pl.ds(row, ch), out] = d.astype(dw_ref.dtype)
        return carry

    lax.fori_loop(0, 3, block, 0)


def silu(h):
    return h * jax.nn.sigmoid(h)


def first_crop(v, gains_ref, w_ref, a3):
    mean, rstd = moments(v)
    a = silu((v - mean) * rstd * gains_ref[0:1, :] + gains_ref[1:2, :])
    fill_three(a3, shifted(a, 1), a, shifted(a, -1))
    return a.astype(BF), conv_rows(a3, w_ref)


def second_crop(v, x, gains_ref, w_ref, l_ref, a3, y32):
    ch = v.shape[1]
    mean, rstd = moments(v)
    a = silu((v - mean) * rstd * gains_ref[2:3, :] + gains_ref[3:4, :])
    fill_three(a3, shifted(a, 1), a, shifted(a, -1))
    put_lanes(y32, slice(None), conv_rows(a3, w_ref) + x)
    even = get_lanes(y32, pl.ds(0, 128, stride=2))
    odd = get_lanes(y32, pl.ds(1, 128, stride=2))
    cell = lax.broadcasted_iota(jnp.int32, odd.shape, 0) & 7
    before = jnp.where(cell == 0, 0.0, pltpu.roll(odd, 1, 0))
    for dx, part in enumerate((before, even, odd)):
        part = part.reshape(8, 2, 8, ch)
        upper = part[:, 0].reshape(64, ch)
        lower = part[:, 1].reshape(64, ch)
        above = jnp.concatenate([jnp.zeros((8, ch), F32), lower[:56]], axis=0)
        for dy, rows in enumerate((above, upper, lower)):
            lane = (dy * 3 + dx) * ch
            l_ref[:, lane : lane + ch] = rows.astype(BF)
    return a.astype(BF)


def down_dot(l_ref, w_ref, s_ref):
    ch = s_ref.shape[1]
    nb = 256

    def block(j, carry):
        lane = pl.ds(pl.multiple_of(j * nb, nb), nb)
        d = jnp.dot(l_ref[...], w_ref[:, lane], preferred_element_type=F32)
        s_ref[:, lane] = d.astype(BF)
        return carry

    lax.fori_loop(0, ch // nb, block, 0)


def crop_rows(i):
    return pl.ds(pl.multiple_of(i * 64, 64), 64)


def first_conv_kernel(x_ref, gains_ref, w_ref, a_ref, c_ref, a3):
    zero_edges(a3)

    def crop(i, carry):
        a_ref[i], c_ref[i] = first_crop(x_ref[i].astype(F32), gains_ref, w_ref, a3)
        return carry

    lax.fori_loop(0, x_ref.shape[0], crop, 0)


def second_conv_kernel(c_in_ref, x_ref, gains_ref, w_ref, w_down_ref, a_ref, l_ref, s_ref, a3, y32):
    zero_edges(a3)

    def crop(i, carry):
        a_ref[i] = second_crop(
            c_in_ref[i],
            x_ref[i].astype(F32),
            gains_ref,
            w_ref,
            l_ref.at[crop_rows(i)],
            a3,
            y32,
        )
        return carry

    lax.fori_loop(0, x_ref.shape[0], crop, 0)
    down_dot(l_ref, w_down_ref, s_ref)


def down_input_grad(ds_ref, w_ref, dc_ref, y32, tick=None):
    cells, ch = ds_ref.shape
    crops = cells // 64

    def dot_t(lhs, tap):
        return lax.dot_general(
            lhs.astype(BF),
            w_ref[tap * ch : (tap + 1) * ch, :],
            (((1,), (1,)), ((), ())),
            preferred_element_type=F32,
        )

    def crop(i, carry):
        if tick is not None:
            tick(i)
        here = ds_ref[pl.ds(pl.multiple_of(i * 64, 64), 64), :].astype(F32)
        at = lax.broadcasted_iota(jnp.int32, here.shape, 0)

        def next_col(v):
            return jnp.where((at & 7) == 7, 0.0, pltpu.roll(v, 63, 0))

        right = next_col(here)
        under = jnp.concatenate([here[8:], jnp.zeros((8, ch), F32)], axis=0)
        corner = next_col(under)
        ee = dot_t(here, 4)
        eo = dot_t(here, 5) + dot_t(right, 3)
        oe = dot_t(here, 7) + dot_t(under, 1)
        oo = dot_t(here, 8) + dot_t(right, 6) + dot_t(under, 2) + dot_t(corner, 0)

        def both_rows(top, bottom):
            top, bottom = top.reshape(8, 1, 8, ch), bottom.reshape(8, 1, 8, ch)
            return jnp.concatenate([top, bottom], axis=1).reshape(128, ch)

        put_lanes(y32, pl.ds(0, 128, stride=2), both_rows(ee, oe))
        put_lanes(y32, pl.ds(1, 128, stride=2), both_rows(eo, oo))
        dc_ref[i] = get_lanes(y32, slice(None)).astype(BF)
        return carry

    lax.fori_loop(0, crops, crop, 0)


def down_weight_grad(l_ref, ds_ref, dw_ref):
    ch = ds_ref.shape[1]

    def block(t, carry):
        lane = pl.multiple_of(t * ch, ch)
        d = lax.dot_general(
            l_ref[:, pl.ds(lane, ch)],
            ds_ref[...],
            (((0,), (0,)), ((), ())),
            preferred_element_type=F32,
        )
        dw_ref[pl.ds(lane, ch), :] = d.astype(BF)
        return carry

    lax.fori_loop(0, 9, block, 0)


def down_back_kernel(ds_ref, l_ref, w_ref, dc_ref, dw_ref, y32):
    down_weight_grad(l_ref, ds_ref, dw_ref)
    down_input_grad(ds_ref, w_ref, dc_ref, y32)


def hidden_grad(v, gain, shift, d_act):
    mean, rstd = moments(v)
    vhat = (v - mean) * rstd
    h = vhat * gain + shift
    sig = jax.nn.sigmoid(h)
    return d_act * sig * (1.0 + h * (1.0 - sig)), vhat, rstd


def shift_all(dc_ref, d3, tick=None):
    def crop(i, carry):
        if tick is not None:
            tick(i)
        d = dc_ref[i].astype(F32)
        slot = d3.at[i]
        zero_edges(slot)
        fill_three(slot, shifted(d, -1), d, shifted(d, 1))
        return carry

    lax.fori_loop(0, dc_ref.shape[0], crop, 0)


def unit_back(v_of, gains_ref, w_ref, dg_ref, d3, row, din_ref=None, tick=None):
    crops, cells, ch = d3.shape[0], 256, d3.shape[3] // 3
    dg_ref[...] = jnp.zeros_like(dg_ref)

    def crop(i, carry):
        if tick is not None:
            tick(i)
        d_act = conv_rows_back(d3.at[i], w_ref)
        gain = gains_ref[row : row + 1, :]
        hg, vhat, rstd = hidden_grad(v_of(i), gain, gains_ref[row + 1 : row + 2, :], d_act)
        one = jnp.sum(hg * vhat, axis=0, keepdims=True)
        two = jnp.sum(hg, axis=0, keepdims=True)
        dg_ref[0:1, :] += one
        dg_ref[1:2, :] += two
        if din_ref is not None:
            count = cells * (ch // GROUPS)
            sums = jnp.concatenate([two * gain, one * gain, jnp.zeros((6, ch), F32)], axis=0)
            sums = group_sum(sums) / count
            din_ref[i] = (rstd * (hg * gain - sums[0:1] - vhat * sums[1:2])).astype(BF)
        return carry

    lax.fori_loop(0, crops, crop, 0)


def unit_back_kernel(dc_ref, v_ref, gains_ref, w_ref, a_ref, *outs, row, inner):
    if inner:
        din_ref, dw_ref, dg_ref, d3 = outs
    else:
        dw_ref, dg_ref, d3 = outs
        din_ref = None

    def v_of(i):
        return v_ref[i].astype(F32)

    shift_all(dc_ref, d3)
    unit_back(v_of, gains_ref, w_ref, dg_ref, d3, row, din_ref)
    for half in range(2):
        conv_weight_grad(a_ref, d3, dw_ref, half)


def kernel_call(body, outs, scratch, flops, *args):
    bytes_accessed = sum(a.size * a.dtype.itemsize for a in args)
    bytes_accessed += sum(o.size * o.dtype.itemsize for o in outs)
    return pl.pallas_call(
        body,
        out_shape=outs,
        in_specs=[VM] * len(args),
        out_specs=[VM] * len(outs),
        scratch_shapes=scratch,
        compiler_params=pltpu.CompilerParams(vmem_limit_bytes=56 * MIB),
        cost_estimate=pl.CostEstimate(
            flops=flops, bytes_accessed=bytes_accessed, transcendentals=0
        ),
    )(*args)


class Place:
    def __init__(self):
        rows, batch = lax.axis_index("rows"), lax.axis_index("batch")
        self.x, self.c = rows // 2, rows % 2
        self.z, self.y = batch // 2, batch % 2
        self.part = self.c * 2 + self.x

    def at(self, x=None, c=None, z=None, y=None):
        x = self.x if x is None else x
        c = self.c if c is None else c
        z = self.z if z is None else z
        y = self.y if y is None else y
        return {"rows": 2 * x + c, "batch": 2 * z + y}

    def row_peers(self):
        return [
            self.at(c=1 - self.c),
            self.at(x=1 - self.x),
            self.at(x=1 - self.x, c=1 - self.c),
        ]

    def z_peers(self):
        return [self.at(z=(self.z + d) % 4) for d in (1, 2, 3)]

    def greet(self):
        barrier = pltpu.get_barrier_semaphore()
        peers = self.row_peers() + self.z_peers() + [self.at(y=1 - self.y)]
        for peer in peers:
            pl.semaphore_signal(barrier, inc=1, device_id=peer, device_id_type=MESH)
        pl.semaphore_wait(barrier, len(peers))


def remote(src, dst, send, recv, peer):
    return pltpu.make_async_remote_copy(
        src_ref=src, dst_ref=dst, send_sem=send, recv_sem=recv, device_id=peer, device_id_type=MESH
    )


class Gather:
    def __init__(self, place, src, dst, send, recv, route):
        self.p, self.src, self.dst, self.send, self.recv = place, src, dst, send, recv
        self.route = "z" + route + "c"
        self.steps = len(self.route)

    def copies(self, step):
        p, src, dst, send, recv = self.p, self.src, self.dst, self.send, self.recv
        axis = self.route[step]
        if axis == "z":
            mine = (p.c, p.x) if "x" in self.route else (p.c,)
            here, there = src.at[mine], dst.at[(p.z, p.y) + mine]
            out = [
                remote(here, there, send.at[k], recv.at[k], q) for k, q in enumerate(p.z_peers())
            ]
            return out + [pltpu.make_async_copy(here, there, recv.at[6])]
        have_y = "y" in self.route[:step]
        have_x = "x" in self.route[:step] or "x" not in self.route
        part = dst.at[:, slice(None) if have_y else p.y, p.c]
        if not have_x:
            part = dst.at[:, slice(None) if have_y else p.y, p.c, p.x]
        k = 3 + "yxc".index(axis)
        peer = {"y": p.at(y=1 - p.y), "x": p.at(x=1 - p.x), "c": p.at(c=1 - p.c)}[axis]
        return [remote(part, part, send.at[k], recv.at[k], peer)]

    def start(self, step):
        for copy in self.copies(step):
            copy.start()

    def arrive(self, step):
        for copy in self.copies(step):
            copy.wait_recv()

    def go(self, step):
        self.arrive(step - 1)
        self.start(step)

    def finish(self):
        for step in range(self.steps):
            for copy in self.copies(step):
                if copy.is_remote:
                    copy.wait_send()


class Reduce:
    steps = 6

    def __init__(self, place, src, out, mine, one, two, three, kept, four, send, recv, turn=True):
        self.p, self.src, self.out = place, src, out
        self.mine, self.one, self.two, self.three, self.four = mine, one, two, three, four
        self.send, self.recv = send, recv
        first_x = (place.c == 0) & turn
        self.turn = turn
        self.f = jnp.where(first_x, place.x, place.y)
        self.g = jnp.where(first_x, place.y, place.x)
        self.f_peer = place.at(
            x=jnp.where(first_x, 1 - place.x, place.x), y=jnp.where(first_x, place.y, 1 - place.y)
        )
        self.g_peer = place.at(
            x=jnp.where(first_x, place.x, 1 - place.x), y=jnp.where(first_x, 1 - place.y, place.y)
        )
        self.slot = 2 * self.f + self.g
        self.kept = kept

    @staticmethod
    def early(rows, lanes):
        return [pltpu.VMEM(lead + (rows, lanes), BF) for lead in ((4, 4), (4, 4), (2, 4), (4,))]

    @staticmethod
    def late(rows, lanes, kept):
        return [pltpu.VMEM(lead + (rows, lanes), BF) for lead in ((4,),) * kept + ((3,),)]

    @staticmethod
    def sems():
        return [pltpu.SemaphoreType.DMA((11,)), pltpu.SemaphoreType.DMA((15,))]

    def copies(self, step):
        p, src, mine, send, recv = self.p, self.src, self.mine, self.send, self.recv
        if step == 0:
            out = []
            for k in range(4):
                y, x = k // 2, k % 2
                there = jnp.where((p.c == 1) & self.turn, 2 * x + y, 2 * y + x)
                here = jnp.where((p.c == 0) & self.turn, 2 * x + y, 2 * y + x)
                part = src.at[:, y, 1 - p.c, x]
                peer = p.at(c=1 - p.c)
                out.append(remote(part, self.one.at[there], send.at[k], recv.at[k], peer))
                local = src.at[:, y, p.c, x]
                out.append(pltpu.make_async_copy(local, mine.at[here], recv.at[10 + k]))
            return out
        if step == 1:
            part = mine.at[pl.ds(2 * (1 - self.f), 2)]
            return [remote(part, self.two, send.at[4], recv.at[4], self.f_peer)]
        if step == 2:
            part = mine.at[2 * self.f + 1 - self.g]
            return [remote(part, self.three, send.at[5], recv.at[5], self.g_peer)]
        if step == 3:
            out = []
            for d, peer in zip((1, 2, 3), p.z_peers()):
                part = self.kept.at[(p.z + d) % 4]
                out.append(remote(part, self.four.at[d - 1], send.at[5 + d], recv.at[5 + d], peer))
            return out
        if step == 4:
            part = self.out.at[p.part]
            return [remote(part, part, send.at[9], recv.at[9], p.at(x=1 - p.x))]
        part = self.out.at[pl.ds(2 * p.c, 2)]
        return [remote(part, part, send.at[10], recv.at[14], p.at(c=1 - p.c))]

    def start(self, step):
        for copy in self.copies(step):
            copy.start()

    def arrive(self, step):
        p, mine = self.p, self.mine
        for copy in self.copies(step):
            copy.wait_recv()

        def add(dst, a, b):
            dst[...] = (a[...].astype(F32) + b[...].astype(F32)).astype(BF)

        if step == 0:

            def body(i, carry):
                at = (i // 4, i % 4)
                add(mine.at[at], mine.at[at], self.one.at[at])
                return carry

            lax.fori_loop(0, 16, body, 0)
        if step == 1:
            for copy in self.copies(step):
                copy.wait_send()

            def body(i, carry):
                at = (2 * self.f + i // 4, i % 4)
                add(mine.at[at], mine.at[at], self.two.at[i // 4, i % 4])
                return carry

            lax.fori_loop(0, 8, body, 0)
        if step == 2:

            def body(i, carry):
                add(self.kept.at[i], mine.at[self.slot, i], self.three.at[i])
                return carry

            lax.fori_loop(0, 4, body, 0)
        if step == 3:
            total = self.kept[p.z].astype(F32)
            for d in range(3):
                total = total + self.four[d].astype(F32)
            self.out[p.part] = total.astype(BF)

    def go(self, step):
        self.arrive(step - 1)
        self.start(step)

    def sent(self, first, last):
        for step in range(first, last):
            if step == 1:
                continue
            for copy in self.copies(step):
                if copy.is_remote:
                    copy.wait_send()


PARTS = (
    ("w0b", "yx", 1, None),
    ("w1a", "yx", 0, None),
    ("w0a", "y", 0, None),
    ("w1b", "yx", 1, None),
    ("w2b", "yx", 1, None),
    ("r0", "y", 0, 0),
    ("r2", "yx", 0, 1),
    ("r1", "yx", 1, 0),
    ("w2a", "y", 0, None),
    ("r3", "y", 1, 1),
)
BEFORE = ("w0b1", "w1a1", "w0b2", "w1a2", "w0a1", "w1b1", "w0b3", "w2b1", "w0a2")
FIRST = {1: ("w1a3", "w1b2"), 2: ("r01",), 4: ("w2b2", "r21"), 7: ("r11", "w1b3")}
BETWEEN = ("r02",)
SECOND = {1: ("r22",), 2: ("w2a1",), 3: ("w2b3", "r12"), 6: ("r31", "r23"), 7: ("w2a2",)}
AFTER = ("r13", "r32")


def forward_kernel(
    feat,
    side,
    conv_ref,
    code_ref,
    proj_ref,
    head_ref,
    gains_ref,
    x_out,
    side_out,
    w_out0,
    w_out1,
    w_out2,
    rest_out,
    a_one_ref,
    c_one_ref,
    a_two_ref,
    l_ref,
    s_ref,
    wt_ref,
    w_mine,
    rest_mine,
    xv,
    wv0,
    wv1,
    wv2,
    a3,
    y32,
    x_send,
    x_recv,
    g_send,
    g_recv,
    o_sem,
):
    place = Place()
    rank = 2 * place.x + place.c
    ch, lat = conv_ref.shape[2], code_ref.shape[1]
    n_code, n_proj, n_head = (v.shape[0] // 4 for v in (code_ref, proj_ref, head_ref))
    wt_ref[...] = jnp.zeros_like(wt_ref)

    def cast_conv(j):
        n = w_mine.shape[3]
        for k in range(4):
            v = conv_ref[j, k * n : (k + 1) * n, :]
            w_mine[j, k // 2, k % 2] = v.astype(BF)
            wt_ref[j : j + 1, :] += jnp.sum(v * v, axis=0, keepdims=True)

    def cast_rest():
        for k in range(4):
            low = 0
            for m, (ref, n) in enumerate(
                ((code_ref, n_code), (proj_ref, n_proj), (head_ref, n_head))
            ):
                v = ref[k * n : (k + 1) * n, :]
                wt_ref[3 + m : 4 + m, :lat] += jnp.sum(v * v, axis=0, keepdims=True)
                if n % 16:
                    v = jnp.concatenate([v, jnp.zeros((-n % 16, lat), F32)], axis=0)
                rest_mine[k // 2, k % 2, low : low + v.shape[0]] = v.astype(BF)
                low += v.shape[0]

    cast_conv(0)
    place.greet()

    def view(ref, lanes):
        n = ref.shape[0] // 32
        return ref.reshape(4, 2, 2, 2, n, ref.shape[1]).at[..., lanes]

    jobs = {}
    views = [view(wv0, slice(None)), view(wv1, slice(None)), view(wv2, slice(None)), rest_out]
    for k, (name, route, lane, row) in enumerate(PARTS):
        rest = name[0] == "r"
        src = rest_mine if rest else w_mine.at[int(name[1])]
        dst = views[3] if rest else views[int(name[1])]
        n, m = src.shape[-2], src.shape[-1] // 2
        rows = pl.ds(0, n) if row is None else pl.ds(row * n // 2, n // 2)
        at = (..., rows, pl.ds(lane * m, m))
        jobs[name] = Gather(place, src.at[at], dst.at[at], g_send.at[k], g_recv.at[k], route)

    def go(words):
        for word in words:
            jobs[word[:-1]].go(int(word[-1]))

    def ticks(table):
        def tick(i):
            for when, words in table.items():

                @pl.when(i == when)
                def _():
                    go(words)

        return tick

    def whole(names):
        for name in names:
            jobs[name].arrive(jobs[name].steps - 1)

    cells = []
    for src, dst, base in ((feat, xv, 0), (side, side_out, 4)):
        for k, q in enumerate(place.row_peers()):
            to = q["rows"]
            cells.append(
                remote(src.at[to], dst.at[:, rank], x_send.at[base + k], x_recv.at[base + k], q)
            )
        cells.append(pltpu.make_async_copy(src.at[rank], dst.at[:, rank], x_recv.at[base + 3]))

    jobs["w0b"].start(0)
    for copy in cells:
        copy.start()
    cast_conv(1)
    for name in ("w1a", "w0a", "w1b"):
        jobs[name].start(0)
    cast_conv(2)
    cast_rest()
    for name, *_ in PARTS[4:]:
        jobs[name].start(0)
    go(BEFORE)
    zero_edges(a3)
    for copy in cells:
        copy.wait_recv()
    keep_x = pltpu.make_async_copy(xv, x_out, o_sem.at[0])
    keep_x.start()
    whole(("w0a", "w0b"))
    keep_w = [
        pltpu.make_async_copy(v, o, o_sem.at[1 + k])
        for k, (v, o) in enumerate(((wv0, w_out0), (wv1, w_out1), (wv2, w_out2)))
    ]
    keep_w[0].start()
    count = xv.shape[0]

    def crop_x(i):
        return xv[i].reshape(256, ch).astype(F32)

    tick_first, tick_second = ticks(FIRST), ticks(SECOND)

    def first(i, carry):
        tick_first(i)
        a_one_ref[i], c_one_ref[i] = first_crop(crop_x(i), gains_ref, wv0, a3)
        return carry

    lax.fori_loop(0, count, first, 0)
    go(BETWEEN)
    whole(("w1a", "w1b"))
    keep_w[1].start()

    def second(i, carry):
        tick_second(i)
        a_two_ref[i] = second_crop(
            c_one_ref[i], crop_x(i), gains_ref, wv1, l_ref.at[crop_rows(i)], a3, y32
        )
        return carry

    lax.fori_loop(0, count, second, 0)
    whole(("w2a", "w2b"))
    keep_w[2].start()
    down_dot(l_ref, wv2, s_ref)
    go(AFTER)
    whole(("r0", "r1", "r2", "r3"))
    for job in jobs.values():
        job.finish()
    for copy in cells:
        if copy.is_remote:
            copy.wait_send()
    keep_x.wait()
    for copy in keep_w:
        copy.wait()


def forward_call(feat, side, conv_w, code_w, proj_w, head_w, gains):
    ranks, crops, cells, ch = feat.shape
    lat = code_w.shape[1]
    lat_cells = crops * ranks * cells // 4
    n_conv = conv_w.shape[1] // 4
    n_rest = code_w.shape[0] // 4 + proj_w.shape[0] // 4 + 16
    whole = 32 * n_conv

    def shape(*dims, dtype=BF):
        return jax.ShapeDtypeStruct(dims, dtype)

    outs = [
        shape(crops, ranks, cells, ch),
        shape(crops, ranks, *side.shape[2:], dtype=F32),
        shape(whole, ch),
        shape(whole, ch),
        shape(whole, ch),
        shape(4, 2, 2, 2, n_rest, lat),
        shape(crops, ranks * cells, ch),
        shape(crops, ranks * cells, ch, dtype=F32),
        shape(crops, ranks * cells, ch),
        shape(lat_cells, 9 * ch),
        shape(lat_cells, ch),
        shape(8, ch, dtype=F32),
    ]
    return pl.pallas_call(
        forward_kernel,
        out_shape=outs,
        in_specs=[ANY] * 2 + [VM] * 5,
        out_specs=[ANY] * 6 + [VM] * 6,
        scratch_shapes=[
            pltpu.VMEM((3, 2, 2, n_conv, ch), BF),
            pltpu.VMEM((2, 2, n_rest, lat), BF),
            pltpu.VMEM((crops, ranks, cells, ch), BF),
        ]
        + [pltpu.VMEM((whole, ch), BF)] * 3
        + [
            pltpu.VMEM((18, 16, 3 * ch), BF),
            pltpu.VMEM((ch // 128, ranks * cells, 128), F32),
            pltpu.SemaphoreType.DMA((8,)),
            pltpu.SemaphoreType.DMA((8,)),
            pltpu.SemaphoreType.DMA((len(PARTS), 8)),
            pltpu.SemaphoreType.DMA((len(PARTS), 8)),
            pltpu.SemaphoreType.DMA((4,)),
        ],
        compiler_params=pltpu.CompilerParams(
            vmem_limit_bytes=58 * MIB, collective_id=2, has_side_effects=True
        ),
        cost_estimate=pl.CostEstimate(
            flops=45 * crops * ranks * cells * ch * ch,
            bytes_accessed=0,
            transcendentals=0,
        ),
    )(feat, side, conv_w, code_w, proj_w, head_w, gains)


def quantizer_kernel(
    consts,
    codes_ref,
    rest,
    side_ref,
    sl_ref,
    l_ref,
    ds_ref,
    loss_ref,
    dp_ref,
    small_ref,
    dw_ref,
    tab,
    stage,
    proj_v,
    head_v,
    e_ref,
    sems,
):
    lat_count, pix_count, rgb, n_code = consts
    cells = sl_ref.shape[0]
    pieces = rest.shape[0]
    slots = stage.shape[0]
    lat = tab.shape[1]
    small = [
        pltpu.make_async_copy(rest.at[:, n_code : n_code + 16], proj_v, sems.at[slots]),
        pltpu.make_async_copy(rest.at[:, n_code + 16 :], head_v, sems.at[slots + 1]),
    ]
    for copy in small:
        copy.start()

    def fetch(p):
        slot = p % slots
        return pltpu.make_async_copy(rest.at[p, :n_code], stage.at[slot], sems.at[slot])

    for p in range(slots):
        fetch(p).start()

    def widen(p, carry):
        fetch(p).wait()
        tab[pl.ds(pl.multiple_of(p * n_code, n_code), n_code), :] = stage[p % slots].astype(F32)

        @pl.when(p + slots < pieces)
        def _():
            fetch(p + slots).start()

        return carry

    lax.fori_loop(0, pieces, widen, 0)
    for copy in small:
        copy.wait()
    proj = proj_v[...].reshape(-1, lat)
    head = head_v[...].astype(F32)[:, :8, :128].reshape(-1, 128).astype(BF)

    def pick(b, carry):
        for j in range(8):
            for k in range(4):
                row = codes_ref[k * cells + b * 8 + j]
                e_ref[k, pl.ds(b * 8 + j, 1), :] = tab[pl.ds(row, 1), :]
        return carry

    lax.fori_loop(0, cells // 8, pick, 0)

    latent = jnp.dot(sl_ref[...], proj, preferred_element_type=F32)
    cum = e_ref[0]
    resid = []
    square = None
    for k in range(4):
        if k:
            cum = cum + e_ref[k]
        r = latent - cum
        resid.append(r)
        part = jnp.sum(r * r, axis=0, keepdims=True)
        square = part if square is None else square + part
    zq = cum.astype(BF)
    side = side_ref[...]
    valid = lax.broadcasted_iota(jnp.int32, side.shape, 1) < rgb
    weight = jnp.where(valid, pltpu.roll(side, 128 - 16, 1), 0.0)
    diff = jnp.where(valid, jnp.dot(zq, head, preferred_element_type=F32) - side, 0.0)
    smooth = jnp.sqrt(diff * diff + 1.0)
    recon = jnp.sum(weight * (smooth - 1.0), axis=0, keepdims=True)
    loss_ref[...] = jnp.zeros_like(loss_ref)
    loss_ref[0:1, 0:lat] = square * ((1.0 + BETA) / lat_count)
    loss_ref[0:1, lat : lat + 128] = recon / pix_count
    d_pred = (weight * (diff / smooth) / pix_count).astype(BF)
    back = (((1,), (1,)), ((), ()))
    rows = (((0,), (0,)), ((), ()))
    d_head = lax.dot_general(zq, d_pred, rows, preferred_element_type=F32)
    total = resid[0] + resid[1] + resid[2] + resid[3]
    d_zq = lax.dot_general(d_pred, head, back, preferred_element_type=F32)
    d_lat = (total * (2.0 * BETA / lat_count) + d_zq).astype(BF)
    d_proj = lax.dot_general(sl_ref[...], d_lat, rows, preferred_element_type=F32)
    d_s = lax.dot_general(d_lat, proj, back, preferred_element_type=F32)
    ds_ref[...] = d_s.astype(BF)
    tail = None
    for k in (3, 2, 1, 0):
        tail = resid[k] if tail is None else tail + resid[k]
        dp_ref[k * cells : (k + 1) * cells, :] = (tail * (-2.0 / lat_count)).astype(BF)
    small_ref[:, :16] = d_proj.astype(BF).reshape(pieces, 16, lat)
    d_head = jnp.concatenate([d_head, jnp.zeros((d_head.shape[0], lat - 128), F32)], axis=1)
    d_head = d_head.reshape(pieces, 8, lat)
    d_head = jnp.concatenate([d_head, jnp.zeros((pieces, 8, lat), F32)], axis=1)
    small_ref[:, 16:] = d_head.astype(BF)
    down_weight_grad(l_ref, ds_ref, dw_ref)


def quantizer_call(codes, rest, side, s_low, windows, lat_count, pix_count, rgb, n_code):
    pieces, rows, lat = rest.shape
    cells, ch = s_low.shape
    outs = [
        jax.ShapeDtypeStruct((cells, ch), BF),
        jax.ShapeDtypeStruct((8, ch), F32),
        jax.ShapeDtypeStruct((4 * cells, lat), BF),
        jax.ShapeDtypeStruct((pieces, 32, lat), BF),
        jax.ShapeDtypeStruct((9 * ch, ch), BF),
    ]
    return pl.pallas_call(
        functools.partial(quantizer_kernel, (lat_count, pix_count, rgb, n_code)),
        out_shape=outs,
        in_specs=[pl.BlockSpec(memory_space=pltpu.SMEM), ANY, VM, VM, VM],
        out_specs=[VM] * 5,
        scratch_shapes=[
            pltpu.VMEM((pieces * n_code, lat), F32),
            pltpu.VMEM((4, n_code, lat), BF),
            pltpu.VMEM((pieces, 16, lat), BF),
            pltpu.VMEM((pieces, rows - n_code - 16, lat), BF),
            pltpu.VMEM((4, cells, lat), F32),
            pltpu.SemaphoreType.DMA((6,)),
        ],
        compiler_params=pltpu.CompilerParams(vmem_limit_bytes=58 * MIB),
        cost_estimate=pl.CostEstimate(flops=10**10, bytes_accessed=10**7, transcendentals=0),
    )(codes, rest, side, s_low, windows)


def second_back_kernel(
    n_code,
    ds_ref,
    w_down_ref,
    w_ref,
    c_ref,
    a_ref,
    gains_ref,
    codes_ref,
    dp_ref,
    down_src,
    small_src,
    din_ref,
    dg_ref,
    g_down0_ref,
    g_down1_ref,
    kept0_ref,
    kept1_ref,
    rest_kept_ref,
    dw,
    d3,
    y32,
    dp_all,
    codes_all,
    quarter,
    quarter_in,
    small_in,
    e_send,
    e_recv,
    *bufs,
):
    place = Place()
    bufs = list(bufs)

    def take(n):
        out = bufs[:n]
        del bufs[:n]
        return out

    half = down_src.shape[-1] // 2
    view = dw.reshape(4, 2, 2, 2, dw.shape[0] // 32, dw.shape[1])
    down0 = Reduce(place, down_src.at[..., :half], g_down0_ref, *take(8), turn=False)
    down1 = Reduce(place, down_src.at[..., half:], g_down1_ref, *take(8), turn=False)
    early, sems = take(4), take(2)
    low = Reduce(place, view.at[..., :half], None, *early, kept0_ref, None, *sems)
    early, sems = take(4), take(2)
    high = Reduce(place, view.at[..., half:], None, *early, kept1_ref, None, *sems)

    across = place.at(x=1 - place.x)
    other = place.at(c=1 - place.c)
    two = pl.ds(2 * place.c, 2)
    entries = [(dp_ref, dp_all, 0), (codes_ref, codes_all, 1)]
    out_x = [
        remote(src, dst.at[place.part], e_send.at[k], e_recv.at[k], across) for src, dst, k in entries
    ]
    out_x += [
        pltpu.make_async_copy(src, dst.at[place.part], e_recv.at[2 + k]) for src, dst, k in entries
    ]
    out_c = [
        remote(dst.at[two], dst.at[two], e_send.at[4 + k], e_recv.at[4 + k], other)
        for _, dst, k in entries
    ]
    small = []
    for k, (x, c) in enumerate(
        ((place.x, 1 - place.c), (1 - place.x, place.c), (1 - place.x, 1 - place.c))
    ):
        small.append(
            remote(
                small_src.at[:, :, c, x],
                small_in.at[k],
                e_send.at[6 + k],
                e_recv.at[6 + k],
                place.at(x=x, c=c),
            )
        )
    small.append(
        pltpu.make_async_copy(small_src.at[:, :, place.c, place.x], small_in.at[3], e_recv.at[9])
    )
    out_y = [
        remote(
            quarter.at[1 - place.y, pl.ds(2 * k, 2)],
            quarter_in.at[pl.ds(2 * k, 2)],
            e_send.at[10 + k],
            e_recv.at[10 + k],
            place.at(y=1 - place.y),
        )
        for k in range(2)
    ]

    place.greet()
    down0.start(0)
    down1.start(0)
    for copy in out_x + small:
        copy.start()

    def piece(z, y):
        base = ((z * 2 + y) * 4 + place.part) * n_code
        row = lax.broadcasted_iota(jnp.int32, (n_code, dp_ref.shape[0]), 0) + base

        def add(k, total):
            hot = jnp.where(row == codes_all[k], 1.0, 0.0).astype(BF)
            return total + jnp.dot(hot, dp_all[k], preferred_element_type=F32)

        total = lax.fori_loop(0, 4, add, jnp.zeros((n_code, dp_ref.shape[1]), F32))
        quarter[y, z, :n_code] = total.astype(BF)
        total = small_in[3, z, y].astype(F32)
        for k in range(3):
            total = total + small_in[k, z, y].astype(F32)
        quarter[y, z, n_code:] = total.astype(BF)

    def codebook_grad():
        def away(z, carry):
            piece(z, 1 - place.y)

            for k in range(2):

                @pl.when(z == 2 * k + 1)
                def _():
                    out_y[k].start()

            return carry

        def here(z, carry):
            piece(z, place.y)

            @pl.when(z == 0)
            def _():
                low.go(2)

            @pl.when(z == 2)
            def _():
                high.go(2)

            return carry

        lax.fori_loop(0, 4, away, 0)
        lax.fori_loop(0, 4, here, 0)

    def tick_down(i):
        @pl.when(i == 5)
        def _():
            down0.go(1)

        @pl.when(i == 6)
        def _():
            down1.go(1)

    def tick_low(dx):
        @pl.when(dx == 2)
        def _():
            down0.go(2)

    def tick_high(dx):
        @pl.when(dx == 1)
        def _():
            low.arrive(0)

    def tick_crop(i):
        @pl.when(i == 0)
        def _():
            low.start(1)

        @pl.when(i == 1)
        def _():
            high.go(1)
            for copy in out_x:
                copy.wait_recv()
            for copy in out_c:
                copy.start()

        @pl.when(i == 3)
        def _():
            down1.go(2)
            down0.go(3)
            for copy in out_c:
                copy.wait_recv()
            for copy in small:
                copy.wait_recv()
            codebook_grad()

        @pl.when(i == 4)
        def _():
            down1.go(3)
            down0.go(4)

        @pl.when(i == 6)
        def _():
            down0.go(5)
            down1.go(4)

        @pl.when(i == 7)
        def _():
            low.arrive(2)
            down1.go(5)

    down_input_grad(ds_ref, w_down_ref, din_ref, y32, tick_down)
    shift_all(din_ref, d3)
    conv_weight_grad(a_ref, d3, dw, 0, tick_low)
    low.start(0)
    conv_weight_grad(a_ref, d3, dw, 1, tick_high)
    high.start(0)
    unit_back(lambda i: c_ref[i], gains_ref, w_ref, dg_ref, d3, 2, din_ref, tick_crop)
    for copy in out_y:
        copy.wait_recv()
    for z in range(4):
        total = quarter[place.y, z].astype(F32) + quarter_in[z].astype(F32)
        rest_kept_ref[z] = total.astype(BF)
    high.arrive(2)
    down0.arrive(5)
    down1.arrive(5)
    for job in (down0, down1):
        job.sent(0, 6)
    for job in (low, high):
        job.sent(0, 3)
    for copy in out_x[:2] + out_c + small[:3] + out_y:
        copy.wait_send()


def second_back_call(n_code, ds, w_down, w, c_one, a_two, gains, codes, dp, down_src, small_src):
    crops, cells, ch = c_one.shape
    n_conv, lat = down_src.shape[-2], dp.shape[-1]
    n_rest = n_code + small_src.shape[-2]

    def shape(*dims, dtype=BF):
        return jax.ShapeDtypeStruct(dims, dtype)

    outs = [
        shape(crops, cells, ch),
        shape(2, ch, dtype=F32),
        shape(4, n_conv, ch // 2),
        shape(4, n_conv, ch // 2),
        shape(4, n_conv, ch // 2),
        shape(4, n_conv, ch // 2),
        shape(4, n_rest, lat),
    ]
    whole = Reduce.early(n_conv, ch // 2) + Reduce.late(n_conv, ch // 2, 1) + Reduce.sems()
    begun = Reduce.early(n_conv, ch // 2) + Reduce.sems()
    return pl.pallas_call(
        functools.partial(second_back_kernel, n_code),
        out_shape=outs,
        in_specs=[VM] * 8 + [ANY] * 2,
        out_specs=[VM] * 7,
        scratch_shapes=[
            pltpu.VMEM(w.shape, BF),
            pltpu.VMEM((crops, 18, 16, 3 * ch), BF),
            pltpu.VMEM((ch // 128, cells, 128), F32),
            pltpu.VMEM((4,) + dp.shape, BF),
            pltpu.VMEM((4,) + codes.shape, jnp.int32),
            pltpu.VMEM((2, 4, n_rest, lat), BF),
            pltpu.VMEM((4, n_rest, lat), BF),
            pltpu.VMEM((4, 4, 2, small_src.shape[-2], lat), BF),
            pltpu.SemaphoreType.DMA((12,)),
            pltpu.SemaphoreType.DMA((12,)),
        ]
        + whole * 2
        + begun * 2,
        compiler_params=pltpu.CompilerParams(
            vmem_limit_bytes=61 * MIB, collective_id=3, has_side_effects=True
        ),
        cost_estimate=pl.CostEstimate(flops=4 * 10**10, bytes_accessed=0, transcendentals=0),
    )(ds, w_down, w, c_one, a_two, gains, codes, dp, down_src, small_src)


def first_back_kernel(
    sizes,
    dc_ref,
    x_ref,
    gains_ref,
    w_ref,
    a_ref,
    kept0_ref,
    kept1_ref,
    rest_kept_ref,
    g_down0,
    g_down1,
    dg_two_ref,
    loss_ref,
    wt_ref,
    conv_row_ref,
    rest_row_ref,
    g_first0,
    g_first1,
    g_second0,
    g_second1,
    g_rest0,
    g_rest1,
    conv_new_ref,
    rest_new_ref,
    tv_ref,
    dw,
    d3,
    dg,
    vec,
    vec_in,
    tv_in,
    s_send,
    s_recv,
    *bufs,
):
    n_code, n_proj, n_head, rgb = sizes
    place = Place()
    bufs = list(bufs)

    def take(n):
        out = bufs[:n]
        del bufs[:n]
        return out

    half = rest_kept_ref.shape[-1] // 2
    ch = tv_ref.shape[1]
    view = dw.reshape(4, 2, 2, 2, dw.shape[0] // 32, ch)
    none = [None] * 4
    second0 = Reduce(place, None, g_second0, *none, kept0_ref, *take(3))
    second1 = Reduce(place, None, g_second1, *none, kept1_ref, *take(3))
    rest0 = Reduce(place, None, g_rest0, *none, rest_kept_ref.at[..., :half], *take(3))
    rest1 = Reduce(place, None, g_rest1, *none, rest_kept_ref.at[..., half:], *take(3))
    low = Reduce(place, view.at[..., : ch // 2], g_first0, *take(8))
    high = Reduce(place, view.at[..., ch // 2 :], g_first1, *take(8))
    late = (second0, second1, rest0, rest1)
    place.greet()
    for job in late:
        job.start(3)

    def tick_high(dx):
        @pl.when(dx == 1)
        def _():
            low.go(1)

        @pl.when(dx == 2)
        def _():
            second0.go(4)

    def tick_crop(i):
        @pl.when(i == 0)
        def _():
            second1.go(4)

        @pl.when(i == 1)
        def _():
            high.go(1)
            second0.go(5)

        @pl.when(i == 2)
        def _():
            low.go(2)

        @pl.when(i == 3)
        def _():
            second1.go(5)

        @pl.when(i == 5)
        def _():
            low.go(3)
            high.go(2)

        @pl.when(i == 6)
        def _():
            rest0.go(4)

        @pl.when(i == 7)
        def _():
            high.go(3)

    def v_of(i):
        return x_ref[i].astype(F32)

    shift_all(dc_ref, d3)
    conv_weight_grad(a_ref, d3, dw, 0)
    low.start(0)
    conv_weight_grad(a_ref, d3, dw, 1, tick_high)
    high.start(0)
    unit_back(v_of, gains_ref, w_ref, dg, d3, 0, None, tick_crop)
    vec[...] = jnp.zeros_like(vec)
    vec[0:2] = dg[...]
    vec[2:4] = dg_two_ref[...]
    vec[4:5] = loss_ref[0:1]
    small = [
        remote(vec, vec_in.at[k], s_send.at[k], s_recv.at[k], q)
        for k, q in enumerate(place.row_peers())
    ]
    for copy in small:
        copy.start()
    tv_ref[...] = jnp.zeros_like(tv_ref)
    for copy in small:
        copy.wait_recv()
    tv_ref[16:24, :] = vec[...] + vec_in[0] + vec_in[1] + vec_in[2]
    tv_ref[24:32, :] = wt_ref[...]

    def fold(parts, row, width):
        squares = [g.astype(F32) for g in parts]
        squares = [g * g for g in squares]
        total = sum(jnp.sum(q, axis=1, keepdims=True) for q in squares)
        new = 0.5 * row + 0.5 * (total / width + EPS_SQ)
        inverse = 1.0 / new
        col = [jnp.sum(q, axis=0, keepdims=True) for q in squares]
        over = [jnp.sum(q * inverse, axis=0, keepdims=True) for q in squares]
        return (
            new,
            jnp.concatenate(col, axis=1),
            jnp.concatenate(over, axis=1),
            jnp.sum(new, axis=0, keepdims=True),
        )

    def fold_conv(j, refs):
        for k in range(4):
            new, col, over, total = fold([r[k] for r in refs], conv_row_ref[j, k], ch)
            conv_new_ref[j, k] = new
            tv_ref[j : j + 1, :] += col
            tv_ref[3 + j : 4 + j, :] += over
            tv_ref[6 + j : 7 + j, :] += total

    def fold_rest():
        lat = 2 * half
        spans = ((0, n_code, lat), (n_code, n_proj, lat), (n_code + n_proj, n_head, rgb))
        for k in range(4):
            both = [r[k] for r in (g_rest0, g_rest1)]
            for m, (start, size, width) in enumerate(spans):
                parts = [v.astype(F32)[start : start + size] for v in both]
                row = rest_row_ref[k, start : start + size]
                new, col, over, total = fold(parts, row, width)
                rest_new_ref[k, start : start + size] = new
                tv_ref[9 + m : 10 + m, :lat] += col
                tv_ref[9 + m : 10 + m, lat:] += over
                tv_ref[12 + m : 13 + m, :] += total
            size = rest_row_ref.shape[1] - n_code - n_proj - n_head
            rest_new_ref[k, rest_row_ref.shape[1] - size :] = jnp.ones((size, 1), F32)

    rest0.go(5)
    fold_conv(2, [g_down0, g_down1])
    second0.arrive(5)
    second1.arrive(5)
    fold_conv(1, [g_second0, g_second1])
    rest1.go(4)
    rest0.arrive(5)
    rest1.go(5)
    low.go(4)
    rest1.arrive(5)
    fold_rest()
    low.go(5)
    high.go(4)
    low.arrive(5)
    high.go(5)
    high.arrive(5)
    fold_conv(0, [g_first0, g_first1])

    across = remote(tv_ref, tv_in.at[0], s_send.at[3], s_recv.at[3], place.at(y=1 - place.y))
    across.start()
    across.wait()
    tv_ref[...] += tv_in[0]
    along = [
        remote(tv_ref, tv_in.at[k], s_send.at[3 + k], s_recv.at[3 + k], q)
        for k, q in zip((1, 2, 3), place.z_peers())
    ]
    for copy in along:
        copy.start()
    for copy in along:
        copy.wait()
    tv_ref[...] += tv_in[1] + tv_in[2] + tv_in[3]
    for copy in small:
        copy.wait_send()
    for job in late:
        job.sent(3, 6)
    for job in (low, high):
        job.sent(0, 6)


def first_back_call(sizes, dc, x, gains, w, a_one, kept, g_down, dg_two, loss, wt, rows):
    crops, cells, ch = x.shape
    n_conv, n_rest = g_down[0].shape[-2], kept[2].shape[-2]

    def shape(*dims, dtype=BF):
        return jax.ShapeDtypeStruct(dims, dtype)

    conv_half = shape(4, n_conv, ch // 2)
    rest_half = shape(4, n_rest, 128)
    outs = [conv_half] * 4 + [rest_half] * 2
    outs += [shape(*v.shape, dtype=F32) for v in rows] + [shape(32, ch, dtype=F32)]
    args = [dc, x, gains, w, a_one, *kept, *g_down, dg_two, loss, wt, *rows]
    whole = Reduce.early(n_conv, ch // 2) + Reduce.late(n_conv, ch // 2, 1) + Reduce.sems()
    return pl.pallas_call(
        functools.partial(first_back_kernel, sizes),
        out_shape=outs,
        in_specs=[VM] * len(args),
        out_specs=[VM] * len(outs),
        scratch_shapes=[
            pltpu.VMEM(w.shape, BF),
            pltpu.VMEM((crops, 18, 16, 3 * ch), BF),
            pltpu.VMEM((2, ch), F32),
            pltpu.VMEM((8, ch), F32),
            pltpu.VMEM((3, 8, ch), F32),
            pltpu.VMEM((4, 32, ch), F32),
            pltpu.SemaphoreType.DMA((7,)),
            pltpu.SemaphoreType.DMA((7,)),
        ]
        + (Reduce.late(n_conv, ch // 2, 0) + Reduce.sems()) * 2
        + (Reduce.late(n_rest, 128, 0) + Reduce.sems()) * 2
        + whole * 2,
        compiler_params=pltpu.CompilerParams(
            vmem_limit_bytes=60 * MIB, collective_id=4, has_side_effects=True
        ),
        cost_estimate=pl.CostEstimate(flops=2 * 10**10, bytes_accessed=0, transcendentals=0),
    )(*args)


def finish_kernel(
    sizes,
    g_first0,
    g_first1,
    g_second0,
    g_second1,
    g_down0,
    g_down1,
    g_rest0,
    g_rest1,
    conv_ref,
    code_ref,
    proj_ref,
    head_ref,
    conv_row_ref,
    rest_row_ref,
    tv_ref,
    conv_col_ref,
    code_col_ref,
    proj_col_ref,
    head_col_ref,
    gains_ref,
    state_ref,
    loss_ref,
    conv_outs,
    rest_outs,
    gain_outs,
):
    n_code, n_proj, n_head, rgb, shards = sizes
    ch = conv_ref.shape[2]
    lat = code_ref.shape[1]

    def scales(col, col_sum, over, row_sum, weights, rows, width):
        rows = rows * shards
        col_new = 0.5 * col + 0.5 * (col_sum / rows + EPS_SQ)
        row_mean = row_sum / rows
        upd_sq = row_mean * jnp.sum(over / col_new, axis=1, keepdims=True)
        rms_u = jnp.sqrt(upd_sq / (rows * width))
        scale = jnp.sqrt(jnp.sum(weights, axis=1, keepdims=True) / (rows * width))
        factor = RATE * scale / jnp.maximum(1.0, rms_u)
        return col_new, factor * lax.rsqrt(col_new), row_mean

    def line(k):
        return tv_ref[k : k + 1, :]

    cg, cc, cn, cl = conv_outs
    for j, parts in enumerate(((g_first0, g_first1), (g_second0, g_second1), (g_down0, g_down1))):
        n = conv_ref.shape[1]
        col_new, q, row_mean = scales(
            conv_col_ref[j : j + 1, :], line(j), line(3 + j), line(6 + j)[:, :1], line(24 + j), n, ch
        )
        cc[j : j + 1, :] = col_new
        m = n // 4
        for k in range(4):
            r = lax.rsqrt(conv_row_ref[j, k] / row_mean)
            rows = slice(k * m, (k + 1) * m)
            for p, part in enumerate(parts):
                width = part.shape[2]
                lanes = slice(p * width, (p + 1) * width)
                g = part[k].astype(F32)
                new = conv_ref[j, rows, lanes] - g * r * q[:, lanes]
                cg[j, rows, lanes] = g
                cn[j, rows, lanes] = new
                cl[j, rows, lanes] = new.astype(BF)
    cols = (code_col_ref, proj_col_ref, head_col_ref)
    spans = ((0, n_code, lat), (n_code, n_proj, lat), (n_code + n_proj, n_head, rgb))
    for m, (w_ref, (start, size, width)) in enumerate(zip((code_ref, proj_ref, head_ref), spans)):
        og, oc, on, ol = rest_outs[m]
        col_new, q, row_mean = scales(
            cols[m][...],
            line(9 + m)[:, :lat],
            line(9 + m)[:, lat:],
            line(12 + m)[:, :1],
            line(27 + m)[:, :lat],
            w_ref.shape[0],
            width,
        )
        oc[...] = col_new
        news = []
        for k in range(4):
            g = jnp.concatenate([g_rest0[k].astype(F32), g_rest1[k].astype(F32)], axis=1)
            g = g[start : start + size]
            r = lax.rsqrt(rest_row_ref[k, start : start + size] / row_mean)
            rows = slice(k * size, (k + 1) * size)
            new = w_ref[rows, :] - g * r * q
            og[rows, :] = g
            on[rows, :] = new
            if size % 16:
                news.append(new)
            else:
                ol[rows, :] = new.astype(BF)
        if news:
            ol[...] = jnp.concatenate(news, axis=0).astype(BF)
    loss_ref[...] = jnp.sum(line(20), axis=1, keepdims=True)
    grad = tv_ref[16:20, :]
    state = 0.5 * state_ref[...] + 0.5 * (grad * grad + EPS_SQ)
    update = grad * lax.rsqrt(state)
    gains = gains_ref[...]

    def rms(v):
        return jnp.sqrt(
            jnp.sum(jnp.sum(v * v, axis=1, keepdims=True), axis=0, keepdims=True) / v.size
        )

    gain_outs[0][...] = grad
    gain_outs[1][...] = state
    gain_outs[2][...] = gains - RATE * rms(gains) * update / jnp.maximum(1.0, rms(update))


def finish_call(sizes, grads, weights, rows, tv, cols, gains, state):
    conv_w, code_w, proj_w, head_w = weights
    lat = code_w.shape[1]

    def shape(dims, dtype=F32):
        return jax.ShapeDtypeStruct(dims, dtype)

    def matrix(w, col):
        return [shape(w.shape), shape(col), shape(w.shape), shape(w.shape, BF)]

    outs = [shape((1, 1)), matrix(conv_w, (3, conv_w.shape[2]))]
    outs += [[matrix(w, (1, lat)) for w in (code_w, proj_w, head_w)]]
    outs += [[shape(gains.shape)] * 3]
    args = [*grads, *weights, *rows, tv, *cols, gains, state]
    return pl.pallas_call(
        functools.partial(finish_kernel, sizes),
        out_shape=outs,
        in_specs=[VM] * len(args),
        out_specs=jax.tree.map(lambda _: VM, outs),
        compiler_params=pltpu.CompilerParams(vmem_limit_bytes=56 * MIB),
        cost_estimate=pl.CostEstimate(flops=10**7, bytes_accessed=2 * 10**7, transcendentals=0),
    )(*args)


def contract_last(left, right):
    return lax.dot_general(left, right, (((1,), (0,)), ((), ())), preferred_element_type=F32)


def contract_back(left, right):
    return lax.dot_general(left, right, (((1,), (1,)), ((), ())), preferred_element_type=F32)


def contract_rows(left, right):
    return lax.dot_general(left, right, (((0,), (0,)), ((), ())), preferred_element_type=F32)


def row_part(grad, row):
    g_sq = grad * grad + EPS_SQ
    row_new = 0.5 * row + 0.5 * jnp.mean(g_sq, axis=2)
    over_row = jnp.sum(grad * grad / row_new[:, :, None], axis=0)
    return row_new, jnp.sum(g_sq, axis=0), jnp.sum(row_new, axis=0), over_row


def finish(grad, weight, row_new, col, col_sum, row_sum, over_row, wt_sq):
    total = grad.shape[0] * lax.axis_size("batch")
    count = total * grad.shape[2]
    col_new = 0.5 * col + 0.5 * col_sum / total
    row_mean = row_sum / total
    upd_sq = row_mean * jnp.sum(over_row / col_new, axis=1)
    rms_u = jnp.sqrt(upd_sq / count)
    scale = jnp.sqrt(wt_sq / count)
    vhat = row_new[:, :, None] * col_new[None] / row_mean[None, :, None]
    update = grad * lax.rsqrt(vhat)
    new = weight - RATE * (scale / jnp.maximum(1.0, rms_u))[None, :, None] * update
    return col_new, new


def local_any(
    features,
    target,
    mask,
    codes,
    conv_w,
    proj_w,
    code_w,
    head_w,
    gains,
    conv_row,
    conv_col,
    proj_row,
    proj_col,
    code_row,
    code_col,
    head_row,
    head_col,
    gain_state,
):
    ranks = lax.axis_size("rows")
    shards = lax.axis_size("batch")
    me = lax.axis_index("rows")
    crops_all = features.shape[0] * shards
    ch = features.shape[3]
    lat = proj_w.shape[1]
    rgb = head_w.shape[1]
    height = features.shape[1] * ranks
    width = features.shape[2]

    def whole_crops(v):
        return lax.all_to_all(v, "rows", split_axis=0, concat_axis=1, tiled=True)

    def my_part(v):
        size = v.shape[0] // ranks
        return lax.dynamic_slice_in_dim(v, me * size, size, 0)

    conv_piece = jnp.transpose(my_part(conv_w).astype(BF), (1, 0, 2))
    head_wide = jnp.pad(head_w, ((0, 0), (0, lat - rgb)))
    rest_piece = jnp.concatenate(
        [my_part(code_w).astype(BF), my_part(proj_w).astype(BF), my_part(head_wide).astype(BF)]
    )
    n_code, n_proj, n_head = (v.shape[0] // ranks for v in (code_w, proj_w, head_w))
    w_all = [lax.all_gather(conv_piece[0], BOTH, axis=0, tiled=True)]
    later = lax.all_gather(conv_piece[1:], BOTH, axis=0)
    later = jnp.transpose(later, (1, 0, 2, 3)).reshape(2, -1, ch)
    w_all += [later[0], later[1]]
    rest = lax.all_gather(rest_piece, BOTH, axis=0)
    code_all = rest[:, :n_code].reshape(-1, lat)
    proj_all = rest[:, n_code : n_code + n_proj].reshape(-1, lat)
    head_all = rest[:, n_code + n_proj :, :rgb].reshape(-1, rgb)

    x = whole_crops(features)
    target, mask, codes = whole_crops(target), whole_crops(mask), whole_crops(codes)
    crops = x.shape[0]
    cells = height * width
    x = x.reshape(crops, cells, ch)
    lat_cells = crops * cells // 4
    target = target.reshape(lat_cells, rgb)
    mask = mask.reshape(lat_cells, -1)
    codes = codes.reshape(lat_cells, -1)

    conv_flops = 2 * crops * cells * 9 * ch * ch
    three = pltpu.VMEM((18, 16, 3 * ch), BF)
    fold = pltpu.VMEM((ch // 128, cells, 128), F32)

    def big(dtype):
        return jax.ShapeDtypeStruct((crops, cells, ch), dtype)

    dw_shape = jax.ShapeDtypeStruct((9 * ch, ch), BF)
    dg_shape = jax.ShapeDtypeStruct((2, ch), F32)

    a_one, c_one = kernel_call(
        first_conv_kernel, [big(BF), big(F32)], [three], conv_flops, x, gains, w_all[0]
    )
    a_two, windows, s_low = kernel_call(
        second_conv_kernel,
        [
            big(BF),
            jax.ShapeDtypeStruct((lat_cells, 9 * ch), BF),
            jax.ShapeDtypeStruct((lat_cells, ch), BF),
        ],
        [three, fold],
        conv_flops,
        c_one,
        x,
        gains,
        w_all[1],
        w_all[2],
    )

    lat_count = crops_all * cells // 4 * lat
    pix_count = crops_all * cells * 3
    latent = contract_last(s_low, proj_all)
    picked = code_all[codes].astype(F32)
    cum = jnp.cumsum(picked, axis=1)
    resid = latent[:, None, :] - cum
    quant_part = (1.0 + BETA) * jnp.sum(resid * resid) / lat_count
    zq_low = cum[:, -1].astype(BF)
    pred = contract_last(zq_low, head_all)
    diff = pred - target
    weight_mask = jnp.repeat(mask.astype(F32), 3, axis=-1)
    smooth = jnp.sqrt(diff * diff + 1.0)
    recon_part = jnp.sum(weight_mask * (smooth - 1.0)) / pix_count
    d_pred = (weight_mask * (diff / smooth) / pix_count).astype(BF)
    d_head = contract_rows(zq_low, d_pred)
    d_zq = contract_back(d_pred, head_all)
    d_cum = -2.0 / lat_count * resid
    d_picked = jnp.flip(jnp.cumsum(jnp.flip(d_cum, 1), axis=1), 1)
    d_code = jax.ops.segment_sum(
        d_picked.reshape(-1, lat), codes.reshape(-1), num_segments=code_all.shape[0]
    )
    d_lat_low = (jnp.sum(resid, axis=1) * (2.0 * BETA / lat_count) + d_zq).astype(BF)
    d_proj = contract_rows(s_low, d_lat_low)
    d_s_low = contract_back(d_lat_low, proj_all).astype(BF)

    d_c_two, d_down = kernel_call(
        down_back_kernel,
        [big(BF), dw_shape],
        [fold],
        conv_flops // 2,
        d_s_low,
        windows,
        w_all[2],
    )
    d_three = pltpu.VMEM((crops, 18, 16, 3 * ch), BF)
    d_c_one, d_second, gain_two = kernel_call(
        functools.partial(unit_back_kernel, row=2, inner=True),
        [big(BF), dw_shape, dg_shape],
        [d_three],
        2 * conv_flops,
        d_c_two,
        c_one,
        gains,
        w_all[1],
        a_two,
    )
    d_first, gain_one = kernel_call(
        functools.partial(unit_back_kernel, row=0, inner=False),
        [dw_shape, dg_shape],
        [d_three],
        2 * conv_flops,
        d_c_one,
        x,
        gains,
        w_all[0],
        a_one,
    )
    d_gains = jnp.concatenate([gain_one, gain_two], axis=0)

    devices = ranks * shards

    def to_owner(v):
        return lax.psum_scatter(v, BOTH, scatter_dimension=0, tiled=True)

    def to_rows(v):
        return lax.all_gather(v, "rows", axis=0)

    pad = jnp.pad(d_head, ((0, 0), (0, lat - rgb)))
    rest_grad = jnp.concatenate(
        [v.astype(BF).reshape(devices, -1, lat) for v in (d_code, d_proj, pad)], axis=1
    )
    rest_mine = to_owner(rest_grad.reshape(-1, lat))
    conv_mine = [to_owner(v) for v in (d_first, d_second, d_down)]
    rest_full = to_rows(rest_mine).astype(F32)
    conv_full = to_rows(jnp.stack(conv_mine)).astype(F32)
    g_conv = jnp.transpose(conv_full, (0, 2, 1, 3)).reshape(-1, 3, ch)
    g_code = rest_full[:, :n_code].reshape(-1, lat)
    g_proj = rest_full[:, n_code : n_code + n_proj].reshape(-1, lat)
    g_head = rest_full[:, n_code + n_proj :, :rgb].reshape(-1, rgb)

    mats = [
        (g_conv, conv_w, conv_row, conv_col),
        (g_proj[:, None, :], proj_w[:, None, :], proj_row[:, None], proj_col[None, :]),
        (g_code[:, None, :], code_w[:, None, :], code_row[:, None], code_col[None, :]),
        (g_head[:, None, :], head_w[:, None, :], head_row[:, None], head_col[None, :]),
    ]
    rows_new = [row_part(grad, row) for grad, weight, row, col in mats]
    wt_sq = [jnp.sum(weight * weight, axis=(0, 2)) for grad, weight, row, col in mats]
    sums = lax.psum([r[1:] + (w,) for r, w in zip(rows_new, wt_sq)], "batch")
    loss, g_gain = lax.psum((recon_part + quant_part, d_gains), BOTH)
    done = [
        finish(m[0], m[1], r[0], m[3], *s) for m, r, s in zip(mats, rows_new, sums)
    ]

    state_new = 0.5 * gain_state + 0.5 * (g_gain * g_gain + EPS_SQ)
    update = g_gain * lax.rsqrt(state_new)
    rms_u = jnp.sqrt(jnp.mean(update * update))
    scale = jnp.sqrt(jnp.mean(gains * gains))
    gains_new = gains - RATE * scale * update / jnp.maximum(1.0, rms_u)
    conv_new = done[0][1]
    proj_new, code_new, head_new = (d[1][:, 0, :] for d in done[1:])
    return (
        loss,
        g_conv,
        rows_new[0][0],
        done[0][0],
        conv_new,
        conv_new.astype(BF),
        g_proj,
        rows_new[1][0][:, 0],
        done[1][0][0],
        proj_new,
        proj_new.astype(BF),
        g_code,
        rows_new[2][0][:, 0],
        done[2][0][0],
        code_new,
        code_new.astype(BF),
        g_head,
        rows_new[3][0][:, 0],
        done[3][0][0],
        head_new,
        head_new.astype(BF),
        g_gain,
        state_new,
        gains_new,
    )


def local_fast(
    features,
    target,
    mask,
    codes,
    conv_w,
    proj_w,
    code_w,
    head_w,
    gains,
    conv_row,
    conv_col,
    proj_row,
    proj_col,
    code_row,
    code_col,
    head_row,
    head_col,
    gain_state,
):
    ranks = lax.axis_size("rows")
    shards = lax.axis_size("batch")
    crops_all = features.shape[0] * shards
    crops = features.shape[0] // ranks
    ch = features.shape[3]
    cells = features.shape[1] * ranks * features.shape[2]
    lat, rgb = proj_w.shape[1], head_w.shape[1]
    lat_cells = crops * cells // 4
    n_code, n_proj, n_head = (v.shape[0] // ranks for v in (code_w, proj_w, head_w))
    sizes = (n_code, n_proj, n_head, rgb)
    conv_rows = jnp.transpose(conv_w, (1, 0, 2))
    head_wide = jnp.pad(head_w, ((0, 0), (0, lat - rgb)))

    def lanes(v, n):
        return jnp.pad(v, ((0, 0),) * (v.ndim - 1) + ((0, n - v.shape[-1]),))

    side = [lanes(target, 16), lanes(jnp.repeat(mask.astype(F32), 3, axis=-1), 16)]
    side = lanes(jnp.concatenate(side + [codes.astype(F32)], axis=-1), 128)
    out = forward_call(
        features.reshape(ranks, crops, -1, ch),
        side.reshape(ranks, crops, -1, 128),
        conv_rows,
        code_w,
        proj_w,
        head_wide,
        gains,
    )
    x = out[0].reshape(crops, cells, ch)
    side = out[1].reshape(lat_cells, 128)
    w_all, rest = out[2:5], out[5]
    a_one, c_one, a_two, windows, s_low, wt = out[6:]
    codes = jnp.transpose(side[:, 32:36]).astype(jnp.int32).reshape(-1)
    n_rest = rest.shape[-2]
    d_s, loss, dp, d_small, d_down = quantizer_call(
        codes,
        rest.reshape(-1, n_rest, lat),
        side,
        s_low,
        windows,
        crops_all * cells // 4 * lat,
        crops_all * cells * 3,
        rgb,
        n_code,
    )

    def shards_of(v):
        return v.reshape(4, 2, 2, 2, -1, v.shape[-1])

    d_c_one, dg_two, g_down0, g_down1, *kept = second_back_call(
        n_code,
        d_s,
        w_all[2],
        w_all[1],
        c_one,
        a_two,
        gains,
        codes[None],
        dp,
        shards_of(d_down),
        d_small.reshape(4, 2, 2, 2, -1, lat),
    )
    conv_row4 = jnp.transpose(conv_row).reshape(3, 4, -1, 1)
    rest_row4 = [v.reshape(4, -1) for v in (code_row, proj_row, head_row)]
    rest_row4.append(jnp.ones((4, n_rest - n_code - n_proj - n_head), F32))
    rest_row4 = jnp.concatenate(rest_row4, axis=1)[:, :, None]
    out = first_back_call(
        sizes,
        d_c_one,
        x,
        gains,
        w_all[0],
        a_one,
        kept,
        (g_down0, g_down1),
        dg_two,
        loss,
        wt,
        (conv_row4, rest_row4),
    )
    conv_rn, rest_rn, tv = out[6:]
    head_col_wide = jnp.pad(head_col, (0, lat - rgb), constant_values=1.0)
    loss, conv_outs, rest_outs, gain_outs = finish_call(
        sizes + (shards,),
        (*out[:4], g_down0, g_down1, *out[4:6]),
        (conv_rows, code_w, proj_w, head_wide),
        (conv_rn, rest_rn),
        tv,
        (conv_col, code_col[None], proj_col[None], head_col_wide[None]),
        gains,
        gain_state,
    )
    conv_g, conv_c, conv_n, conv_l = conv_outs
    code_o, proj_o, head_o = rest_outs
    cuts = (n_code, n_code + n_proj, n_code + n_proj + n_head)
    code_r, proj_r, head_r = (
        v.reshape(-1) for v in jnp.split(rest_rn[:, :, 0], cuts, axis=1)[:3]
    )

    def back(v):
        return jnp.transpose(v, (1, 0, 2))

    return (
        loss[0, 0],
        back(conv_g),
        jnp.transpose(conv_rn.reshape(3, -1)),
        conv_c,
        back(conv_n),
        back(conv_l),
        proj_o[0],
        proj_r,
        proj_o[1][0],
        proj_o[2],
        proj_o[3],
        code_o[0],
        code_r,
        code_o[1][0],
        code_o[2],
        code_o[3],
        head_o[0][:, :rgb],
        head_r,
        head_o[1][0, :rgb],
        head_o[2][:, :rgb],
        head_o[3][:, :rgb],
        *gain_outs,
    )


def solution(mesh):
    cell = P("batch", "rows", None, None)
    mat, vec = P("batch", None), P("batch")
    placed = (cell,) * 4 + (P("batch", None, None), mat, mat, mat, P())
    placed += (mat, P()) + (vec, P()) * 3 + (P(),)
    conv_outs = (P("batch", None, None), mat, P(), P("batch", None, None), P("batch", None, None))
    mat_outs = (mat, vec, P(), mat, mat)
    fast = (mesh.shape["rows"], mesh.shape["batch"]) == (4, 8)
    return jax.shard_map(
        local_fast if fast else local_any,
        mesh=mesh,
        in_specs=placed,
        out_specs=(P(),) + conv_outs + mat_outs * 3 + (P(),) * 3,
        check_vma=False,
    )
```

```python
import functools

import jax
import jax.numpy as jnp
from jax import lax
from jax.experimental import pallas as pl
from jax.experimental.pallas import tpu as pltpu
from jax.sharding import PartitionSpec as P

GROUPS = 32
BETA = 0.25
RATE = 0.5
EPS_NORM = 1e-05
EPS_SQ = 1e-30
BF = jnp.bfloat16
F32 = jnp.float32
BOTH = ("batch", "rows")
MIB = 1 << 20
VM = pl.BlockSpec(memory_space=pltpu.VMEM)
ANY = pl.BlockSpec(memory_space=pl.ANY)
MESH = pl.DeviceIdType.MESH


def group_sum(v):
    lane = lax.broadcasted_iota(jnp.int32, v.shape, 1)
    width = v.shape[1]
    for k in (1, 2, 4, 8):
        up = pltpu.roll(v, k, 1)
        down = pltpu.roll(v, width - k, 1)
        v = v + jnp.where((lane & k) != 0, up, down)
    return v


def moments(v):
    count = v.shape[0] * (v.shape[1] // GROUPS)
    sums = jnp.concatenate(
        [jnp.sum(v, axis=0, keepdims=True), jnp.sum(v * v, axis=0, keepdims=True)]
        + [jnp.zeros((6, v.shape[1]), F32)],
        axis=0,
    )
    sums = group_sum(sums) / count
    mean = sums[0:1]
    return mean, lax.rsqrt(sums[1:2] - mean * mean + EPS_NORM)


def shifted(v, by):
    cells = v.shape[0]
    col = lax.broadcasted_iota(jnp.int32, v.shape, 0) & 15
    edge = 0 if by == 1 else 15
    return jnp.where(col == edge, 0.0, pltpu.roll(v, by % cells, 0))


def fill_three(dst, left, mid, right):
    ch = mid.shape[1]
    for k, v in enumerate((left, mid, right)):
        dst[1:17, :, k * ch : (k + 1) * ch] = v.astype(BF).reshape(16, 16, ch)


def zero_edges(dst):
    dst[0] = jnp.zeros(dst.shape[1:], dst.dtype)
    dst[17] = jnp.zeros(dst.shape[1:], dst.dtype)


def put_lanes(dst, rows, v):
    for k in range(dst.shape[0]):
        dst[k, rows, :] = v[:, k * 128 : (k + 1) * 128]


def get_lanes(src, rows):
    return jnp.concatenate([src[k, rows, :] for k in range(src.shape[0])], axis=1)


def conv_rows(src, w_ref):
    acc = None
    width = src.shape[2]
    for dy in range(3):
        lhs = src[dy : dy + 16].reshape(256, width)
        d = jnp.dot(lhs, w_ref[dy * width : (dy + 1) * width, :], preferred_element_type=F32)
        acc = d if acc is None else acc + d
    return acc


def conv_rows_back(src, w_ref):
    acc = None
    ch = src.shape[2] // 3
    for dy in range(3):
        for dx in range(3):
            lhs = src[2 - dy : 18 - dy, :, dx * ch : (dx + 1) * ch].reshape(256, ch)
            t = (dy * 3 + dx) * ch
            d = lax.dot_general(
                lhs, w_ref[t : t + ch, :], (((1,), (1,)), ((), ())), preferred_element_type=F32
            )
            acc = d if acc is None else acc + d
    return acc


def conv_weight_grad(a_ref, d3_ref, dw_ref, half, tick=None):
    crops, cells, ch = a_ref.shape
    nb = 256
    out = slice(half * nb, (half + 1) * nb)

    def block(dx, carry):
        if tick is not None:
            tick(dx)
        lane = pl.multiple_of(dx * ch + half * nb, nb)
        for dy in range(3):
            rhs = d3_ref[:, 2 - dy : 18 - dy, :, pl.ds(lane, nb)].reshape(crops * cells, nb)
            d = lax.dot_general(
                a_ref[...].reshape(crops * cells, ch),
                rhs,
                (((0,), (0,)), ((), ())),
                preferred_element_type=F32,
            )
            row = pl.multiple_of((dy * 3 + dx) * ch, ch)
            dw_ref[pl.ds(row, ch), out] = d.astype(dw_ref.dtype)
        return carry

    lax.fori_loop(0, 3, block, 0)


def silu(h):
    return h * jax.nn.sigmoid(h)


def first_crop(v, gains_ref, w_ref, a3):
    mean, rstd = moments(v)
    a = silu((v - mean) * rstd * gains_ref[0:1, :] + gains_ref[1:2, :])
    fill_three(a3, shifted(a, 1), a, shifted(a, -1))
    return a.astype(BF), conv_rows(a3, w_ref)


def second_crop(v, x, gains_ref, w_ref, l_ref, a3, y32):
    ch = v.shape[1]
    mean, rstd = moments(v)
    a = silu((v - mean) * rstd * gains_ref[2:3, :] + gains_ref[3:4, :])
    fill_three(a3, shifted(a, 1), a, shifted(a, -1))
    put_lanes(y32, slice(None), conv_rows(a3, w_ref) + x)
    even = get_lanes(y32, pl.ds(0, 128, stride=2))
    odd = get_lanes(y32, pl.ds(1, 128, stride=2))
    cell = lax.broadcasted_iota(jnp.int32, odd.shape, 0) & 7
    before = jnp.where(cell == 0, 0.0, pltpu.roll(odd, 1, 0))
    for dx, part in enumerate((before, even, odd)):
        part = part.reshape(8, 2, 8, ch)
        upper = part[:, 0].reshape(64, ch)
        lower = part[:, 1].reshape(64, ch)
        above = jnp.concatenate([jnp.zeros((8, ch), F32), lower[:56]], axis=0)
        for dy, rows in enumerate((above, upper, lower)):
            lane = (dy * 3 + dx) * ch
            l_ref[:, lane : lane + ch] = rows.astype(BF)
    return a.astype(BF)


def down_dot(l_ref, w_ref, s_ref):
    ch = s_ref.shape[1]
    nb = 256

    def block(j, carry):
        lane = pl.ds(pl.multiple_of(j * nb, nb), nb)
        d = jnp.dot(l_ref[...], w_ref[:, lane], preferred_element_type=F32)
        s_ref[:, lane] = d.astype(BF)
        return carry

    lax.fori_loop(0, ch // nb, block, 0)


def crop_rows(i):
    return pl.ds(pl.multiple_of(i * 64, 64), 64)


def first_conv_kernel(x_ref, gains_ref, w_ref, a_ref, c_ref, a3):
    zero_edges(a3)

    def crop(i, carry):
        a_ref[i], c_ref[i] = first_crop(x_ref[i].astype(F32), gains_ref, w_ref, a3)
        return carry

    lax.fori_loop(0, x_ref.shape[0], crop, 0)


def second_conv_kernel(c_in_ref, x_ref, gains_ref, w_ref, w_down_ref, a_ref, l_ref, s_ref, a3, y32):
    zero_edges(a3)

    def crop(i, carry):
        a_ref[i] = second_crop(
            c_in_ref[i],
            x_ref[i].astype(F32),
            gains_ref,
            w_ref,
            l_ref.at[crop_rows(i)],
            a3,
            y32,
        )
        return carry

    lax.fori_loop(0, x_ref.shape[0], crop, 0)
    down_dot(l_ref, w_down_ref, s_ref)


def down_input_grad(ds_ref, w_ref, dc_ref, y32, tick=None):
    cells, ch = ds_ref.shape
    crops = cells // 64

    def dot_t(lhs, tap):
        return lax.dot_general(
            lhs.astype(BF),
            w_ref[tap * ch : (tap + 1) * ch, :],
            (((1,), (1,)), ((), ())),
            preferred_element_type=F32,
        )

    def crop(i, carry):
        if tick is not None:
            tick(i)
        here = ds_ref[pl.ds(pl.multiple_of(i * 64, 64), 64), :].astype(F32)
        at = lax.broadcasted_iota(jnp.int32, here.shape, 0)

        def next_col(v):
            return jnp.where((at & 7) == 7, 0.0, pltpu.roll(v, 63, 0))

        right = next_col(here)
        under = jnp.concatenate([here[8:], jnp.zeros((8, ch), F32)], axis=0)
        corner = next_col(under)
        ee = dot_t(here, 4)
        eo = dot_t(here, 5) + dot_t(right, 3)
        oe = dot_t(here, 7) + dot_t(under, 1)
        oo = dot_t(here, 8) + dot_t(right, 6) + dot_t(under, 2) + dot_t(corner, 0)

        def both_rows(top, bottom):
            top, bottom = top.reshape(8, 1, 8, ch), bottom.reshape(8, 1, 8, ch)
            return jnp.concatenate([top, bottom], axis=1).reshape(128, ch)

        put_lanes(y32, pl.ds(0, 128, stride=2), both_rows(ee, oe))
        put_lanes(y32, pl.ds(1, 128, stride=2), both_rows(eo, oo))
        dc_ref[i] = get_lanes(y32, slice(None)).astype(BF)
        return carry

    lax.fori_loop(0, crops, crop, 0)


def down_weight_grad(l_ref, ds_ref, dw_ref):
    ch = ds_ref.shape[1]

    def block(t, carry):
        lane = pl.multiple_of(t * ch, ch)
        d = lax.dot_general(
            l_ref[:, pl.ds(lane, ch)],
            ds_ref[...],
            (((0,), (0,)), ((), ())),
            preferred_element_type=F32,
        )
        dw_ref[pl.ds(lane, ch), :] = d.astype(BF)
        return carry

    lax.fori_loop(0, 9, block, 0)


def down_back_kernel(ds_ref, l_ref, w_ref, dc_ref, dw_ref, y32):
    down_weight_grad(l_ref, ds_ref, dw_ref)
    down_input_grad(ds_ref, w_ref, dc_ref, y32)


def hidden_grad(v, gain, shift, d_act):
    mean, rstd = moments(v)
    vhat = (v - mean) * rstd
    h = vhat * gain + shift
    sig = jax.nn.sigmoid(h)
    return d_act * sig * (1.0 + h * (1.0 - sig)), vhat, rstd


def shift_all(dc_ref, d3, tick=None):
    def crop(i, carry):
        if tick is not None:
            tick(i)
        d = dc_ref[i].astype(F32)
        slot = d3.at[i]
        zero_edges(slot)
        fill_three(slot, shifted(d, -1), d, shifted(d, 1))
        return carry

    lax.fori_loop(0, dc_ref.shape[0], crop, 0)


def unit_back(v_of, gains_ref, w_ref, dg_ref, d3, row, din_ref=None, tick=None):
    crops, cells, ch = d3.shape[0], 256, d3.shape[3] // 3
    dg_ref[...] = jnp.zeros_like(dg_ref)

    def crop(i, carry):
        if tick is not None:
            tick(i)
        d_act = conv_rows_back(d3.at[i], w_ref)
        gain = gains_ref[row : row + 1, :]
        hg, vhat, rstd = hidden_grad(v_of(i), gain, gains_ref[row + 1 : row + 2, :], d_act)
        one = jnp.sum(hg * vhat, axis=0, keepdims=True)
        two = jnp.sum(hg, axis=0, keepdims=True)
        dg_ref[0:1, :] += one
        dg_ref[1:2, :] += two
        if din_ref is not None:
            count = cells * (ch // GROUPS)
            sums = jnp.concatenate([two * gain, one * gain, jnp.zeros((6, ch), F32)], axis=0)
            sums = group_sum(sums) / count
            din_ref[i] = (rstd * (hg * gain - sums[0:1] - vhat * sums[1:2])).astype(BF)
        return carry

    lax.fori_loop(0, crops, crop, 0)


def unit_back_kernel(dc_ref, v_ref, gains_ref, w_ref, a_ref, *outs, row, inner):
    if inner:
        din_ref, dw_ref, dg_ref, d3 = outs
    else:
        dw_ref, dg_ref, d3 = outs
        din_ref = None

    def v_of(i):
        return v_ref[i].astype(F32)

    shift_all(dc_ref, d3)
    unit_back(v_of, gains_ref, w_ref, dg_ref, d3, row, din_ref)
    for half in range(2):
        conv_weight_grad(a_ref, d3, dw_ref, half)


def kernel_call(body, outs, scratch, flops, *args):
    bytes_accessed = sum(a.size * a.dtype.itemsize for a in args)
    bytes_accessed += sum(o.size * o.dtype.itemsize for o in outs)
    return pl.pallas_call(
        body,
        out_shape=outs,
        in_specs=[VM] * len(args),
        out_specs=[VM] * len(outs),
        scratch_shapes=scratch,
        compiler_params=pltpu.CompilerParams(vmem_limit_bytes=56 * MIB),
        cost_estimate=pl.CostEstimate(
            flops=flops, bytes_accessed=bytes_accessed, transcendentals=0
        ),
    )(*args)


class Place:
    def __init__(self):
        rows, batch = lax.axis_index("rows"), lax.axis_index("batch")
        self.x, self.c = rows // 2, rows % 2
        self.z, self.y = batch // 2, batch % 2
        self.part = self.c * 2 + self.x

    def at(self, x=None, c=None, z=None, y=None):
        x = self.x if x is None else x
        c = self.c if c is None else c
        z = self.z if z is None else z
        y = self.y if y is None else y
        return {"rows": 2 * x + c, "batch": 2 * z + y}

    def row_peers(self):
        return [
            self.at(c=1 - self.c),
            self.at(x=1 - self.x),
            self.at(x=1 - self.x, c=1 - self.c),
        ]

    def z_peers(self):
        return [self.at(z=(self.z + d) % 4) for d in (1, 2, 3)]

    def greet(self):
        barrier = pltpu.get_barrier_semaphore()
        peers = self.row_peers() + self.z_peers() + [self.at(y=1 - self.y)]
        for peer in peers:
            pl.semaphore_signal(barrier, inc=1, device_id=peer, device_id_type=MESH)
        pl.semaphore_wait(barrier, len(peers))


def remote(src, dst, send, recv, peer):
    return pltpu.make_async_remote_copy(
        src_ref=src, dst_ref=dst, send_sem=send, recv_sem=recv, device_id=peer, device_id_type=MESH
    )


class Gather:
    def __init__(self, place, src, dst, send, recv, route):
        self.p, self.src, self.dst, self.send, self.recv = place, src, dst, send, recv
        self.route = "z" + route + "c"
        self.steps = len(self.route)

    def copies(self, step):
        p, src, dst, send, recv = self.p, self.src, self.dst, self.send, self.recv
        axis = self.route[step]
        if axis == "z":
            mine = (p.c, p.x) if "x" in self.route else (p.c,)
            here, there = src.at[mine], dst.at[(p.z, p.y) + mine]
            out = [
                remote(here, there, send.at[k], recv.at[k], q) for k, q in enumerate(p.z_peers())
            ]
            return out + [pltpu.make_async_copy(here, there, recv.at[6])]
        have_y = "y" in self.route[:step]
        have_x = "x" in self.route[:step] or "x" not in self.route
        part = dst.at[:, slice(None) if have_y else p.y, p.c]
        if not have_x:
            part = dst.at[:, slice(None) if have_y else p.y, p.c, p.x]
        k = 3 + "yxc".index(axis)
        peer = {"y": p.at(y=1 - p.y), "x": p.at(x=1 - p.x), "c": p.at(c=1 - p.c)}[axis]
        return [remote(part, part, send.at[k], recv.at[k], peer)]

    def start(self, step):
        for copy in self.copies(step):
            copy.start()

    def arrive(self, step):
        for copy in self.copies(step):
            copy.wait_recv()

    def go(self, step):
        self.arrive(step - 1)
        self.start(step)

    def finish(self):
        for step in range(self.steps):
            for copy in self.copies(step):
                if copy.is_remote:
                    copy.wait_send()


class Reduce:
    steps = 6

    def __init__(self, place, src, out, mine, one, two, three, kept, four, send, recv, turn=True):
        self.p, self.src, self.out = place, src, out
        self.mine, self.one, self.two, self.three, self.four = mine, one, two, three, four
        self.send, self.recv = send, recv
        first_x = (place.c == 0) & turn
        self.turn = turn
        self.f = jnp.where(first_x, place.x, place.y)
        self.g = jnp.where(first_x, place.y, place.x)
        self.f_peer = place.at(
            x=jnp.where(first_x, 1 - place.x, place.x), y=jnp.where(first_x, place.y, 1 - place.y)
        )
        self.g_peer = place.at(
            x=jnp.where(first_x, place.x, 1 - place.x), y=jnp.where(first_x, 1 - place.y, place.y)
        )
        self.slot = 2 * self.f + self.g
        self.kept = kept

    @staticmethod
    def early(rows, lanes):
        return [pltpu.VMEM(lead + (rows, lanes), BF) for lead in ((4, 4), (4, 4), (2, 4), (4,))]

    @staticmethod
    def late(rows, lanes, kept):
        return [pltpu.VMEM(lead + (rows, lanes), BF) for lead in ((4,),) * kept + ((3,),)]

    @staticmethod
    def sems():
        return [pltpu.SemaphoreType.DMA((11,)), pltpu.SemaphoreType.DMA((15,))]

    def copies(self, step):
        p, src, mine, send, recv = self.p, self.src, self.mine, self.send, self.recv
        if step == 0:
            out = []
            for k in range(4):
                y, x = k // 2, k % 2
                there = jnp.where((p.c == 1) & self.turn, 2 * x + y, 2 * y + x)
                here = jnp.where((p.c == 0) & self.turn, 2 * x + y, 2 * y + x)
                part = src.at[:, y, 1 - p.c, x]
                peer = p.at(c=1 - p.c)
                out.append(remote(part, self.one.at[there], send.at[k], recv.at[k], peer))
                local = src.at[:, y, p.c, x]
                out.append(pltpu.make_async_copy(local, mine.at[here], recv.at[10 + k]))
            return out
        if step == 1:
            part = mine.at[pl.ds(2 * (1 - self.f), 2)]
            return [remote(part, self.two, send.at[4], recv.at[4], self.f_peer)]
        if step == 2:
            part = mine.at[2 * self.f + 1 - self.g]
            return [remote(part, self.three, send.at[5], recv.at[5], self.g_peer)]
        if step == 3:
            out = []
            for d, peer in zip((1, 2, 3), p.z_peers()):
                part = self.kept.at[(p.z + d) % 4]
                out.append(remote(part, self.four.at[d - 1], send.at[5 + d], recv.at[5 + d], peer))
            return out
        if step == 4:
            part = self.out.at[p.part]
            return [remote(part, part, send.at[9], recv.at[9], p.at(x=1 - p.x))]
        part = self.out.at[pl.ds(2 * p.c, 2)]
        return [remote(part, part, send.at[10], recv.at[14], p.at(c=1 - p.c))]

    def start(self, step):
        for copy in self.copies(step):
            copy.start()

    def arrive(self, step):
        p, mine = self.p, self.mine
        for copy in self.copies(step):
            copy.wait_recv()

        def add(dst, a, b):
            dst[...] = (a[...].astype(F32) + b[...].astype(F32)).astype(BF)

        if step == 0:

            def body(i, carry):
                at = (i // 4, i % 4)
                add(mine.at[at], mine.at[at], self.one.at[at])
                return carry

            lax.fori_loop(0, 16, body, 0)
        if step == 1:
            for copy in self.copies(step):
                copy.wait_send()

            def body(i, carry):
                at = (2 * self.f + i // 4, i % 4)
                add(mine.at[at], mine.at[at], self.two.at[i // 4, i % 4])
                return carry

            lax.fori_loop(0, 8, body, 0)
        if step == 2:

            def body(i, carry):
                add(self.kept.at[i], mine.at[self.slot, i], self.three.at[i])
                return carry

            lax.fori_loop(0, 4, body, 0)
        if step == 3:
            total = self.kept[p.z].astype(F32)
            for d in range(3):
                total = total + self.four[d].astype(F32)
            self.out[p.part] = total.astype(BF)

    def go(self, step):
        self.arrive(step - 1)
        self.start(step)

    def sent(self, first, last):
        for step in range(first, last):
            if step == 1:
                continue
            for copy in self.copies(step):
                if copy.is_remote:
                    copy.wait_send()


class ReduceZ(Reduce):
    def copies(self, step):
        p, send, recv = self.p, self.send, self.recv
        if step == 1:
            out = []
            for d, peer in zip((1, 2, 3), p.z_peers()):
                part = self.mine.at[:, (p.z + d) % 4]
                out.append(remote(part, self.four.at[d - 1], send.at[5 + d], recv.at[5 + d], peer))
            return out
        if step == 2:
            part = self.kept.at[pl.ds(2 * (1 - self.f), 2)]
            return [remote(part, self.two, send.at[4], recv.at[4], self.f_peer)]
        if step == 3:
            part = self.pair.at[1 - self.g]
            return [remote(part, self.three, send.at[5], recv.at[5], self.g_peer)]
        return super().copies(step)

    def arrive(self, step):
        if step not in (1, 2, 3):
            super().arrive(step)
            return
        for copy in self.copies(step):
            copy.wait_recv()
        if step == 1:

            def body(i, carry):
                total = self.mine[i, self.p.z].astype(F32)
                for d in range(3):
                    total = total + self.four[d, i].astype(F32)
                self.kept[i] = total.astype(BF)
                return carry

            lax.fori_loop(0, 4, body, 0)
        if step == 2:
            for copy in self.copies(step):
                copy.wait_send()
            for k in range(2):
                at = 2 * self.f + k
                self.pair[k] = (self.kept[at].astype(F32) + self.two[k].astype(F32)).astype(BF)
        if step == 3:
            total = self.pair[self.g].astype(F32) + self.three[...].astype(F32)
            self.out[self.p.part] = total.astype(BF)

    def sent(self, first, last):
        for step in range(first, last):
            if step == 2:
                continue
            for copy in self.copies(step):
                if copy.is_remote:
                    copy.wait_send()


PARTS = (('w0b', 'yx', 1, None), ('w0a', 'yx', 0, None), ('r1', 'yx', 1, 0), ('w1b', 'yx', 1, None), ('w2b', 'yx', 1, None), ('w2a', 'yx', 0, None), ('w1a', 'y', 0, None), ('r3', 'y', 1, 1), ('r0', 'y', 0, 0), ('r2', 'y', 0, 1))
BEFORE = ('w0b1', 'w0a1', 'w0b2', 'r11', 'w0a2', 'w1b1', 'r12', 'w2b1', 'w0b3', 'w1b2', 'w2a1', 'w2b2', 'w0a3', 'w2a2', 'w1a1')
FIRST = {3: ('r13',), 4: ('r31',), 6: ('w1a2',), 7: ('w1b3',)}
BETWEEN = ('r01',)
SECOND = {1: ('r32',), 3: ('w2b3', 'r21'), 5: ('r02',), 6: ('w2a3',)}
AFTER = ('r22',)


def forward_kernel(
    feat,
    side,
    conv_ref,
    code_ref,
    proj_ref,
    head_ref,
    gains_ref,
    x_out,
    side_out,
    w_out0,
    w_out1,
    w_out2,
    rest_out,
    a_one_out,
    c_one_out,
    a_two_out,
    l_out,
    s_ref,
    wt_ref,
    a_one_ref,
    c_one_ref,
    a_two_ref,
    l_ref,
    k_sem,
    w_mine,
    rest_mine,
    xv,
    wv0,
    wv1,
    wv2,
    a3,
    y32,
    x_send,
    x_recv,
    g_send,
    g_recv,
    o_sem,
):
    place = Place()
    rank = 2 * place.x + place.c
    ch, lat = conv_ref.shape[2], code_ref.shape[1]
    n_code, n_proj, n_head = (v.shape[0] // 4 for v in (code_ref, proj_ref, head_ref))
    wt_ref[...] = jnp.zeros_like(wt_ref)

    def cast_conv(j):
        n = w_mine.shape[3]
        for k in range(4):
            v = conv_ref[j, k * n : (k + 1) * n, :]
            w_mine[j, k // 2, k % 2] = v.astype(BF)
            wt_ref[j : j + 1, :] += jnp.sum(v * v, axis=0, keepdims=True)

    def cast_rest():
        for k in range(4):
            low = 0
            for m, (ref, n) in enumerate(
                ((code_ref, n_code), (proj_ref, n_proj), (head_ref, n_head))
            ):
                v = ref[k * n : (k + 1) * n, :]
                wt_ref[3 + m : 4 + m, :lat] += jnp.sum(v * v, axis=0, keepdims=True)
                if n % 16:
                    v = jnp.concatenate([v, jnp.zeros((-n % 16, lat), F32)], axis=0)
                rest_mine[k // 2, k % 2, low : low + v.shape[0]] = v.astype(BF)
                low += v.shape[0]

    cast_conv(0)
    place.greet()

    def view(ref, lanes):
        n = ref.shape[0] // 32
        return ref.reshape(4, 2, 2, 2, n, ref.shape[1]).at[..., lanes]

    jobs = {}
    views = [view(wv0, slice(None)), view(wv1, slice(None)), view(wv2, slice(None)), rest_out]
    for k, (name, route, lane, row) in enumerate(PARTS):
        rest = name[0] == "r"
        src = rest_mine if rest else w_mine.at[int(name[1])]
        dst = views[3] if rest else views[int(name[1])]
        n = src.shape[-2]
        parts, which = (2, lane) if row is None else (4, 2 * row + lane)
        cut = [k * n // (16 * parts) * 16 for k in range(parts)] + [n]
        at = (..., pl.ds(cut[which], cut[which + 1] - cut[which]), slice(None))
        jobs[name] = Gather(place, src.at[at], dst.at[at], g_send.at[k], g_recv.at[k], route)

    def go(words):
        for word in words:
            jobs[word[:-1]].go(int(word[-1]))

    def ticks(table):
        def tick(i):
            for when, words in table.items():

                @pl.when(i == when)
                def _():
                    go(words)

        return tick

    def whole(names):
        for name in names:
            jobs[name].arrive(jobs[name].steps - 1)

    cells = []
    for src, dst, base in ((feat, xv, 0), (side, side_out, 4)):
        for k, q in enumerate(place.row_peers()):
            to = q["rows"]
            cells.append(
                remote(src.at[to], dst.at[:, rank], x_send.at[base + k], x_recv.at[base + k], q)
            )
        cells.append(pltpu.make_async_copy(src.at[rank], dst.at[:, rank], x_recv.at[base + 3]))

    started = PARTS[0][0]
    jobs[started].start(0)
    for copy in cells:
        copy.start()
    cast = {"0"}
    for name, *_ in PARTS[1:]:
        which = name[1] if name[0] == "w" else "rest"
        if which not in cast:
            cast_rest() if which == "rest" else cast_conv(int(which))
            cast.add(which)
        jobs[name].start(0)
    go(BEFORE)
    zero_edges(a3)
    for copy in cells:
        copy.wait_recv()
    keep_x = pltpu.make_async_copy(xv, x_out, o_sem.at[0])
    keep_x.start()
    whole(("w0a", "w0b"))
    keep_w = [
        pltpu.make_async_copy(v, o, o_sem.at[1 + k])
        for k, (v, o) in enumerate(((wv0, w_out0), (wv1, w_out1), (wv2, w_out2)))
    ]
    keep_w[0].start()
    count = xv.shape[0]

    def crop_x(i):
        return xv[i].reshape(256, ch).astype(F32)

    tick_first, tick_second = ticks(FIRST), ticks(SECOND)

    def keep_first(i):
        return [
            pltpu.make_async_copy(v.at[i], o.at[i], k_sem.at[k, i])
            for k, (v, o) in enumerate(((a_one_ref, a_one_out), (c_one_ref, c_one_out)))
        ]

    def keep_second(i):
        rows = crop_rows(i)
        return [
            pltpu.make_async_copy(a_two_ref.at[i], a_two_out.at[i], k_sem.at[2, i]),
            pltpu.make_async_copy(l_ref.at[rows], l_out.at[rows], k_sem.at[3, i]),
        ]

    def first(i, carry):
        tick_first(i)
        a_one_ref[i], c_one_ref[i] = first_crop(crop_x(i), gains_ref, wv0, a3)
        for copy in keep_first(i):
            copy.start()
        return carry

    lax.fori_loop(0, count, first, 0)
    go(BETWEEN)
    whole(("w1a", "w1b"))
    keep_w[1].start()

    def second(i, carry):
        tick_second(i)
        a_two_ref[i] = second_crop(
            c_one_ref[i], crop_x(i), gains_ref, wv1, l_ref.at[crop_rows(i)], a3, y32
        )
        for copy in keep_second(i):
            copy.start()
        return carry

    lax.fori_loop(0, count, second, 0)
    whole(("w2a", "w2b"))
    keep_w[2].start()
    down_dot(l_ref, wv2, s_ref)
    go(AFTER)
    whole(("r0", "r1", "r2", "r3"))
    for job in jobs.values():
        job.finish()
    for copy in cells:
        if copy.is_remote:
            copy.wait_send()
    keep_x.wait()
    for copy in keep_w:
        copy.wait()

    def kept(i, carry):
        for copy in keep_first(i) + keep_second(i):
            copy.wait()
        return carry

    lax.fori_loop(0, count, kept, 0)


def forward_call(feat, side, conv_w, code_w, proj_w, head_w, gains):
    ranks, crops, cells, ch = feat.shape
    lat = code_w.shape[1]
    lat_cells = crops * ranks * cells // 4
    n_conv = conv_w.shape[1] // 4
    n_rest = code_w.shape[0] // 4 + proj_w.shape[0] // 4 + 16
    whole = 32 * n_conv

    def shape(*dims, dtype=BF):
        return jax.ShapeDtypeStruct(dims, dtype)

    outs = [
        shape(crops, ranks, cells, ch),
        shape(crops, ranks, *side.shape[2:], dtype=F32),
        shape(whole, ch),
        shape(whole, ch),
        shape(whole, ch),
        shape(4, 2, 2, 2, n_rest, lat),
        shape(crops, ranks * cells, ch),
        shape(crops, ranks * cells, ch, dtype=F32),
        shape(crops, ranks * cells, ch),
        shape(lat_cells, 9 * ch),
        shape(lat_cells, ch),
        shape(8, ch, dtype=F32),
    ]
    return pl.pallas_call(
        forward_kernel,
        out_shape=outs,
        in_specs=[ANY] * 2 + [VM] * 5,
        out_specs=[ANY] * 10 + [VM] * 2,
        scratch_shapes=[
            pltpu.VMEM((crops, ranks * cells, ch), BF),
            pltpu.VMEM((crops, ranks * cells, ch), F32),
            pltpu.VMEM((crops, ranks * cells, ch), BF),
            pltpu.VMEM((lat_cells, 9 * ch), BF),
            pltpu.SemaphoreType.DMA((4, crops)),
            pltpu.VMEM((3, 2, 2, n_conv, ch), BF),
            pltpu.VMEM((2, 2, n_rest, lat), BF),
            pltpu.VMEM((crops, ranks, cells, ch), BF),
        ]
        + [pltpu.VMEM((whole, ch), BF)] * 3
        + [
            pltpu.VMEM((18, 16, 3 * ch), BF),
            pltpu.VMEM((ch // 128, ranks * cells, 128), F32),
            pltpu.SemaphoreType.DMA((8,)),
            pltpu.SemaphoreType.DMA((8,)),
            pltpu.SemaphoreType.DMA((len(PARTS), 8)),
            pltpu.SemaphoreType.DMA((len(PARTS), 8)),
            pltpu.SemaphoreType.DMA((4,)),
        ],
        compiler_params=pltpu.CompilerParams(
            vmem_limit_bytes=58 * MIB, collective_id=2, has_side_effects=True
        ),
        cost_estimate=pl.CostEstimate(
            flops=45 * crops * ranks * cells * ch * ch,
            bytes_accessed=0,
            transcendentals=0,
        ),
    )(feat, side, conv_w, code_w, proj_w, head_w, gains)


def quantizer_kernel(
    consts,
    codes_ref,
    rest,
    side_ref,
    sl_ref,
    l_ref,
    ds_ref,
    loss_ref,
    dp_ref,
    small_ref,
    dw_ref,
    tab,
    stage,
    proj_v,
    head_v,
    e_ref,
    sems,
):
    lat_count, pix_count, rgb, n_code = consts
    cells = sl_ref.shape[0]
    pieces = rest.shape[0]
    slots = stage.shape[0]
    lat = tab.shape[1]
    small = [
        pltpu.make_async_copy(rest.at[:, n_code : n_code + 16], proj_v, sems.at[slots]),
        pltpu.make_async_copy(rest.at[:, n_code + 16 :], head_v, sems.at[slots + 1]),
    ]
    for copy in small:
        copy.start()

    def fetch(p):
        slot = p % slots
        return pltpu.make_async_copy(rest.at[p, :n_code], stage.at[slot], sems.at[slot])

    for p in range(slots):
        fetch(p).start()

    def widen(p, carry):
        fetch(p).wait()
        tab[pl.ds(pl.multiple_of(p * n_code, n_code), n_code), :] = stage[p % slots].astype(F32)

        @pl.when(p + slots < pieces)
        def _():
            fetch(p + slots).start()

        return carry

    lax.fori_loop(0, pieces, widen, 0)
    for copy in small:
        copy.wait()
    proj = proj_v[...].reshape(-1, lat)
    head = head_v[...].astype(F32)[:, :8, :128].reshape(-1, 128).astype(BF)

    def pick(b, carry):
        for j in range(8):
            for k in range(4):
                row = codes_ref[k * cells + b * 8 + j]
                e_ref[k, pl.ds(b * 8 + j, 1), :] = tab[pl.ds(row, 1), :]
        return carry

    lax.fori_loop(0, cells // 8, pick, 0)

    latent = jnp.dot(sl_ref[...], proj, preferred_element_type=F32)
    cum = e_ref[0]
    resid = []
    square = None
    for k in range(4):
        if k:
            cum = cum + e_ref[k]
        r = latent - cum
        resid.append(r)
        part = jnp.sum(r * r, axis=0, keepdims=True)
        square = part if square is None else square + part
    zq = cum.astype(BF)
    side = side_ref[...]
    valid = lax.broadcasted_iota(jnp.int32, side.shape, 1) < rgb
    weight = jnp.where(valid, pltpu.roll(side, 128 - 16, 1), 0.0)
    diff = jnp.where(valid, jnp.dot(zq, head, preferred_element_type=F32) - side, 0.0)
    smooth = jnp.sqrt(diff * diff + 1.0)
    recon = jnp.sum(weight * (smooth - 1.0), axis=0, keepdims=True)
    loss_ref[...] = jnp.zeros_like(loss_ref)
    loss_ref[0:1, 0:lat] = square * ((1.0 + BETA) / lat_count)
    loss_ref[0:1, lat : lat + 128] = recon / pix_count
    d_pred = (weight * (diff / smooth) / pix_count).astype(BF)
    back = (((1,), (1,)), ((), ()))
    rows = (((0,), (0,)), ((), ()))
    d_head = lax.dot_general(zq, d_pred, rows, preferred_element_type=F32)
    total = resid[0] + resid[1] + resid[2] + resid[3]
    d_zq = lax.dot_general(d_pred, head, back, preferred_element_type=F32)
    d_lat = (total * (2.0 * BETA / lat_count) + d_zq).astype(BF)
    d_proj = lax.dot_general(sl_ref[...], d_lat, rows, preferred_element_type=F32)
    d_s = lax.dot_general(d_lat, proj, back, preferred_element_type=F32)
    ds_ref[...] = d_s.astype(BF)
    tail = None
    for k in (3, 2, 1, 0):
        tail = resid[k] if tail is None else tail + resid[k]
        dp_ref[k * cells : (k + 1) * cells, :] = (tail * (-2.0 / lat_count)).astype(BF)
    small_ref[:, :16] = d_proj.astype(BF).reshape(pieces, 16, lat)
    d_head = jnp.concatenate([d_head, jnp.zeros((d_head.shape[0], lat - 128), F32)], axis=1)
    d_head = d_head.reshape(pieces, 8, lat)
    d_head = jnp.concatenate([d_head, jnp.zeros((pieces, 8, lat), F32)], axis=1)
    small_ref[:, 16:] = d_head.astype(BF)
    down_weight_grad(l_ref, ds_ref, dw_ref)


def quantizer_call(codes, rest, side, s_low, windows, lat_count, pix_count, rgb, n_code):
    pieces, rows, lat = rest.shape
    cells, ch = s_low.shape
    outs = [
        jax.ShapeDtypeStruct((cells, ch), BF),
        jax.ShapeDtypeStruct((8, ch), F32),
        jax.ShapeDtypeStruct((4 * cells, lat), BF),
        jax.ShapeDtypeStruct((pieces, 32, lat), BF),
        jax.ShapeDtypeStruct((9 * ch, ch), BF),
    ]
    return pl.pallas_call(
        functools.partial(quantizer_kernel, (lat_count, pix_count, rgb, n_code)),
        out_shape=outs,
        in_specs=[pl.BlockSpec(memory_space=pltpu.SMEM), ANY, VM, VM, VM],
        out_specs=[VM] * 5,
        scratch_shapes=[
            pltpu.VMEM((pieces * n_code, lat), F32),
            pltpu.VMEM((4, n_code, lat), BF),
            pltpu.VMEM((pieces, 16, lat), BF),
            pltpu.VMEM((pieces, rows - n_code - 16, lat), BF),
            pltpu.VMEM((4, cells, lat), F32),
            pltpu.SemaphoreType.DMA((6,)),
        ],
        compiler_params=pltpu.CompilerParams(vmem_limit_bytes=58 * MIB),
        cost_estimate=pl.CostEstimate(flops=10**10, bytes_accessed=10**7, transcendentals=0),
    )(codes, rest, side, s_low, windows)


def second_back_kernel(
    n_code,
    ds_ref,
    gains_ref,
    codes_ref,
    dp_ref,
    w_down_in,
    w_in,
    c_in,
    a_in,
    down_src,
    small_src,
    din_ref,
    dg_ref,
    down_kept_ref,
    kept0_ref,
    kept1_ref,
    rest_kept_ref,
    w_down_ref,
    w_ref,
    c_ref,
    a_ref,
    l_sem,
    dw,
    d3,
    y32,
    dp_all,
    codes_all,
    quarter,
    quarter_in,
    small_in,
    e_send,
    e_recv,
    *bufs,
):
    place = Place()
    bufs = list(bufs)

    def take(n):
        out = bufs[:n]
        del bufs[:n]
        return out

    loads = [
        pltpu.make_async_copy(src, dst, l_sem.at[k])
        for k, (src, dst) in enumerate(
            ((w_down_in, w_down_ref), (a_in, a_ref), (w_in, w_ref), (c_in, c_ref))
        )
    ]
    for copy in loads:
        copy.start()
    half = down_src.shape[-1] // 2
    view = dw.reshape(4, 2, 2, 2, dw.shape[0] // 32, dw.shape[1])
    mine, one, four, send, recv = take(5)
    down = ReduceZ(place, down_src, None, mine, one, None, None, down_kept_ref, four, send, recv)
    early, sems = take(4), take(2)
    low = Reduce(place, view.at[..., :half], None, *early, kept0_ref, None, *sems)
    early, sems = take(4), take(2)
    high = Reduce(place, view.at[..., half:], None, *early, kept1_ref, None, *sems)

    across = place.at(x=1 - place.x)
    other = place.at(c=1 - place.c)
    two = pl.ds(2 * place.c, 2)
    entries = [(dp_ref, dp_all, 0), (codes_ref, codes_all, 1)]
    out_x = [
        remote(src, dst.at[place.part], e_send.at[k], e_recv.at[k], across) for src, dst, k in entries
    ]
    out_x += [
        pltpu.make_async_copy(src, dst.at[place.part], e_recv.at[2 + k]) for src, dst, k in entries
    ]
    out_c = [
        remote(dst.at[two], dst.at[two], e_send.at[4 + k], e_recv.at[4 + k], other)
        for _, dst, k in entries
    ]
    small = []
    for k, (x, c) in enumerate(
        ((place.x, 1 - place.c), (1 - place.x, place.c), (1 - place.x, 1 - place.c))
    ):
        small.append(
            remote(
                small_src.at[:, :, c, x],
                small_in.at[k],
                e_send.at[6 + k],
                e_recv.at[6 + k],
                place.at(x=x, c=c),
            )
        )
    small.append(
        pltpu.make_async_copy(small_src.at[:, :, place.c, place.x], small_in.at[3], e_recv.at[9])
    )
    out_y = [
        remote(
            quarter.at[1 - place.y, pl.ds(2 * k, 2)],
            quarter_in.at[pl.ds(2 * k, 2)],
            e_send.at[10 + k],
            e_recv.at[10 + k],
            place.at(y=1 - place.y),
        )
        for k in range(2)
    ]

    place.greet()
    down.start(0)
    for copy in out_x + small:
        copy.start()

    def piece(z, y):
        base = ((z * 2 + y) * 4 + place.part) * n_code
        row = lax.broadcasted_iota(jnp.int32, (n_code, dp_ref.shape[0]), 0) + base

        def add(k, total):
            hot = jnp.where(row == codes_all[k], 1.0, 0.0).astype(BF)
            return total + jnp.dot(hot, dp_all[k], preferred_element_type=F32)

        total = lax.fori_loop(0, 4, add, jnp.zeros((n_code, dp_ref.shape[1]), F32))
        quarter[y, z, :n_code] = total.astype(BF)
        total = small_in[3, z, y].astype(F32)
        for k in range(3):
            total = total + small_in[k, z, y].astype(F32)
        quarter[y, z, n_code:] = total.astype(BF)

    def codebook_grad():
        def away(z, carry):
            piece(z, 1 - place.y)

            for k in range(2):

                @pl.when(z == 2 * k + 1)
                def _():
                    out_y[k].start()

            return carry

        def here(z, carry):
            piece(z, place.y)

            @pl.when(z == 0)
            def _():
                low.go(2)

            @pl.when(z == 2)
            def _():
                high.go(2)

            return carry

        lax.fori_loop(0, 4, away, 0)
        lax.fori_loop(0, 4, here, 0)

    def tick_down(i):
        @pl.when(i == 4)
        def _():
            down.go(1)

    def tick_high(dx):
        @pl.when(dx == 2)
        def _():
            low.go(1)

    def tick_crop(i):
        @pl.when(i == 1)
        def _():
            high.go(1)
            for copy in out_x:
                copy.wait_recv()
            for copy in out_c:
                copy.start()

        @pl.when(i == 3)
        def _():
            for copy in out_c:
                copy.wait_recv()
            for copy in small:
                copy.wait_recv()
            codebook_grad()

        @pl.when(i == 7)
        def _():
            low.arrive(2)
            down.arrive(1)

    loads[0].wait()
    down_input_grad(ds_ref, w_down_ref, din_ref, y32, tick_down)
    shift_all(din_ref, d3)
    loads[1].wait()
    conv_weight_grad(a_ref, d3, dw, 0)
    low.start(0)
    conv_weight_grad(a_ref, d3, dw, 1, tick_high)
    high.start(0)
    loads[2].wait()
    loads[3].wait()
    unit_back(lambda i: c_ref[i], gains_ref, w_ref, dg_ref, d3, 2, din_ref, tick_crop)
    for copy in out_y:
        copy.wait_recv()
    for z in range(4):
        total = quarter[place.y, z].astype(F32) + quarter_in[z].astype(F32)
        rest_kept_ref[z] = total.astype(BF)
    high.arrive(2)
    down.sent(0, 2)
    for job in (low, high):
        job.sent(0, 3)
    for copy in out_x[:2] + out_c + small[:3] + out_y:
        copy.wait_send()


def second_back_call(n_code, ds, w_down, w, c_one, a_two, gains, codes, dp, down_src, small_src):
    crops, cells, ch = c_one.shape
    n_conv, lat = down_src.shape[-2], dp.shape[-1]
    n_rest = n_code + small_src.shape[-2]

    def shape(*dims, dtype=BF):
        return jax.ShapeDtypeStruct(dims, dtype)

    outs = [
        shape(crops, cells, ch),
        shape(2, ch, dtype=F32),
        shape(4, n_conv, ch),
        shape(4, n_conv, ch // 2),
        shape(4, n_conv, ch // 2),
        shape(4, n_rest, lat),
    ]
    begun = Reduce.early(n_conv, ch // 2) + Reduce.sems()
    return pl.pallas_call(
        functools.partial(second_back_kernel, n_code),
        out_shape=outs,
        in_specs=[VM] * 4 + [ANY] * 6,
        out_specs=[VM] * 6,
        scratch_shapes=[
            pltpu.VMEM(w_down.shape, BF),
            pltpu.VMEM(w.shape, BF),
            pltpu.VMEM(c_one.shape, F32),
            pltpu.VMEM(a_two.shape, BF),
            pltpu.SemaphoreType.DMA((4,)),
            pltpu.VMEM(w.shape, BF),
            pltpu.VMEM((crops, 18, 16, 3 * ch), BF),
            pltpu.VMEM((ch // 128, cells, 128), F32),
            pltpu.VMEM((4,) + dp.shape, BF),
            pltpu.VMEM((4,) + codes.shape, jnp.int32),
            pltpu.VMEM((2, 4, n_rest, lat), BF),
            pltpu.VMEM((4, n_rest, lat), BF),
            pltpu.VMEM((4, 4, 2, small_src.shape[-2], lat), BF),
            pltpu.SemaphoreType.DMA((12,)),
            pltpu.SemaphoreType.DMA((12,)),
        ]
        + [pltpu.VMEM((k, 4, n_conv, ch), BF) for k in (4, 4, 3)]
        + Reduce.sems()
        + begun * 2,
        compiler_params=pltpu.CompilerParams(
            vmem_limit_bytes=61 * MIB, collective_id=3, has_side_effects=True
        ),
        cost_estimate=pl.CostEstimate(flops=4 * 10**10, bytes_accessed=0, transcendentals=0),
    )(ds, gains, codes, dp, w_down, w, c_one, a_two, down_src, small_src)


def first_back_kernel(
    sizes,
    dc_in,
    x_in,
    w_in,
    a_in,
    gains_ref,
    kept0_ref,
    kept1_ref,
    rest_kept_ref,
    down_kept_ref,
    dg_two_ref,
    loss_ref,
    wt_ref,
    conv_row_ref,
    rest_row_ref,
    g_first0,
    g_first1,
    g_second0,
    g_second1,
    g_down,
    g_rest0,
    g_rest1,
    conv_new_ref,
    rest_new_ref,
    tv_ref,
    dc_ref,
    x_ref,
    w_ref,
    a_ref,
    l_sem,
    dw,
    d3,
    dg,
    vec,
    vec_in,
    tv_in,
    s_send,
    s_recv,
    *bufs,
):
    n_code, n_proj, n_head, rgb = sizes
    place = Place()
    bufs = list(bufs)

    def take(n):
        out = bufs[:n]
        del bufs[:n]
        return out

    loads = [
        pltpu.make_async_copy(src, dst, l_sem.at[k])
        for k, (src, dst) in enumerate(
            ((dc_in, dc_ref), (a_in, a_ref), (w_in, w_ref), (x_in, x_ref))
        )
    ]
    for copy in loads:
        copy.start()
    half = rest_kept_ref.shape[-1] // 2
    ch = tv_ref.shape[1]
    view = dw.reshape(4, 2, 2, 2, dw.shape[0] // 32, ch)
    none = [None] * 4
    second0 = Reduce(place, None, g_second0, *none, kept0_ref, *take(3))
    second1 = Reduce(place, None, g_second1, *none, kept1_ref, *take(3))
    rest0 = Reduce(place, None, g_rest0, *none, rest_kept_ref.at[..., :half], *take(3))
    rest1 = Reduce(place, None, g_rest1, *none, rest_kept_ref.at[..., half:], *take(3))
    low = Reduce(place, view.at[..., : ch // 2], g_first0, *take(8))
    high = Reduce(place, view.at[..., ch // 2 :], g_first1, *take(8))
    late = (second0, second1, rest0, rest1)
    two, three, pair, send, recv = take(5)
    down = ReduceZ(place, None, g_down, None, None, two, three, down_kept_ref, None, send, recv)
    down.pair = pair
    place.greet()
    for job in late:
        job.start(3)
    down.start(2)

    def tick_low(dx):
        @pl.when(dx == 2)
        def _():
            down.go(4)

    def tick_high(dx):
        @pl.when(dx == 1)
        def _():
            low.go(1)

        @pl.when(dx == 2)
        def _():
            second0.go(4)
            down.go(5)

    def tick_crop(i):
        @pl.when(i == 0)
        def _():
            second1.go(4)

        @pl.when(i == 1)
        def _():
            high.go(1)
            second0.go(5)

        @pl.when(i == 2)
        def _():
            low.go(2)

        @pl.when(i == 3)
        def _():
            second1.go(5)

        @pl.when(i == 5)
        def _():
            low.go(3)
            high.go(2)

        @pl.when(i == 6)
        def _():
            rest0.go(4)

        @pl.when(i == 7)
        def _():
            high.go(3)

    def v_of(i):
        return x_ref[i].astype(F32)

    loads[0].wait()
    shift_all(dc_ref, d3)
    loads[1].wait()
    down.go(3)
    conv_weight_grad(a_ref, d3, dw, 0, tick_low)
    low.start(0)
    conv_weight_grad(a_ref, d3, dw, 1, tick_high)
    high.start(0)
    loads[2].wait()
    loads[3].wait()
    unit_back(v_of, gains_ref, w_ref, dg, d3, 0, None, tick_crop)
    vec[...] = jnp.zeros_like(vec)
    vec[0:2] = dg[...]
    vec[2:4] = dg_two_ref[...]
    vec[4:5] = loss_ref[0:1]
    small = [
        remote(vec, vec_in.at[k], s_send.at[k], s_recv.at[k], q)
        for k, q in enumerate(place.row_peers())
    ]
    for copy in small:
        copy.start()
    tv_ref[...] = jnp.zeros_like(tv_ref)
    for copy in small:
        copy.wait_recv()
    tv_ref[16:24, :] = vec[...] + vec_in[0] + vec_in[1] + vec_in[2]
    tv_ref[24:32, :] = wt_ref[...]

    def fold(parts, row, width):
        squares = [g.astype(F32) for g in parts]
        squares = [g * g for g in squares]
        total = sum(jnp.sum(q, axis=1, keepdims=True) for q in squares)
        new = 0.5 * row + 0.5 * (total / width + EPS_SQ)
        inverse = 1.0 / new
        col = [jnp.sum(q, axis=0, keepdims=True) for q in squares]
        over = [jnp.sum(q * inverse, axis=0, keepdims=True) for q in squares]
        return (
            new,
            jnp.concatenate(col, axis=1),
            jnp.concatenate(over, axis=1),
            jnp.sum(new, axis=0, keepdims=True),
        )

    def fold_conv(j, refs):
        for k in range(4):
            new, col, over, total = fold([r[k] for r in refs], conv_row_ref[j, k], ch)
            conv_new_ref[j, k] = new
            tv_ref[j : j + 1, :] += col
            tv_ref[3 + j : 4 + j, :] += over
            tv_ref[6 + j : 7 + j, :] += total

    def fold_rest():
        lat = 2 * half
        spans = ((0, n_code, lat), (n_code, n_proj, lat), (n_code + n_proj, n_head, rgb))
        for k in range(4):
            both = [r[k] for r in (g_rest0, g_rest1)]
            for m, (start, size, width) in enumerate(spans):
                parts = [v.astype(F32)[start : start + size] for v in both]
                row = rest_row_ref[k, start : start + size]
                new, col, over, total = fold(parts, row, width)
                rest_new_ref[k, start : start + size] = new
                tv_ref[9 + m : 10 + m, :lat] += col
                tv_ref[9 + m : 10 + m, lat:] += over
                tv_ref[12 + m : 13 + m, :] += total
            size = rest_row_ref.shape[1] - n_code - n_proj - n_head
            rest_new_ref[k, rest_row_ref.shape[1] - size :] = jnp.ones((size, 1), F32)

    rest0.go(5)
    down.arrive(5)
    fold_conv(2, [g_down])
    second0.arrive(5)
    second1.arrive(5)
    fold_conv(1, [g_second0, g_second1])
    rest1.go(4)
    rest0.arrive(5)
    rest1.go(5)
    low.go(4)
    rest1.arrive(5)
    fold_rest()
    low.go(5)
    high.go(4)
    low.arrive(5)
    high.go(5)
    high.arrive(5)
    fold_conv(0, [g_first0, g_first1])

    across = remote(tv_ref, tv_in.at[0], s_send.at[3], s_recv.at[3], place.at(y=1 - place.y))
    across.start()
    across.wait()
    tv_ref[...] += tv_in[0]
    along = [
        remote(tv_ref, tv_in.at[k], s_send.at[3 + k], s_recv.at[3 + k], q)
        for k, q in zip((1, 2, 3), place.z_peers())
    ]
    for copy in along:
        copy.start()
    for copy in along:
        copy.wait()
    tv_ref[...] += tv_in[1] + tv_in[2] + tv_in[3]
    for copy in small:
        copy.wait_send()
    down.sent(2, 6)
    for job in late:
        job.sent(3, 6)
    for job in (low, high):
        job.sent(0, 6)


def first_back_call(sizes, dc, x, gains, w, a_one, kept, down_kept, dg_two, loss, wt, rows):
    crops, cells, ch = x.shape
    n_conv, n_rest = down_kept.shape[-2], kept[2].shape[-2]

    def shape(*dims, dtype=BF):
        return jax.ShapeDtypeStruct(dims, dtype)

    conv_half = shape(4, n_conv, ch // 2)
    rest_half = shape(4, n_rest, 128)
    outs = [conv_half] * 4 + [shape(4, n_conv, ch)] + [rest_half] * 2
    outs += [shape(*v.shape, dtype=F32) for v in rows] + [shape(32, ch, dtype=F32)]
    args = [dc, x, w, a_one, gains, *kept, down_kept, dg_two, loss, wt, *rows]
    whole = Reduce.early(n_conv, ch // 2) + Reduce.late(n_conv, ch // 2, 1) + Reduce.sems()
    return pl.pallas_call(
        functools.partial(first_back_kernel, sizes),
        out_shape=outs,
        in_specs=[ANY] * 4 + [VM] * (len(args) - 4),
        out_specs=[VM] * len(outs),
        scratch_shapes=[
            pltpu.VMEM(dc.shape, BF),
            pltpu.VMEM(x.shape, BF),
            pltpu.VMEM(w.shape, BF),
            pltpu.VMEM(a_one.shape, BF),
            pltpu.SemaphoreType.DMA((4,)),
            pltpu.VMEM(w.shape, BF),
            pltpu.VMEM((crops, 18, 16, 3 * ch), BF),
            pltpu.VMEM((2, ch), F32),
            pltpu.VMEM((8, ch), F32),
            pltpu.VMEM((3, 8, ch), F32),
            pltpu.VMEM((4, 32, ch), F32),
            pltpu.SemaphoreType.DMA((7,)),
            pltpu.SemaphoreType.DMA((7,)),
        ]
        + (Reduce.late(n_conv, ch // 2, 0) + Reduce.sems()) * 2
        + (Reduce.late(n_rest, 128, 0) + Reduce.sems()) * 2
        + whole * 2
        + [
            pltpu.VMEM((2, n_conv, ch), BF),
            pltpu.VMEM((n_conv, ch), BF),
            pltpu.VMEM((2, n_conv, ch), BF),
        ]
        + Reduce.sems(),
        compiler_params=pltpu.CompilerParams(
            vmem_limit_bytes=60 * MIB, collective_id=4, has_side_effects=True
        ),
        cost_estimate=pl.CostEstimate(flops=2 * 10**10, bytes_accessed=0, transcendentals=0),
    )(*args)


def finish_kernel(
    sizes,
    g_first0,
    g_first1,
    g_second0,
    g_second1,
    g_down,
    g_rest0,
    g_rest1,
    conv_ref,
    code_ref,
    proj_ref,
    head_ref,
    conv_row_ref,
    rest_row_ref,
    tv_ref,
    conv_col_ref,
    code_col_ref,
    proj_col_ref,
    head_col_ref,
    gains_ref,
    state_ref,
    loss_ref,
    conv_outs,
    rest_outs,
    gain_outs,
):
    n_code, n_proj, n_head, rgb, shards = sizes
    ch = conv_ref.shape[2]
    lat = code_ref.shape[1]

    def scales(col, col_sum, over, row_sum, weights, rows, width):
        rows = rows * shards
        col_new = 0.5 * col + 0.5 * (col_sum / rows + EPS_SQ)
        row_mean = row_sum / rows
        upd_sq = row_mean * jnp.sum(over / col_new, axis=1, keepdims=True)
        rms_u = jnp.sqrt(upd_sq / (rows * width))
        scale = jnp.sqrt(jnp.sum(weights, axis=1, keepdims=True) / (rows * width))
        factor = RATE * scale / jnp.maximum(1.0, rms_u)
        return col_new, factor * lax.rsqrt(col_new), row_mean

    def line(k):
        return tv_ref[k : k + 1, :]

    cg, cc, cn, cl = conv_outs
    for j, parts in enumerate(((g_first0, g_first1), (g_second0, g_second1), (g_down,))):
        n = conv_ref.shape[1]
        col_new, q, row_mean = scales(
            conv_col_ref[j : j + 1, :], line(j), line(3 + j), line(6 + j)[:, :1], line(24 + j), n, ch
        )
        cc[j : j + 1, :] = col_new
        m = n // 4
        for k in range(4):
            r = lax.rsqrt(conv_row_ref[j, k] / row_mean)
            rows = slice(k * m, (k + 1) * m)
            for p, part in enumerate(parts):
                width = part.shape[2]
                lanes = slice(p * width, (p + 1) * width)
                g = part[k].astype(F32)
                new = conv_ref[j, rows, lanes] - g * r * q[:, lanes]
                cg[j, rows, lanes] = g
                cn[j, rows, lanes] = new
                cl[j, rows, lanes] = new.astype(BF)
    cols = (code_col_ref, proj_col_ref, head_col_ref)
    spans = ((0, n_code, lat), (n_code, n_proj, lat), (n_code + n_proj, n_head, rgb))
    for m, (w_ref, (start, size, width)) in enumerate(zip((code_ref, proj_ref, head_ref), spans)):
        og, oc, on, ol = rest_outs[m]
        col_new, q, row_mean = scales(
            cols[m][...],
            line(9 + m)[:, :lat],
            line(9 + m)[:, lat:],
            line(12 + m)[:, :1],
            line(27 + m)[:, :lat],
            w_ref.shape[0],
            width,
        )
        oc[...] = col_new
        news = []
        for k in range(4):
            g = jnp.concatenate([g_rest0[k].astype(F32), g_rest1[k].astype(F32)], axis=1)
            g = g[start : start + size]
            r = lax.rsqrt(rest_row_ref[k, start : start + size] / row_mean)
            rows = slice(k * size, (k + 1) * size)
            new = w_ref[rows, :] - g * r * q
            og[rows, :] = g
            on[rows, :] = new
            if size % 16:
                news.append(new)
            else:
                ol[rows, :] = new.astype(BF)
        if news:
            ol[...] = jnp.concatenate(news, axis=0).astype(BF)
    loss_ref[...] = jnp.sum(line(20), axis=1, keepdims=True)
    grad = tv_ref[16:20, :]
    state = 0.5 * state_ref[...] + 0.5 * (grad * grad + EPS_SQ)
    update = grad * lax.rsqrt(state)
    gains = gains_ref[...]

    def rms(v):
        return jnp.sqrt(
            jnp.sum(jnp.sum(v * v, axis=1, keepdims=True), axis=0, keepdims=True) / v.size
        )

    gain_outs[0][...] = grad
    gain_outs[1][...] = state
    gain_outs[2][...] = gains - RATE * rms(gains) * update / jnp.maximum(1.0, rms(update))


def finish_call(sizes, grads, weights, rows, tv, cols, gains, state):
    conv_w, code_w, proj_w, head_w = weights
    lat = code_w.shape[1]

    def shape(dims, dtype=F32):
        return jax.ShapeDtypeStruct(dims, dtype)

    def matrix(w, col):
        return [shape(w.shape), shape(col), shape(w.shape), shape(w.shape, BF)]

    outs = [shape((1, 1)), matrix(conv_w, (3, conv_w.shape[2]))]
    outs += [[matrix(w, (1, lat)) for w in (code_w, proj_w, head_w)]]
    outs += [[shape(gains.shape)] * 3]
    args = [*grads, *weights, *rows, tv, *cols, gains, state]
    return pl.pallas_call(
        functools.partial(finish_kernel, sizes),
        out_shape=outs,
        in_specs=[VM] * len(args),
        out_specs=jax.tree.map(lambda _: VM, outs),
        compiler_params=pltpu.CompilerParams(vmem_limit_bytes=56 * MIB),
        cost_estimate=pl.CostEstimate(flops=10**7, bytes_accessed=2 * 10**7, transcendentals=0),
    )(*args)


def contract_last(left, right):
    return lax.dot_general(left, right, (((1,), (0,)), ((), ())), preferred_element_type=F32)


def contract_back(left, right):
    return lax.dot_general(left, right, (((1,), (1,)), ((), ())), preferred_element_type=F32)


def contract_rows(left, right):
    return lax.dot_general(left, right, (((0,), (0,)), ((), ())), preferred_element_type=F32)


def row_part(grad, row):
    g_sq = grad * grad + EPS_SQ
    row_new = 0.5 * row + 0.5 * jnp.mean(g_sq, axis=2)
    over_row = jnp.sum(grad * grad / row_new[:, :, None], axis=0)
    return row_new, jnp.sum(g_sq, axis=0), jnp.sum(row_new, axis=0), over_row


def finish(grad, weight, row_new, col, col_sum, row_sum, over_row, wt_sq):
    total = grad.shape[0] * lax.axis_size("batch")
    count = total * grad.shape[2]
    col_new = 0.5 * col + 0.5 * col_sum / total
    row_mean = row_sum / total
    upd_sq = row_mean * jnp.sum(over_row / col_new, axis=1)
    rms_u = jnp.sqrt(upd_sq / count)
    scale = jnp.sqrt(wt_sq / count)
    vhat = row_new[:, :, None] * col_new[None] / row_mean[None, :, None]
    update = grad * lax.rsqrt(vhat)
    new = weight - RATE * (scale / jnp.maximum(1.0, rms_u))[None, :, None] * update
    return col_new, new


def local_any(
    features,
    target,
    mask,
    codes,
    conv_w,
    proj_w,
    code_w,
    head_w,
    gains,
    conv_row,
    conv_col,
    proj_row,
    proj_col,
    code_row,
    code_col,
    head_row,
    head_col,
    gain_state,
):
    ranks = lax.axis_size("rows")
    shards = lax.axis_size("batch")
    me = lax.axis_index("rows")
    crops_all = features.shape[0] * shards
    ch = features.shape[3]
    lat = proj_w.shape[1]
    rgb = head_w.shape[1]
    height = features.shape[1] * ranks
    width = features.shape[2]

    def whole_crops(v):
        return lax.all_to_all(v, "rows", split_axis=0, concat_axis=1, tiled=True)

    def my_part(v):
        size = v.shape[0] // ranks
        return lax.dynamic_slice_in_dim(v, me * size, size, 0)

    conv_piece = jnp.transpose(my_part(conv_w).astype(BF), (1, 0, 2))
    head_wide = jnp.pad(head_w, ((0, 0), (0, lat - rgb)))
    rest_piece = jnp.concatenate(
        [my_part(code_w).astype(BF), my_part(proj_w).astype(BF), my_part(head_wide).astype(BF)]
    )
    n_code, n_proj, n_head = (v.shape[0] // ranks for v in (code_w, proj_w, head_w))
    w_all = [lax.all_gather(conv_piece[0], BOTH, axis=0, tiled=True)]
    later = lax.all_gather(conv_piece[1:], BOTH, axis=0)
    later = jnp.transpose(later, (1, 0, 2, 3)).reshape(2, -1, ch)
    w_all += [later[0], later[1]]
    rest = lax.all_gather(rest_piece, BOTH, axis=0)
    code_all = rest[:, :n_code].reshape(-1, lat)
    proj_all = rest[:, n_code : n_code + n_proj].reshape(-1, lat)
    head_all = rest[:, n_code + n_proj :, :rgb].reshape(-1, rgb)

    x = whole_crops(features)
    target, mask, codes = whole_crops(target), whole_crops(mask), whole_crops(codes)
    crops = x.shape[0]
    cells = height * width
    x = x.reshape(crops, cells, ch)
    lat_cells = crops * cells // 4
    target = target.reshape(lat_cells, rgb)
    mask = mask.reshape(lat_cells, -1)
    codes = codes.reshape(lat_cells, -1)

    conv_flops = 2 * crops * cells * 9 * ch * ch
    three = pltpu.VMEM((18, 16, 3 * ch), BF)
    fold = pltpu.VMEM((ch // 128, cells, 128), F32)

    def big(dtype):
        return jax.ShapeDtypeStruct((crops, cells, ch), dtype)

    dw_shape = jax.ShapeDtypeStruct((9 * ch, ch), BF)
    dg_shape = jax.ShapeDtypeStruct((2, ch), F32)

    a_one, c_one = kernel_call(
        first_conv_kernel, [big(BF), big(F32)], [three], conv_flops, x, gains, w_all[0]
    )
    a_two, windows, s_low = kernel_call(
        second_conv_kernel,
        [
            big(BF),
            jax.ShapeDtypeStruct((lat_cells, 9 * ch), BF),
            jax.ShapeDtypeStruct((lat_cells, ch), BF),
        ],
        [three, fold],
        conv_flops,
        c_one,
        x,
        gains,
        w_all[1],
        w_all[2],
    )

    lat_count = crops_all * cells // 4 * lat
    pix_count = crops_all * cells * 3
    latent = contract_last(s_low, proj_all)
    picked = code_all[codes].astype(F32)
    cum = jnp.cumsum(picked, axis=1)
    resid = latent[:, None, :] - cum
    quant_part = (1.0 + BETA) * jnp.sum(resid * resid) / lat_count
    zq_low = cum[:, -1].astype(BF)
    pred = contract_last(zq_low, head_all)
    diff = pred - target
    weight_mask = jnp.repeat(mask.astype(F32), 3, axis=-1)
    smooth = jnp.sqrt(diff * diff + 1.0)
    recon_part = jnp.sum(weight_mask * (smooth - 1.0)) / pix_count
    d_pred = (weight_mask * (diff / smooth) / pix_count).astype(BF)
    d_head = contract_rows(zq_low, d_pred)
    d_zq = contract_back(d_pred, head_all)
    d_cum = -2.0 / lat_count * resid
    d_picked = jnp.flip(jnp.cumsum(jnp.flip(d_cum, 1), axis=1), 1)
    d_code = jax.ops.segment_sum(
        d_picked.reshape(-1, lat), codes.reshape(-1), num_segments=code_all.shape[0]
    )
    d_lat_low = (jnp.sum(resid, axis=1) * (2.0 * BETA / lat_count) + d_zq).astype(BF)
    d_proj = contract_rows(s_low, d_lat_low)
    d_s_low = contract_back(d_lat_low, proj_all).astype(BF)

    d_c_two, d_down = kernel_call(
        down_back_kernel,
        [big(BF), dw_shape],
        [fold],
        conv_flops // 2,
        d_s_low,
        windows,
        w_all[2],
    )
    d_three = pltpu.VMEM((crops, 18, 16, 3 * ch), BF)
    d_c_one, d_second, gain_two = kernel_call(
        functools.partial(unit_back_kernel, row=2, inner=True),
        [big(BF), dw_shape, dg_shape],
        [d_three],
        2 * conv_flops,
        d_c_two,
        c_one,
        gains,
        w_all[1],
        a_two,
    )
    d_first, gain_one = kernel_call(
        functools.partial(unit_back_kernel, row=0, inner=False),
        [dw_shape, dg_shape],
        [d_three],
        2 * conv_flops,
        d_c_one,
        x,
        gains,
        w_all[0],
        a_one,
    )
    d_gains = jnp.concatenate([gain_one, gain_two], axis=0)

    devices = ranks * shards

    def to_owner(v):
        return lax.psum_scatter(v, BOTH, scatter_dimension=0, tiled=True)

    def to_rows(v):
        return lax.all_gather(v, "rows", axis=0)

    pad = jnp.pad(d_head, ((0, 0), (0, lat - rgb)))
    rest_grad = jnp.concatenate(
        [v.astype(BF).reshape(devices, -1, lat) for v in (d_code, d_proj, pad)], axis=1
    )
    rest_mine = to_owner(rest_grad.reshape(-1, lat))
    conv_mine = [to_owner(v) for v in (d_first, d_second, d_down)]
    rest_full = to_rows(rest_mine).astype(F32)
    conv_full = to_rows(jnp.stack(conv_mine)).astype(F32)
    g_conv = jnp.transpose(conv_full, (0, 2, 1, 3)).reshape(-1, 3, ch)
    g_code = rest_full[:, :n_code].reshape(-1, lat)
    g_proj = rest_full[:, n_code : n_code + n_proj].reshape(-1, lat)
    g_head = rest_full[:, n_code + n_proj :, :rgb].reshape(-1, rgb)

    mats = [
        (g_conv, conv_w, conv_row, conv_col),
        (g_proj[:, None, :], proj_w[:, None, :], proj_row[:, None], proj_col[None, :]),
        (g_code[:, None, :], code_w[:, None, :], code_row[:, None], code_col[None, :]),
        (g_head[:, None, :], head_w[:, None, :], head_row[:, None], head_col[None, :]),
    ]
    rows_new = [row_part(grad, row) for grad, weight, row, col in mats]
    wt_sq = [jnp.sum(weight * weight, axis=(0, 2)) for grad, weight, row, col in mats]
    sums = lax.psum([r[1:] + (w,) for r, w in zip(rows_new, wt_sq)], "batch")
    loss, g_gain = lax.psum((recon_part + quant_part, d_gains), BOTH)
    done = [
        finish(m[0], m[1], r[0], m[3], *s) for m, r, s in zip(mats, rows_new, sums)
    ]

    state_new = 0.5 * gain_state + 0.5 * (g_gain * g_gain + EPS_SQ)
    update = g_gain * lax.rsqrt(state_new)
    rms_u = jnp.sqrt(jnp.mean(update * update))
    scale = jnp.sqrt(jnp.mean(gains * gains))
    gains_new = gains - RATE * scale * update / jnp.maximum(1.0, rms_u)
    conv_new = done[0][1]
    proj_new, code_new, head_new = (d[1][:, 0, :] for d in done[1:])
    return (
        loss,
        g_conv,
        rows_new[0][0],
        done[0][0],
        conv_new,
        conv_new.astype(BF),
        g_proj,
        rows_new[1][0][:, 0],
        done[1][0][0],
        proj_new,
        proj_new.astype(BF),
        g_code,
        rows_new[2][0][:, 0],
        done[2][0][0],
        code_new,
        code_new.astype(BF),
        g_head,
        rows_new[3][0][:, 0],
        done[3][0][0],
        head_new,
        head_new.astype(BF),
        g_gain,
        state_new,
        gains_new,
    )


def local_fast(
    features,
    target,
    mask,
    codes,
    conv_w,
    proj_w,
    code_w,
    head_w,
    gains,
    conv_row,
    conv_col,
    proj_row,
    proj_col,
    code_row,
    code_col,
    head_row,
    head_col,
    gain_state,
):
    ranks = lax.axis_size("rows")
    shards = lax.axis_size("batch")
    crops_all = features.shape[0] * shards
    crops = features.shape[0] // ranks
    ch = features.shape[3]
    cells = features.shape[1] * ranks * features.shape[2]
    lat, rgb = proj_w.shape[1], head_w.shape[1]
    lat_cells = crops * cells // 4
    n_code, n_proj, n_head = (v.shape[0] // ranks for v in (code_w, proj_w, head_w))
    sizes = (n_code, n_proj, n_head, rgb)
    conv_rows = jnp.transpose(conv_w, (1, 0, 2))
    head_wide = jnp.pad(head_w, ((0, 0), (0, lat - rgb)))

    def lanes(v, n):
        return jnp.pad(v, ((0, 0),) * (v.ndim - 1) + ((0, n - v.shape[-1]),))

    side = [lanes(target, 16), lanes(jnp.repeat(mask.astype(F32), 3, axis=-1), 16)]
    side = lanes(jnp.concatenate(side + [codes.astype(F32)], axis=-1), 128)
    out = forward_call(
        features.reshape(ranks, crops, -1, ch),
        side.reshape(ranks, crops, -1, 128),
        conv_rows,
        code_w,
        proj_w,
        head_wide,
        gains,
    )
    x = out[0].reshape(crops, cells, ch)
    side = out[1].reshape(lat_cells, 128)
    w_all, rest = out[2:5], out[5]
    a_one, c_one, a_two, windows, s_low, wt = out[6:]
    codes = jnp.transpose(side[:, 32:36]).astype(jnp.int32).reshape(-1)
    n_rest = rest.shape[-2]
    d_s, loss, dp, d_small, d_down = quantizer_call(
        codes,
        rest.reshape(-1, n_rest, lat),
        side,
        s_low,
        windows,
        crops_all * cells // 4 * lat,
        crops_all * cells * 3,
        rgb,
        n_code,
    )

    def shards_of(v):
        return v.reshape(4, 2, 2, 2, -1, v.shape[-1])

    d_c_one, dg_two, down_kept, *kept = second_back_call(
        n_code,
        d_s,
        w_all[2],
        w_all[1],
        c_one,
        a_two,
        gains,
        codes[None],
        dp,
        shards_of(d_down),
        d_small.reshape(4, 2, 2, 2, -1, lat),
    )
    conv_row4 = jnp.transpose(conv_row).reshape(3, 4, -1, 1)
    rest_row4 = [v.reshape(4, -1) for v in (code_row, proj_row, head_row)]
    rest_row4.append(jnp.ones((4, n_rest - n_code - n_proj - n_head), F32))
    rest_row4 = jnp.concatenate(rest_row4, axis=1)[:, :, None]
    out = first_back_call(
        sizes,
        d_c_one,
        x,
        gains,
        w_all[0],
        a_one,
        kept,
        down_kept,
        dg_two,
        loss,
        wt,
        (conv_row4, rest_row4),
    )
    conv_rn, rest_rn, tv = out[7:]
    head_col_wide = jnp.pad(head_col, (0, lat - rgb), constant_values=1.0)
    loss, conv_outs, rest_outs, gain_outs = finish_call(
        sizes + (shards,),
        out[:7],
        (conv_rows, code_w, proj_w, head_wide),
        (conv_rn, rest_rn),
        tv,
        (conv_col, code_col[None], proj_col[None], head_col_wide[None]),
        gains,
        gain_state,
    )
    conv_g, conv_c, conv_n, conv_l = conv_outs
    code_o, proj_o, head_o = rest_outs
    cuts = (n_code, n_code + n_proj, n_code + n_proj + n_head)
    code_r, proj_r, head_r = (
        v.reshape(-1) for v in jnp.split(rest_rn[:, :, 0], cuts, axis=1)[:3]
    )

    def back(v):
        return jnp.transpose(v, (1, 0, 2))

    return (
        loss[0, 0],
        back(conv_g),
        jnp.transpose(conv_rn.reshape(3, -1)),
        conv_c,
        back(conv_n),
        back(conv_l),
        proj_o[0],
        proj_r,
        proj_o[1][0],
        proj_o[2],
        proj_o[3],
        code_o[0],
        code_r,
        code_o[1][0],
        code_o[2],
        code_o[3],
        head_o[0][:, :rgb],
        head_r,
        head_o[1][0, :rgb],
        head_o[2][:, :rgb],
        head_o[3][:, :rgb],
        *gain_outs,
    )


def solution(mesh):
    cell = P("batch", "rows", None, None)
    mat, vec = P("batch", None), P("batch")
    placed = (cell,) * 4 + (P("batch", None, None), mat, mat, mat, P())
    placed += (mat, P()) + (vec, P()) * 3 + (P(),)
    conv_outs = (P("batch", None, None), mat, P(), P("batch", None, None), P("batch", None, None))
    mat_outs = (mat, vec, P(), mat, mat)
    fast = (mesh.shape["rows"], mesh.shape["batch"]) == (4, 8)
    return jax.shard_map(
        local_fast if fast else local_any,
        mesh=mesh,
        in_specs=placed,
        out_specs=(P(),) + conv_outs + mat_outs * 3 + (P(),) * 3,
        check_vma=False,
    )
```

```python
import functools

import jax
import jax.numpy as jnp
from jax import lax
from jax.experimental import pallas as pl
from jax.experimental.pallas import tpu as pltpu
from jax.sharding import PartitionSpec as P

GROUPS = 32
BETA = 0.25
RATE = 0.5
EPS_NORM = 1e-05
EPS_SQ = 1e-30
BF = jnp.bfloat16
F32 = jnp.float32
BOTH = ("batch", "rows")
MIB = 1 << 20
VM = pl.BlockSpec(memory_space=pltpu.VMEM)
ANY = pl.BlockSpec(memory_space=pl.ANY)
MESH = pl.DeviceIdType.MESH


def group_sum(v):
    lane = lax.broadcasted_iota(jnp.int32, v.shape, 1)
    width = v.shape[1]
    for k in (1, 2, 4, 8):
        up = pltpu.roll(v, k, 1)
        down = pltpu.roll(v, width - k, 1)
        v = v + jnp.where((lane & k) != 0, up, down)
    return v


def moments(v):
    count = v.shape[0] * (v.shape[1] // GROUPS)
    sums = jnp.concatenate(
        [jnp.sum(v, axis=0, keepdims=True), jnp.sum(v * v, axis=0, keepdims=True)]
        + [jnp.zeros((6, v.shape[1]), F32)],
        axis=0,
    )
    sums = group_sum(sums) / count
    mean = sums[0:1]
    return mean, lax.rsqrt(sums[1:2] - mean * mean + EPS_NORM)


def shifted(v, by):
    cells = v.shape[0]
    col = lax.broadcasted_iota(jnp.int32, v.shape, 0) & 15
    edge = 0 if by == 1 else 15
    return jnp.where(col == edge, 0.0, pltpu.roll(v, by % cells, 0))


def fill_three(dst, left, mid, right):
    ch = mid.shape[1]
    for k, v in enumerate((left, mid, right)):
        dst[1:17, :, k * ch : (k + 1) * ch] = v.astype(BF).reshape(16, 16, ch)


def zero_edges(dst):
    dst[0] = jnp.zeros(dst.shape[1:], dst.dtype)
    dst[17] = jnp.zeros(dst.shape[1:], dst.dtype)


def put_lanes(dst, rows, v):
    for k in range(dst.shape[0]):
        dst[k, rows, :] = v[:, k * 128 : (k + 1) * 128]


def get_lanes(src, rows):
    return jnp.concatenate([src[k, rows, :] for k in range(src.shape[0])], axis=1)


def conv_rows(src, w_ref):
    acc = None
    width = src.shape[2]
    for dy in range(3):
        lhs = src[dy : dy + 16].reshape(256, width)
        d = jnp.dot(lhs, w_ref[dy * width : (dy + 1) * width, :], preferred_element_type=F32)
        acc = d if acc is None else acc + d
    return acc


def conv_rows_back(src, w_ref):
    acc = None
    ch = src.shape[2] // 3
    for dy in range(3):
        for dx in range(3):
            lhs = src[2 - dy : 18 - dy, :, dx * ch : (dx + 1) * ch].reshape(256, ch)
            t = (dy * 3 + dx) * ch
            d = lax.dot_general(
                lhs, w_ref[t : t + ch, :], (((1,), (1,)), ((), ())), preferred_element_type=F32
            )
            acc = d if acc is None else acc + d
    return acc


def conv_weight_grad(a_ref, d3_ref, dw_ref, half, tick=None):
    crops, cells, ch = a_ref.shape
    nb = 256
    out = slice(half * nb, (half + 1) * nb)

    def block(dx, carry):
        if tick is not None:
            tick(dx)
        lane = pl.multiple_of(dx * ch + half * nb, nb)
        for dy in range(3):
            rhs = d3_ref[:, 2 - dy : 18 - dy, :, pl.ds(lane, nb)].reshape(crops * cells, nb)
            d = lax.dot_general(
                a_ref[...].reshape(crops * cells, ch),
                rhs,
                (((0,), (0,)), ((), ())),
                preferred_element_type=F32,
            )
            row = pl.multiple_of((dy * 3 + dx) * ch, ch)
            dw_ref[pl.ds(row, ch), out] = d.astype(dw_ref.dtype)
        return carry

    lax.fori_loop(0, 3, block, 0)


def silu(h):
    return h * jax.nn.sigmoid(h)


def first_crop(v, gains_ref, w_ref, a3):
    mean, rstd = moments(v)
    a = silu((v - mean) * rstd * gains_ref[0:1, :] + gains_ref[1:2, :])
    fill_three(a3, shifted(a, 1), a, shifted(a, -1))
    return a.astype(BF), conv_rows(a3, w_ref)


def second_crop(v, x, gains_ref, w_ref, l_ref, a3, y32):
    ch = v.shape[1]
    mean, rstd = moments(v)
    a = silu((v - mean) * rstd * gains_ref[2:3, :] + gains_ref[3:4, :])
    fill_three(a3, shifted(a, 1), a, shifted(a, -1))
    put_lanes(y32, slice(None), conv_rows(a3, w_ref) + x)
    even = get_lanes(y32, pl.ds(0, 128, stride=2))
    odd = get_lanes(y32, pl.ds(1, 128, stride=2))
    cell = lax.broadcasted_iota(jnp.int32, odd.shape, 0) & 7
    before = jnp.where(cell == 0, 0.0, pltpu.roll(odd, 1, 0))
    for dx, part in enumerate((before, even, odd)):
        part = part.reshape(8, 2, 8, ch)
        upper = part[:, 0].reshape(64, ch)
        lower = part[:, 1].reshape(64, ch)
        above = jnp.concatenate([jnp.zeros((8, ch), F32), lower[:56]], axis=0)
        for dy, rows in enumerate((above, upper, lower)):
            lane = (dy * 3 + dx) * ch
            l_ref[:, lane : lane + ch] = rows.astype(BF)
    return a.astype(BF)


def down_dot(l_ref, w_ref, s_ref):
    ch = s_ref.shape[1]
    nb = 256

    def block(j, carry):
        lane = pl.ds(pl.multiple_of(j * nb, nb), nb)
        d = jnp.dot(l_ref[...], w_ref[:, lane], preferred_element_type=F32)
        s_ref[:, lane] = d.astype(BF)
        return carry

    lax.fori_loop(0, ch // nb, block, 0)


def crop_rows(i):
    return pl.ds(pl.multiple_of(i * 64, 64), 64)


def first_conv_kernel(x_ref, gains_ref, w_ref, a_ref, c_ref, a3):
    zero_edges(a3)

    def crop(i, carry):
        a_ref[i], c_ref[i] = first_crop(x_ref[i].astype(F32), gains_ref, w_ref, a3)
        return carry

    lax.fori_loop(0, x_ref.shape[0], crop, 0)


def second_conv_kernel(c_in_ref, x_ref, gains_ref, w_ref, w_down_ref, a_ref, l_ref, s_ref, a3, y32):
    zero_edges(a3)

    def crop(i, carry):
        a_ref[i] = second_crop(
            c_in_ref[i],
            x_ref[i].astype(F32),
            gains_ref,
            w_ref,
            l_ref.at[crop_rows(i)],
            a3,
            y32,
        )
        return carry

    lax.fori_loop(0, x_ref.shape[0], crop, 0)
    down_dot(l_ref, w_down_ref, s_ref)


def down_input_grad(ds_ref, w_ref, dc_ref, y32):
    cells, ch = ds_ref.shape
    group = 4 if cells % 256 == 0 else 1
    size = 64 * group

    def dot_t(lhs, tap):
        return lax.dot_general(
            lhs.astype(BF),
            w_ref[tap * ch : (tap + 1) * ch, :],
            (((1,), (1,)), ((), ())),
            preferred_element_type=F32,
        )

    def crops(i, carry):
        here = ds_ref[pl.ds(pl.multiple_of(i * size, size), size), :].astype(F32)
        at = lax.broadcasted_iota(jnp.int32, here.shape, 0)

        def next_col(v):
            return jnp.where((at & 7) == 7, 0.0, pltpu.roll(v, size - 1, 0))

        right = next_col(here)
        under = jnp.where((at & 63) >= 56, 0.0, pltpu.roll(here, size - 8, 0))
        corner = next_col(under)
        ee = dot_t(here, 4)
        eo = dot_t(here, 5) + dot_t(right, 3)
        oe = dot_t(here, 7) + dot_t(under, 1)
        oo = dot_t(here, 8) + dot_t(right, 6) + dot_t(under, 2) + dot_t(corner, 0)

        def both_rows(top, bottom):
            top, bottom = top.reshape(8, 1, 8, ch), bottom.reshape(8, 1, 8, ch)
            return jnp.concatenate([top, bottom], axis=1).reshape(128, ch)

        for k in range(group):
            rows = slice(64 * k, 64 * k + 64)
            put_lanes(y32, pl.ds(0, 128, stride=2), both_rows(ee[rows], oe[rows]))
            put_lanes(y32, pl.ds(1, 128, stride=2), both_rows(eo[rows], oo[rows]))
            dc_ref[i * group + k] = get_lanes(y32, slice(None)).astype(BF)
        return carry

    lax.fori_loop(0, cells // size, crops, 0)


def down_weight_grad(l_ref, ds_ref, dw_ref):
    ch = ds_ref.shape[1]

    def block(t, carry):
        lane = pl.multiple_of(t * ch, ch)
        d = lax.dot_general(
            l_ref[:, pl.ds(lane, ch)],
            ds_ref[...],
            (((0,), (0,)), ((), ())),
            preferred_element_type=F32,
        )
        dw_ref[pl.ds(lane, ch), :] = d.astype(BF)
        return carry

    lax.fori_loop(0, 9, block, 0)


def down_back_kernel(ds_ref, l_ref, w_ref, dc_ref, dw_ref, y32):
    down_weight_grad(l_ref, ds_ref, dw_ref)
    down_input_grad(ds_ref, w_ref, dc_ref, y32)


def hidden_grad(v, gain, shift, d_act):
    mean, rstd = moments(v)
    vhat = (v - mean) * rstd
    h = vhat * gain + shift
    sig = jax.nn.sigmoid(h)
    return d_act * sig * (1.0 + h * (1.0 - sig)), vhat, rstd


def shift_all(dc_ref, d3, tick=None):
    def crop(i, carry):
        if tick is not None:
            tick(i)
        d = dc_ref[i].astype(F32)
        slot = d3.at[i]
        zero_edges(slot)
        fill_three(slot, shifted(d, -1), d, shifted(d, 1))
        return carry

    lax.fori_loop(0, dc_ref.shape[0], crop, 0)


def unit_back(v_of, gains_ref, w_ref, dg_ref, d3, row, din_ref=None, tick=None):
    crops, cells, ch = d3.shape[0], 256, d3.shape[3] // 3
    dg_ref[...] = jnp.zeros_like(dg_ref)

    def crop(i, carry):
        if tick is not None:
            tick(i)
        d_act = conv_rows_back(d3.at[i], w_ref)
        gain = gains_ref[row : row + 1, :]
        hg, vhat, rstd = hidden_grad(v_of(i), gain, gains_ref[row + 1 : row + 2, :], d_act)
        one = jnp.sum(hg * vhat, axis=0, keepdims=True)
        two = jnp.sum(hg, axis=0, keepdims=True)
        dg_ref[0:1, :] += one
        dg_ref[1:2, :] += two
        if din_ref is not None:
            count = cells * (ch // GROUPS)
            sums = jnp.concatenate([two * gain, one * gain, jnp.zeros((6, ch), F32)], axis=0)
            sums = group_sum(sums) / count
            din_ref[i] = (rstd * (hg * gain - sums[0:1] - vhat * sums[1:2])).astype(BF)
        return carry

    lax.fori_loop(0, crops, crop, 0)


def unit_back_kernel(dc_ref, v_ref, gains_ref, w_ref, a_ref, *outs, row, inner):
    if inner:
        din_ref, dw_ref, dg_ref, d3 = outs
    else:
        dw_ref, dg_ref, d3 = outs
        din_ref = None

    def v_of(i):
        return v_ref[i].astype(F32)

    shift_all(dc_ref, d3)
    unit_back(v_of, gains_ref, w_ref, dg_ref, d3, row, din_ref)
    for half in range(2):
        conv_weight_grad(a_ref, d3, dw_ref, half)


def kernel_call(body, outs, scratch, flops, *args):
    bytes_accessed = sum(a.size * a.dtype.itemsize for a in args)
    bytes_accessed += sum(o.size * o.dtype.itemsize for o in outs)
    return pl.pallas_call(
        body,
        out_shape=outs,
        in_specs=[VM] * len(args),
        out_specs=[VM] * len(outs),
        scratch_shapes=scratch,
        compiler_params=pltpu.CompilerParams(vmem_limit_bytes=56 * MIB),
        cost_estimate=pl.CostEstimate(
            flops=flops, bytes_accessed=bytes_accessed, transcendentals=0
        ),
    )(*args)


class Place:
    def __init__(self):
        rows, batch = lax.axis_index("rows"), lax.axis_index("batch")
        self.x, self.c = rows // 2, rows % 2
        self.z, self.y = batch // 2, batch % 2
        self.part = self.c * 2 + self.x

    def at(self, x=None, c=None, z=None, y=None):
        x = self.x if x is None else x
        c = self.c if c is None else c
        z = self.z if z is None else z
        y = self.y if y is None else y
        return {"rows": 2 * x + c, "batch": 2 * z + y}

    def row_peers(self):
        return [
            self.at(c=1 - self.c),
            self.at(x=1 - self.x),
            self.at(x=1 - self.x, c=1 - self.c),
        ]

    def z_peers(self):
        return [self.at(z=(self.z + d) % 4) for d in (1, 2, 3)]

    def greet(self):
        barrier = pltpu.get_barrier_semaphore()
        peers = self.row_peers() + self.z_peers() + [self.at(y=1 - self.y)]
        for peer in peers:
            pl.semaphore_signal(barrier, inc=1, device_id=peer, device_id_type=MESH)
        pl.semaphore_wait(barrier, len(peers))


def remote(src, dst, send, recv, peer):
    return pltpu.make_async_remote_copy(
        src_ref=src, dst_ref=dst, send_sem=send, recv_sem=recv, device_id=peer, device_id_type=MESH
    )


class Gather:
    def __init__(self, place, src, dst, send, recv, route):
        self.p, self.src, self.dst, self.send, self.recv = place, src, dst, send, recv
        self.route = "z" + route + "c"
        self.steps = len(self.route)

    def copies(self, step):
        p, src, dst, send, recv = self.p, self.src, self.dst, self.send, self.recv
        axis = self.route[step]
        if axis == "z":
            mine = (p.c, p.x) if "x" in self.route else (p.c,)
            here, there = src.at[mine], dst.at[(p.z, p.y) + mine]
            out = [
                remote(here, there, send.at[k], recv.at[k], q) for k, q in enumerate(p.z_peers())
            ]
            return out + [pltpu.make_async_copy(here, there, recv.at[6])]
        have_y = "y" in self.route[:step]
        have_x = "x" in self.route[:step] or "x" not in self.route
        part = dst.at[:, slice(None) if have_y else p.y, p.c]
        if not have_x:
            part = dst.at[:, slice(None) if have_y else p.y, p.c, p.x]
        k = 3 + "yxc".index(axis)
        peer = {"y": p.at(y=1 - p.y), "x": p.at(x=1 - p.x), "c": p.at(c=1 - p.c)}[axis]
        return [remote(part, part, send.at[k], recv.at[k], peer)]

    def start(self, step):
        for copy in self.copies(step):
            copy.start()

    def arrive(self, step):
        for copy in self.copies(step):
            copy.wait_recv()

    def go(self, step):
        self.arrive(step - 1)
        self.start(step)

    def finish(self):
        for step in range(self.steps):
            for copy in self.copies(step):
                if copy.is_remote:
                    copy.wait_send()


class Reduce:
    steps = 6

    def __init__(self, place, src, out, mine, one, two, three, kept, four, send, recv, turn=True):
        self.p, self.src, self.out = place, src, out
        self.mine, self.one, self.two, self.three, self.four = mine, one, two, three, four
        self.send, self.recv = send, recv
        first_x = (place.c == 0) & turn
        self.turn = turn
        self.f = jnp.where(first_x, place.x, place.y)
        self.g = jnp.where(first_x, place.y, place.x)
        self.f_peer = place.at(
            x=jnp.where(first_x, 1 - place.x, place.x), y=jnp.where(first_x, place.y, 1 - place.y)
        )
        self.g_peer = place.at(
            x=jnp.where(first_x, place.x, 1 - place.x), y=jnp.where(first_x, 1 - place.y, place.y)
        )
        self.slot = 2 * self.f + self.g
        self.kept = kept

    @staticmethod
    def early(rows, lanes):
        return [pltpu.VMEM(lead + (rows, lanes), BF) for lead in ((4, 4), (4, 4), (2, 4), (4,))]

    @staticmethod
    def late(rows, lanes, kept):
        return [pltpu.VMEM(lead + (rows, lanes), BF) for lead in ((4,),) * kept + ((3,),)]

    @staticmethod
    def sems():
        return [pltpu.SemaphoreType.DMA((11,)), pltpu.SemaphoreType.DMA((15,))]

    def copies(self, step):
        p, src, mine, send, recv = self.p, self.src, self.mine, self.send, self.recv
        if step == 0:
            out = []
            for k in range(4):
                y, x = k // 2, k % 2
                there = jnp.where((p.c == 1) & self.turn, 2 * x + y, 2 * y + x)
                here = jnp.where((p.c == 0) & self.turn, 2 * x + y, 2 * y + x)
                part = src.at[:, y, 1 - p.c, x]
                peer = p.at(c=1 - p.c)
                out.append(remote(part, self.one.at[there], send.at[k], recv.at[k], peer))
                local = src.at[:, y, p.c, x]
                out.append(pltpu.make_async_copy(local, mine.at[here], recv.at[10 + k]))
            return out
        if step == 1:
            part = mine.at[pl.ds(2 * (1 - self.f), 2)]
            return [remote(part, self.two, send.at[4], recv.at[4], self.f_peer)]
        if step == 2:
            part = mine.at[2 * self.f + 1 - self.g]
            return [remote(part, self.three, send.at[5], recv.at[5], self.g_peer)]
        if step == 3:
            out = []
            for d, peer in zip((1, 2, 3), p.z_peers()):
                part = self.kept.at[(p.z + d) % 4]
                out.append(remote(part, self.four.at[d - 1], send.at[5 + d], recv.at[5 + d], peer))
            return out
        if step == 4:
            part = self.out.at[p.part]
            return [remote(part, part, send.at[9], recv.at[9], p.at(x=1 - p.x))]
        part = self.out.at[pl.ds(2 * p.c, 2)]
        return [remote(part, part, send.at[10], recv.at[14], p.at(c=1 - p.c))]

    def start(self, step):
        for copy in self.copies(step):
            copy.start()

    def arrive(self, step):
        p, mine = self.p, self.mine
        for copy in self.copies(step):
            copy.wait_recv()

        def add(dst, a, b):
            dst[...] = (a[...].astype(F32) + b[...].astype(F32)).astype(BF)

        if step == 0:

            def body(i, carry):
                at = (i // 4, i % 4)
                add(mine.at[at], mine.at[at], self.one.at[at])
                return carry

            lax.fori_loop(0, 16, body, 0)
        if step == 1:
            for copy in self.copies(step):
                copy.wait_send()

            def body(i, carry):
                at = (2 * self.f + i // 4, i % 4)
                add(mine.at[at], mine.at[at], self.two.at[i // 4, i % 4])
                return carry

            lax.fori_loop(0, 8, body, 0)
        if step == 2:

            def body(i, carry):
                add(self.kept.at[i], mine.at[self.slot, i], self.three.at[i])
                return carry

            lax.fori_loop(0, 4, body, 0)
        if step == 3:
            total = self.kept[p.z].astype(F32)
            for d in range(3):
                total = total + self.four[d].astype(F32)
            self.out[p.part] = total.astype(BF)

    def go(self, step):
        self.arrive(step - 1)
        self.start(step)

    def sent(self, first, last):
        for step in range(first, last):
            if step == 1:
                continue
            for copy in self.copies(step):
                if copy.is_remote:
                    copy.wait_send()


class ReduceZ(Reduce):
    def copies(self, step):
        p, send, recv = self.p, self.send, self.recv
        if step == 1:
            out = []
            for d, peer in zip((1, 2, 3), p.z_peers()):
                part = self.mine.at[:, (p.z + d) % 4]
                out.append(remote(part, self.four.at[d - 1], send.at[5 + d], recv.at[5 + d], peer))
            return out
        if step == 2:
            part = self.kept.at[pl.ds(2 * (1 - self.f), 2)]
            return [remote(part, self.two, send.at[4], recv.at[4], self.f_peer)]
        if step == 3:
            part = self.pair.at[1 - self.g]
            return [remote(part, self.three, send.at[5], recv.at[5], self.g_peer)]
        return super().copies(step)

    def arrive(self, step):
        if step not in (1, 2, 3):
            super().arrive(step)
            return
        for copy in self.copies(step):
            copy.wait_recv()
        if step == 1:

            def body(i, carry):
                total = self.mine[i, self.p.z].astype(F32)
                for d in range(3):
                    total = total + self.four[d, i].astype(F32)
                self.kept[i] = total.astype(BF)
                return carry

            lax.fori_loop(0, 4, body, 0)
        if step == 2:
            for copy in self.copies(step):
                copy.wait_send()
            for k in range(2):
                at = 2 * self.f + k
                self.pair[k] = (self.kept[at].astype(F32) + self.two[k].astype(F32)).astype(BF)
        if step == 3:
            total = self.pair[self.g].astype(F32) + self.three[...].astype(F32)
            self.out[self.p.part] = total.astype(BF)

    def sent(self, first, last):
        for step in range(first, last):
            if step == 2:
                continue
            for copy in self.copies(step):
                if copy.is_remote:
                    copy.wait_send()


def stand(flat_ref, pad_ref, width):
    rows, lanes = flat_ref.shape
    pad_ref[...] = jnp.zeros_like(pad_ref)
    pad_ref[:rows, :lanes] = flat_ref[...]
    turned = jnp.transpose(pad_ref[...])[:lanes]
    return jnp.concatenate([turned, jnp.zeros((lanes, width - turned.shape[1]), F32)], axis=1)


PARTS = (('w0b', 'yx', 1, None), ('w0a', 'yx', 0, None), ('r1', 'yx', 1, 0), ('w1b', 'yx', 1, None), ('w2b', 'yx', 1, None), ('w2a', 'yx', 0, None), ('w1a', 'y', 0, None), ('r3', 'y', 1, 1), ('r0', 'y', 0, 0), ('r2', 'y', 0, 1))
BEFORE = ('w0b1', 'w0a1', 'w0b2', 'r11', 'w0a2', 'w1b1', 'r12', 'w2b1', 'w0b3', 'w1b2', 'w2a1', 'w2b2', 'w0a3', 'w2a2', 'w1a1')
FIRST = {3: ('r13',), 4: ('r31',), 6: ('w1a2',), 7: ('w1b3',)}
BETWEEN = ('r01',)
SECOND = {1: ('r32',), 3: ('w2b3', 'r21'), 5: ('r02',), 6: ('w2a3',)}
AFTER = ('r22',)


def forward_kernel(
    feat,
    side,
    conv_ref,
    code_ref,
    proj_ref,
    head_flat_ref,
    gains_ref,
    x_out,
    side_out,
    w_out0,
    w_out1,
    w_out2,
    rest_out,
    a_one_out,
    c_one_out,
    a_two_out,
    l_out,
    s_ref,
    wt_ref,
    a_one_ref,
    c_one_ref,
    a_two_ref,
    l_ref,
    k_sem,
    head_pad,
    head_ref,
    w_mine,
    rest_mine,
    xv,
    wv0,
    wv1,
    wv2,
    a3,
    y32,
    x_send,
    x_recv,
    g_send,
    g_recv,
    o_sem,
):
    place = Place()
    rank = 2 * place.x + place.c
    ch, lat = conv_ref.shape[2], code_ref.shape[1]
    n_code, n_proj, n_head = (v.shape[0] // 4 for v in (code_ref, proj_ref, head_ref))
    wt_ref[...] = jnp.zeros_like(wt_ref)

    def cast_conv(j):
        n = w_mine.shape[3]
        for k in range(4):
            v = conv_ref[j, k * n : (k + 1) * n, :]
            w_mine[j, k // 2, k % 2] = v.astype(BF)
            wt_ref[j : j + 1, :] += jnp.sum(v * v, axis=0, keepdims=True)

    def cast_rest():
        head_ref[...] = stand(head_flat_ref, head_pad, lat)
        for k in range(4):
            low = 0
            for m, (ref, n) in enumerate(
                ((code_ref, n_code), (proj_ref, n_proj), (head_ref, n_head))
            ):
                v = ref[k * n : (k + 1) * n, :]
                wt_ref[3 + m : 4 + m, :lat] += jnp.sum(v * v, axis=0, keepdims=True)
                if n % 16:
                    v = jnp.concatenate([v, jnp.zeros((-n % 16, lat), F32)], axis=0)
                rest_mine[k // 2, k % 2, low : low + v.shape[0]] = v.astype(BF)
                low += v.shape[0]

    cast_conv(0)
    place.greet()

    def view(ref, lanes):
        n = ref.shape[0] // 32
        return ref.reshape(4, 2, 2, 2, n, ref.shape[1]).at[..., lanes]

    jobs = {}
    views = [view(wv0, slice(None)), view(wv1, slice(None)), view(wv2, slice(None)), rest_out]
    for k, (name, route, lane, row) in enumerate(PARTS):
        rest = name[0] == "r"
        src = rest_mine if rest else w_mine.at[int(name[1])]
        dst = views[3] if rest else views[int(name[1])]
        n = src.shape[-2]
        parts, which = (2, lane) if row is None else (4, 2 * row + lane)
        cut = [k * n // (16 * parts) * 16 for k in range(parts)] + [n]
        at = (..., pl.ds(cut[which], cut[which + 1] - cut[which]), slice(None))
        jobs[name] = Gather(place, src.at[at], dst.at[at], g_send.at[k], g_recv.at[k], route)

    def go(words):
        for word in words:
            jobs[word[:-1]].go(int(word[-1]))

    def ticks(table):
        def tick(i):
            for when, words in table.items():

                @pl.when(i == when)
                def _():
                    go(words)

        return tick

    def whole(names):
        for name in names:
            jobs[name].arrive(jobs[name].steps - 1)

    cells = []
    for src, dst, base in ((feat, xv, 0), (side, side_out, 4)):
        for k, q in enumerate(place.row_peers()):
            to = q["rows"]
            cells.append(
                remote(src.at[to], dst.at[:, rank], x_send.at[base + k], x_recv.at[base + k], q)
            )
        cells.append(pltpu.make_async_copy(src.at[rank], dst.at[:, rank], x_recv.at[base + 3]))

    started = PARTS[0][0]
    jobs[started].start(0)
    for copy in cells:
        copy.start()
    cast = {"0"}
    for name, *_ in PARTS[1:]:
        which = name[1] if name[0] == "w" else "rest"
        if which not in cast:
            cast_rest() if which == "rest" else cast_conv(int(which))
            cast.add(which)
        jobs[name].start(0)
    go(BEFORE)
    zero_edges(a3)
    for copy in cells:
        copy.wait_recv()
    keep_x = pltpu.make_async_copy(xv, x_out, o_sem.at[0])
    keep_x.start()
    whole(("w0a", "w0b"))
    keep_w = [
        pltpu.make_async_copy(v, o, o_sem.at[1 + k])
        for k, (v, o) in enumerate(((wv0, w_out0), (wv1, w_out1), (wv2, w_out2)))
    ]
    keep_w[0].start()
    count = xv.shape[0]

    def crop_x(i):
        return xv[i].reshape(256, ch).astype(F32)

    tick_first, tick_second = ticks(FIRST), ticks(SECOND)

    def keep_first(i):
        return [
            pltpu.make_async_copy(v.at[i], o.at[i], k_sem.at[k, i])
            for k, (v, o) in enumerate(((a_one_ref, a_one_out), (c_one_ref, c_one_out)))
        ]

    def keep_second(i):
        rows = crop_rows(i)
        return [
            pltpu.make_async_copy(a_two_ref.at[i], a_two_out.at[i], k_sem.at[2, i]),
            pltpu.make_async_copy(l_ref.at[rows], l_out.at[rows], k_sem.at[3, i]),
        ]

    def first(i, carry):
        tick_first(i)
        a_one_ref[i], c_one_ref[i] = first_crop(crop_x(i), gains_ref, wv0, a3)
        for copy in keep_first(i):
            copy.start()
        return carry

    lax.fori_loop(0, count, first, 0)
    go(BETWEEN)
    whole(("w1a", "w1b"))
    keep_w[1].start()

    def second(i, carry):
        tick_second(i)
        a_two_ref[i] = second_crop(
            c_one_ref[i], crop_x(i), gains_ref, wv1, l_ref.at[crop_rows(i)], a3, y32
        )
        for copy in keep_second(i):
            copy.start()
        return carry

    lax.fori_loop(0, count, second, 0)
    whole(("w2a", "w2b"))
    keep_w[2].start()
    down_dot(l_ref, wv2, s_ref)
    go(AFTER)
    whole(("r0", "r1", "r2", "r3"))
    for job in jobs.values():
        job.finish()
    for copy in cells:
        if copy.is_remote:
            copy.wait_send()
    keep_x.wait()
    for copy in keep_w:
        copy.wait()

    def kept(i, carry):
        for copy in keep_first(i) + keep_second(i):
            copy.wait()
        return carry

    lax.fori_loop(0, count, kept, 0)


def forward_call(feat, side, conv_w, code_w, proj_w, head_w, gains):
    ranks, crops, cells, ch = feat.shape
    lat = code_w.shape[1]
    lat_cells = crops * ranks * cells // 4
    n_conv = conv_w.shape[1] // 4
    n_rest = code_w.shape[0] // 4 + proj_w.shape[0] // 4 + 16
    whole = 32 * n_conv

    def shape(*dims, dtype=BF):
        return jax.ShapeDtypeStruct(dims, dtype)

    outs = [
        shape(crops, ranks, cells, ch),
        shape(crops, ranks, *side.shape[2:], dtype=F32),
        shape(whole, ch),
        shape(whole, ch),
        shape(whole, ch),
        shape(4, 2, 2, 2, n_rest, lat),
        shape(crops, ranks * cells, ch),
        shape(crops, ranks * cells, ch, dtype=F32),
        shape(crops, ranks * cells, ch),
        shape(lat_cells, 9 * ch),
        shape(lat_cells, ch),
        shape(8, ch, dtype=F32),
    ]
    return pl.pallas_call(
        forward_kernel,
        out_shape=outs,
        in_specs=[ANY] * 2 + [VM] * 5,
        out_specs=[ANY] * 10 + [VM] * 2,
        scratch_shapes=[
            pltpu.VMEM((crops, ranks * cells, ch), BF),
            pltpu.VMEM((crops, ranks * cells, ch), F32),
            pltpu.VMEM((crops, ranks * cells, ch), BF),
            pltpu.VMEM((lat_cells, 9 * ch), BF),
            pltpu.SemaphoreType.DMA((4, crops)),
            pltpu.VMEM((128, 128), F32),
            pltpu.VMEM((head_w.shape[1], lat), F32),
            pltpu.VMEM((3, 2, 2, n_conv, ch), BF),
            pltpu.VMEM((2, 2, n_rest, lat), BF),
            pltpu.VMEM((crops, ranks, cells, ch), BF),
        ]
        + [pltpu.VMEM((whole, ch), BF)] * 3
        + [
            pltpu.VMEM((18, 16, 3 * ch), BF),
            pltpu.VMEM((ch // 128, ranks * cells, 128), F32),
            pltpu.SemaphoreType.DMA((8,)),
            pltpu.SemaphoreType.DMA((8,)),
            pltpu.SemaphoreType.DMA((len(PARTS), 8)),
            pltpu.SemaphoreType.DMA((len(PARTS), 8)),
            pltpu.SemaphoreType.DMA((4,)),
        ],
        compiler_params=pltpu.CompilerParams(
            vmem_limit_bytes=58 * MIB, collective_id=2, has_side_effects=True
        ),
        cost_estimate=pl.CostEstimate(
            flops=45 * crops * ranks * cells * ch * ch,
            bytes_accessed=0,
            transcendentals=0,
        ),
    )(feat, side, conv_w, code_w, proj_w, head_w, gains)


def quantizer_kernel(
    consts,
    codes_ref,
    rest,
    side_ref,
    sl_ref,
    l_in,
    ds_ref,
    loss_ref,
    dp_ref,
    small_ref,
    dw_ref,
    tab,
    stage,
    proj_v,
    head_v,
    e_ref,
    l_ref,
    sems,
):
    lat_count, pix_count, rgb, n_code = consts
    cells = sl_ref.shape[0]
    pieces = rest.shape[0]
    slots = stage.shape[0]
    lat = tab.shape[1]
    small = [
        pltpu.make_async_copy(rest.at[:, n_code : n_code + 16], proj_v, sems.at[slots]),
        pltpu.make_async_copy(rest.at[:, n_code + 16 :], head_v, sems.at[slots + 1]),
    ]
    windows = pltpu.make_async_copy(l_in, l_ref, sems.at[slots + 2])
    for copy in small:
        copy.start()

    def fetch(p):
        slot = p % slots
        return pltpu.make_async_copy(rest.at[p, :n_code], stage.at[slot], sems.at[slot])

    for p in range(slots):
        fetch(p).start()
    windows.start()

    def widen(p, carry):
        fetch(p).wait()
        tab[pl.ds(pl.multiple_of(p * n_code, n_code), n_code), :] = stage[p % slots].astype(F32)

        @pl.when(p + slots < pieces)
        def _():
            fetch(p + slots).start()

        return carry

    lax.fori_loop(0, pieces, widen, 0)
    for copy in small:
        copy.wait()
    proj = proj_v[...].reshape(-1, lat)
    head = head_v[...].astype(F32)[:, :8, :128].reshape(-1, 128).astype(BF)

    def pick(b, carry):
        for j in range(8):
            for k in range(4):
                row = codes_ref[k * cells + b * 8 + j]
                e_ref[k, pl.ds(b * 8 + j, 1), :] = tab[pl.ds(row, 1), :]
        return carry

    lax.fori_loop(0, cells // 8, pick, 0)

    latent = jnp.dot(sl_ref[...], proj, preferred_element_type=F32)
    cum = e_ref[0]
    resid = []
    square = None
    for k in range(4):
        if k:
            cum = cum + e_ref[k]
        r = latent - cum
        resid.append(r)
        part = jnp.sum(r * r, axis=0, keepdims=True)
        square = part if square is None else square + part
    zq = cum.astype(BF)
    side = side_ref[...]
    valid = lax.broadcasted_iota(jnp.int32, side.shape, 1) < rgb
    weight = jnp.where(valid, pltpu.roll(side, 128 - 16, 1), 0.0)
    diff = jnp.where(valid, jnp.dot(zq, head, preferred_element_type=F32) - side, 0.0)
    smooth = jnp.sqrt(diff * diff + 1.0)
    recon = jnp.sum(weight * (smooth - 1.0), axis=0, keepdims=True)
    loss_ref[...] = jnp.zeros_like(loss_ref)
    loss_ref[0:1, 0:lat] = square * ((1.0 + BETA) / lat_count)
    loss_ref[0:1, lat : lat + 128] = recon / pix_count
    d_pred = (weight * (diff / smooth) / pix_count).astype(BF)
    back = (((1,), (1,)), ((), ()))
    rows = (((0,), (0,)), ((), ()))
    d_head = lax.dot_general(zq, d_pred, rows, preferred_element_type=F32)
    total = resid[0] + resid[1] + resid[2] + resid[3]
    d_zq = lax.dot_general(d_pred, head, back, preferred_element_type=F32)
    d_lat = (total * (2.0 * BETA / lat_count) + d_zq).astype(BF)
    d_proj = lax.dot_general(sl_ref[...], d_lat, rows, preferred_element_type=F32)
    d_s = lax.dot_general(d_lat, proj, back, preferred_element_type=F32)
    ds_ref[...] = d_s.astype(BF)
    tail = None
    for k in (3, 2, 1, 0):
        tail = resid[k] if tail is None else tail + resid[k]
        dp_ref[k * cells : (k + 1) * cells, :] = (tail * (-2.0 / lat_count)).astype(BF)
    small_ref[:, :16] = d_proj.astype(BF).reshape(pieces, 16, lat)
    d_head = jnp.concatenate([d_head, jnp.zeros((d_head.shape[0], lat - 128), F32)], axis=1)
    d_head = d_head.reshape(pieces, 8, lat)
    d_head = jnp.concatenate([d_head, jnp.zeros((pieces, 8, lat), F32)], axis=1)
    small_ref[:, 16:] = d_head.astype(BF)
    windows.wait()
    down_weight_grad(l_ref, ds_ref, dw_ref)


def quantizer_call(codes, rest, side, s_low, windows, lat_count, pix_count, rgb, n_code):
    pieces, rows, lat = rest.shape
    cells, ch = s_low.shape
    outs = [
        jax.ShapeDtypeStruct((cells, ch), BF),
        jax.ShapeDtypeStruct((8, ch), F32),
        jax.ShapeDtypeStruct((4 * cells, lat), BF),
        jax.ShapeDtypeStruct((pieces, 32, lat), BF),
        jax.ShapeDtypeStruct((9 * ch, ch), BF),
    ]
    return pl.pallas_call(
        functools.partial(quantizer_kernel, (lat_count, pix_count, rgb, n_code)),
        out_shape=outs,
        in_specs=[pl.BlockSpec(memory_space=pltpu.SMEM), ANY, VM, VM, ANY],
        out_specs=[VM] * 5,
        scratch_shapes=[
            pltpu.VMEM((pieces * n_code, lat), F32),
            pltpu.VMEM((4, n_code, lat), BF),
            pltpu.VMEM((pieces, 16, lat), BF),
            pltpu.VMEM((pieces, rows - n_code - 16, lat), BF),
            pltpu.VMEM((4, cells, lat), F32),
            pltpu.VMEM(windows.shape, BF),
            pltpu.SemaphoreType.DMA((7,)),
        ],
        compiler_params=pltpu.CompilerParams(vmem_limit_bytes=58 * MIB),
        cost_estimate=pl.CostEstimate(flops=10**10, bytes_accessed=10**7, transcendentals=0),
    )(codes, rest, side, s_low, windows)


def second_back_kernel(
    n_code,
    ds_ref,
    gains_ref,
    codes_ref,
    dp_ref,
    w_down_in,
    w_in,
    c_in,
    a_in,
    down_src,
    small_src,
    din_ref,
    dg_ref,
    down_kept_ref,
    kept0_ref,
    kept1_ref,
    rest_kept_ref,
    w_down_ref,
    w_ref,
    c_ref,
    a_ref,
    l_sem,
    dw,
    d3,
    y32,
    dp_all,
    codes_all,
    quarter,
    quarter_in,
    small_in,
    e_send,
    e_recv,
    *bufs,
):
    place = Place()
    bufs = list(bufs)

    def take(n):
        out = bufs[:n]
        del bufs[:n]
        return out

    loads = [
        pltpu.make_async_copy(src, dst, l_sem.at[k])
        for k, (src, dst) in enumerate(
            ((w_down_in, w_down_ref), (a_in, a_ref), (w_in, w_ref), (c_in, c_ref))
        )
    ]
    for copy in loads:
        copy.start()
    half = down_src.shape[-1] // 2
    view = dw.reshape(4, 2, 2, 2, dw.shape[0] // 32, dw.shape[1])
    mine, one, four, send, recv = take(5)
    down = ReduceZ(place, down_src, None, mine, one, None, None, down_kept_ref, four, send, recv)
    early, sems = take(4), take(2)
    low = Reduce(place, view.at[..., :half], None, *early, kept0_ref, None, *sems)
    early, sems = take(4), take(2)
    high = Reduce(place, view.at[..., half:], None, *early, kept1_ref, None, *sems)

    across = place.at(x=1 - place.x)
    other = place.at(c=1 - place.c)
    two = pl.ds(2 * place.c, 2)
    entries = [(dp_ref, dp_all, 0), (codes_ref, codes_all, 1)]
    out_x = [
        remote(src, dst.at[place.part], e_send.at[k], e_recv.at[k], across) for src, dst, k in entries
    ]
    out_x += [
        pltpu.make_async_copy(src, dst.at[place.part], e_recv.at[2 + k]) for src, dst, k in entries
    ]
    out_c = [
        remote(dst.at[two], dst.at[two], e_send.at[4 + k], e_recv.at[4 + k], other)
        for _, dst, k in entries
    ]
    small = []
    for k, (x, c) in enumerate(
        ((place.x, 1 - place.c), (1 - place.x, place.c), (1 - place.x, 1 - place.c))
    ):
        small.append(
            remote(
                small_src.at[:, :, c, x],
                small_in.at[k],
                e_send.at[6 + k],
                e_recv.at[6 + k],
                place.at(x=x, c=c),
            )
        )
    small.append(
        pltpu.make_async_copy(small_src.at[:, :, place.c, place.x], small_in.at[3], e_recv.at[9])
    )
    out_y = [
        remote(
            quarter.at[1 - place.y, pl.ds(2 * k, 2)],
            quarter_in.at[pl.ds(2 * k, 2)],
            e_send.at[10 + k],
            e_recv.at[10 + k],
            place.at(y=1 - place.y),
        )
        for k in range(2)
    ]

    place.greet()
    down.start(0)
    for copy in out_x + small:
        copy.start()

    def piece(z, y):
        base = ((z * 2 + y) * 4 + place.part) * n_code
        row = lax.broadcasted_iota(jnp.int32, (n_code, dp_ref.shape[0]), 0) + base

        def add(k, total):
            hot = jnp.where(row == codes_all[k], 1.0, 0.0).astype(BF)
            return total + jnp.dot(hot, dp_all[k], preferred_element_type=F32)

        total = lax.fori_loop(0, 4, add, jnp.zeros((n_code, dp_ref.shape[1]), F32))
        quarter[y, z, :n_code] = total.astype(BF)
        total = small_in[3, z, y].astype(F32)
        for k in range(3):
            total = total + small_in[k, z, y].astype(F32)
        quarter[y, z, n_code:] = total.astype(BF)

    def codebook_grad():
        def away(z, carry):
            piece(z, 1 - place.y)

            for k in range(2):

                @pl.when(z == 2 * k + 1)
                def _():
                    out_y[k].start()

            return carry

        def here(z, carry):
            piece(z, place.y)

            @pl.when(z == 0)
            def _():
                low.go(2)

            @pl.when(z == 2)
            def _():
                high.go(2)

            return carry

        lax.fori_loop(0, 4, away, 0)
        lax.fori_loop(0, 4, here, 0)

    def tick_high(dx):
        @pl.when(dx == 2)
        def _():
            low.go(1)

    def tick_crop(i):
        @pl.when(i == 1)
        def _():
            high.go(1)
            for copy in out_x:
                copy.wait_recv()
            for copy in out_c:
                copy.start()

        @pl.when(i == 3)
        def _():
            for copy in out_c:
                copy.wait_recv()
            for copy in small:
                copy.wait_recv()
            codebook_grad()

        @pl.when(i == 7)
        def _():
            low.arrive(2)
            down.arrive(1)

    loads[0].wait()
    down_input_grad(ds_ref, w_down_ref, din_ref, y32)
    down.go(1)
    shift_all(din_ref, d3)
    loads[1].wait()
    conv_weight_grad(a_ref, d3, dw, 0)
    low.start(0)
    conv_weight_grad(a_ref, d3, dw, 1, tick_high)
    high.start(0)
    loads[2].wait()
    loads[3].wait()
    unit_back(lambda i: c_ref[i], gains_ref, w_ref, dg_ref, d3, 2, din_ref, tick_crop)
    for copy in out_y:
        copy.wait_recv()
    for z in range(4):
        total = quarter[place.y, z].astype(F32) + quarter_in[z].astype(F32)
        rest_kept_ref[z] = total.astype(BF)
    high.arrive(2)
    down.sent(0, 2)
    for job in (low, high):
        job.sent(0, 3)
    for copy in out_x[:2] + out_c + small[:3] + out_y:
        copy.wait_send()


def second_back_call(n_code, ds, w_down, w, c_one, a_two, gains, codes, dp, down_src, small_src):
    crops, cells, ch = c_one.shape
    n_conv, lat = down_src.shape[-2], dp.shape[-1]
    n_rest = n_code + small_src.shape[-2]

    def shape(*dims, dtype=BF):
        return jax.ShapeDtypeStruct(dims, dtype)

    outs = [
        shape(crops, cells, ch),
        shape(2, ch, dtype=F32),
        shape(4, n_conv, ch),
        shape(4, n_conv, ch // 2),
        shape(4, n_conv, ch // 2),
        shape(4, n_rest, lat),
    ]
    begun = Reduce.early(n_conv, ch // 2) + Reduce.sems()
    return pl.pallas_call(
        functools.partial(second_back_kernel, n_code),
        out_shape=outs,
        in_specs=[VM] * 4 + [ANY] * 6,
        out_specs=[VM] * 6,
        scratch_shapes=[
            pltpu.VMEM(w_down.shape, BF),
            pltpu.VMEM(w.shape, BF),
            pltpu.VMEM(c_one.shape, F32),
            pltpu.VMEM(a_two.shape, BF),
            pltpu.SemaphoreType.DMA((4,)),
            pltpu.VMEM(w.shape, BF),
            pltpu.VMEM((crops, 18, 16, 3 * ch), BF),
            pltpu.VMEM((ch // 128, cells, 128), F32),
            pltpu.VMEM((4,) + dp.shape, BF),
            pltpu.VMEM((4,) + codes.shape, jnp.int32),
            pltpu.VMEM((2, 4, n_rest, lat), BF),
            pltpu.VMEM((4, n_rest, lat), BF),
            pltpu.VMEM((4, 4, 2, small_src.shape[-2], lat), BF),
            pltpu.SemaphoreType.DMA((12,)),
            pltpu.SemaphoreType.DMA((12,)),
        ]
        + [pltpu.VMEM((k, 4, n_conv, ch), BF) for k in (4, 4, 3)]
        + Reduce.sems()
        + begun * 2,
        compiler_params=pltpu.CompilerParams(
            vmem_limit_bytes=61 * MIB, collective_id=3, has_side_effects=True
        ),
        cost_estimate=pl.CostEstimate(flops=4 * 10**10, bytes_accessed=0, transcendentals=0),
    )(ds, gains, codes, dp, w_down, w, c_one, a_two, down_src, small_src)


def first_back_kernel(
    sizes,
    dc_in,
    x_in,
    w_in,
    a_in,
    gains_ref,
    kept0_ref,
    kept1_ref,
    rest_kept_ref,
    down_kept_ref,
    dg_two_ref,
    loss_ref,
    wt_ref,
    conv_row_ref,
    rest_row_ref,
    g_first0,
    g_first1,
    g_second0,
    g_second1,
    g_down,
    g_rest0,
    g_rest1,
    conv_new_ref,
    rest_new_ref,
    tv_ref,
    dc_ref,
    x_ref,
    w_ref,
    a_ref,
    l_sem,
    dw,
    d3,
    dg,
    vec,
    vec_in,
    tv_in,
    s_send,
    s_recv,
    *bufs,
):
    n_code, n_proj, n_head, rgb = sizes
    place = Place()
    bufs = list(bufs)

    def take(n):
        out = bufs[:n]
        del bufs[:n]
        return out

    loads = [
        pltpu.make_async_copy(src, dst, l_sem.at[k])
        for k, (src, dst) in enumerate(
            ((dc_in, dc_ref), (a_in, a_ref), (w_in, w_ref), (x_in, x_ref))
        )
    ]
    for copy in loads:
        copy.start()
    half = rest_kept_ref.shape[-1] // 2
    ch = tv_ref.shape[1]
    view = dw.reshape(4, 2, 2, 2, dw.shape[0] // 32, ch)
    none = [None] * 4
    second0 = Reduce(place, None, g_second0, *none, kept0_ref, *take(3))
    second1 = Reduce(place, None, g_second1, *none, kept1_ref, *take(3))
    rest0 = Reduce(place, None, g_rest0, *none, rest_kept_ref.at[..., :half], *take(3))
    rest1 = Reduce(place, None, g_rest1, *none, rest_kept_ref.at[..., half:], *take(3))
    low = Reduce(place, view.at[..., : ch // 2], g_first0, *take(8))
    high = Reduce(place, view.at[..., ch // 2 :], g_first1, *take(8))
    late = (second0, second1, rest0, rest1)
    two, three, pair, send, recv = take(5)
    down = ReduceZ(place, None, g_down, None, None, two, three, down_kept_ref, None, send, recv)
    down.pair = pair
    place.greet()
    for job in late:
        job.start(3)
    down.start(2)

    def tick_low(dx):
        @pl.when(dx == 2)
        def _():
            down.go(4)

    def tick_high(dx):
        @pl.when(dx == 1)
        def _():
            low.go(1)

        @pl.when(dx == 2)
        def _():
            second0.go(4)
            down.go(5)

    def tick_crop(i):
        @pl.when(i == 0)
        def _():
            second1.go(4)

        @pl.when(i == 1)
        def _():
            high.go(1)
            second0.go(5)

        @pl.when(i == 2)
        def _():
            low.go(2)

        @pl.when(i == 3)
        def _():
            second1.go(5)

        @pl.when(i == 5)
        def _():
            low.go(3)
            high.go(2)

        @pl.when(i == 6)
        def _():
            rest0.go(4)

        @pl.when(i == 7)
        def _():
            high.go(3)

    def v_of(i):
        return x_ref[i].astype(F32)

    loads[0].wait()
    shift_all(dc_ref, d3)
    loads[1].wait()
    down.go(3)
    conv_weight_grad(a_ref, d3, dw, 0, tick_low)
    low.start(0)
    conv_weight_grad(a_ref, d3, dw, 1, tick_high)
    high.start(0)
    loads[2].wait()
    loads[3].wait()
    unit_back(v_of, gains_ref, w_ref, dg, d3, 0, None, tick_crop)
    vec[...] = jnp.zeros_like(vec)
    vec[0:2] = dg[...]
    vec[2:4] = dg_two_ref[...]
    vec[4:5] = loss_ref[0:1]
    small = [
        remote(vec, vec_in.at[k], s_send.at[k], s_recv.at[k], q)
        for k, q in enumerate(place.row_peers())
    ]
    for copy in small:
        copy.start()
    tv_ref[...] = jnp.zeros_like(tv_ref)
    for copy in small:
        copy.wait_recv()
    tv_ref[16:24, :] = vec[...] + vec_in[0] + vec_in[1] + vec_in[2]
    tv_ref[24:32, :] = wt_ref[...]

    def fold(parts, row, width):
        squares = [g.astype(F32) for g in parts]
        squares = [g * g for g in squares]
        total = sum(jnp.sum(q, axis=1, keepdims=True) for q in squares)
        new = 0.5 * row + 0.5 * (total / width + EPS_SQ)
        inverse = 1.0 / new
        col = [jnp.sum(q, axis=0, keepdims=True) for q in squares]
        over = [jnp.sum(q * inverse, axis=0, keepdims=True) for q in squares]
        return (
            new,
            jnp.concatenate(col, axis=1),
            jnp.concatenate(over, axis=1),
            jnp.sum(new, axis=0, keepdims=True),
        )

    def fold_conv(j, refs):
        for k in range(4):
            new, col, over, total = fold([r[k] for r in refs], conv_row_ref[j, k], ch)
            conv_new_ref[j, k] = new
            tv_ref[j : j + 1, :] += col
            tv_ref[3 + j : 4 + j, :] += over
            tv_ref[6 + j : 7 + j, :] += total

    def fold_rest():
        lat = 2 * half
        spans = ((0, n_code, lat), (n_code, n_proj, lat), (n_code + n_proj, n_head, rgb))
        for k in range(4):
            both = [r[k] for r in (g_rest0, g_rest1)]
            for m, (start, size, width) in enumerate(spans):
                parts = [v.astype(F32)[start : start + size] for v in both]
                row = rest_row_ref[k, start : start + size]
                new, col, over, total = fold(parts, row, width)
                rest_new_ref[k, start : start + size] = new
                tv_ref[9 + m : 10 + m, :lat] += col
                tv_ref[9 + m : 10 + m, lat:] += over
                tv_ref[12 + m : 13 + m, :] += total
            size = rest_row_ref.shape[1] - n_code - n_proj - n_head
            rest_new_ref[k, rest_row_ref.shape[1] - size :] = jnp.ones((size, 1), F32)

    rest0.go(5)
    down.arrive(5)
    fold_conv(2, [g_down])
    second0.arrive(5)
    second1.arrive(5)
    fold_conv(1, [g_second0, g_second1])
    rest1.go(4)
    rest0.arrive(5)
    rest1.go(5)
    low.go(4)
    rest1.arrive(5)
    fold_rest()
    low.go(5)
    high.go(4)
    low.arrive(5)
    high.go(5)
    high.arrive(5)
    fold_conv(0, [g_first0, g_first1])

    across = remote(tv_ref, tv_in.at[0], s_send.at[3], s_recv.at[3], place.at(y=1 - place.y))
    across.start()
    across.wait()
    tv_ref[...] += tv_in[0]
    along = [
        remote(tv_ref, tv_in.at[k], s_send.at[3 + k], s_recv.at[3 + k], q)
        for k, q in zip((1, 2, 3), place.z_peers())
    ]
    for copy in along:
        copy.start()
    for copy in along:
        copy.wait()
    tv_ref[...] += tv_in[1] + tv_in[2] + tv_in[3]
    for copy in small:
        copy.wait_send()
    down.sent(2, 6)
    for job in late:
        job.sent(3, 6)
    for job in (low, high):
        job.sent(0, 6)


def first_back_call(sizes, dc, x, gains, w, a_one, kept, down_kept, dg_two, loss, wt, rows):
    crops, cells, ch = x.shape
    n_conv, n_rest = down_kept.shape[-2], kept[2].shape[-2]

    def shape(*dims, dtype=BF):
        return jax.ShapeDtypeStruct(dims, dtype)

    conv_half = shape(4, n_conv, ch // 2)
    rest_half = shape(4, n_rest, 128)
    outs = [conv_half] * 4 + [shape(4, n_conv, ch)] + [rest_half] * 2
    outs += [shape(*v.shape, dtype=F32) for v in rows] + [shape(32, ch, dtype=F32)]
    args = [dc, x, w, a_one, gains, *kept, down_kept, dg_two, loss, wt, *rows]
    whole = Reduce.early(n_conv, ch // 2) + Reduce.late(n_conv, ch // 2, 1) + Reduce.sems()
    return pl.pallas_call(
        functools.partial(first_back_kernel, sizes),
        out_shape=outs,
        in_specs=[ANY] * 4 + [VM] * (len(args) - 4),
        out_specs=[VM] * len(outs),
        scratch_shapes=[
            pltpu.VMEM(dc.shape, BF),
            pltpu.VMEM(x.shape, BF),
            pltpu.VMEM(w.shape, BF),
            pltpu.VMEM(a_one.shape, BF),
            pltpu.SemaphoreType.DMA((4,)),
            pltpu.VMEM(w.shape, BF),
            pltpu.VMEM((crops, 18, 16, 3 * ch), BF),
            pltpu.VMEM((2, ch), F32),
            pltpu.VMEM((8, ch), F32),
            pltpu.VMEM((3, 8, ch), F32),
            pltpu.VMEM((4, 32, ch), F32),
            pltpu.SemaphoreType.DMA((7,)),
            pltpu.SemaphoreType.DMA((7,)),
        ]
        + (Reduce.late(n_conv, ch // 2, 0) + Reduce.sems()) * 2
        + (Reduce.late(n_rest, 128, 0) + Reduce.sems()) * 2
        + whole * 2
        + [
            pltpu.VMEM((2, n_conv, ch), BF),
            pltpu.VMEM((n_conv, ch), BF),
            pltpu.VMEM((2, n_conv, ch), BF),
        ]
        + Reduce.sems(),
        compiler_params=pltpu.CompilerParams(
            vmem_limit_bytes=60 * MIB, collective_id=4, has_side_effects=True
        ),
        cost_estimate=pl.CostEstimate(flops=2 * 10**10, bytes_accessed=0, transcendentals=0),
    )(*args)


def finish_kernel(
    sizes,
    g_first0,
    g_first1,
    g_second0,
    g_second1,
    g_down,
    g_rest0,
    g_rest1,
    conv_in,
    code_in,
    proj_ref,
    head_flat_ref,
    conv_row_ref,
    rest_row_ref,
    tv_ref,
    conv_col_ref,
    code_col_ref,
    proj_col_ref,
    head_col_ref,
    gains_ref,
    state_ref,
    loss_ref,
    conv_outs,
    rest_outs,
    gain_outs,
    conv_ref,
    code_ref,
    head_ref,
    head_pad,
    cg,
    cn,
    cl,
    kg,
    kn,
    kl,
    l_sem,
    s_sem,
):
    n_code, n_proj, n_head, rgb, shards = sizes
    loads = [pltpu.make_async_copy(conv_in.at[j], conv_ref.at[j], l_sem.at[j]) for j in range(3)]
    loads.append(pltpu.make_async_copy(code_in, code_ref, l_sem.at[3]))
    for copy in loads:
        copy.start()
    stores = []

    def store(src, dst):
        stores.append(pltpu.make_async_copy(src, dst, s_sem.at[len(stores)]))
        stores[-1].start()

    ch = conv_ref.shape[2]
    lat = code_ref.shape[1]

    def scales(col, col_sum, over, row_sum, weights, rows, width):
        rows = rows * shards
        col_new = 0.5 * col + 0.5 * (col_sum / rows + EPS_SQ)
        row_mean = row_sum / rows
        upd_sq = row_mean * jnp.sum(over / col_new, axis=1, keepdims=True)
        rms_u = jnp.sqrt(upd_sq / (rows * width))
        scale = jnp.sqrt(jnp.sum(weights, axis=1, keepdims=True) / (rows * width))
        factor = RATE * scale / jnp.maximum(1.0, rms_u)
        return col_new, factor * lax.rsqrt(col_new), row_mean

    def line(k):
        return tv_ref[k : k + 1, :]

    cg_out, cc, cn_out, cl_out = conv_outs
    for j, parts in enumerate(((g_first0, g_first1), (g_second0, g_second1), (g_down,))):
        n = conv_ref.shape[1]
        col_new, q, row_mean = scales(
            conv_col_ref[j : j + 1, :], line(j), line(3 + j), line(6 + j)[:, :1], line(24 + j), n, ch
        )
        cc[j : j + 1, :] = col_new
        m = n // 4
        loads[j].wait()
        for k in range(4):
            r = lax.rsqrt(conv_row_ref[j, k] / row_mean)
            rows = slice(k * m, (k + 1) * m)
            for p, part in enumerate(parts):
                width = part.shape[2]
                lanes = slice(p * width, (p + 1) * width)
                g = part[k].astype(F32)
                new = conv_ref[j, rows, lanes] - g * r * q[:, lanes]
                cg[j, rows, lanes] = g
                cn[j, rows, lanes] = new
                cl[j, rows, lanes] = new.astype(BF)
        for src, dst in ((cg, cg_out), (cn, cn_out), (cl, cl_out)):
            store(src.at[j], dst.at[j])
    loads[3].wait()
    head_ref[...] = stand(head_flat_ref, head_pad, lat)
    cols = (code_col_ref, proj_col_ref, head_col_ref)
    spans = ((0, n_code, lat), (n_code, n_proj, lat), (n_code + n_proj, n_head, rgb))
    for m, (w_ref, (start, size, width)) in enumerate(zip((code_ref, proj_ref, head_ref), spans)):
        og, oc, on, ol = rest_outs[m]
        if m == 0:
            code_outs, (og, on, ol) = (og, on, ol), (kg, kn, kl)
        col_new, q, row_mean = scales(
            cols[m][...],
            line(9 + m)[:, :lat],
            line(9 + m)[:, lat:],
            line(12 + m)[:, :1],
            line(27 + m)[:, :lat],
            w_ref.shape[0],
            width,
        )
        oc[...] = col_new
        both = []
        for k in range(4):
            g = jnp.concatenate([g_rest0[k].astype(F32), g_rest1[k].astype(F32)], axis=1)
            g = g[start : start + size]
            r = lax.rsqrt(rest_row_ref[k, start : start + size] / row_mean)
            rows = slice(k * size, (k + 1) * size)
            new = w_ref[rows, :] - g * r * q
            if m == 2:
                both.append((g, new))
            else:
                og[rows, :] = g
                on[rows, :] = new
                ol[rows, :] = new.astype(BF)
        if m == 0:
            for src, dst in zip((og, on, ol), code_outs):
                store(src, dst)
        if m == 2:
            for ref, values in zip((og, on), zip(*both)):
                tall = jnp.concatenate(values, axis=0)[:, :128]
                tall = jnp.concatenate([tall, jnp.zeros((128 - tall.shape[0], 128), F32)], axis=0)
                head_pad[...] = jnp.transpose(tall)
                ref[...] = head_pad[: ref.shape[0], : ref.shape[1]]
            ol[...] = on[...].astype(BF)
    loss_ref[...] = jnp.sum(line(20), axis=1, keepdims=True)
    grad = tv_ref[16:20, :]
    state = 0.5 * state_ref[...] + 0.5 * (grad * grad + EPS_SQ)
    update = grad * lax.rsqrt(state)
    gains = gains_ref[...]

    def rms(v):
        return jnp.sqrt(
            jnp.sum(jnp.sum(v * v, axis=1, keepdims=True), axis=0, keepdims=True) / v.size
        )

    gain_outs[0][...] = grad
    gain_outs[1][...] = state
    gain_outs[2][...] = gains - RATE * rms(gains) * update / jnp.maximum(1.0, rms(update))
    for copy in stores:
        copy.wait()


def finish_call(sizes, grads, weights, rows, tv, cols, gains, state):
    conv_w, code_w, proj_w, head_w = weights
    lat = code_w.shape[1]

    def shape(dims, dtype=F32):
        return jax.ShapeDtypeStruct(dims, dtype)

    def matrix(w, col):
        return [shape(w.shape), shape(col), shape(w.shape), shape(w.shape, BF)]

    outs = [shape((1, 1)), matrix(conv_w, (3, conv_w.shape[2]))]
    outs += [[matrix(w, (1, lat)) for w in (code_w, proj_w, head_w)]]
    outs += [[shape(gains.shape)] * 3]
    args = [*grads, *weights, *rows, tv, *cols, gains, state]
    specs = jax.tree.map(lambda _: VM, outs)
    streamed = [ANY, VM, ANY, ANY]
    specs[1] = streamed
    specs[2] = [streamed] + specs[2][1:]
    in_specs = [VM] * len(args)
    in_specs[len(grads)] = in_specs[len(grads) + 1] = ANY
    return pl.pallas_call(
        functools.partial(finish_kernel, sizes),
        out_shape=outs,
        in_specs=in_specs,
        out_specs=specs,
        scratch_shapes=[
            pltpu.VMEM(conv_w.shape, F32),
            pltpu.VMEM(code_w.shape, F32),
            pltpu.VMEM((head_w.shape[1], lat), F32),
            pltpu.VMEM((128, 128), F32),
        ]
        + [pltpu.VMEM(w.shape, t) for w in (conv_w, code_w) for t in (F32, F32, BF)]
        + [pltpu.SemaphoreType.DMA((4,)), pltpu.SemaphoreType.DMA((12,))],
        compiler_params=pltpu.CompilerParams(vmem_limit_bytes=56 * MIB),
        cost_estimate=pl.CostEstimate(flops=10**7, bytes_accessed=2 * 10**7, transcendentals=0),
    )(*args)


def contract_last(left, right):
    return lax.dot_general(left, right, (((1,), (0,)), ((), ())), preferred_element_type=F32)


def contract_back(left, right):
    return lax.dot_general(left, right, (((1,), (1,)), ((), ())), preferred_element_type=F32)


def contract_rows(left, right):
    return lax.dot_general(left, right, (((0,), (0,)), ((), ())), preferred_element_type=F32)


def row_part(grad, row):
    g_sq = grad * grad + EPS_SQ
    row_new = 0.5 * row + 0.5 * jnp.mean(g_sq, axis=2)
    over_row = jnp.sum(grad * grad / row_new[:, :, None], axis=0)
    return row_new, jnp.sum(g_sq, axis=0), jnp.sum(row_new, axis=0), over_row


def finish(grad, weight, row_new, col, col_sum, row_sum, over_row, wt_sq):
    total = grad.shape[0] * lax.axis_size("batch")
    count = total * grad.shape[2]
    col_new = 0.5 * col + 0.5 * col_sum / total
    row_mean = row_sum / total
    upd_sq = row_mean * jnp.sum(over_row / col_new, axis=1)
    rms_u = jnp.sqrt(upd_sq / count)
    scale = jnp.sqrt(wt_sq / count)
    vhat = row_new[:, :, None] * col_new[None] / row_mean[None, :, None]
    update = grad * lax.rsqrt(vhat)
    new = weight - RATE * (scale / jnp.maximum(1.0, rms_u))[None, :, None] * update
    return col_new, new


def local_any(
    features,
    target,
    mask,
    codes,
    conv_w,
    proj_w,
    code_w,
    head_w,
    gains,
    conv_row,
    conv_col,
    proj_row,
    proj_col,
    code_row,
    code_col,
    head_row,
    head_col,
    gain_state,
):
    ranks = lax.axis_size("rows")
    shards = lax.axis_size("batch")
    me = lax.axis_index("rows")
    crops_all = features.shape[0] * shards
    ch = features.shape[3]
    lat = proj_w.shape[1]
    rgb = head_w.shape[1]
    height = features.shape[1] * ranks
    width = features.shape[2]

    def whole_crops(v):
        return lax.all_to_all(v, "rows", split_axis=0, concat_axis=1, tiled=True)

    def my_part(v):
        size = v.shape[0] // ranks
        return lax.dynamic_slice_in_dim(v, me * size, size, 0)

    conv_piece = jnp.transpose(my_part(conv_w).astype(BF), (1, 0, 2))
    head_wide = jnp.pad(head_w, ((0, 0), (0, lat - rgb)))
    rest_piece = jnp.concatenate(
        [my_part(code_w).astype(BF), my_part(proj_w).astype(BF), my_part(head_wide).astype(BF)]
    )
    n_code, n_proj, n_head = (v.shape[0] // ranks for v in (code_w, proj_w, head_w))
    w_all = [lax.all_gather(conv_piece[0], BOTH, axis=0, tiled=True)]
    later = lax.all_gather(conv_piece[1:], BOTH, axis=0)
    later = jnp.transpose(later, (1, 0, 2, 3)).reshape(2, -1, ch)
    w_all += [later[0], later[1]]
    rest = lax.all_gather(rest_piece, BOTH, axis=0)
    code_all = rest[:, :n_code].reshape(-1, lat)
    proj_all = rest[:, n_code : n_code + n_proj].reshape(-1, lat)
    head_all = rest[:, n_code + n_proj :, :rgb].reshape(-1, rgb)

    x = whole_crops(features)
    target, mask, codes = whole_crops(target), whole_crops(mask), whole_crops(codes)
    crops = x.shape[0]
    cells = height * width
    x = x.reshape(crops, cells, ch)
    lat_cells = crops * cells // 4
    target = target.reshape(lat_cells, rgb)
    mask = mask.reshape(lat_cells, -1)
    codes = codes.reshape(lat_cells, -1)

    conv_flops = 2 * crops * cells * 9 * ch * ch
    three = pltpu.VMEM((18, 16, 3 * ch), BF)
    fold = pltpu.VMEM((ch // 128, cells, 128), F32)

    def big(dtype):
        return jax.ShapeDtypeStruct((crops, cells, ch), dtype)

    dw_shape = jax.ShapeDtypeStruct((9 * ch, ch), BF)
    dg_shape = jax.ShapeDtypeStruct((2, ch), F32)

    a_one, c_one = kernel_call(
        first_conv_kernel, [big(BF), big(F32)], [three], conv_flops, x, gains, w_all[0]
    )
    a_two, windows, s_low = kernel_call(
        second_conv_kernel,
        [
            big(BF),
            jax.ShapeDtypeStruct((lat_cells, 9 * ch), BF),
            jax.ShapeDtypeStruct((lat_cells, ch), BF),
        ],
        [three, fold],
        conv_flops,
        c_one,
        x,
        gains,
        w_all[1],
        w_all[2],
    )

    lat_count = crops_all * cells // 4 * lat
    pix_count = crops_all * cells * 3
    latent = contract_last(s_low, proj_all)
    picked = code_all[codes].astype(F32)
    cum = jnp.cumsum(picked, axis=1)
    resid = latent[:, None, :] - cum
    quant_part = (1.0 + BETA) * jnp.sum(resid * resid) / lat_count
    zq_low = cum[:, -1].astype(BF)
    pred = contract_last(zq_low, head_all)
    diff = pred - target
    weight_mask = jnp.repeat(mask.astype(F32), 3, axis=-1)
    smooth = jnp.sqrt(diff * diff + 1.0)
    recon_part = jnp.sum(weight_mask * (smooth - 1.0)) / pix_count
    d_pred = (weight_mask * (diff / smooth) / pix_count).astype(BF)
    d_head = contract_rows(zq_low, d_pred)
    d_zq = contract_back(d_pred, head_all)
    d_cum = -2.0 / lat_count * resid
    d_picked = jnp.flip(jnp.cumsum(jnp.flip(d_cum, 1), axis=1), 1)
    d_code = jax.ops.segment_sum(
        d_picked.reshape(-1, lat), codes.reshape(-1), num_segments=code_all.shape[0]
    )
    d_lat_low = (jnp.sum(resid, axis=1) * (2.0 * BETA / lat_count) + d_zq).astype(BF)
    d_proj = contract_rows(s_low, d_lat_low)
    d_s_low = contract_back(d_lat_low, proj_all).astype(BF)

    d_c_two, d_down = kernel_call(
        down_back_kernel,
        [big(BF), dw_shape],
        [fold],
        conv_flops // 2,
        d_s_low,
        windows,
        w_all[2],
    )
    d_three = pltpu.VMEM((crops, 18, 16, 3 * ch), BF)
    d_c_one, d_second, gain_two = kernel_call(
        functools.partial(unit_back_kernel, row=2, inner=True),
        [big(BF), dw_shape, dg_shape],
        [d_three],
        2 * conv_flops,
        d_c_two,
        c_one,
        gains,
        w_all[1],
        a_two,
    )
    d_first, gain_one = kernel_call(
        functools.partial(unit_back_kernel, row=0, inner=False),
        [dw_shape, dg_shape],
        [d_three],
        2 * conv_flops,
        d_c_one,
        x,
        gains,
        w_all[0],
        a_one,
    )
    d_gains = jnp.concatenate([gain_one, gain_two], axis=0)

    devices = ranks * shards

    def to_owner(v):
        return lax.psum_scatter(v, BOTH, scatter_dimension=0, tiled=True)

    def to_rows(v):
        return lax.all_gather(v, "rows", axis=0)

    pad = jnp.pad(d_head, ((0, 0), (0, lat - rgb)))
    rest_grad = jnp.concatenate(
        [v.astype(BF).reshape(devices, -1, lat) for v in (d_code, d_proj, pad)], axis=1
    )
    rest_mine = to_owner(rest_grad.reshape(-1, lat))
    conv_mine = [to_owner(v) for v in (d_first, d_second, d_down)]
    rest_full = to_rows(rest_mine).astype(F32)
    conv_full = to_rows(jnp.stack(conv_mine)).astype(F32)
    g_conv = jnp.transpose(conv_full, (0, 2, 1, 3)).reshape(-1, 3, ch)
    g_code = rest_full[:, :n_code].reshape(-1, lat)
    g_proj = rest_full[:, n_code : n_code + n_proj].reshape(-1, lat)
    g_head = rest_full[:, n_code + n_proj :, :rgb].reshape(-1, rgb)

    mats = [
        (g_conv, conv_w, conv_row, conv_col),
        (g_proj[:, None, :], proj_w[:, None, :], proj_row[:, None], proj_col[None, :]),
        (g_code[:, None, :], code_w[:, None, :], code_row[:, None], code_col[None, :]),
        (g_head[:, None, :], head_w[:, None, :], head_row[:, None], head_col[None, :]),
    ]
    rows_new = [row_part(grad, row) for grad, weight, row, col in mats]
    wt_sq = [jnp.sum(weight * weight, axis=(0, 2)) for grad, weight, row, col in mats]
    sums = lax.psum([r[1:] + (w,) for r, w in zip(rows_new, wt_sq)], "batch")
    loss, g_gain = lax.psum((recon_part + quant_part, d_gains), BOTH)
    done = [
        finish(m[0], m[1], r[0], m[3], *s) for m, r, s in zip(mats, rows_new, sums)
    ]

    state_new = 0.5 * gain_state + 0.5 * (g_gain * g_gain + EPS_SQ)
    update = g_gain * lax.rsqrt(state_new)
    rms_u = jnp.sqrt(jnp.mean(update * update))
    scale = jnp.sqrt(jnp.mean(gains * gains))
    gains_new = gains - RATE * scale * update / jnp.maximum(1.0, rms_u)
    conv_new = done[0][1]
    proj_new, code_new, head_new = (d[1][:, 0, :] for d in done[1:])
    return (
        loss,
        g_conv,
        rows_new[0][0],
        done[0][0],
        conv_new,
        conv_new.astype(BF),
        g_proj,
        rows_new[1][0][:, 0],
        done[1][0][0],
        proj_new,
        proj_new.astype(BF),
        g_code,
        rows_new[2][0][:, 0],
        done[2][0][0],
        code_new,
        code_new.astype(BF),
        g_head,
        rows_new[3][0][:, 0],
        done[3][0][0],
        head_new,
        head_new.astype(BF),
        g_gain,
        state_new,
        gains_new,
    )


def local_fast(
    features,
    target,
    mask,
    codes,
    conv_w,
    proj_w,
    code_w,
    head_w,
    gains,
    conv_row,
    conv_col,
    proj_row,
    proj_col,
    code_row,
    code_col,
    head_row,
    head_col,
    gain_state,
):
    ranks = lax.axis_size("rows")
    shards = lax.axis_size("batch")
    crops_all = features.shape[0] * shards
    crops = features.shape[0] // ranks
    ch = features.shape[3]
    cells = features.shape[1] * ranks * features.shape[2]
    lat, rgb = proj_w.shape[1], head_w.shape[1]
    lat_cells = crops * cells // 4
    n_code, n_proj, n_head = (v.shape[0] // ranks for v in (code_w, proj_w, head_w))
    sizes = (n_code, n_proj, n_head, rgb)
    conv_rows = jnp.transpose(conv_w, (1, 0, 2))
    head_flat = jnp.transpose(head_w)

    def lanes(v, n):
        return jnp.pad(v, ((0, 0),) * (v.ndim - 1) + ((0, n - v.shape[-1]),))

    side = [lanes(target, 16), lanes(jnp.repeat(mask.astype(F32), 3, axis=-1), 16)]
    side = lanes(jnp.concatenate(side + [codes.astype(F32)], axis=-1), 128)
    out = forward_call(
        features.reshape(ranks, crops, -1, ch),
        side.reshape(ranks, crops, -1, 128),
        conv_rows,
        code_w,
        proj_w,
        head_flat,
        gains,
    )
    x = out[0].reshape(crops, cells, ch)
    side = out[1].reshape(lat_cells, 128)
    w_all, rest = out[2:5], out[5]
    a_one, c_one, a_two, windows, s_low, wt = out[6:]
    codes = jnp.transpose(side[:, 32:36]).astype(jnp.int32).reshape(-1)
    n_rest = rest.shape[-2]
    d_s, loss, dp, d_small, d_down = quantizer_call(
        codes,
        rest.reshape(-1, n_rest, lat),
        side,
        s_low,
        windows,
        crops_all * cells // 4 * lat,
        crops_all * cells * 3,
        rgb,
        n_code,
    )

    def shards_of(v):
        return v.reshape(4, 2, 2, 2, -1, v.shape[-1])

    d_c_one, dg_two, down_kept, *kept = second_back_call(
        n_code,
        d_s,
        w_all[2],
        w_all[1],
        c_one,
        a_two,
        gains,
        codes[None],
        dp,
        shards_of(d_down),
        d_small.reshape(4, 2, 2, 2, -1, lat),
    )
    conv_row4 = jnp.transpose(conv_row).reshape(3, 4, -1, 1)
    rest_row4 = [v.reshape(4, -1) for v in (code_row, proj_row, head_row)]
    rest_row4.append(jnp.ones((4, n_rest - n_code - n_proj - n_head), F32))
    rest_row4 = jnp.concatenate(rest_row4, axis=1)[:, :, None]
    out = first_back_call(
        sizes,
        d_c_one,
        x,
        gains,
        w_all[0],
        a_one,
        kept,
        down_kept,
        dg_two,
        loss,
        wt,
        (conv_row4, rest_row4),
    )
    conv_rn, rest_rn, tv = out[7:]
    head_col_wide = jnp.pad(head_col, (0, lat - rgb), constant_values=1.0)
    loss, conv_outs, rest_outs, gain_outs = finish_call(
        sizes + (shards,),
        out[:7],
        (conv_rows, code_w, proj_w, head_flat),
        (conv_rn, rest_rn),
        tv,
        (conv_col, code_col[None], proj_col[None], head_col_wide[None]),
        gains,
        gain_state,
    )
    conv_g, conv_c, conv_n, conv_l = conv_outs
    code_o, proj_o, head_o = rest_outs
    cuts = (n_code, n_code + n_proj, n_code + n_proj + n_head)
    code_r, proj_r, head_r = (
        v.reshape(-1) for v in jnp.split(rest_rn[:, :, 0], cuts, axis=1)[:3]
    )

    def back(v):
        return jnp.transpose(v, (1, 0, 2))

    return (
        loss[0, 0],
        back(conv_g),
        jnp.transpose(conv_rn.reshape(3, -1)),
        conv_c,
        back(conv_n),
        back(conv_l),
        proj_o[0],
        proj_r,
        proj_o[1][0],
        proj_o[2],
        proj_o[3],
        code_o[0],
        code_r,
        code_o[1][0],
        code_o[2],
        code_o[3],
        jnp.transpose(head_o[0]),
        head_r,
        head_o[1][0, :rgb],
        jnp.transpose(head_o[2]),
        jnp.transpose(head_o[3]),
        *gain_outs,
    )


def solution(mesh):
    cell = P("batch", "rows", None, None)
    mat, vec = P("batch", None), P("batch")
    placed = (cell,) * 4 + (P("batch", None, None), mat, mat, mat, P())
    placed += (mat, P()) + (vec, P()) * 3 + (P(),)
    conv_outs = (P("batch", None, None), mat, P(), P("batch", None, None), P("batch", None, None))
    mat_outs = (mat, vec, P(), mat, mat)
    fast = (mesh.shape["rows"], mesh.shape["batch"]) == (4, 8)
    return jax.shard_map(
        local_fast if fast else local_any,
        mesh=mesh,
        in_specs=placed,
        out_specs=(P(),) + conv_outs + mat_outs * 3 + (P(),) * 3,
        check_vma=False,
    )
```

```python
import functools

import jax
import jax.numpy as jnp
from jax import lax
from jax.experimental import pallas as pl
from jax.experimental.pallas import tpu as pltpu
from jax.sharding import PartitionSpec as P

GROUPS = 32
BETA = 0.25
RATE = 0.5
EPS_NORM = 1e-05
EPS_SQ = 1e-30
BF = jnp.bfloat16
F32 = jnp.float32
BOTH = ("batch", "rows")
MIB = 1 << 20
VM = pl.BlockSpec(memory_space=pltpu.VMEM)
ANY = pl.BlockSpec(memory_space=pl.ANY)
MESH = pl.DeviceIdType.MESH


def group_sum(v):
    lane = lax.broadcasted_iota(jnp.int32, v.shape, 1)
    width = v.shape[1]
    for k in (1, 2, 4, 8):
        up = pltpu.roll(v, k, 1)
        down = pltpu.roll(v, width - k, 1)
        v = v + jnp.where((lane & k) != 0, up, down)
    return v


def moments(v):
    count = v.shape[0] * (v.shape[1] // GROUPS)
    sums = jnp.concatenate(
        [jnp.sum(v, axis=0, keepdims=True), jnp.sum(v * v, axis=0, keepdims=True)]
        + [jnp.zeros((6, v.shape[1]), F32)],
        axis=0,
    )
    sums = group_sum(sums) / count
    mean = sums[0:1]
    return mean, lax.rsqrt(sums[1:2] - mean * mean + EPS_NORM)


def shifted(v, by):
    cells = v.shape[0]
    col = lax.broadcasted_iota(jnp.int32, v.shape, 0) & 15
    edge = 0 if by == 1 else 15
    return jnp.where(col == edge, 0.0, pltpu.roll(v, by % cells, 0))


def fill_three(dst, left, mid, right):
    ch = mid.shape[1]
    for k, v in enumerate((left, mid, right)):
        dst[1:17, :, k * ch : (k + 1) * ch] = v.astype(BF).reshape(16, 16, ch)


def zero_edges(dst):
    dst[0] = jnp.zeros(dst.shape[1:], dst.dtype)
    dst[17] = jnp.zeros(dst.shape[1:], dst.dtype)


def put_lanes(dst, rows, v):
    for k in range(dst.shape[0]):
        dst[k, rows, :] = v[:, k * 128 : (k + 1) * 128]


def get_lanes(src, rows):
    return jnp.concatenate([src[k, rows, :] for k in range(src.shape[0])], axis=1)


def conv_rows(src, w_ref):
    acc = None
    width = src.shape[2]
    for dy in range(3):
        lhs = src[dy : dy + 16].reshape(256, width)
        d = jnp.dot(lhs, w_ref[dy * width : (dy + 1) * width, :], preferred_element_type=F32)
        acc = d if acc is None else acc + d
    return acc


def conv_rows_back(src, w_ref):
    acc = None
    ch = src.shape[2] // 3
    for dy in range(3):
        for dx in range(3):
            lhs = src[2 - dy : 18 - dy, :, dx * ch : (dx + 1) * ch].reshape(256, ch)
            t = (dy * 3 + dx) * ch
            d = lax.dot_general(
                lhs, w_ref[t : t + ch, :], (((1,), (1,)), ((), ())), preferred_element_type=F32
            )
            acc = d if acc is None else acc + d
    return acc


def conv_weight_grad(a_ref, d3_ref, dw_ref, half, tick=None):
    crops, cells, ch = a_ref.shape
    nb = 256
    out = slice(half * nb, (half + 1) * nb)

    def block(dx, carry):
        if tick is not None:
            tick(dx)
        lane = pl.multiple_of(dx * ch + half * nb, nb)
        for dy in range(3):
            rhs = d3_ref[:, 2 - dy : 18 - dy, :, pl.ds(lane, nb)].reshape(crops * cells, nb)
            d = lax.dot_general(
                a_ref[...].reshape(crops * cells, ch),
                rhs,
                (((0,), (0,)), ((), ())),
                preferred_element_type=F32,
            )
            row = pl.multiple_of((dy * 3 + dx) * ch, ch)
            dw_ref[pl.ds(row, ch), out] = d.astype(dw_ref.dtype)
        return carry

    lax.fori_loop(0, 3, block, 0)


def silu(h):
    return h * jax.nn.sigmoid(h)


def first_crop(v, gains_ref, w_ref, a3):
    mean, rstd = moments(v)
    a = silu((v - mean) * rstd * gains_ref[0:1, :] + gains_ref[1:2, :])
    fill_three(a3, shifted(a, 1), a, shifted(a, -1))
    return a.astype(BF), conv_rows(a3, w_ref)


def second_crop(v, x, gains_ref, w_ref, l_ref, a3, y32):
    ch = v.shape[1]
    mean, rstd = moments(v)
    a = silu((v - mean) * rstd * gains_ref[2:3, :] + gains_ref[3:4, :])
    fill_three(a3, shifted(a, 1), a, shifted(a, -1))
    put_lanes(y32, slice(None), conv_rows(a3, w_ref) + x)
    even = get_lanes(y32, pl.ds(0, 128, stride=2))
    odd = get_lanes(y32, pl.ds(1, 128, stride=2))
    cell = lax.broadcasted_iota(jnp.int32, odd.shape, 0) & 7
    before = jnp.where(cell == 0, 0.0, pltpu.roll(odd, 1, 0))
    for dx, part in enumerate((before, even, odd)):
        part = part.reshape(8, 2, 8, ch)
        upper = part[:, 0].reshape(64, ch)
        lower = part[:, 1].reshape(64, ch)
        above = jnp.concatenate([jnp.zeros((8, ch), F32), lower[:56]], axis=0)
        for dy, rows in enumerate((above, upper, lower)):
            lane = (dy * 3 + dx) * ch
            l_ref[:, lane : lane + ch] = rows.astype(BF)
    return a.astype(BF)


def down_dot(l_ref, w_ref, s_ref):
    ch = s_ref.shape[1]
    nb = 256

    def block(j, carry):
        lane = pl.ds(pl.multiple_of(j * nb, nb), nb)
        d = jnp.dot(l_ref[...], w_ref[:, lane], preferred_element_type=F32)
        s_ref[:, lane] = d.astype(BF)
        return carry

    lax.fori_loop(0, ch // nb, block, 0)


def crop_rows(i):
    return pl.ds(pl.multiple_of(i * 64, 64), 64)


def first_conv_kernel(x_ref, gains_ref, w_ref, a_ref, c_ref, a3):
    zero_edges(a3)

    def crop(i, carry):
        a_ref[i], c_ref[i] = first_crop(x_ref[i].astype(F32), gains_ref, w_ref, a3)
        return carry

    lax.fori_loop(0, x_ref.shape[0], crop, 0)


def second_conv_kernel(c_in_ref, x_ref, gains_ref, w_ref, w_down_ref, a_ref, l_ref, s_ref, a3, y32):
    zero_edges(a3)

    def crop(i, carry):
        a_ref[i] = second_crop(
            c_in_ref[i],
            x_ref[i].astype(F32),
            gains_ref,
            w_ref,
            l_ref.at[crop_rows(i)],
            a3,
            y32,
        )
        return carry

    lax.fori_loop(0, x_ref.shape[0], crop, 0)
    down_dot(l_ref, w_down_ref, s_ref)


def down_input_grad(ds_ref, w_ref, dc_ref, y32):
    cells, ch = ds_ref.shape
    group = 4 if cells % 256 == 0 else 1
    size = 64 * group

    def dot_t(lhs, tap):
        return lax.dot_general(
            lhs.astype(BF),
            w_ref[tap * ch : (tap + 1) * ch, :],
            (((1,), (1,)), ((), ())),
            preferred_element_type=F32,
        )

    def crops(i, carry):
        here = ds_ref[pl.ds(pl.multiple_of(i * size, size), size), :].astype(F32)
        at = lax.broadcasted_iota(jnp.int32, here.shape, 0)

        def next_col(v):
            return jnp.where((at & 7) == 7, 0.0, pltpu.roll(v, size - 1, 0))

        right = next_col(here)
        under = jnp.where((at & 63) >= 56, 0.0, pltpu.roll(here, size - 8, 0))
        corner = next_col(under)
        ee = dot_t(here, 4)
        eo = dot_t(here, 5) + dot_t(right, 3)
        oe = dot_t(here, 7) + dot_t(under, 1)
        oo = dot_t(here, 8) + dot_t(right, 6) + dot_t(under, 2) + dot_t(corner, 0)

        def both_rows(top, bottom):
            top, bottom = top.reshape(8, 1, 8, ch), bottom.reshape(8, 1, 8, ch)
            return jnp.concatenate([top, bottom], axis=1).reshape(128, ch)

        for k in range(group):
            rows = slice(64 * k, 64 * k + 64)
            put_lanes(y32, pl.ds(0, 128, stride=2), both_rows(ee[rows], oe[rows]))
            put_lanes(y32, pl.ds(1, 128, stride=2), both_rows(eo[rows], oo[rows]))
            dc_ref[i * group + k] = get_lanes(y32, slice(None)).astype(BF)
        return carry

    lax.fori_loop(0, cells // size, crops, 0)


def down_weight_grad(l_ref, ds_ref, dw_ref, after=None):
    ch = ds_ref.shape[1]

    def block(t, carry):
        lane = pl.multiple_of(t * ch, ch)
        d = lax.dot_general(
            l_ref[:, pl.ds(lane, ch)],
            ds_ref[...],
            (((0,), (0,)), ((), ())),
            preferred_element_type=F32,
        )
        dw_ref[pl.ds(lane, ch), :] = d.astype(BF)
        if after is not None:
            after(t)
        return carry

    lax.fori_loop(0, 9, block, 0)


def down_back_kernel(ds_ref, l_ref, w_ref, dc_ref, dw_ref, y32):
    down_weight_grad(l_ref, ds_ref, dw_ref)
    down_input_grad(ds_ref, w_ref, dc_ref, y32)


def hidden_grad(v, gain, shift, d_act):
    mean, rstd = moments(v)
    vhat = (v - mean) * rstd
    h = vhat * gain + shift
    sig = jax.nn.sigmoid(h)
    return d_act * sig * (1.0 + h * (1.0 - sig)), vhat, rstd


def shift_all(dc_ref, d3, tick=None):
    def crop(i, carry):
        if tick is not None:
            tick(i)
        d = dc_ref[i].astype(F32)
        slot = d3.at[i]
        zero_edges(slot)
        fill_three(slot, shifted(d, -1), d, shifted(d, 1))
        return carry

    lax.fori_loop(0, dc_ref.shape[0], crop, 0)


def unit_back(v_of, gains_ref, w_ref, dg_ref, d3, row, din_ref=None, tick=None):
    crops, cells, ch = d3.shape[0], 256, d3.shape[3] // 3
    dg_ref[...] = jnp.zeros_like(dg_ref)

    def crop(i, carry):
        if tick is not None:
            tick(i)
        d_act = conv_rows_back(d3.at[i], w_ref)
        gain = gains_ref[row : row + 1, :]
        hg, vhat, rstd = hidden_grad(v_of(i), gain, gains_ref[row + 1 : row + 2, :], d_act)
        one = jnp.sum(hg * vhat, axis=0, keepdims=True)
        two = jnp.sum(hg, axis=0, keepdims=True)
        dg_ref[0:1, :] += one
        dg_ref[1:2, :] += two
        if din_ref is not None:
            count = cells * (ch // GROUPS)
            sums = jnp.concatenate([two * gain, one * gain, jnp.zeros((6, ch), F32)], axis=0)
            sums = group_sum(sums) / count
            din_ref[i] = (rstd * (hg * gain - sums[0:1] - vhat * sums[1:2])).astype(BF)
        return carry

    lax.fori_loop(0, crops, crop, 0)


def unit_back_kernel(dc_ref, v_ref, gains_ref, w_ref, a_ref, *outs, row, inner):
    if inner:
        din_ref, dw_ref, dg_ref, d3 = outs
    else:
        dw_ref, dg_ref, d3 = outs
        din_ref = None

    def v_of(i):
        return v_ref[i].astype(F32)

    shift_all(dc_ref, d3)
    unit_back(v_of, gains_ref, w_ref, dg_ref, d3, row, din_ref)
    for half in range(2):
        conv_weight_grad(a_ref, d3, dw_ref, half)


def kernel_call(body, outs, scratch, flops, *args):
    bytes_accessed = sum(a.size * a.dtype.itemsize for a in args)
    bytes_accessed += sum(o.size * o.dtype.itemsize for o in outs)
    return pl.pallas_call(
        body,
        out_shape=outs,
        in_specs=[VM] * len(args),
        out_specs=[VM] * len(outs),
        scratch_shapes=scratch,
        compiler_params=pltpu.CompilerParams(vmem_limit_bytes=56 * MIB),
        cost_estimate=pl.CostEstimate(
            flops=flops, bytes_accessed=bytes_accessed, transcendentals=0
        ),
    )(*args)


class Place:
    def __init__(self):
        rows, batch = lax.axis_index("rows"), lax.axis_index("batch")
        self.x, self.c = rows // 2, rows % 2
        self.z, self.y = batch // 2, batch % 2
        self.part = self.c * 2 + self.x

    def at(self, x=None, c=None, z=None, y=None):
        x = self.x if x is None else x
        c = self.c if c is None else c
        z = self.z if z is None else z
        y = self.y if y is None else y
        return {"rows": 2 * x + c, "batch": 2 * z + y}

    def row_peers(self):
        return [
            self.at(c=1 - self.c),
            self.at(x=1 - self.x),
            self.at(x=1 - self.x, c=1 - self.c),
        ]

    def z_peers(self):
        return [self.at(z=(self.z + d) % 4) for d in (1, 2, 3)]

    def greet(self):
        barrier = pltpu.get_barrier_semaphore()
        peers = self.row_peers() + self.z_peers() + [self.at(y=1 - self.y)]
        for peer in peers:
            pl.semaphore_signal(barrier, inc=1, device_id=peer, device_id_type=MESH)
        pl.semaphore_wait(barrier, len(peers))


def remote(src, dst, send, recv, peer):
    return pltpu.make_async_remote_copy(
        src_ref=src, dst_ref=dst, send_sem=send, recv_sem=recv, device_id=peer, device_id_type=MESH
    )


class Gather:
    def __init__(self, place, src, dst, send, recv, route):
        self.p, self.src, self.dst, self.send, self.recv = place, src, dst, send, recv
        self.route = "z" + route + "c"
        self.steps = len(self.route)

    def copies(self, step):
        p, src, dst, send, recv = self.p, self.src, self.dst, self.send, self.recv
        axis = self.route[step]
        if axis == "z":
            mine = (p.c, p.x) if "x" in self.route else (p.c,)
            here, there = src.at[mine], dst.at[(p.z, p.y) + mine]
            out = [
                remote(here, there, send.at[k], recv.at[k], q) for k, q in enumerate(p.z_peers())
            ]
            return out + [pltpu.make_async_copy(here, there, recv.at[6])]
        have_y = "y" in self.route[:step]
        have_x = "x" in self.route[:step] or "x" not in self.route
        part = dst.at[:, slice(None) if have_y else p.y, p.c]
        if not have_x:
            part = dst.at[:, slice(None) if have_y else p.y, p.c, p.x]
        k = 3 + "yxc".index(axis)
        peer = {"y": p.at(y=1 - p.y), "x": p.at(x=1 - p.x), "c": p.at(c=1 - p.c)}[axis]
        return [remote(part, part, send.at[k], recv.at[k], peer)]

    def start(self, step):
        for copy in self.copies(step):
            copy.start()

    def arrive(self, step):
        for copy in self.copies(step):
            copy.wait_recv()

    def go(self, step):
        self.arrive(step - 1)
        self.start(step)

    def finish(self):
        for step in range(self.steps):
            for copy in self.copies(step):
                if copy.is_remote:
                    copy.wait_send()


class Reduce:
    steps = 6

    def __init__(self, place, src, out, mine, one, two, three, kept, four, send, recv, turn=True):
        self.p, self.src, self.out = place, src, out
        self.mine, self.one, self.two, self.three, self.four = mine, one, two, three, four
        self.send, self.recv = send, recv
        first_x = (place.c == 0) & turn
        self.turn = turn
        self.f = jnp.where(first_x, place.x, place.y)
        self.g = jnp.where(first_x, place.y, place.x)
        self.f_peer = place.at(
            x=jnp.where(first_x, 1 - place.x, place.x), y=jnp.where(first_x, place.y, 1 - place.y)
        )
        self.g_peer = place.at(
            x=jnp.where(first_x, place.x, 1 - place.x), y=jnp.where(first_x, 1 - place.y, place.y)
        )
        self.slot = 2 * self.f + self.g
        self.kept = kept

    @staticmethod
    def early(rows, lanes):
        return [pltpu.VMEM(lead + (rows, lanes), BF) for lead in ((4, 4), (4, 4), (2, 4), (4,))]

    @staticmethod
    def late(rows, lanes, kept):
        return [pltpu.VMEM(lead + (rows, lanes), BF) for lead in ((4,),) * kept + ((3,),)]

    @staticmethod
    def sems():
        return [pltpu.SemaphoreType.DMA((11,)), pltpu.SemaphoreType.DMA((15,))]

    def copies(self, step):
        p, src, mine, send, recv = self.p, self.src, self.mine, self.send, self.recv
        if step == 0:
            out = []
            for k in range(4):
                y, x = k // 2, k % 2
                there = jnp.where((p.c == 1) & self.turn, 2 * x + y, 2 * y + x)
                here = jnp.where((p.c == 0) & self.turn, 2 * x + y, 2 * y + x)
                part = src.at[:, y, 1 - p.c, x]
                peer = p.at(c=1 - p.c)
                out.append(remote(part, self.one.at[there], send.at[k], recv.at[k], peer))
                local = src.at[:, y, p.c, x]
                out.append(pltpu.make_async_copy(local, mine.at[here], recv.at[10 + k]))
            return out
        if step == 1:
            part = mine.at[pl.ds(2 * (1 - self.f), 2)]
            return [remote(part, self.two, send.at[4], recv.at[4], self.f_peer)]
        if step == 2:
            part = mine.at[2 * self.f + 1 - self.g]
            return [remote(part, self.three, send.at[5], recv.at[5], self.g_peer)]
        if step == 3:
            out = []
            for d, peer in zip((1, 2, 3), p.z_peers()):
                part = self.kept.at[(p.z + d) % 4]
                out.append(remote(part, self.four.at[d - 1], send.at[5 + d], recv.at[5 + d], peer))
            return out
        if step == 4:
            part = self.out.at[p.part]
            return [remote(part, part, send.at[9], recv.at[9], p.at(x=1 - p.x))]
        part = self.out.at[pl.ds(2 * p.c, 2)]
        return [remote(part, part, send.at[10], recv.at[14], p.at(c=1 - p.c))]

    def start(self, step):
        for copy in self.copies(step):
            copy.start()

    def arrive(self, step):
        p, mine = self.p, self.mine
        for copy in self.copies(step):
            copy.wait_recv()

        def add(dst, a, b):
            dst[...] = (a[...].astype(F32) + b[...].astype(F32)).astype(BF)

        if step == 0:

            def body(i, carry):
                at = (i // 4, i % 4)
                add(mine.at[at], mine.at[at], self.one.at[at])
                return carry

            lax.fori_loop(0, 16, body, 0)
        if step == 1:
            for copy in self.copies(step):
                copy.wait_send()

            def body(i, carry):
                at = (2 * self.f + i // 4, i % 4)
                add(mine.at[at], mine.at[at], self.two.at[i // 4, i % 4])
                return carry

            lax.fori_loop(0, 8, body, 0)
        if step == 2:

            def body(i, carry):
                add(self.kept.at[i], mine.at[self.slot, i], self.three.at[i])
                return carry

            lax.fori_loop(0, 4, body, 0)
        if step == 3:
            total = self.kept[p.z].astype(F32)
            for d in range(3):
                total = total + self.four[d].astype(F32)
            self.out[p.part] = total.astype(BF)

    def go(self, step):
        self.arrive(step - 1)
        self.start(step)

    def sent(self, first, last):
        for step in range(first, last):
            if step == 1:
                continue
            for copy in self.copies(step):
                if copy.is_remote:
                    copy.wait_send()


class ReduceZ(Reduce):
    def copies(self, step):
        p, send, recv = self.p, self.send, self.recv
        if step == 1:
            out = []
            for d, peer in zip((1, 2, 3), p.z_peers()):
                part = self.mine.at[:, (p.z + d) % 4]
                out.append(remote(part, self.four.at[d - 1], send.at[5 + d], recv.at[5 + d], peer))
            return out
        if step == 2:
            part = self.kept.at[pl.ds(2 * (1 - self.f), 2)]
            return [remote(part, self.two, send.at[4], recv.at[4], self.f_peer)]
        if step == 3:
            part = self.pair.at[1 - self.g]
            return [remote(part, self.three, send.at[5], recv.at[5], self.g_peer)]
        return super().copies(step)

    def arrive(self, step):
        if step not in (1, 2, 3):
            super().arrive(step)
            return
        for copy in self.copies(step):
            copy.wait_recv()
        if step == 1:

            def body(i, carry):
                total = self.mine[i, self.p.z].astype(F32)
                for d in range(3):
                    total = total + self.four[d, i].astype(F32)
                self.kept[i] = total.astype(BF)
                return carry

            lax.fori_loop(0, 4, body, 0)
        if step == 2:
            for copy in self.copies(step):
                copy.wait_send()
            for k in range(2):
                at = 2 * self.f + k
                self.pair[k] = (self.kept[at].astype(F32) + self.two[k].astype(F32)).astype(BF)
        if step == 3:
            total = self.pair[self.g].astype(F32) + self.three[...].astype(F32)
            self.out[self.p.part] = total.astype(BF)

    def sent(self, first, last):
        for step in range(first, last):
            if step == 2:
                continue
            for copy in self.copies(step):
                if copy.is_remote:
                    copy.wait_send()


def stand(flat_ref, pad_ref, width):
    rows, lanes = flat_ref.shape
    pad_ref[...] = jnp.zeros_like(pad_ref)
    pad_ref[:rows, :lanes] = flat_ref[...]
    turned = jnp.transpose(pad_ref[...])[:lanes]
    return jnp.concatenate([turned, jnp.zeros((lanes, width - turned.shape[1]), F32)], axis=1)


PARTS = (('w0b', 'yx', 1, None), ('w0a', 'yx', 0, None), ('r1', 'yx', 1, 0), ('w1b', 'yx', 1, None), ('w2b', 'yx', 1, None), ('w2a', 'yx', 0, None), ('w1a', 'y', 0, None), ('r3', 'y', 1, 1), ('r0', 'y', 0, 0), ('r2', 'y', 0, 1))
BEFORE = ('w0b1', 'w0a1', 'w0b2', 'r11', 'w0a2', 'w1b1', 'r12', 'w2b1', 'w0b3', 'w1b2', 'w2a1', 'w2b2', 'w0a3', 'w2a2', 'w1a1')
FIRST = {3: ('r13',), 4: ('r31',), 6: ('w1a2',), 7: ('w1b3',)}
BETWEEN = ('r01',)
SECOND = {1: ('r32',), 3: ('w2b3', 'r21'), 5: ('r02',), 6: ('w2a3',)}
AFTER = ('r22',)


def forward_kernel(
    feat,
    side,
    conv_ref,
    code_ref,
    proj_ref,
    head_flat_ref,
    gains_ref,
    x_out,
    side_out,
    w_out0,
    w_out1,
    w_out2,
    rest_out,
    a_one_out,
    c_one_out,
    a_two_out,
    l_out,
    s_ref,
    wt_ref,
    a_one_ref,
    c_one_ref,
    a_two_ref,
    l_ref,
    k_sem,
    head_pad,
    head_ref,
    w_mine,
    rest_mine,
    xv,
    wv0,
    wv1,
    wv2,
    a3,
    y32,
    x_send,
    x_recv,
    g_send,
    g_recv,
    o_sem,
):
    place = Place()
    rank = 2 * place.x + place.c
    ch, lat = conv_ref.shape[2], code_ref.shape[1]
    n_code, n_proj, n_head = (v.shape[0] // 4 for v in (code_ref, proj_ref, head_ref))
    wt_ref[...] = jnp.zeros_like(wt_ref)

    def cast_conv(j):
        n = w_mine.shape[3]
        for k in range(4):
            v = conv_ref[j, k * n : (k + 1) * n, :]
            w_mine[j, k // 2, k % 2] = v.astype(BF)
            wt_ref[j : j + 1, :] += jnp.sum(v * v, axis=0, keepdims=True)

    def cast_rest():
        head_ref[...] = stand(head_flat_ref, head_pad, lat)
        for k in range(4):
            low = 0
            for m, (ref, n) in enumerate(
                ((code_ref, n_code), (proj_ref, n_proj), (head_ref, n_head))
            ):
                v = ref[k * n : (k + 1) * n, :]
                wt_ref[3 + m : 4 + m, :lat] += jnp.sum(v * v, axis=0, keepdims=True)
                if n % 16:
                    v = jnp.concatenate([v, jnp.zeros((-n % 16, lat), F32)], axis=0)
                rest_mine[k // 2, k % 2, low : low + v.shape[0]] = v.astype(BF)
                low += v.shape[0]

    cast_conv(0)
    place.greet()

    def view(ref, lanes):
        n = ref.shape[0] // 32
        return ref.reshape(4, 2, 2, 2, n, ref.shape[1]).at[..., lanes]

    jobs = {}
    views = [view(wv0, slice(None)), view(wv1, slice(None)), view(wv2, slice(None)), rest_out]
    for k, (name, route, lane, row) in enumerate(PARTS):
        rest = name[0] == "r"
        src = rest_mine if rest else w_mine.at[int(name[1])]
        dst = views[3] if rest else views[int(name[1])]
        n = src.shape[-2]
        parts, which = (2, lane) if row is None else (4, 2 * row + lane)
        cut = [k * n // (16 * parts) * 16 for k in range(parts)] + [n]
        at = (..., pl.ds(cut[which], cut[which + 1] - cut[which]), slice(None))
        jobs[name] = Gather(place, src.at[at], dst.at[at], g_send.at[k], g_recv.at[k], route)

    def go(words):
        for word in words:
            jobs[word[:-1]].go(int(word[-1]))

    def ticks(table):
        def tick(i):
            for when, words in table.items():

                @pl.when(i == when)
                def _():
                    go(words)

        return tick

    def whole(names):
        for name in names:
            jobs[name].arrive(jobs[name].steps - 1)

    cells = []
    for src, dst, base in ((feat, xv, 0), (side, side_out, 4)):
        for k, q in enumerate(place.row_peers()):
            to = q["rows"]
            cells.append(
                remote(src.at[to], dst.at[:, rank], x_send.at[base + k], x_recv.at[base + k], q)
            )
        cells.append(pltpu.make_async_copy(src.at[rank], dst.at[:, rank], x_recv.at[base + 3]))

    started = PARTS[0][0]
    jobs[started].start(0)
    for copy in cells:
        copy.start()
    cast = {"0"}
    for name, *_ in PARTS[1:]:
        which = name[1] if name[0] == "w" else "rest"
        if which not in cast:
            cast_rest() if which == "rest" else cast_conv(int(which))
            cast.add(which)
        jobs[name].start(0)
    go(BEFORE)
    zero_edges(a3)
    for copy in cells:
        copy.wait_recv()
    keep_x = pltpu.make_async_copy(xv, x_out, o_sem.at[0])
    keep_x.start()
    whole(("w0a", "w0b"))
    keep_w = [
        pltpu.make_async_copy(v, o, o_sem.at[1 + k])
        for k, (v, o) in enumerate(((wv0, w_out0), (wv1, w_out1), (wv2, w_out2)))
    ]
    keep_w[0].start()
    count = xv.shape[0]

    def crop_x(i):
        return xv[i].reshape(256, ch).astype(F32)

    tick_first, tick_second = ticks(FIRST), ticks(SECOND)

    def keep_first(i):
        return [
            pltpu.make_async_copy(v.at[i], o.at[i], k_sem.at[k, i])
            for k, (v, o) in enumerate(((a_one_ref, a_one_out), (c_one_ref, c_one_out)))
        ]

    def keep_second(i):
        rows = crop_rows(i)
        return [
            pltpu.make_async_copy(a_two_ref.at[i], a_two_out.at[i], k_sem.at[2, i]),
            pltpu.make_async_copy(l_ref.at[rows], l_out.at[rows], k_sem.at[3, i]),
        ]

    def first(i, carry):
        tick_first(i)
        a_one_ref[i], c_one_ref[i] = first_crop(crop_x(i), gains_ref, wv0, a3)
        for copy in keep_first(i):
            copy.start()
        return carry

    lax.fori_loop(0, count, first, 0)
    go(BETWEEN)
    whole(("w1a", "w1b"))
    keep_w[1].start()

    def second(i, carry):
        tick_second(i)
        a_two_ref[i] = second_crop(
            c_one_ref[i], crop_x(i), gains_ref, wv1, l_ref.at[crop_rows(i)], a3, y32
        )
        for copy in keep_second(i):
            copy.start()
        return carry

    lax.fori_loop(0, count, second, 0)
    whole(("w2a", "w2b"))
    keep_w[2].start()
    down_dot(l_ref, wv2, s_ref)
    go(AFTER)
    whole(("r0", "r1", "r2", "r3"))
    for job in jobs.values():
        job.finish()
    for copy in cells:
        if copy.is_remote:
            copy.wait_send()
    keep_x.wait()
    for copy in keep_w:
        copy.wait()

    def kept(i, carry):
        for copy in keep_first(i) + keep_second(i):
            copy.wait()
        return carry

    lax.fori_loop(0, count, kept, 0)


def forward_call(feat, side, conv_w, code_w, proj_w, head_w, gains):
    ranks, crops, cells, ch = feat.shape
    lat = code_w.shape[1]
    lat_cells = crops * ranks * cells // 4
    n_conv = conv_w.shape[1] // 4
    n_rest = code_w.shape[0] // 4 + proj_w.shape[0] // 4 + 16
    whole = 32 * n_conv

    def shape(*dims, dtype=BF):
        return jax.ShapeDtypeStruct(dims, dtype)

    outs = [
        shape(crops, ranks, cells, ch),
        shape(crops, ranks, *side.shape[2:], dtype=F32),
        shape(whole, ch),
        shape(whole, ch),
        shape(whole, ch),
        shape(4, 2, 2, 2, n_rest, lat),
        shape(crops, ranks * cells, ch),
        shape(crops, ranks * cells, ch, dtype=F32),
        shape(crops, ranks * cells, ch),
        shape(lat_cells, 9 * ch),
        shape(lat_cells, ch),
        shape(8, ch, dtype=F32),
    ]
    return pl.pallas_call(
        forward_kernel,
        out_shape=outs,
        in_specs=[ANY] * 2 + [VM] * 5,
        out_specs=[ANY] * 10 + [VM] * 2,
        scratch_shapes=[
            pltpu.VMEM((crops, ranks * cells, ch), BF),
            pltpu.VMEM((crops, ranks * cells, ch), F32),
            pltpu.VMEM((crops, ranks * cells, ch), BF),
            pltpu.VMEM((lat_cells, 9 * ch), BF),
            pltpu.SemaphoreType.DMA((4, crops)),
            pltpu.VMEM((128, 128), F32),
            pltpu.VMEM((head_w.shape[1], lat), F32),
            pltpu.VMEM((3, 2, 2, n_conv, ch), BF),
            pltpu.VMEM((2, 2, n_rest, lat), BF),
            pltpu.VMEM((crops, ranks, cells, ch), BF),
        ]
        + [pltpu.VMEM((whole, ch), BF)] * 3
        + [
            pltpu.VMEM((18, 16, 3 * ch), BF),
            pltpu.VMEM((ch // 128, ranks * cells, 128), F32),
            pltpu.SemaphoreType.DMA((8,)),
            pltpu.SemaphoreType.DMA((8,)),
            pltpu.SemaphoreType.DMA((len(PARTS), 8)),
            pltpu.SemaphoreType.DMA((len(PARTS), 8)),
            pltpu.SemaphoreType.DMA((4,)),
        ],
        compiler_params=pltpu.CompilerParams(
            vmem_limit_bytes=58 * MIB, collective_id=2, has_side_effects=True
        ),
        cost_estimate=pl.CostEstimate(
            flops=45 * crops * ranks * cells * ch * ch,
            bytes_accessed=0,
            transcendentals=0,
        ),
    )(feat, side, conv_w, code_w, proj_w, head_w, gains)


def quantizer_kernel(
    consts,
    codes_ref,
    rest,
    side_ref,
    sl_ref,
    l_in,
    ds_ref,
    loss_ref,
    dp_ref,
    small_ref,
    dw_out,
    tab,
    stage,
    proj_v,
    head_v,
    e_ref,
    l_ref,
    dw_ref,
    sems,
    w_sems,
):
    lat_count, pix_count, rgb, n_code = consts
    cells = sl_ref.shape[0]
    pieces = rest.shape[0]
    slots = stage.shape[0]
    lat = tab.shape[1]
    small = [
        pltpu.make_async_copy(rest.at[:, n_code : n_code + 16], proj_v, sems.at[slots]),
        pltpu.make_async_copy(rest.at[:, n_code + 16 :], head_v, sems.at[slots + 1]),
    ]
    windows = pltpu.make_async_copy(l_in, l_ref, sems.at[slots + 2])
    for copy in small:
        copy.start()

    def fetch(p):
        slot = p % slots
        return pltpu.make_async_copy(rest.at[p, :n_code], stage.at[slot], sems.at[slot])

    for p in range(slots):
        fetch(p).start()
    windows.start()

    def widen(p, carry):
        fetch(p).wait()
        tab[pl.ds(pl.multiple_of(p * n_code, n_code), n_code), :] = stage[p % slots].astype(F32)

        @pl.when(p + slots < pieces)
        def _():
            fetch(p + slots).start()

        return carry

    lax.fori_loop(0, pieces, widen, 0)
    for copy in small:
        copy.wait()
    proj = proj_v[...].reshape(-1, lat)
    head = head_v[...].astype(F32)[:, :8, :128].reshape(-1, 128).astype(BF)

    def pick(b, carry):
        for j in range(8):
            for k in range(4):
                row = codes_ref[k * cells + b * 8 + j]
                e_ref[k, pl.ds(b * 8 + j, 1), :] = tab[pl.ds(row, 1), :]
        return carry

    lax.fori_loop(0, cells // 8, pick, 0)

    latent = jnp.dot(sl_ref[...], proj, preferred_element_type=F32)
    cum = e_ref[0]
    resid = []
    square = None
    for k in range(4):
        if k:
            cum = cum + e_ref[k]
        r = latent - cum
        resid.append(r)
        part = jnp.sum(r * r, axis=0, keepdims=True)
        square = part if square is None else square + part
    zq = cum.astype(BF)
    side = side_ref[...]
    valid = lax.broadcasted_iota(jnp.int32, side.shape, 1) < rgb
    weight = jnp.where(valid, pltpu.roll(side, 128 - 16, 1), 0.0)
    diff = jnp.where(valid, jnp.dot(zq, head, preferred_element_type=F32) - side, 0.0)
    smooth = jnp.sqrt(diff * diff + 1.0)
    recon = jnp.sum(weight * (smooth - 1.0), axis=0, keepdims=True)
    loss_ref[...] = jnp.zeros_like(loss_ref)
    loss_ref[0:1, 0:lat] = square * ((1.0 + BETA) / lat_count)
    loss_ref[0:1, lat : lat + 128] = recon / pix_count
    d_pred = (weight * (diff / smooth) / pix_count).astype(BF)
    back = (((1,), (1,)), ((), ()))
    rows = (((0,), (0,)), ((), ()))
    d_head = lax.dot_general(zq, d_pred, rows, preferred_element_type=F32)
    total = resid[0] + resid[1] + resid[2] + resid[3]
    d_zq = lax.dot_general(d_pred, head, back, preferred_element_type=F32)
    d_lat = (total * (2.0 * BETA / lat_count) + d_zq).astype(BF)
    d_proj = lax.dot_general(sl_ref[...], d_lat, rows, preferred_element_type=F32)
    d_s = lax.dot_general(d_lat, proj, back, preferred_element_type=F32)
    ds_ref[...] = d_s.astype(BF)
    tail = None
    for k in (3, 2, 1, 0):
        tail = resid[k] if tail is None else tail + resid[k]
        dp_ref[k * cells : (k + 1) * cells, :] = (tail * (-2.0 / lat_count)).astype(BF)
    small_ref[:, :16] = d_proj.astype(BF).reshape(pieces, 16, lat)
    d_head = jnp.concatenate([d_head, jnp.zeros((d_head.shape[0], lat - 128), F32)], axis=1)
    d_head = d_head.reshape(pieces, 8, lat)
    d_head = jnp.concatenate([d_head, jnp.zeros((pieces, 8, lat), F32)], axis=1)
    small_ref[:, 16:] = d_head.astype(BF)
    windows.wait()

    def keep(t):
        ch = dw_ref.shape[1]
        rows = pl.ds(pl.multiple_of(t * ch, ch), ch)
        return pltpu.make_async_copy(dw_ref.at[rows], dw_out.at[rows], w_sems.at[t])

    down_weight_grad(l_ref, ds_ref, dw_ref, lambda t: keep(t).start())
    for t in range(9):
        keep(t).wait()


def quantizer_call(codes, rest, side, s_low, windows, lat_count, pix_count, rgb, n_code):
    pieces, rows, lat = rest.shape
    cells, ch = s_low.shape
    outs = [
        jax.ShapeDtypeStruct((cells, ch), BF),
        jax.ShapeDtypeStruct((8, ch), F32),
        jax.ShapeDtypeStruct((4 * cells, lat), BF),
        jax.ShapeDtypeStruct((pieces, 32, lat), BF),
        jax.ShapeDtypeStruct((9 * ch, ch), BF),
    ]
    return pl.pallas_call(
        functools.partial(quantizer_kernel, (lat_count, pix_count, rgb, n_code)),
        out_shape=outs,
        in_specs=[pl.BlockSpec(memory_space=pltpu.SMEM), ANY, VM, VM, ANY],
        out_specs=[VM] * 4 + [ANY],
        scratch_shapes=[
            pltpu.VMEM((pieces * n_code, lat), F32),
            pltpu.VMEM((4, n_code, lat), BF),
            pltpu.VMEM((pieces, 16, lat), BF),
            pltpu.VMEM((pieces, rows - n_code - 16, lat), BF),
            pltpu.VMEM((4, cells, lat), F32),
            pltpu.VMEM(windows.shape, BF),
            pltpu.VMEM((9 * ch, ch), BF),
            pltpu.SemaphoreType.DMA((7,)),
            pltpu.SemaphoreType.DMA((9,)),
        ],
        compiler_params=pltpu.CompilerParams(vmem_limit_bytes=58 * MIB),
        cost_estimate=pl.CostEstimate(flops=10**10, bytes_accessed=10**7, transcendentals=0),
    )(codes, rest, side, s_low, windows)


def second_back_kernel(
    n_code,
    ds_ref,
    gains_ref,
    codes_ref,
    dp_ref,
    w_down_in,
    w_in,
    c_in,
    a_in,
    down_src,
    small_src,
    din_ref,
    dg_ref,
    down_kept_ref,
    kept0_ref,
    kept1_ref,
    rest_kept_ref,
    w_down_ref,
    w_ref,
    c_ref,
    a_ref,
    l_sem,
    dw,
    d3,
    y32,
    dp_all,
    codes_all,
    quarter,
    quarter_in,
    small_in,
    e_send,
    e_recv,
    *bufs,
):
    place = Place()
    bufs = list(bufs)

    def take(n):
        out = bufs[:n]
        del bufs[:n]
        return out

    loads = [
        pltpu.make_async_copy(src, dst, l_sem.at[k])
        for k, (src, dst) in enumerate(
            ((w_down_in, w_down_ref), (a_in, a_ref), (w_in, w_ref), (c_in, c_ref))
        )
    ]
    for copy in loads:
        copy.start()
    half = down_src.shape[-1] // 2
    view = dw.reshape(4, 2, 2, 2, dw.shape[0] // 32, dw.shape[1])
    mine, one, four, send, recv = take(5)
    down = ReduceZ(place, down_src, None, mine, one, None, None, down_kept_ref, four, send, recv)
    early, sems = take(4), take(2)
    low = Reduce(place, view.at[..., :half], None, *early, kept0_ref, None, *sems)
    early, sems = take(4), take(2)
    high = Reduce(place, view.at[..., half:], None, *early, kept1_ref, None, *sems)

    across = place.at(x=1 - place.x)
    other = place.at(c=1 - place.c)
    two = pl.ds(2 * place.c, 2)
    entries = [(dp_ref, dp_all, 0), (codes_ref, codes_all, 1)]
    out_x = [
        remote(src, dst.at[place.part], e_send.at[k], e_recv.at[k], across) for src, dst, k in entries
    ]
    out_x += [
        pltpu.make_async_copy(src, dst.at[place.part], e_recv.at[2 + k]) for src, dst, k in entries
    ]
    out_c = [
        remote(dst.at[two], dst.at[two], e_send.at[4 + k], e_recv.at[4 + k], other)
        for _, dst, k in entries
    ]
    small = []
    for k, (x, c) in enumerate(
        ((place.x, 1 - place.c), (1 - place.x, place.c), (1 - place.x, 1 - place.c))
    ):
        small.append(
            remote(
                small_src.at[:, :, c, x],
                small_in.at[k],
                e_send.at[6 + k],
                e_recv.at[6 + k],
                place.at(x=x, c=c),
            )
        )
    small.append(
        pltpu.make_async_copy(small_src.at[:, :, place.c, place.x], small_in.at[3], e_recv.at[9])
    )
    out_y = [
        remote(
            quarter.at[1 - place.y, pl.ds(2 * k, 2)],
            quarter_in.at[pl.ds(2 * k, 2)],
            e_send.at[10 + k],
            e_recv.at[10 + k],
            place.at(y=1 - place.y),
        )
        for k in range(2)
    ]

    place.greet()
    down.start(0)
    for copy in out_x + small:
        copy.start()

    def piece(z, y):
        base = ((z * 2 + y) * 4 + place.part) * n_code
        row = lax.broadcasted_iota(jnp.int32, (n_code, dp_ref.shape[0]), 0) + base

        def add(k, total):
            hot = jnp.where(row == codes_all[k], 1.0, 0.0).astype(BF)
            return total + jnp.dot(hot, dp_all[k], preferred_element_type=F32)

        total = lax.fori_loop(0, 4, add, jnp.zeros((n_code, dp_ref.shape[1]), F32))
        quarter[y, z, :n_code] = total.astype(BF)
        total = small_in[3, z, y].astype(F32)
        for k in range(3):
            total = total + small_in[k, z, y].astype(F32)
        quarter[y, z, n_code:] = total.astype(BF)

    def codebook_grad():
        def away(z, carry):
            piece(z, 1 - place.y)

            for k in range(2):

                @pl.when(z == 2 * k + 1)
                def _():
                    out_y[k].start()

            return carry

        def here(z, carry):
            piece(z, place.y)

            @pl.when(z == 0)
            def _():
                low.go(2)

            @pl.when(z == 2)
            def _():
                high.go(2)

            return carry

        lax.fori_loop(0, 4, away, 0)
        lax.fori_loop(0, 4, here, 0)

    def tick_high(dx):
        @pl.when(dx == 2)
        def _():
            low.go(1)

    def tick_crop(i):
        @pl.when(i == 1)
        def _():
            high.go(1)
            for copy in out_x:
                copy.wait_recv()
            for copy in out_c:
                copy.start()

        @pl.when(i == 3)
        def _():
            for copy in out_c:
                copy.wait_recv()
            for copy in small:
                copy.wait_recv()
            codebook_grad()

        @pl.when(i == 7)
        def _():
            low.arrive(2)
            down.arrive(1)

    loads[0].wait()
    down_input_grad(ds_ref, w_down_ref, din_ref, y32)
    down.go(1)
    shift_all(din_ref, d3)
    loads[1].wait()
    conv_weight_grad(a_ref, d3, dw, 0)
    low.start(0)
    conv_weight_grad(a_ref, d3, dw, 1, tick_high)
    high.start(0)
    loads[2].wait()
    loads[3].wait()
    unit_back(lambda i: c_ref[i], gains_ref, w_ref, dg_ref, d3, 2, din_ref, tick_crop)
    for copy in out_y:
        copy.wait_recv()
    for z in range(4):
        total = quarter[place.y, z].astype(F32) + quarter_in[z].astype(F32)
        rest_kept_ref[z] = total.astype(BF)
    high.arrive(2)
    down.sent(0, 2)
    for job in (low, high):
        job.sent(0, 3)
    for copy in out_x[:2] + out_c + small[:3] + out_y:
        copy.wait_send()


def second_back_call(n_code, ds, w_down, w, c_one, a_two, gains, codes, dp, down_src, small_src):
    crops, cells, ch = c_one.shape
    n_conv, lat = down_src.shape[-2], dp.shape[-1]
    n_rest = n_code + small_src.shape[-2]

    def shape(*dims, dtype=BF):
        return jax.ShapeDtypeStruct(dims, dtype)

    outs = [
        shape(crops, cells, ch),
        shape(2, ch, dtype=F32),
        shape(4, n_conv, ch),
        shape(4, n_conv, ch // 2),
        shape(4, n_conv, ch // 2),
        shape(4, n_rest, lat),
    ]
    begun = Reduce.early(n_conv, ch // 2) + Reduce.sems()
    return pl.pallas_call(
        functools.partial(second_back_kernel, n_code),
        out_shape=outs,
        in_specs=[VM] * 4 + [ANY] * 6,
        out_specs=[VM] * 6,
        scratch_shapes=[
            pltpu.VMEM(w_down.shape, BF),
            pltpu.VMEM(w.shape, BF),
            pltpu.VMEM(c_one.shape, F32),
            pltpu.VMEM(a_two.shape, BF),
            pltpu.SemaphoreType.DMA((4,)),
            pltpu.VMEM(w.shape, BF),
            pltpu.VMEM((crops, 18, 16, 3 * ch), BF),
            pltpu.VMEM((ch // 128, cells, 128), F32),
            pltpu.VMEM((4,) + dp.shape, BF),
            pltpu.VMEM((4,) + codes.shape, jnp.int32),
            pltpu.VMEM((2, 4, n_rest, lat), BF),
            pltpu.VMEM((4, n_rest, lat), BF),
            pltpu.VMEM((4, 4, 2, small_src.shape[-2], lat), BF),
            pltpu.SemaphoreType.DMA((12,)),
            pltpu.SemaphoreType.DMA((12,)),
        ]
        + [pltpu.VMEM((k, 4, n_conv, ch), BF) for k in (4, 4, 3)]
        + Reduce.sems()
        + begun * 2,
        compiler_params=pltpu.CompilerParams(
            vmem_limit_bytes=61 * MIB, collective_id=3, has_side_effects=True
        ),
        cost_estimate=pl.CostEstimate(flops=4 * 10**10, bytes_accessed=0, transcendentals=0),
    )(ds, gains, codes, dp, w_down, w, c_one, a_two, down_src, small_src)


def first_back_kernel(
    sizes,
    dc_in,
    x_in,
    w_in,
    a_in,
    gains_ref,
    kept0_ref,
    kept1_ref,
    rest_kept_ref,
    down_kept_ref,
    dg_two_ref,
    loss_ref,
    wt_ref,
    conv_row_ref,
    rest_row_ref,
    g_first0,
    g_first1,
    g_second0,
    g_second1,
    g_down,
    g_rest0,
    g_rest1,
    conv_new_ref,
    rest_new_ref,
    tv_ref,
    dc_ref,
    x_ref,
    w_ref,
    a_ref,
    l_sem,
    dw,
    d3,
    dg,
    vec,
    vec_in,
    tv_in,
    s_send,
    s_recv,
    *bufs,
):
    n_code, n_proj, n_head, rgb = sizes
    place = Place()
    bufs = list(bufs)

    def take(n):
        out = bufs[:n]
        del bufs[:n]
        return out

    loads = [
        pltpu.make_async_copy(src, dst, l_sem.at[k])
        for k, (src, dst) in enumerate(
            ((dc_in, dc_ref), (a_in, a_ref), (w_in, w_ref), (x_in, x_ref))
        )
    ]
    for copy in loads:
        copy.start()
    half = rest_kept_ref.shape[-1] // 2
    ch = tv_ref.shape[1]
    view = dw.reshape(4, 2, 2, 2, dw.shape[0] // 32, ch)
    none = [None] * 4
    second0 = Reduce(place, None, g_second0, *none, kept0_ref, *take(3))
    second1 = Reduce(place, None, g_second1, *none, kept1_ref, *take(3))
    rest0 = Reduce(place, None, g_rest0, *none, rest_kept_ref.at[..., :half], *take(3))
    rest1 = Reduce(place, None, g_rest1, *none, rest_kept_ref.at[..., half:], *take(3))
    low = Reduce(place, view.at[..., : ch // 2], g_first0, *take(8))
    high = Reduce(place, view.at[..., ch // 2 :], g_first1, *take(8))
    late = (second0, second1, rest0, rest1)
    two, three, pair, send, recv = take(5)
    down = ReduceZ(place, None, g_down, None, None, two, three, down_kept_ref, None, send, recv)
    down.pair = pair
    place.greet()
    for job in late:
        job.start(3)
    down.start(2)

    def tick_low(dx):
        @pl.when(dx == 2)
        def _():
            down.go(4)

    def tick_high(dx):
        @pl.when(dx == 1)
        def _():
            low.go(1)

        @pl.when(dx == 2)
        def _():
            second0.go(4)
            down.go(5)

    def tick_crop(i):
        @pl.when(i == 0)
        def _():
            second1.go(4)

        @pl.when(i == 1)
        def _():
            high.go(1)
            second0.go(5)

        @pl.when(i == 2)
        def _():
            low.go(2)

        @pl.when(i == 3)
        def _():
            second1.go(5)

        @pl.when(i == 5)
        def _():
            low.go(3)
            high.go(2)

        @pl.when(i == 6)
        def _():
            rest0.go(4)

        @pl.when(i == 7)
        def _():
            high.go(3)

    def v_of(i):
        return x_ref[i].astype(F32)

    loads[0].wait()
    shift_all(dc_ref, d3)
    loads[1].wait()
    down.go(3)
    conv_weight_grad(a_ref, d3, dw, 0, tick_low)
    low.start(0)
    conv_weight_grad(a_ref, d3, dw, 1, tick_high)
    high.start(0)
    loads[2].wait()
    loads[3].wait()
    unit_back(v_of, gains_ref, w_ref, dg, d3, 0, None, tick_crop)
    vec[...] = jnp.zeros_like(vec)
    vec[0:2] = dg[...]
    vec[2:4] = dg_two_ref[...]
    vec[4:5] = loss_ref[0:1]
    small = [
        remote(vec, vec_in.at[k], s_send.at[k], s_recv.at[k], q)
        for k, q in enumerate(place.row_peers())
    ]
    for copy in small:
        copy.start()
    tv_ref[...] = jnp.zeros_like(tv_ref)
    for copy in small:
        copy.wait_recv()
    tv_ref[16:24, :] = vec[...] + vec_in[0] + vec_in[1] + vec_in[2]
    tv_ref[24:32, :] = wt_ref[...]

    def fold(parts, row, width):
        squares = [g.astype(F32) for g in parts]
        squares = [g * g for g in squares]
        total = sum(jnp.sum(q, axis=1, keepdims=True) for q in squares)
        new = 0.5 * row + 0.5 * (total / width + EPS_SQ)
        inverse = 1.0 / new
        col = [jnp.sum(q, axis=0, keepdims=True) for q in squares]
        over = [jnp.sum(q * inverse, axis=0, keepdims=True) for q in squares]
        return (
            new,
            jnp.concatenate(col, axis=1),
            jnp.concatenate(over, axis=1),
            jnp.sum(new, axis=0, keepdims=True),
        )

    def fold_conv(j, refs):
        for k in range(4):
            new, col, over, total = fold([r[k] for r in refs], conv_row_ref[j, k], ch)
            conv_new_ref[j, k] = new
            tv_ref[j : j + 1, :] += col
            tv_ref[3 + j : 4 + j, :] += over
            tv_ref[6 + j : 7 + j, :] += total

    def fold_rest():
        lat = 2 * half
        spans = ((0, n_code, lat), (n_code, n_proj, lat), (n_code + n_proj, n_head, rgb))
        for k in range(4):
            both = [r[k] for r in (g_rest0, g_rest1)]
            for m, (start, size, width) in enumerate(spans):
                parts = [v.astype(F32)[start : start + size] for v in both]
                row = rest_row_ref[k, start : start + size]
                new, col, over, total = fold(parts, row, width)
                rest_new_ref[k, start : start + size] = new
                tv_ref[9 + m : 10 + m, :lat] += col
                tv_ref[9 + m : 10 + m, lat:] += over
                tv_ref[12 + m : 13 + m, :] += total
            size = rest_row_ref.shape[1] - n_code - n_proj - n_head
            rest_new_ref[k, rest_row_ref.shape[1] - size :] = jnp.ones((size, 1), F32)

    rest0.go(5)
    down.arrive(5)
    fold_conv(2, [g_down])
    second0.arrive(5)
    second1.arrive(5)
    fold_conv(1, [g_second0, g_second1])
    rest1.go(4)
    rest0.arrive(5)
    rest1.go(5)
    low.go(4)
    rest1.arrive(5)
    fold_rest()
    low.go(5)
    high.go(4)
    low.arrive(5)
    high.go(5)
    high.arrive(5)
    fold_conv(0, [g_first0, g_first1])

    across = remote(tv_ref, tv_in.at[0], s_send.at[3], s_recv.at[3], place.at(y=1 - place.y))
    across.start()
    across.wait()
    tv_ref[...] += tv_in[0]
    along = [
        remote(tv_ref, tv_in.at[k], s_send.at[3 + k], s_recv.at[3 + k], q)
        for k, q in zip((1, 2, 3), place.z_peers())
    ]
    for copy in along:
        copy.start()
    for copy in along:
        copy.wait()
    tv_ref[...] += tv_in[1] + tv_in[2] + tv_in[3]
    for copy in small:
        copy.wait_send()
    down.sent(2, 6)
    for job in late:
        job.sent(3, 6)
    for job in (low, high):
        job.sent(0, 6)


def first_back_call(sizes, dc, x, gains, w, a_one, kept, down_kept, dg_two, loss, wt, rows):
    crops, cells, ch = x.shape
    n_conv, n_rest = down_kept.shape[-2], kept[2].shape[-2]

    def shape(*dims, dtype=BF):
        return jax.ShapeDtypeStruct(dims, dtype)

    conv_half = shape(4, n_conv, ch // 2)
    rest_half = shape(4, n_rest, 128)
    outs = [conv_half] * 4 + [shape(4, n_conv, ch)] + [rest_half] * 2
    outs += [shape(*v.shape, dtype=F32) for v in rows] + [shape(32, ch, dtype=F32)]
    args = [dc, x, w, a_one, gains, *kept, down_kept, dg_two, loss, wt, *rows]
    whole = Reduce.early(n_conv, ch // 2) + Reduce.late(n_conv, ch // 2, 1) + Reduce.sems()
    return pl.pallas_call(
        functools.partial(first_back_kernel, sizes),
        out_shape=outs,
        in_specs=[ANY] * 4 + [VM] * (len(args) - 4),
        out_specs=[VM] * len(outs),
        scratch_shapes=[
            pltpu.VMEM(dc.shape, BF),
            pltpu.VMEM(x.shape, BF),
            pltpu.VMEM(w.shape, BF),
            pltpu.VMEM(a_one.shape, BF),
            pltpu.SemaphoreType.DMA((4,)),
            pltpu.VMEM(w.shape, BF),
            pltpu.VMEM((crops, 18, 16, 3 * ch), BF),
            pltpu.VMEM((2, ch), F32),
            pltpu.VMEM((8, ch), F32),
            pltpu.VMEM((3, 8, ch), F32),
            pltpu.VMEM((4, 32, ch), F32),
            pltpu.SemaphoreType.DMA((7,)),
            pltpu.SemaphoreType.DMA((7,)),
        ]
        + (Reduce.late(n_conv, ch // 2, 0) + Reduce.sems()) * 2
        + (Reduce.late(n_rest, 128, 0) + Reduce.sems()) * 2
        + whole * 2
        + [
            pltpu.VMEM((2, n_conv, ch), BF),
            pltpu.VMEM((n_conv, ch), BF),
            pltpu.VMEM((2, n_conv, ch), BF),
        ]
        + Reduce.sems(),
        compiler_params=pltpu.CompilerParams(
            vmem_limit_bytes=60 * MIB, collective_id=4, has_side_effects=True
        ),
        cost_estimate=pl.CostEstimate(flops=2 * 10**10, bytes_accessed=0, transcendentals=0),
    )(*args)


def finish_kernel(
    sizes,
    g_first0,
    g_first1,
    g_second0,
    g_second1,
    g_down,
    g_rest0,
    g_rest1,
    conv_in,
    code_in,
    proj_ref,
    head_flat_ref,
    conv_row_ref,
    rest_row_ref,
    tv_ref,
    conv_col_ref,
    code_col_ref,
    proj_col_ref,
    head_col_ref,
    gains_ref,
    state_ref,
    loss_ref,
    conv_outs,
    rest_outs,
    gain_outs,
    conv_ref,
    code_ref,
    head_ref,
    head_pad,
    cg,
    cn,
    cl,
    kg,
    kn,
    kl,
    l_sem,
    s_sem,
):
    n_code, n_proj, n_head, rgb, shards = sizes
    loads = [pltpu.make_async_copy(conv_in.at[j], conv_ref.at[j], l_sem.at[j]) for j in range(3)]
    loads.append(pltpu.make_async_copy(code_in, code_ref, l_sem.at[3]))
    for copy in loads:
        copy.start()
    stores = []

    def store(src, dst):
        stores.append(pltpu.make_async_copy(src, dst, s_sem.at[len(stores)]))
        stores[-1].start()

    ch = conv_ref.shape[2]
    lat = code_ref.shape[1]

    def scales(col, col_sum, over, row_sum, weights, rows, width):
        rows = rows * shards
        col_new = 0.5 * col + 0.5 * (col_sum / rows + EPS_SQ)
        row_mean = row_sum / rows
        upd_sq = row_mean * jnp.sum(over / col_new, axis=1, keepdims=True)
        rms_u = jnp.sqrt(upd_sq / (rows * width))
        scale = jnp.sqrt(jnp.sum(weights, axis=1, keepdims=True) / (rows * width))
        factor = RATE * scale / jnp.maximum(1.0, rms_u)
        return col_new, factor * lax.rsqrt(col_new), row_mean

    def line(k):
        return tv_ref[k : k + 1, :]

    cg_out, cc, cn_out, cl_out = conv_outs
    for j, parts in enumerate(((g_first0, g_first1), (g_second0, g_second1), (g_down,))):
        n = conv_ref.shape[1]
        col_new, q, row_mean = scales(
            conv_col_ref[j : j + 1, :], line(j), line(3 + j), line(6 + j)[:, :1], line(24 + j), n, ch
        )
        cc[j : j + 1, :] = col_new
        m = n // 4
        loads[j].wait()
        for k in range(4):
            r = lax.rsqrt(conv_row_ref[j, k] / row_mean)
            rows = slice(k * m, (k + 1) * m)
            for p, part in enumerate(parts):
                width = part.shape[2]
                lanes = slice(p * width, (p + 1) * width)
                g = part[k].astype(F32)
                new = conv_ref[j, rows, lanes] - g * r * q[:, lanes]
                cg[j, rows, lanes] = g
                cn[j, rows, lanes] = new
                cl[j, rows, lanes] = new.astype(BF)
        for src, dst in ((cg, cg_out), (cn, cn_out), (cl, cl_out)):
            store(src.at[j], dst.at[j])
    loads[3].wait()
    head_ref[...] = stand(head_flat_ref, head_pad, lat)
    cols = (code_col_ref, proj_col_ref, head_col_ref)
    spans = ((0, n_code, lat), (n_code, n_proj, lat), (n_code + n_proj, n_head, rgb))
    for m, (w_ref, (start, size, width)) in enumerate(zip((code_ref, proj_ref, head_ref), spans)):
        og, oc, on, ol = rest_outs[m]
        if m == 0:
            code_outs, (og, on, ol) = (og, on, ol), (kg, kn, kl)
        col_new, q, row_mean = scales(
            cols[m][...],
            line(9 + m)[:, :lat],
            line(9 + m)[:, lat:],
            line(12 + m)[:, :1],
            line(27 + m)[:, :lat],
            w_ref.shape[0],
            width,
        )
        oc[...] = col_new
        both = []
        for k in range(4):
            g = jnp.concatenate([g_rest0[k].astype(F32), g_rest1[k].astype(F32)], axis=1)
            g = g[start : start + size]
            r = lax.rsqrt(rest_row_ref[k, start : start + size] / row_mean)
            rows = slice(k * size, (k + 1) * size)
            new = w_ref[rows, :] - g * r * q
            if m == 2:
                both.append((g, new))
            else:
                og[rows, :] = g
                on[rows, :] = new
                ol[rows, :] = new.astype(BF)
        if m == 0:
            for src, dst in zip((og, on, ol), code_outs):
                store(src, dst)
        if m == 2:
            for ref, values in zip((og, on), zip(*both)):
                tall = jnp.concatenate(values, axis=0)[:, :128]
                tall = jnp.concatenate([tall, jnp.zeros((128 - tall.shape[0], 128), F32)], axis=0)
                head_pad[...] = jnp.transpose(tall)
                ref[...] = head_pad[: ref.shape[0], : ref.shape[1]]
            ol[...] = on[...].astype(BF)
    loss_ref[...] = jnp.sum(line(20), axis=1, keepdims=True)
    grad = tv_ref[16:20, :]
    state = 0.5 * state_ref[...] + 0.5 * (grad * grad + EPS_SQ)
    update = grad * lax.rsqrt(state)
    gains = gains_ref[...]

    def rms(v):
        return jnp.sqrt(
            jnp.sum(jnp.sum(v * v, axis=1, keepdims=True), axis=0, keepdims=True) / v.size
        )

    gain_outs[0][...] = grad
    gain_outs[1][...] = state
    gain_outs[2][...] = gains - RATE * rms(gains) * update / jnp.maximum(1.0, rms(update))
    for copy in stores:
        copy.wait()


def finish_call(sizes, grads, weights, rows, tv, cols, gains, state):
    conv_w, code_w, proj_w, head_w = weights
    lat = code_w.shape[1]

    def shape(dims, dtype=F32):
        return jax.ShapeDtypeStruct(dims, dtype)

    def matrix(w, col):
        return [shape(w.shape), shape(col), shape(w.shape), shape(w.shape, BF)]

    outs = [shape((1, 1)), matrix(conv_w, (3, conv_w.shape[2]))]
    outs += [[matrix(w, (1, lat)) for w in (code_w, proj_w, head_w)]]
    outs += [[shape(gains.shape)] * 3]
    args = [*grads, *weights, *rows, tv, *cols, gains, state]
    specs = jax.tree.map(lambda _: VM, outs)
    streamed = [ANY, VM, ANY, ANY]
    specs[1] = streamed
    specs[2] = [streamed] + specs[2][1:]
    in_specs = [VM] * len(args)
    in_specs[len(grads)] = in_specs[len(grads) + 1] = ANY
    return pl.pallas_call(
        functools.partial(finish_kernel, sizes),
        out_shape=outs,
        in_specs=in_specs,
        out_specs=specs,
        scratch_shapes=[
            pltpu.VMEM(conv_w.shape, F32),
            pltpu.VMEM(code_w.shape, F32),
            pltpu.VMEM((head_w.shape[1], lat), F32),
            pltpu.VMEM((128, 128), F32),
        ]
        + [pltpu.VMEM(w.shape, t) for w in (conv_w, code_w) for t in (F32, F32, BF)]
        + [pltpu.SemaphoreType.DMA((4,)), pltpu.SemaphoreType.DMA((12,))],
        compiler_params=pltpu.CompilerParams(vmem_limit_bytes=56 * MIB),
        cost_estimate=pl.CostEstimate(flops=10**7, bytes_accessed=2 * 10**7, transcendentals=0),
    )(*args)


def contract_last(left, right):
    return lax.dot_general(left, right, (((1,), (0,)), ((), ())), preferred_element_type=F32)


def contract_back(left, right):
    return lax.dot_general(left, right, (((1,), (1,)), ((), ())), preferred_element_type=F32)


def contract_rows(left, right):
    return lax.dot_general(left, right, (((0,), (0,)), ((), ())), preferred_element_type=F32)


def row_part(grad, row):
    g_sq = grad * grad + EPS_SQ
    row_new = 0.5 * row + 0.5 * jnp.mean(g_sq, axis=2)
    over_row = jnp.sum(grad * grad / row_new[:, :, None], axis=0)
    return row_new, jnp.sum(g_sq, axis=0), jnp.sum(row_new, axis=0), over_row


def finish(grad, weight, row_new, col, col_sum, row_sum, over_row, wt_sq):
    total = grad.shape[0] * lax.axis_size("batch")
    count = total * grad.shape[2]
    col_new = 0.5 * col + 0.5 * col_sum / total
    row_mean = row_sum / total
    upd_sq = row_mean * jnp.sum(over_row / col_new, axis=1)
    rms_u = jnp.sqrt(upd_sq / count)
    scale = jnp.sqrt(wt_sq / count)
    vhat = row_new[:, :, None] * col_new[None] / row_mean[None, :, None]
    update = grad * lax.rsqrt(vhat)
    new = weight - RATE * (scale / jnp.maximum(1.0, rms_u))[None, :, None] * update
    return col_new, new


def local_any(
    features,
    target,
    mask,
    codes,
    conv_w,
    proj_w,
    code_w,
    head_w,
    gains,
    conv_row,
    conv_col,
    proj_row,
    proj_col,
    code_row,
    code_col,
    head_row,
    head_col,
    gain_state,
):
    ranks = lax.axis_size("rows")
    shards = lax.axis_size("batch")
    me = lax.axis_index("rows")
    crops_all = features.shape[0] * shards
    ch = features.shape[3]
    lat = proj_w.shape[1]
    rgb = head_w.shape[1]
    height = features.shape[1] * ranks
    width = features.shape[2]

    def whole_crops(v):
        return lax.all_to_all(v, "rows", split_axis=0, concat_axis=1, tiled=True)

    def my_part(v):
        size = v.shape[0] // ranks
        return lax.dynamic_slice_in_dim(v, me * size, size, 0)

    conv_piece = jnp.transpose(my_part(conv_w).astype(BF), (1, 0, 2))
    head_wide = jnp.pad(head_w, ((0, 0), (0, lat - rgb)))
    rest_piece = jnp.concatenate(
        [my_part(code_w).astype(BF), my_part(proj_w).astype(BF), my_part(head_wide).astype(BF)]
    )
    n_code, n_proj, n_head = (v.shape[0] // ranks for v in (code_w, proj_w, head_w))
    w_all = [lax.all_gather(conv_piece[0], BOTH, axis=0, tiled=True)]
    later = lax.all_gather(conv_piece[1:], BOTH, axis=0)
    later = jnp.transpose(later, (1, 0, 2, 3)).reshape(2, -1, ch)
    w_all += [later[0], later[1]]
    rest = lax.all_gather(rest_piece, BOTH, axis=0)
    code_all = rest[:, :n_code].reshape(-1, lat)
    proj_all = rest[:, n_code : n_code + n_proj].reshape(-1, lat)
    head_all = rest[:, n_code + n_proj :, :rgb].reshape(-1, rgb)

    x = whole_crops(features)
    target, mask, codes = whole_crops(target), whole_crops(mask), whole_crops(codes)
    crops = x.shape[0]
    cells = height * width
    x = x.reshape(crops, cells, ch)
    lat_cells = crops * cells // 4
    target = target.reshape(lat_cells, rgb)
    mask = mask.reshape(lat_cells, -1)
    codes = codes.reshape(lat_cells, -1)

    conv_flops = 2 * crops * cells * 9 * ch * ch
    three = pltpu.VMEM((18, 16, 3 * ch), BF)
    fold = pltpu.VMEM((ch // 128, cells, 128), F32)

    def big(dtype):
        return jax.ShapeDtypeStruct((crops, cells, ch), dtype)

    dw_shape = jax.ShapeDtypeStruct((9 * ch, ch), BF)
    dg_shape = jax.ShapeDtypeStruct((2, ch), F32)

    a_one, c_one = kernel_call(
        first_conv_kernel, [big(BF), big(F32)], [three], conv_flops, x, gains, w_all[0]
    )
    a_two, windows, s_low = kernel_call(
        second_conv_kernel,
        [
            big(BF),
            jax.ShapeDtypeStruct((lat_cells, 9 * ch), BF),
            jax.ShapeDtypeStruct((lat_cells, ch), BF),
        ],
        [three, fold],
        conv_flops,
        c_one,
        x,
        gains,
        w_all[1],
        w_all[2],
    )

    lat_count = crops_all * cells // 4 * lat
    pix_count = crops_all * cells * 3
    latent = contract_last(s_low, proj_all)
    picked = code_all[codes].astype(F32)
    cum = jnp.cumsum(picked, axis=1)
    resid = latent[:, None, :] - cum
    quant_part = (1.0 + BETA) * jnp.sum(resid * resid) / lat_count
    zq_low = cum[:, -1].astype(BF)
    pred = contract_last(zq_low, head_all)
    diff = pred - target
    weight_mask = jnp.repeat(mask.astype(F32), 3, axis=-1)
    smooth = jnp.sqrt(diff * diff + 1.0)
    recon_part = jnp.sum(weight_mask * (smooth - 1.0)) / pix_count
    d_pred = (weight_mask * (diff / smooth) / pix_count).astype(BF)
    d_head = contract_rows(zq_low, d_pred)
    d_zq = contract_back(d_pred, head_all)
    d_cum = -2.0 / lat_count * resid
    d_picked = jnp.flip(jnp.cumsum(jnp.flip(d_cum, 1), axis=1), 1)
    d_code = jax.ops.segment_sum(
        d_picked.reshape(-1, lat), codes.reshape(-1), num_segments=code_all.shape[0]
    )
    d_lat_low = (jnp.sum(resid, axis=1) * (2.0 * BETA / lat_count) + d_zq).astype(BF)
    d_proj = contract_rows(s_low, d_lat_low)
    d_s_low = contract_back(d_lat_low, proj_all).astype(BF)

    d_c_two, d_down = kernel_call(
        down_back_kernel,
        [big(BF), dw_shape],
        [fold],
        conv_flops // 2,
        d_s_low,
        windows,
        w_all[2],
    )
    d_three = pltpu.VMEM((crops, 18, 16, 3 * ch), BF)
    d_c_one, d_second, gain_two = kernel_call(
        functools.partial(unit_back_kernel, row=2, inner=True),
        [big(BF), dw_shape, dg_shape],
        [d_three],
        2 * conv_flops,
        d_c_two,
        c_one,
        gains,
        w_all[1],
        a_two,
    )
    d_first, gain_one = kernel_call(
        functools.partial(unit_back_kernel, row=0, inner=False),
        [dw_shape, dg_shape],
        [d_three],
        2 * conv_flops,
        d_c_one,
        x,
        gains,
        w_all[0],
        a_one,
    )
    d_gains = jnp.concatenate([gain_one, gain_two], axis=0)

    devices = ranks * shards

    def to_owner(v):
        return lax.psum_scatter(v, BOTH, scatter_dimension=0, tiled=True)

    def to_rows(v):
        return lax.all_gather(v, "rows", axis=0)

    pad = jnp.pad(d_head, ((0, 0), (0, lat - rgb)))
    rest_grad = jnp.concatenate(
        [v.astype(BF).reshape(devices, -1, lat) for v in (d_code, d_proj, pad)], axis=1
    )
    rest_mine = to_owner(rest_grad.reshape(-1, lat))
    conv_mine = [to_owner(v) for v in (d_first, d_second, d_down)]
    rest_full = to_rows(rest_mine).astype(F32)
    conv_full = to_rows(jnp.stack(conv_mine)).astype(F32)
    g_conv = jnp.transpose(conv_full, (0, 2, 1, 3)).reshape(-1, 3, ch)
    g_code = rest_full[:, :n_code].reshape(-1, lat)
    g_proj = rest_full[:, n_code : n_code + n_proj].reshape(-1, lat)
    g_head = rest_full[:, n_code + n_proj :, :rgb].reshape(-1, rgb)

    mats = [
        (g_conv, conv_w, conv_row, conv_col),
        (g_proj[:, None, :], proj_w[:, None, :], proj_row[:, None], proj_col[None, :]),
        (g_code[:, None, :], code_w[:, None, :], code_row[:, None], code_col[None, :]),
        (g_head[:, None, :], head_w[:, None, :], head_row[:, None], head_col[None, :]),
    ]
    rows_new = [row_part(grad, row) for grad, weight, row, col in mats]
    wt_sq = [jnp.sum(weight * weight, axis=(0, 2)) for grad, weight, row, col in mats]
    sums = lax.psum([r[1:] + (w,) for r, w in zip(rows_new, wt_sq)], "batch")
    loss, g_gain = lax.psum((recon_part + quant_part, d_gains), BOTH)
    done = [
        finish(m[0], m[1], r[0], m[3], *s) for m, r, s in zip(mats, rows_new, sums)
    ]

    state_new = 0.5 * gain_state + 0.5 * (g_gain * g_gain + EPS_SQ)
    update = g_gain * lax.rsqrt(state_new)
    rms_u = jnp.sqrt(jnp.mean(update * update))
    scale = jnp.sqrt(jnp.mean(gains * gains))
    gains_new = gains - RATE * scale * update / jnp.maximum(1.0, rms_u)
    conv_new = done[0][1]
    proj_new, code_new, head_new = (d[1][:, 0, :] for d in done[1:])
    return (
        loss,
        g_conv,
        rows_new[0][0],
        done[0][0],
        conv_new,
        conv_new.astype(BF),
        g_proj,
        rows_new[1][0][:, 0],
        done[1][0][0],
        proj_new,
        proj_new.astype(BF),
        g_code,
        rows_new[2][0][:, 0],
        done[2][0][0],
        code_new,
        code_new.astype(BF),
        g_head,
        rows_new[3][0][:, 0],
        done[3][0][0],
        head_new,
        head_new.astype(BF),
        g_gain,
        state_new,
        gains_new,
    )


def local_fast(
    features,
    target,
    mask,
    codes,
    conv_w,
    proj_w,
    code_w,
    head_w,
    gains,
    conv_row,
    conv_col,
    proj_row,
    proj_col,
    code_row,
    code_col,
    head_row,
    head_col,
    gain_state,
):
    ranks = lax.axis_size("rows")
    shards = lax.axis_size("batch")
    crops_all = features.shape[0] * shards
    crops = features.shape[0] // ranks
    ch = features.shape[3]
    cells = features.shape[1] * ranks * features.shape[2]
    lat, rgb = proj_w.shape[1], head_w.shape[1]
    lat_cells = crops * cells // 4
    n_code, n_proj, n_head = (v.shape[0] // ranks for v in (code_w, proj_w, head_w))
    sizes = (n_code, n_proj, n_head, rgb)
    conv_rows = jnp.transpose(conv_w, (1, 0, 2))
    head_flat = jnp.transpose(head_w)

    def lanes(v, n):
        return jnp.pad(v, ((0, 0),) * (v.ndim - 1) + ((0, n - v.shape[-1]),))

    side = [lanes(target, 16), lanes(jnp.repeat(mask.astype(F32), 3, axis=-1), 16)]
    side = lanes(jnp.concatenate(side + [codes.astype(F32)], axis=-1), 128)
    out = forward_call(
        features.reshape(ranks, crops, -1, ch),
        side.reshape(ranks, crops, -1, 128),
        conv_rows,
        code_w,
        proj_w,
        head_flat,
        gains,
    )
    x = out[0].reshape(crops, cells, ch)
    side = out[1].reshape(lat_cells, 128)
    w_all, rest = out[2:5], out[5]
    a_one, c_one, a_two, windows, s_low, wt = out[6:]
    codes = jnp.transpose(side[:, 32:36]).astype(jnp.int32).reshape(-1)
    n_rest = rest.shape[-2]
    d_s, loss, dp, d_small, d_down = quantizer_call(
        codes,
        rest.reshape(-1, n_rest, lat),
        side,
        s_low,
        windows,
        crops_all * cells // 4 * lat,
        crops_all * cells * 3,
        rgb,
        n_code,
    )

    def shards_of(v):
        return v.reshape(4, 2, 2, 2, -1, v.shape[-1])

    d_c_one, dg_two, down_kept, *kept = second_back_call(
        n_code,
        d_s,
        w_all[2],
        w_all[1],
        c_one,
        a_two,
        gains,
        codes[None],
        dp,
        shards_of(d_down),
        d_small.reshape(4, 2, 2, 2, -1, lat),
    )
    conv_row4 = jnp.transpose(conv_row).reshape(3, 4, -1, 1)
    rest_row4 = [v.reshape(4, -1) for v in (code_row, proj_row, head_row)]
    rest_row4.append(jnp.ones((4, n_rest - n_code - n_proj - n_head), F32))
    rest_row4 = jnp.concatenate(rest_row4, axis=1)[:, :, None]
    out = first_back_call(
        sizes,
        d_c_one,
        x,
        gains,
        w_all[0],
        a_one,
        kept,
        down_kept,
        dg_two,
        loss,
        wt,
        (conv_row4, rest_row4),
    )
    conv_rn, rest_rn, tv = out[7:]
    head_col_wide = jnp.pad(head_col, (0, lat - rgb), constant_values=1.0)
    loss, conv_outs, rest_outs, gain_outs = finish_call(
        sizes + (shards,),
        out[:7],
        (conv_rows, code_w, proj_w, head_flat),
        (conv_rn, rest_rn),
        tv,
        (conv_col, code_col[None], proj_col[None], head_col_wide[None]),
        gains,
        gain_state,
    )
    conv_g, conv_c, conv_n, conv_l = conv_outs
    code_o, proj_o, head_o = rest_outs
    cuts = (n_code, n_code + n_proj, n_code + n_proj + n_head)
    code_r, proj_r, head_r = (
        v.reshape(-1) for v in jnp.split(rest_rn[:, :, 0], cuts, axis=1)[:3]
    )

    def back(v):
        return jnp.transpose(v, (1, 0, 2))

    return (
        loss[0, 0],
        back(conv_g),
        jnp.transpose(conv_rn.reshape(3, -1)),
        conv_c,
        back(conv_n),
        back(conv_l),
        proj_o[0],
        proj_r,
        proj_o[1][0],
        proj_o[2],
        proj_o[3],
        code_o[0],
        code_r,
        code_o[1][0],
        code_o[2],
        code_o[3],
        jnp.transpose(head_o[0]),
        head_r,
        head_o[1][0, :rgb],
        jnp.transpose(head_o[2]),
        jnp.transpose(head_o[3]),
        *gain_outs,
    )


def solution(mesh):
    cell = P("batch", "rows", None, None)
    mat, vec = P("batch", None), P("batch")
    placed = (cell,) * 4 + (P("batch", None, None), mat, mat, mat, P())
    placed += (mat, P()) + (vec, P()) * 3 + (P(),)
    conv_outs = (P("batch", None, None), mat, P(), P("batch", None, None), P("batch", None, None))
    mat_outs = (mat, vec, P(), mat, mat)
    fast = (mesh.shape["rows"], mesh.shape["batch"]) == (4, 8)
    return jax.shard_map(
        local_fast if fast else local_any,
        mesh=mesh,
        in_specs=placed,
        out_specs=(P(),) + conv_outs + mat_outs * 3 + (P(),) * 3,
        check_vma=False,
    )
```
